32 devices in a mesh: src: 8 (over z, y), tgt: 4 (over x, core).
Axes of the slice: x: 2, y: 2, z: 4, core: 2. Of those that a mesh axis runs over, the one named last changes fastest.
Arguments:
- particle_position: float32 [3, 12288], P(None, ('src', 'tgt')), may hold values from 0 to 1, as said below
- particle_strength: float32 [3, 12288], P(None, ('src', 'tgt')), may hold values from -6 to 6
- core_radius: float32 [1, 12288], P(None, ('src', 'tgt')), may hold values from 0.05 to 0.12
- boundary_points: float32 [3, 8, 256], P(None, None, 'tgt'), may hold values from 0 to 1, as said below
- vorticity: float32 [8, 3, 256, 128], P('src', None, 'tgt'), may hold values from -6 to 6
- swirl: float32 [8, 256, 128], P('src', 'tgt'), may hold values from -0.5 to 0.5
- diffusivity: float32 [8, 256, 128], P('src', 'tgt'), may hold values from 0.05 to 0.2
- intersection_source: int32 [8, 4, 9], P('src', 'tgt'), may hold values from 0 to 191
- intersection_target: int32 [8, 4, 9], P('src', 'tgt'), may hold values from -1 to 35, as said below
Outputs:
- wall_velocity: float32 [3, 8, 256], P(None, 'src', 'tgt')
- grid_vorticity: float32 [8, 3, 256, 128], P('src', None, 'tgt')
- new_strength: float32 [3, 12288], P(None, ('src', 'tgt'))
The draws below stay inside these ranges and needn't reach their ends.
Inputs may be any that keep to these rules, and one draw needn't show every extreme that they name: `particle_position`: every coordinate of every particle lies in [0, 1). `boundary_points`: point (z, a) has its first two coordinates in [0, 1) and its third in [z / 8, (z + 1) / 8). `intersection_target`: an entry of list (s, t) is -1 or owner * 9 + block, naming particle block block of device (s, owner). Live entries stand before the -1 entries. Over all lists of one src index each particle block of each device is named at most once. No list names one owner in more than 4 live entries, and some list names some owner in exactly 4; some list has 9 live entries.
All inputs are finite; a program needn't handle non-finite values.
Results may differ from the reference program's by a relative error of at most 0.0003.
Values sent between devices are 32-bit elements; how exact they have to be, the bound alone decides.
No kernel may reach another device: no remote copies, remote signals or barrier semaphores. Data moves between devices by JAX's collectives and lax.ppermute only.
A program may use at most 64 MiB of HBM per device.

```python
import math
import jax
import jax.numpy as jnp
from jax import lax

P_DEV = 384
ZD = 1
AD = 64
NR = 128
SUBSTEPS = 3
NPART = 12288
NZ = 8
NA = 256
DENSITY = 12288
PB = 9
GB = 192
N_SRC = 8
N_TGT = 4


def vertical_coordinate(key):
    return jax.random.uniform(jax.random.fold_in(key, 12), (1, NPART), jnp.float32)


def draw_particle_position(key, part):
    first = jax.random.fold_in(key, 11)
    across = jax.random.uniform(first, (2, NPART), jnp.float32)
    vertical = vertical_coordinate(key)
    return jnp.concatenate([across, vertical], axis=0).astype(jnp.float32)


def draw_particle_strength(key, part):
    vertical = vertical_coordinate(key)[0]
    phase = jax.random.uniform(jax.random.fold_in(key, 41), (), jnp.float32) * (2.0 * math.pi)
    noise_key = jax.random.fold_in(key, 42)
    noise = jax.random.normal(noise_key, (3, NPART), jnp.float32)
    amplitude = 8.0 / math.sqrt(DENSITY)
    turning = math.pi
    heading = phase + turning * vertical
    coherent = amplitude * jnp.stack([jnp.cos(heading), jnp.sin(heading), jnp.zeros_like(heading)])
    return jnp.clip(noise + coherent, -6.0, 6.0).astype(jnp.float32)


def draw_boundary_points(key, part):
    first = jax.random.fold_in(key, 21)
    second = jax.random.fold_in(key, 22)
    across = jax.random.uniform(first, (2, NZ, NA), jnp.float32)
    within = jax.random.uniform(second, (NZ, NA), jnp.float32)
    planes = jnp.arange(NZ, dtype=jnp.float32)[:, None]
    vertical = ((planes + within) / NZ)[None]
    return jnp.concatenate([across, vertical], axis=0).astype(jnp.float32)


def one_row(rowkey):
    subkeys = jax.random.split(rowkey, 4)
    senders_order = jax.random.permutation(subkeys[0], N_TGT)
    anchor = jax.random.randint(subkeys[1], (), 0, N_TGT)
    halfway = (PB + 1) // 2
    receivers = jnp.arange(N_TGT, dtype=jnp.int32)
    offsets = (anchor - receivers) % N_TGT
    forced = offsets < min(N_TGT, halfway)
    filled = jnp.minimum(PB, 2 * (offsets + N_TGT * ((halfway - 1 - offsets) // N_TGT)) + 2)
    loose = jax.random.randint(subkeys[2], (N_TGT,), 2, PB // 2 + 3)
    loads = jnp.where(forced, filled, jnp.minimum(loose, PB))
    block_keys = jax.random.split(subkeys[3], N_TGT)
    shuffled = jax.vmap(jax.random.permutation, in_axes=(0, None))(block_keys, PB)
    indices = jnp.arange(PB, dtype=jnp.int32)
    active = indices[None, :] < loads[:, None]
    senders = senders_order[(receivers[:, None] + indices[None, :] // 2) % N_TGT]
    codes = receivers[:, None] * PB + shuffled
    flat_active = active.reshape(-1)
    flat_senders = senders.reshape(-1)
    flat_codes = codes.reshape(-1)
    positions = jnp.arange(N_TGT * PB, dtype=jnp.int32)

    def per_sender(sender):
        chosen = flat_active & (flat_senders == sender)
        scores = jnp.where(chosen, positions, positions + N_TGT * PB)
        selection = jnp.argsort(scores)[:PB]
        return jnp.where(chosen[selection], flat_codes[selection], -1)
    return jax.vmap(per_sender)(receivers)


def draw_intersection_target(key, part):
    rowkeys = jax.random.split(jax.random.fold_in(key, 31), N_SRC)
    return jax.vmap(one_row)(rowkeys).astype(jnp.int32)


def with_ends(result, key, low, top_value):
    longest = result.shape.index(max(result.shape))
    spots = []
    for shift in (0, 1):
        where = [jax.random.randint(jax.random.fold_in(key, axis), (), 0, length) for axis, length in enumerate(result.shape)]
        where[longest] = (where[longest] + shift) % result.shape[longest]
        spots.append(tuple(where))
    return result.at[spots[0]].set(low).at[spots[1]].set(top_value)


def level_of(key, shape, cuts, least, top_value):
    def one(dim, blocks):
        draws = jax.random.uniform(jax.random.fold_in(jax.random.fold_in(key, 6), dim), (blocks,), jnp.float32, least / len(cuts), top_value / len(cuts))
        return jnp.repeat(jnp.exp(draws), shape[dim] // blocks).reshape((-1,) + (1,) * (len(shape) - dim - 1))

    loudness = one(*cuts[0])
    for cut in cuts[1:]:
        loudness = loudness * one(*cut)
    return loudness


def scatter_about(rng, shape, deviation, reach, cuts=(), held_as=jnp.bfloat16):
    result = deviation * jax.random.normal(rng, shape, jnp.float32)
    if cuts:
        result = result * level_of(rng, shape, cuts, -0.22, 0.18)
    return jnp.clip(result, -reach, reach).astype(held_as)


def setup_inputs(seed: int = 0) -> dict:
    arg_keys = jax.random.split(jax.random.key(seed), 10)
    particle_position = draw_particle_position(jax.random.fold_in(arg_keys[9], 71), 0)
    particle_strength = draw_particle_strength(jax.random.fold_in(arg_keys[9], 71), 0)
    core_radius = jnp.clip(jnp.exp(math.log(0.12) - 0.8754687 * jax.random.uniform(arg_keys[2], (1, NPART), jnp.float32) ** level_of(arg_keys[2], (1, NPART), ((1, 32),), -0.2, 0.2)), 0.05, 0.12)
    boundary_points = draw_boundary_points(jax.random.fold_in(arg_keys[9], 71), 0)
    vorticity = scatter_about(arg_keys[4], (NZ, 3, NA, NR), 1.0, 6.0, ((0, 8), (2, 4)), jnp.float32)
    swirl = jnp.clip(jax.random.uniform(arg_keys[5], (NZ, NA, NR), jnp.float32, -0.5, 0.5) * level_of(arg_keys[5], (NZ, NA, NR), ((0, 8), (1, 4)), -0.4, 0.0), -0.5, 0.5)
    diffusivity = jnp.clip(0.05 + 0.15 * jax.random.uniform(arg_keys[6], (NZ, NA, NR), jnp.float32) ** level_of(arg_keys[6], (NZ, NA, NR), ((0, 8), (1, 4)), -0.2, 0.2), 0.05, 0.2)
    intersection_source = with_ends(jax.random.randint(arg_keys[7], (N_SRC, N_TGT, PB), 0, GB), jax.random.fold_in(arg_keys[7], 1), 0, GB - 1).astype(jnp.int32)
    intersection_target = draw_intersection_target(jax.random.fold_in(arg_keys[9], 71), 0)
    return {"particle_position": particle_position, "particle_strength": particle_strength, "core_radius": core_radius, "boundary_points": boundary_points, "vorticity": vorticity, "swirl": swirl, "diffusivity": diffusivity, "intersection_source": intersection_source, "intersection_target": intersection_target}


swirl_gain = 0.2

def divisor(number, limit):
    return max([candidate for candidate in range(1, min(number, limit) + 1) if number % candidate == 0])

def induced(targets, position, strength, radius):
    target_total = targets.shape[1]
    particle_total = position.shape[1]
    particle_step = divisor(particle_total, 2048)
    target_step = divisor(target_total, max(256, (1 << 22) // particle_step))
    target_blocks = targets.reshape(3, target_total // target_step, target_step).transpose(1, 0, 2)
    packed = jnp.concatenate([position, strength, radius], axis=0)
    particle_blocks = packed.reshape(7, particle_total // particle_step, particle_step).transpose(1, 0, 2)

    def per_target(target_block):

        def absorb(running_sum, particle_block):
            delta_x = target_block[0][:, None] - particle_block[0][None, :]
            delta_y = target_block[1][:, None] - particle_block[1][None, :]
            delta_z = target_block[2][:, None] - particle_block[2][None, :]
            distance = delta_x * delta_x + delta_y * delta_y + delta_z * delta_z + (particle_block[6] * particle_block[6])[None, :]
            inverse = lax.rsqrt(distance)
            weight = inverse * inverse * inverse
            along_x = particle_block[3][None, :]
            along_y = particle_block[4][None, :]
            along_z = particle_block[5][None, :]
            velocity_x = lax.optimization_barrier(jnp.sum(weight * (along_y * delta_z - along_z * delta_y), axis=1))
            velocity_y = lax.optimization_barrier(jnp.sum(weight * (along_z * delta_x - along_x * delta_z), axis=1))
            velocity_z = lax.optimization_barrier(jnp.sum(weight * (along_x * delta_y - along_y * delta_x), axis=1))
            return (running_sum + jnp.stack([velocity_x, velocity_y, velocity_z]), None)
        running_sum, unused = lax.scan(absorb, jnp.zeros((3, target_step), jnp.float32), particle_blocks)
        return running_sum
    blocked = lax.map(per_target, target_blocks)
    return blocked.transpose(1, 0, 2).reshape(3, target_total)

def substep(field, wall_ghost, local_swirl, local_diff):
    eastern = jnp.roll(field, -1, axis=2)
    western = jnp.roll(field, 1, axis=2)
    outward = jnp.concatenate([field[..., 1:], jnp.zeros_like(field[..., :1])], axis=3)
    inward = jnp.concatenate([wall_ghost[..., None], field[..., :-1]], axis=3)
    transport = local_swirl + swirl_gain * field[:, 2]
    return field + local_diff[:, None] * (eastern + western + outward + inward - 4.0 * field) - 0.5 * transport[:, None] * (eastern - western)

def reference(particle_position, particle_strength, core_radius, boundary_points, vorticity, swirl, diffusivity, intersection_source, intersection_target):
    prefactor = 1.6 / (4.0 * math.pi * math.sqrt(DENSITY))
    targets = boundary_points.reshape(3, NZ * NA)
    wall_speed = (induced(targets, particle_position, particle_strength, core_radius) * prefactor).reshape(3, NZ, NA)
    wall_ghost = wall_speed.transpose(1, 0, 2)
    field = vorticity
    for counter in range(SUBSTEPS):
        field = substep(field, wall_ghost, swirl, diffusivity)
    grid_blocks = field.reshape(N_SRC, ZD, 3, N_TGT, AD, NR).transpose(0, 3, 1, 2, 4, 5).reshape(N_SRC, N_TGT, GB, NR)
    rows_src = jnp.arange(N_SRC, dtype=jnp.int32)[:, None, None]
    rows_tgt = jnp.arange(N_TGT, dtype=jnp.int32)[None, :, None]
    picked = grid_blocks[rows_src, rows_tgt, intersection_source].reshape(N_SRC, N_TGT * PB, NR)
    labels = intersection_target.reshape(N_SRC, N_TGT * PB)
    matches = labels[:, None, :] == jnp.arange(N_TGT * PB, dtype=jnp.int32)[None, :, None]
    incoming = jnp.einsum('sde,sen->sdn', matches.astype(jnp.float32), picked.astype(jnp.float32), precision=lax.Precision.HIGHEST)
    covered = jnp.any(matches, axis=2)
    current = particle_strength.reshape(3, N_SRC, N_TGT, P_DEV // NR, NR).transpose(1, 2, 0, 3, 4).reshape(N_SRC, N_TGT * PB, NR)
    renewed = jnp.where(covered[..., None], incoming, current)
    new_strength = renewed.reshape(N_SRC, N_TGT, 3, P_DEV // NR, NR).transpose(2, 0, 1, 3, 4).reshape(3, NPART)
    return (wall_speed, field, new_strength)
```

```python
import functools
import math

import jax
import jax.numpy as jnp
from jax import lax
from jax.experimental import pallas as pl
from jax.experimental.pallas import tpu as pltpu
from jax.sharding import PartitionSpec as P

SUBSTEPS = 3
LANES = 128
ROWS = 8
GROUP_SET = 3
swirl_gain = 0.2

VMEM = pltpu.VMEM
SMEM = pltpu.SMEM


def vmem():
    return pl.BlockSpec(memory_space=VMEM)


def smem():
    return pl.BlockSpec(memory_space=SMEM)


def divisor(number, limit):
    return max(c for c in range(1, min(number, limit) + 1) if number % c == 0)


def pack_kernel(pos, strength, radius, points, vort, swirl, diff, particles, first, last, columns):
    particles[0:3, :] = pos[...]
    particles[3:6, :] = strength[...]
    particles[6:7, :] = radius[...] * radius[...]
    particles[7:8, :] = jnp.zeros_like(radius)
    angles = vort.shape[2]
    plane = lax.axis_index("src")
    diagonal = lax.broadcasted_iota(jnp.int32, (angles, angles), 0) == lax.broadcasted_iota(
        jnp.int32, (angles, angles), 1
    )
    lane = lax.broadcasted_iota(jnp.int32, (angles, LANES), 1)
    packed = jnp.zeros((angles, LANES), jnp.float32)
    for m in range(3):
        row = points[m, pl.ds(plane, 1), :]
        column = jnp.sum(jnp.where(diagonal, row, 0.0), axis=1, keepdims=True)
        packed = jnp.where(lane == m, column, packed)
    columns[...] = packed
    for m in range(3):
        first[m] = vort[0, m, 0:ROWS]
        last[m] = vort[0, m, angles - ROWS : angles]
    first[3] = swirl[0, 0:ROWS]
    last[3] = swirl[0, angles - ROWS : angles]
    first[4] = diff[0, 0:ROWS]
    last[4] = diff[0, angles - ROWS : angles]
    first[5] = packed[0:ROWS]
    last[5] = packed[angles - ROWS : angles]


def field_kernel(
    scale, particles, columns, low, high, vort, swirl, diff, source, target,
    wall, grid, message, extended_points,
):
    device_total, unused, per_device = particles.shape
    angles = vort.shape[2]
    height = angles + ROWS
    blocks = source.shape[2]
    halo_row = lax.broadcasted_iota(jnp.int32, (ROWS, LANES), 0)

    def halo(index):
        return jnp.where(halo_row < ROWS // 2, high[index], low[index])

    extended_points[0:angles, :] = columns[...]
    extended_points[angles:height, :] = halo(5)

    unroll = divisor(device_total, 4)
    groups = height // ROWS
    walls = [[None] * groups for m in range(3)]
    for start in range(0, groups, GROUP_SET):
        members = list(range(start, min(start + GROUP_SET, groups)))
        where_at = [
            [
                jnp.broadcast_to(extended_points[g * ROWS : (g + 1) * ROWS, m : m + 1], (ROWS, LANES))
                for m in range(3)
            ]
            for g in members
        ]

        def absorb(step, sums):
            sums = list(sums)
            for u in range(unroll):
                for k in range(per_device // LANES):
                    px, py, pz, sx, sy, sz, cc = [
                        particles[step * unroll + u, r : r + 1, k * LANES : (k + 1) * LANES]
                        for r in range(7)
                    ]
                    for i, (tx, ty, tz) in enumerate(where_at):
                        dx = tx - px
                        dy = ty - py
                        dz = tz - pz
                        inverse = lax.rsqrt(dx * dx + dy * dy + (dz * dz + cc))
                        weight = inverse * inverse * inverse
                        dx = dx * weight
                        dy = dy * weight
                        dz = dz * weight
                        sums[3 * i] += sy * dz - sz * dy
                        sums[3 * i + 1] += sz * dx - sx * dz
                        sums[3 * i + 2] += sx * dy - sy * dx
            return tuple(sums)

        zero = jnp.zeros((ROWS, LANES), jnp.float32)
        sums = lax.fori_loop(0, device_total // unroll, absorb, (zero,) * (3 * len(members)))
        for i, g in enumerate(members):
            for m in range(3):
                walls[m][g] = jnp.broadcast_to(
                    jnp.sum(sums[3 * i + m], axis=1, keepdims=True) * scale, (ROWS, LANES)
                )

    wall_columns = [jnp.concatenate(walls[m], axis=0) for m in range(3)]
    own = lax.broadcasted_iota(jnp.int32, (angles, LANES), 0)
    across = lax.broadcasted_iota(jnp.int32, (angles, LANES), 1)
    for m in range(3):
        turned = jnp.sum(jnp.where(own == across, wall_columns[m][0:angles], 0.0), axis=0, keepdims=True)
        wall[m] = turned[:, 0:angles]

    lane = lax.broadcasted_iota(jnp.int32, (height, LANES), 1)
    field = [jnp.concatenate([vort[0, m], halo(m)], axis=0) for m in range(3)]
    local_swirl = jnp.concatenate([swirl[0], halo(3)], axis=0)
    local_diff = jnp.concatenate([diff[0], halo(4)], axis=0)
    for counter in range(SUBSTEPS):
        transport = 0.5 * (local_swirl + swirl_gain * field[2])
        renewed = []
        for m in range(3):
            center = field[m]
            eastern = pltpu.roll(center, height - 1, 0)
            western = pltpu.roll(center, 1, 0)
            outward = jnp.where(lane == LANES - 1, 0.0, pltpu.roll(center, LANES - 1, 1))
            inward = jnp.where(lane == 0, wall_columns[m], pltpu.roll(center, 1, 1))
            renewed.append(
                center
                + local_diff * (eastern + western + outward + inward - 4.0 * center)
                - transport * (eastern - western)
            )
        field = renewed
    for m in range(3):
        grid[0, m] = field[m][0:angles]

    message[0] = jnp.zeros(message.shape[1:], jnp.float32)
    message[1] = jnp.full(message.shape[1:], -1.0, jnp.float32)
    for i in range(blocks):
        q = source[0, 0, i]
        message[0, i : i + 1, :] = grid[0, q // angles, pl.ds(q % angles, 1), :]
        message[1, i : i + 1, :] = jnp.full((1, LANES), target[0, 0, i].astype(jnp.float32))


def deliver_kernel(strength, *rest):
    messages, result = rest[:-1], rest[-1]
    per_device = strength.shape[1]
    pieces = per_device // LANES
    blocks = 3 * pieces
    me = lax.axis_index("tgt")
    for b in range(blocks):
        name = (me * blocks + b).astype(jnp.float32)
        value = None
        for arrived in messages:
            match = arrived[1] == name
            here = jnp.where(match, arrived[0], 0.0)
            count = jnp.where(match, 1.0, 0.0)
            value = here if value is None else value + here
            hits = count if arrived is messages[0] else hits + count
        value = jnp.sum(value, axis=0, keepdims=True)
        hits = jnp.sum(hits, axis=0, keepdims=True)
        c, k = b // pieces, (b % pieces) * LANES
        result[c : c + 1, k : k + LANES] = jnp.where(
            hits > 0.0, value, strength[c : c + 1, k : k + LANES]
        )


def shift(block, axis, distance):
    count = lax.axis_size(axis)
    return lax.ppermute(block, axis, [(i, (i + distance) % count) for i in range(count)])


def on_device(
    particle_position,
    particle_strength,
    core_radius,
    boundary_points,
    vorticity,
    swirl,
    diffusivity,
    intersection_source,
    intersection_target,
):
    source_count = lax.axis_size("src")
    target_count = lax.axis_size("tgt")
    planes, comps, angles, radial = vorticity.shape
    per_device = particle_position.shape[1]
    blocks = intersection_source.shape[2]
    f32 = jnp.float32
    scale = 1.6 / (4.0 * math.pi * math.sqrt(per_device * target_count * source_count))
    particles, first, last, columns = pl.pallas_call(
        pack_kernel,
        out_shape=(
            jax.ShapeDtypeStruct((ROWS, per_device), f32),
            jax.ShapeDtypeStruct((6, ROWS, LANES), f32),
            jax.ShapeDtypeStruct((6, ROWS, LANES), f32),
            jax.ShapeDtypeStruct((angles, LANES), f32),
        ),
        in_specs=[vmem()] * 7,
        out_specs=(vmem(),) * 4,
        name="pack",
    )(
        particle_position, particle_strength, core_radius, boundary_points,
        vorticity, swirl, diffusivity,
    )
    low = shift(last, "tgt", 1)
    high = shift(first, "tgt", -1)
    everyone = lax.all_gather(particles, ("src", "tgt"))
    message_rows = 16 * ((blocks + 15) // 16)
    wall, grid, message = pl.pallas_call(
        functools.partial(field_kernel, scale),
        out_shape=(
            jax.ShapeDtypeStruct((3, planes, angles), f32),
            jax.ShapeDtypeStruct(vorticity.shape, f32),
            jax.ShapeDtypeStruct((2, message_rows, LANES), f32),
        ),
        in_specs=[vmem()] * 7 + [smem()] * 2,
        out_specs=(vmem(),) * 3,
        scratch_shapes=[pltpu.VMEM((angles + ROWS, LANES), f32)],
        compiler_params=pltpu.CompilerParams(
            vmem_limit_bytes=(16 << 20) + 2 * everyone.size * 4
        ),
        name="field",
    )(
        everyone, columns, low, high, vorticity, swirl, diffusivity,
        intersection_source, intersection_target,
    )
    arrived = [message] + [shift(message, "tgt", d) for d in range(1, target_count)]
    new_strength = pl.pallas_call(
        deliver_kernel,
        out_shape=jax.ShapeDtypeStruct(particle_strength.shape, f32),
        in_specs=[vmem()] * (1 + target_count),
        out_specs=vmem(),
        name="deliver",
    )(particle_strength, *arrived)
    return (wall, grid, new_strength)


def solution(mesh):
    in_specs = (
        P(None, ("src", "tgt")),
        P(None, ("src", "tgt")),
        P(None, ("src", "tgt")),
        P(None, None, "tgt"),
        P("src", None, "tgt", None),
        P("src", "tgt", None),
        P("src", "tgt", None),
        P("src", "tgt", None),
        P("src", "tgt", None),
    )
    out_specs = (P(None, "src", "tgt"), P("src", None, "tgt", None), P(None, ("src", "tgt")))
    return jax.shard_map(
        on_device, mesh=mesh, in_specs=in_specs, out_specs=out_specs, check_vma=False
    )
```

```python
import functools
import math

import jax
import jax.numpy as jnp
from jax import lax
from jax.experimental import pallas as pl
from jax.experimental.pallas import tpu as pltpu
from jax.sharding import PartitionSpec as P

SUBSTEPS = 3
LANES = 128
ROWS = 8
GROUP_SET = 4
swirl_gain = 0.2
f32 = jnp.float32


def vmem():
    return pl.BlockSpec(memory_space=pltpu.VMEM)


def smem():
    return pl.BlockSpec(memory_space=pltpu.SMEM)


def shape(*dims):
    return jax.ShapeDtypeStruct(dims, f32)


def limit(megabytes):
    return pltpu.CompilerParams(vmem_limit_bytes=megabytes << 20)


def cost(flops, size):
    return pl.CostEstimate(flops=flops, bytes_accessed=size, transcendentals=0)


def divisor(number, most):
    return max(c for c in range(1, min(number, most) + 1) if number % c == 0)


def power_of_two(number):
    return number & (number - 1) == 0


def partner(index, step, count):
    return index ^ step if power_of_two(count) else (index + step) % count


def source_of(index, step, count):
    return index ^ step if power_of_two(count) else (index - step) % count


def particles_kernel(inner, pos, strength, radius, points, *messages):
    outer = len(messages)
    tiles = pos.shape[1] // LANES
    angles = points.shape[2]
    src = lax.axis_index("src")
    core = radius[...] * radius[...]
    for step, message in enumerate(messages):
        plane = partner(src // inner, step, outer) * inner + src % inner
        for k in range(tiles):
            part = slice(k * LANES, (k + 1) * LANES)
            message[k, 0:3, :] = pos[:, part]
            message[k, 3:6, :] = strength[:, part]
            message[k, 6:7, :] = core[:, part]
            message[k, 7:8, :] = jnp.zeros((1, LANES), f32)
        message[tiles] = jnp.zeros((ROWS, LANES), f32)
        for m in range(3):
            message[tiles, m : m + 1, 0:angles] = points[m, pl.ds(plane, 1), :]


def plane_kernel(vort, swirl, diff, source, target, plane):
    angles = vort.shape[2]
    total = angles * lax.axis_size("tgt")
    blocks = source.shape[2]
    for m in range(3):
        plane[m * angles : (m + 1) * angles, :] = vort[0, m]
    plane[3 * angles : 4 * angles, :] = swirl[0]
    plane[4 * angles : 5 * angles, :] = diff[0]
    plane[5 * angles : 5 * angles + ROWS, :] = jnp.full((ROWS, LANES), -1.0, f32)
    q = source[0]
    row = (q // angles) * total + lax.axis_index("tgt") * angles + q % angles
    plane[5 * angles : 5 * angles + 1, 0:blocks] = row.astype(f32)
    plane[5 * angles + 1 : 5 * angles + 2, 0:blocks] = target[0].astype(f32)


def join_kernel(ways, outer, *refs):
    messages, (particles, columns), tiled = refs[:outer], refs[outer : outer + 2], refs[outer + 2]
    tiles = messages[0].shape[0] - 1
    angles = columns.shape[1] // ways
    me = lax.axis_index("tgt")
    for step, message in enumerate(messages):
        for k in range(tiles):
            particles[step * tiles + k] = message[k]
    tiled[...] = jnp.zeros(tiled.shape, f32)
    for step in range(ways):
        place = source_of(me, step, ways)
        tiled[pl.ds(pl.multiple_of(place * ROWS, ROWS), ROWS), :] = messages[step][tiles]
    turned = jnp.transpose(tiled[...])
    for t in range(ways):
        for m in range(3):
            lane = t * ROWS + m
            columns[m, t * angles : (t + 1) * angles, :] = jnp.broadcast_to(
                turned[0:angles, lane : lane + 1], (angles, LANES)
            )


def pairs_kernel(scale, particles, columns, *refs):
    before, (result, sums) = refs[:-2], refs[-2:]
    tiles = particles.shape[0]
    angles = columns.shape[1]
    together = divisor(angles // ROWS, GROUP_SET)
    unroll = divisor(tiles, 12)

    def one_set(index, unused):
        base = index * (together * ROWS)
        rows = [pl.ds(pl.multiple_of(base + i * ROWS, ROWS), ROWS) for i in range(together)]
        targets = [[columns[m, r, :] for m in range(3)] for r in rows]

        def absorb(step, carried):
            carried = list(carried)
            for u in range(unroll):
                px, py, pz, sx, sy, sz, cc = [
                    particles[step * unroll + u, r : r + 1, :] for r in range(7)
                ]
                for i, (tx, ty, tz) in enumerate(targets):
                    dx = tx - px
                    dy = ty - py
                    dz = tz - pz
                    inverse = lax.rsqrt(dx * dx + dy * dy + (dz * dz + cc))
                    weight = inverse * inverse * inverse
                    dx = dx * weight
                    dy = dy * weight
                    dz = dz * weight
                    carried[3 * i] += sy * dz - sz * dy
                    carried[3 * i + 1] += sz * dx - sx * dz
                    carried[3 * i + 2] += sx * dy - sy * dx
            return tuple(carried)

        zero = jnp.zeros((ROWS, LANES), f32)
        carried = (zero,) * (3 * together)
        if tiles == unroll:
            carried = absorb(0, carried)
        else:
            carried = lax.fori_loop(0, tiles // unroll, absorb, carried)
        for i, r in enumerate(rows):
            for m in range(3):
                sums[m, r, :] = carried[3 * i + m]
        return unused

    lax.fori_loop(0, angles // (together * ROWS), one_set, 0)
    result[...] = jnp.zeros(result.shape, f32)
    ones = jnp.full((ROWS, LANES), scale, f32)
    for m in range(3):
        total = lax.dot_general(
            ones, sums[m], (((1,), (1,)), ((), ())),
            precision=lax.Precision.HIGHEST, preferred_element_type=f32,
        )[0:1]
        for other in before:
            total = total + other[m : m + 1, :]
        result[m : m + 1, :] = total


def lists_kernel(blocks, *refs):
    planes, result = refs[:-1], refs[-1]
    me = lax.axis_index("tgt")
    result_rows = result.shape[0]
    name = (
        me * blocks + lax.broadcasted_iota(jnp.int32, (result_rows, LANES), 0)
    ).astype(f32)
    found = jnp.full((result_rows, LANES), -1.0, f32)
    for plane in planes:
        piece = plane.shape[0] - ROWS
        row = plane[piece : piece + 1, :]
        code = plane[piece + 1 : piece + 2, :]
        found = jnp.maximum(found, jnp.where(code == name, row, -1.0))
    found = jnp.max(found, axis=1, keepdims=True)
    result[...] = jnp.broadcast_to(found, (result_rows, LANES)).astype(jnp.int32)


def field_kernel(steps, *refs):
    count = len(steps)
    partials, planes = refs[:count], refs[count : 2 * count]
    strength, rows, wall, grid, new_strength, whole, stepped = refs[2 * count :]
    angles = grid.shape[2]
    total = angles * count
    me = lax.axis_index("tgt")
    for step, plane in zip(steps, planes):
        place = pl.multiple_of(source_of(me, step, count) * angles, ROWS)
        for m in range(5):
            whole[m, pl.ds(place, angles), :] = plane[m * angles : (m + 1) * angles, :]
    speed = partials[0][...]
    for partial in partials[1:]:
        speed = speed + partial[...]
    own = pltpu.roll(speed, total - me * angles, 1)
    for m in range(3):
        wall[m] = own[m : m + 1, 0:angles]
    padded = jnp.concatenate([speed, jnp.zeros((LANES - ROWS, total), f32)], axis=0)
    turned = jnp.concatenate(
        [
            jnp.transpose(padded[:, k * LANES : (k + 1) * LANES])
            for k in range(total // LANES)
        ],
        axis=0,
    )
    lane = lax.broadcasted_iota(jnp.int32, (total, LANES), 1)
    walls = [jnp.broadcast_to(turned[:, m : m + 1], (total, LANES)) for m in range(3)]
    field = [whole[m] for m in range(3)]
    local_swirl = whole[3]
    local_diff = whole[4]
    for counter in range(SUBSTEPS):
        transport = 0.5 * (local_swirl + swirl_gain * field[2])
        renewed = []
        for m in range(3):
            center = field[m]
            eastern = pltpu.roll(center, total - 1, 0)
            western = pltpu.roll(center, 1, 0)
            outward = jnp.where(lane == LANES - 1, 0.0, pltpu.roll(center, LANES - 1, 1))
            inward = jnp.where(lane == 0, walls[m], pltpu.roll(center, 1, 1))
            renewed.append(
                center
                + local_diff * (eastern + western + outward + inward - 4.0 * center)
                - transport * (eastern - western)
            )
        field = renewed
    for m in range(3):
        stepped[m * total : (m + 1) * total, :] = field[m]
    for m in range(3):
        place = pl.multiple_of(m * total + me * angles, ROWS)
        grid[0, m] = stepped[pl.ds(place, angles), :]
    pieces = strength.shape[1] // LANES
    for b in range(3 * pieces):
        q = rows[b, 0]
        c, part = b // pieces, slice((b % pieces) * LANES, (b % pieces + 1) * LANES)
        row = stepped[pl.ds(jnp.maximum(q, 0), 1), :]
        new_strength[c : c + 1, part] = jnp.where(q >= 0, row, strength[c : c + 1, part])


def send(block, pairs):
    return lax.ppermute(block, ("src", "tgt"), pairs)


def on_device(
    particle_position,
    particle_strength,
    core_radius,
    boundary_points,
    vorticity,
    swirl,
    diffusivity,
    intersection_source,
    intersection_target,
):
    sources = lax.axis_size("src")
    ways = lax.axis_size("tgt")
    planes, comps, angles, radial = vorticity.shape
    per_device = particle_position.shape[1]
    tiles = per_device // LANES
    blocks = intersection_source.shape[2]
    inner = 2 if sources % 2 == 0 else 1
    outer = sources // inner
    total = angles * ways
    scale = 1.6 / (4.0 * math.pi * math.sqrt(per_device * ways * sources))

    def pairs(move):
        found = []
        for s in range(sources):
            for t in range(ways):
                o, i, u = move(s // inner, s % inner, t)
                found.append((s * ways + t, (o * inner + i) * ways + u))
        return found

    def over_tgt(block, step):
        return send(block, pairs(lambda o, i, t: (o, i, partner(t, step, ways))))

    messages = pl.pallas_call(
        functools.partial(particles_kernel, inner),
        out_shape=(shape(tiles + 1, ROWS, LANES),) * outer,
        in_specs=[vmem()] * 4,
        out_specs=(vmem(),) * outer,
        compiler_params=limit(4),
        name="particles",
    )(particle_position, particle_strength, core_radius, boundary_points)
    line = [messages[0]] + [
        send(
            messages[k],
            pairs(lambda o, i, t: (partner(o, k, outer), i, partner(t, k % ways, ways))),
        )
        for k in range(1, outer)
    ]

    piece = 5 * angles + ROWS
    vorticity_late, held = lax.optimization_barrier((vorticity, messages[0]))
    own_plane = pl.pallas_call(
        plane_kernel,
        out_shape=shape(piece, LANES),
        in_specs=[vmem()] * 5,
        out_specs=vmem(),
        compiler_params=limit(4),
        name="plane",
    )(vorticity_late, swirl, diffusivity, intersection_source, intersection_target)
    whole = [own_plane] + [over_tgt(own_plane, k) for k in range(1, ways)]

    near, columns = pl.pallas_call(
        functools.partial(join_kernel, ways, outer),
        out_shape=(shape(outer * tiles, ROWS, LANES), shape(3, total, LANES)),
        in_specs=[vmem()] * outer,
        out_specs=(vmem(), vmem()),
        scratch_shapes=[pltpu.VMEM((LANES, LANES), f32)],
        compiler_params=limit(8),
        name="join",
    )(*line)

    def induced(particles, *before):
        return pl.pallas_call(
            functools.partial(pairs_kernel, scale),
            out_shape=shape(ROWS, total),
            in_specs=[vmem()] * (2 + len(before)),
            out_specs=vmem(),
            scratch_shapes=[pltpu.VMEM((3, total, LANES), f32)],
            compiler_params=limit(12),
            cost_estimate=cost(26 * total * particles.shape[0] * LANES, 1 << 20),
            name="pairs",
        )(particles, columns, *before)

    if inner > 1:
        far = send(near, pairs(lambda o, i, t: (o, 1 - i, t)))
        partial_sum = induced(far, induced(near))
    else:
        partial_sum = induced(near)
    partials = [partial_sum] + [over_tgt(partial_sum, k) for k in range(1, ways)]

    rows = pl.pallas_call(
        functools.partial(lists_kernel, blocks),
        out_shape=jax.ShapeDtypeStruct((16 * ((blocks + 15) // 16), LANES), jnp.int32),
        in_specs=[vmem()] * ways,
        out_specs=vmem(),
        compiler_params=limit(8),
        name="lists",
    )(*whole)

    wall, grid, new_strength = pl.pallas_call(
        functools.partial(field_kernel, range(ways)),
        out_shape=(shape(3, planes, angles), shape(*vorticity.shape), shape(3, per_device)),
        in_specs=[vmem()] * (2 * ways + 1) + [smem()],
        out_specs=(vmem(),) * 3,
        scratch_shapes=[
            pltpu.VMEM((5, total, LANES), f32),
            pltpu.VMEM((3 * total, LANES), f32),
        ],
        compiler_params=limit(24),
        name="field",
    )(*partials, *whole, particle_strength, rows)
    return (wall, grid, new_strength)


def solution(mesh):
    in_specs = (
        P(None, ("src", "tgt")),
        P(None, ("src", "tgt")),
        P(None, ("src", "tgt")),
        P(None, None, "tgt"),
        P("src", None, "tgt", None),
        P("src", "tgt", None),
        P("src", "tgt", None),
        P("src", "tgt", None),
        P("src", "tgt", None),
    )
    out_specs = (P(None, "src", "tgt"), P("src", None, "tgt", None), P(None, ("src", "tgt")))
    return jax.shard_map(
        on_device, mesh=mesh, in_specs=in_specs, out_specs=out_specs, check_vma=False
    )
```

```python
import functools
import math

import jax
import jax.numpy as jnp
from jax import lax
from jax.experimental import pallas as pl
from jax.experimental.pallas import tpu as pltpu
from jax.sharding import PartitionSpec as P

SUBSTEPS = 3
LANES = 128
ROWS = 8
GROUP_SET = 4
swirl_gain = 0.2
f32 = jnp.float32


def vmem():
    return pl.BlockSpec(memory_space=pltpu.VMEM)


def smem():
    return pl.BlockSpec(memory_space=pltpu.SMEM)


def hbm():
    return pl.BlockSpec(memory_space=pltpu.HBM)


def fetch(refs, held, sems):
    copies = [pltpu.make_async_copy(r, h, sems.at[i]) for i, (r, h) in enumerate(zip(refs, held))]
    for copy in copies:
        copy.start()
    for copy in copies:
        copy.wait()


def shape(*dims):
    return jax.ShapeDtypeStruct(dims, f32)


def limit(megabytes):
    return pltpu.CompilerParams(vmem_limit_bytes=megabytes << 20)


def cost(flops, size):
    return pl.CostEstimate(flops=flops, bytes_accessed=size, transcendentals=0)


def divisor(number, most):
    return max(c for c in range(1, min(number, most) + 1) if number % c == 0)


def power_of_two(number):
    return number & (number - 1) == 0


def partner(index, step, count):
    return index ^ step if power_of_two(count) else (index + step) % count


def source_of(index, step, count):
    return index ^ step if power_of_two(count) else (index - step) % count


def particles_kernel(inner, outer, *refs):
    given, messages, held, sems = refs[:4], refs[4 : 4 + outer], refs[4 + outer : -1], refs[-1]
    fetch(given, held, sems)
    pos, strength, radius, points = held
    tiles = pos.shape[1] // LANES
    angles = points.shape[2]
    src = lax.axis_index("src")
    core = radius[...] * radius[...]
    for step, message in enumerate(messages):
        plane = partner(src // inner, step, outer) * inner + src % inner
        for k in range(tiles):
            part = slice(k * LANES, (k + 1) * LANES)
            message[k, 0:3, :] = pos[:, part]
            message[k, 3:6, :] = strength[:, part]
            message[k, 6:7, :] = core[:, part]
            message[k, 7:8, :] = jnp.zeros((1, LANES), f32)
        message[tiles] = jnp.zeros((ROWS, LANES), f32)
        for m in range(3):
            message[tiles, m : m + 1, 0:angles] = points[m, pl.ds(plane, 1), :]


def edges_kernel(vort, swirl, diff, source, target, after, message, own, own_source, own_target, sems):
    angles = vort.shape[2]
    blocks = source.shape[2]
    total = angles * lax.axis_size("tgt")
    fetch(
        (vort.at[0], swirl, diff, source, target),
        (own.at[0:3], own.at[3:4], own.at[4:5], own_source, own_target),
        sems,
    )
    half = ROWS // 2
    for c in range(5):
        message[c, :, 0:angles] = jnp.transpose(own[c])[0:ROWS, :]
        message[c, :, angles:LANES] = jnp.zeros((ROWS, LANES - angles), f32)
        message[6 + c, 0:half, :] = own[c, 0:half]
        message[6 + c, half:ROWS, :] = own[c, angles - half : angles]
    message[5] = jnp.full((ROWS, LANES), -1.0, f32)
    q = own_source[0]
    row = (q // angles) * total + lax.axis_index("tgt") * angles + q % angles
    message[5, 0:1, 0:blocks] = row.astype(f32)
    message[5, 1:2, 0:blocks] = own_target[0].astype(f32)


def still_kernel(ways, *refs):
    messages = refs[:ways]
    own, source, after, grid, picks, inner_cells, index, placed = refs[ways:]
    angles = own.shape[1]
    height = angles + ROWS
    blocks = source.shape[2]
    me = lax.axis_index("tgt")
    for step, message in enumerate(messages):
        placed[source_of(me, step, ways)] = message[...]

    for c in range(5):
        inner_cells[c] = jnp.concatenate(
            [placed[t, c, :, 0:angles] for t in range(ways)], axis=1
        )

    shaped = index.shape
    name = (me * blocks + lax.broadcasted_iota(jnp.int32, shaped, 0)).astype(f32)
    lane = lax.broadcasted_iota(jnp.int32, shaped, 1).astype(f32)
    row = jnp.full(shaped, -1.0, f32)
    slot = jnp.zeros(shaped, f32)
    for step, message in enumerate(messages):
        match = message[5, 1:2, :] == name
        row = jnp.maximum(row, jnp.where(match, message[5, 0:1, :], -1.0))
        slot = jnp.maximum(slot, jnp.where(match, lane + float(step * picks.shape[0]), 0.0))
    row = jnp.max(row, axis=1, keepdims=True)
    slot = jnp.max(slot, axis=1, keepdims=True)
    index[...] = jnp.where(lane < 1.0, row, slot).astype(jnp.int32)

    upper = lax.broadcasted_iota(jnp.int32, (ROWS, LANES), 0) < ROWS // 2
    east = lax.rem(me + 1, ways)
    west = lax.rem(me + ways - 1, ways)
    cells = [
        jnp.concatenate(
            [own[c], jnp.where(upper, placed[east, 6 + c], placed[west, 6 + c])], axis=0
        )
        for c in range(5)
    ]
    field, local_swirl, local_diff = cells[0:3], cells[3], cells[4]
    lane = lax.broadcasted_iota(jnp.int32, (height, LANES), 1)
    for counter in range(SUBSTEPS):
        transport = 0.5 * (local_swirl + swirl_gain * field[2])
        renewed = []
        for m in range(3):
            center = field[m]
            eastern = pltpu.roll(center, height - 1, 0)
            western = pltpu.roll(center, 1, 0)
            outward = jnp.where(lane == LANES - 1, 0.0, pltpu.roll(center, LANES - 1, 1))
            inward = jnp.where(lane == 0, 0.0, pltpu.roll(center, 1, 1))
            renewed.append(
                center
                + local_diff * (eastern + western + outward + inward - 4.0 * center)
                - transport * (eastern - western)
            )
        field = renewed
    for m in range(3):
        grid[m] = field[m][0:angles]
    picks[...] = jnp.zeros(picks.shape, f32)
    for i in range(blocks):
        q = source[0, 0, i]
        picks[i : i + 1, :] = grid[q // angles, pl.ds(q % angles, 1), :]


def join_kernel(ways, outer, *refs):
    messages, (particles, columns), tiled = refs[:outer], refs[outer : outer + 2], refs[outer + 2]
    tiles = messages[0].shape[0] - 1
    angles = columns.shape[1] // ways
    me = lax.axis_index("tgt")
    for step, message in enumerate(messages):
        for k in range(tiles):
            particles[step * tiles + k] = message[k]
    tiled[...] = jnp.zeros(tiled.shape, f32)
    for step in range(ways):
        place = source_of(me, step, ways)
        tiled[pl.ds(pl.multiple_of(place * ROWS, ROWS), ROWS), :] = messages[step][tiles]
    turned = jnp.transpose(tiled[...])
    for t in range(ways):
        for m in range(3):
            lane = t * ROWS + m
            columns[m, t * angles : (t + 1) * angles, :] = jnp.broadcast_to(
                turned[0:angles, lane : lane + 1], (angles, LANES)
            )


def pairs_kernel(scale, particles, columns, *refs):
    before, (result, sums) = refs[:-2], refs[-2:]
    spread = len(before) > 0
    tiles = particles.shape[0]
    angles = columns.shape[1]
    together = divisor(angles // ROWS, GROUP_SET)
    unroll = divisor(tiles, 12)

    def one_set(index, unused):
        base = index * (together * ROWS)
        rows = [pl.ds(pl.multiple_of(base + i * ROWS, ROWS), ROWS) for i in range(together)]
        targets = [[columns[m, r, :] for m in range(3)] for r in rows]

        def absorb(step, carried):
            carried = list(carried)
            for u in range(unroll):
                px, py, pz, sx, sy, sz, cc = [
                    particles[step * unroll + u, r : r + 1, :] for r in range(7)
                ]
                for i, (tx, ty, tz) in enumerate(targets):
                    dx = tx - px
                    dy = ty - py
                    dz = tz - pz
                    inverse = lax.rsqrt(dx * dx + dy * dy + (dz * dz + cc))
                    weight = inverse * inverse * inverse
                    dx = dx * weight
                    dy = dy * weight
                    dz = dz * weight
                    carried[3 * i] += sy * dz - sz * dy
                    carried[3 * i + 1] += sz * dx - sx * dz
                    carried[3 * i + 2] += sx * dy - sy * dx
            return tuple(carried)

        zero = jnp.zeros((ROWS, LANES), f32)
        carried = (zero,) * (3 * together)
        if tiles == unroll:
            carried = absorb(0, carried)
        else:
            carried = lax.fori_loop(0, tiles // unroll, absorb, carried)
        for i, r in enumerate(rows):
            for m in range(3):
                sums[m, r, :] = carried[3 * i + m]
        return unused

    lax.fori_loop(0, angles // (together * ROWS), one_set, 0)
    result[...] = jnp.zeros(result.shape, f32)
    parts = angles // LANES
    if spread:
        result[parts * ROWS :, :] = before[1][...]
    ones = jnp.full((ROWS, LANES), scale, f32)
    for m in range(3):
        total = lax.dot_general(
            ones, sums[m], (((1,), (1,)), ((), ())),
            precision=lax.Precision.HIGHEST, preferred_element_type=f32,
        )[0:1]
        for k in range(parts):
            row = slice(k * ROWS + m, k * ROWS + m + 1)
            value = total[:, k * LANES : (k + 1) * LANES]
            result[row, :] = value + before[0][row, :] if spread else value


def wall_kernel(ways, *refs):
    partials = refs[:ways]
    (still, inner_cells, strength, index, wall, grid, new_strength,
     fixed, picked, rows, sem) = refs[ways:]
    angles = grid.shape[2]
    total = angles * ways
    parts = total // LANES
    slots = picked.shape[0] // ways
    me = lax.axis_index("tgt")
    copy = pltpu.make_async_copy(index, rows, sem)
    copy.start()
    for step, partial in enumerate(partials):
        picked[step * slots : (step + 1) * slots, :] = partial[parts * ROWS :, :]
    speed = partials[0][0 : parts * ROWS, :]
    for partial in partials[1:]:
        speed = speed + partial[0 : parts * ROWS, :]
    speed = jnp.concatenate([speed[k * ROWS : (k + 1) * ROWS] for k in range(parts)], axis=1)
    own = pltpu.roll(speed, total - me * angles, 1)
    for m in range(3):
        wall[m] = own[m : m + 1, 0:angles]

    first = lax.broadcasted_iota(jnp.int32, (ROWS, total), 0) == 0
    field = [inner_cells[m] for m in range(3)]
    local_swirl = inner_cells[3]
    local_diff = inner_cells[4]
    for counter in range(SUBSTEPS):
        transport = 0.5 * (local_swirl + swirl_gain * field[2])
        renewed = []
        for m in range(3):
            center = field[m]
            eastern = pltpu.roll(center, total - 1, 1)
            western = pltpu.roll(center, 1, 1)
            outward = pltpu.roll(center, ROWS - 1, 0)
            inward = jnp.where(first, speed[m : m + 1, :], pltpu.roll(center, 1, 0))
            renewed.append(
                center
                + local_diff * (eastern + western + outward + inward - 4.0 * center)
                - transport * (eastern - western)
            )
        field = renewed
    stacked = jnp.concatenate(field + [jnp.zeros((LANES - 3 * ROWS, total), f32)], axis=0)
    for k in range(parts):
        turned = jnp.transpose(stacked[:, k * LANES : (k + 1) * LANES])
        for m in range(3):
            place = m * total + k * LANES
            fixed[place : place + LANES, :] = turned if m == 0 else pltpu.roll(
                turned, LANES - m * ROWS, 1
            )
    near = lax.broadcasted_iota(jnp.int32, (angles, LANES), 1) < SUBSTEPS
    for m in range(3):
        place = pl.multiple_of(m * total + me * angles, ROWS)
        grid[0, m] = jnp.where(near, fixed[pl.ds(place, angles), :], still[m])
    near = lax.broadcasted_iota(jnp.int32, (1, LANES), 1) < SUBSTEPS
    pieces = strength.shape[1] // LANES
    copy.wait()
    for b in range(3 * pieces):
        q = rows[b, 0]
        c, part = b // pieces, slice((b % pieces) * LANES, (b % pieces + 1) * LANES)
        row = jnp.where(
            near, fixed[pl.ds(jnp.maximum(q, 0), 1), :], picked[pl.ds(rows[b, 1], 1), :]
        )
        new_strength[c : c + 1, part] = jnp.where(q >= 0, row, strength[c : c + 1, part])


def send(block, pairs):
    return lax.ppermute(block, ("src", "tgt"), pairs)


def on_device(
    particle_position,
    particle_strength,
    core_radius,
    boundary_points,
    vorticity,
    swirl,
    diffusivity,
    intersection_source,
    intersection_target,
):
    sources = lax.axis_size("src")
    ways = lax.axis_size("tgt")
    planes, comps, angles, radial = vorticity.shape
    per_device = particle_position.shape[1]
    tiles = per_device // LANES
    blocks = intersection_source.shape[2]
    inner = 2 if sources % 2 == 0 else 1
    outer = sources // inner
    total = angles * ways
    scale = 1.6 / (4.0 * math.pi * math.sqrt(per_device * ways * sources))

    def pairs(move):
        found = []
        for s in range(sources):
            for t in range(ways):
                o, i, u = move(s // inner, s % inner, t)
                found.append((s * ways + t, (o * inner + i) * ways + u))
        return found

    def over_tgt(block, step):
        return send(block, pairs(lambda o, i, t: (o, i, partner(t, step, ways))))

    messages = pl.pallas_call(
        functools.partial(particles_kernel, inner, outer),
        out_shape=(shape(tiles + 1, ROWS, LANES),) * outer,
        in_specs=[hbm()] * 4,
        out_specs=(vmem(),) * outer,
        scratch_shapes=[
            pltpu.VMEM(particle_position.shape, f32),
            pltpu.VMEM(particle_strength.shape, f32),
            pltpu.VMEM(core_radius.shape, f32),
            pltpu.VMEM(boundary_points.shape, f32),
            pltpu.SemaphoreType.DMA((4,)),
        ],
        compiler_params=limit(4),
        name="particles",
    )(particle_position, particle_strength, core_radius, boundary_points)
    line = [messages[0]] + [
        send(
            messages[k],
            pairs(lambda o, i, t: (partner(o, k, outer), i, partner(t, k % ways, ways))),
        )
        for k in range(1, outer)
    ]

    edges, own = pl.pallas_call(
        edges_kernel,
        out_shape=(shape(11, ROWS, LANES), shape(5, angles, LANES)),
        in_specs=[hbm()] * 5 + [vmem()],
        out_specs=(vmem(), vmem()),
        scratch_shapes=[
            pltpu.VMEM(intersection_source.shape, jnp.int32),
            pltpu.VMEM(intersection_target.shape, jnp.int32),
            pltpu.SemaphoreType.DMA((5,)),
        ],
        compiler_params=limit(4),
        name="edges",
    )(vorticity, swirl, diffusivity, intersection_source, intersection_target, line[1])
    around = [edges] + [over_tgt(edges, k) for k in range(1, ways)]

    near, columns = pl.pallas_call(
        functools.partial(join_kernel, ways, outer),
        out_shape=(shape(outer * tiles, ROWS, LANES), shape(3, total, LANES)),
        in_specs=[vmem()] * outer,
        out_specs=(vmem(), vmem()),
        scratch_shapes=[pltpu.VMEM((LANES, LANES), f32)],
        compiler_params=limit(8),
        name="join",
    )(*line)

    def induced(particles, *before):
        rows = total // LANES * ROWS
        return pl.pallas_call(
            functools.partial(pairs_kernel, scale),
            out_shape=shape(rows + (before[1].shape[0] if before else 0), LANES),
            in_specs=[vmem()] * (2 + len(before)),
            out_specs=vmem(),
            scratch_shapes=[pltpu.VMEM((3, total, LANES), f32)],
            compiler_params=limit(12),
            cost_estimate=cost(26 * total * particles.shape[0] * LANES, 1 << 20),
            name="pairs",
        )(particles, columns, *before)

    near_sum = induced(near)
    far = send(near, pairs(lambda o, i, t: (o, inner - 1 - i, t)))
    slots = 16 * ((blocks + 15) // 16)
    still, picks, inner_cells, index = pl.pallas_call(
        functools.partial(still_kernel, ways),
        out_shape=(
            shape(3, angles, LANES),
            shape(slots, LANES),
            shape(5, ROWS, total),
            jax.ShapeDtypeStruct((slots, LANES), jnp.int32),
        ),
        in_specs=[vmem()] * (ways + 1) + [smem(), vmem()],
        out_specs=(vmem(),) * 4,
        scratch_shapes=[pltpu.VMEM((ways,) + edges.shape, f32)],
        compiler_params=limit(8),
        name="still",
    )(*around, own, intersection_source, near_sum)
    partial_sum = induced(far, near_sum, picks)
    partials = [partial_sum] + [over_tgt(partial_sum, k) for k in range(1, ways)]

    wall, grid, new_strength = pl.pallas_call(
        functools.partial(wall_kernel, ways),
        out_shape=(shape(3, planes, angles), shape(*vorticity.shape), shape(3, per_device)),
        in_specs=[vmem()] * (ways + 4),
        out_specs=(vmem(),) * 3,
        scratch_shapes=[
            pltpu.VMEM((3 * total, LANES), f32),
            pltpu.VMEM((slots * ways, LANES), f32),
            pltpu.SMEM((slots, LANES), jnp.int32),
            pltpu.SemaphoreType.DMA,
        ],
        compiler_params=limit(16),
        name="wall",
    )(*partials, still, inner_cells, particle_strength, index)
    return (wall, grid, new_strength)


def solution(mesh):
    in_specs = (
        P(None, ("src", "tgt")),
        P(None, ("src", "tgt")),
        P(None, ("src", "tgt")),
        P(None, None, "tgt"),
        P("src", None, "tgt", None),
        P("src", "tgt", None),
        P("src", "tgt", None),
        P("src", "tgt", None),
        P("src", "tgt", None),
    )
    out_specs = (P(None, "src", "tgt"), P("src", None, "tgt", None), P(None, ("src", "tgt")))
    return jax.shard_map(
        on_device, mesh=mesh, in_specs=in_specs, out_specs=out_specs, check_vma=False
    )
```

```python
import functools
import math

import jax
import jax.numpy as jnp
from jax import lax
from jax.experimental import pallas as pl
from jax.experimental.pallas import tpu as pltpu
from jax.sharding import PartitionSpec as P

SUBSTEPS = 3
LANES = 128
ROWS = 8
GROUP_SET = 4
swirl_gain = 0.2
f32 = jnp.float32


def vmem():
    return pl.BlockSpec(memory_space=pltpu.VMEM)


def smem():
    return pl.BlockSpec(memory_space=pltpu.SMEM)


def hbm():
    return pl.BlockSpec(memory_space=pltpu.HBM)


def stay(*arrays):
    return [pltpu.with_memory_space_constraint(a, pltpu.HBM) for a in arrays]


def fetch(refs, held, sems):
    copies = [pltpu.make_async_copy(r, h, sems.at[i]) for i, (r, h) in enumerate(zip(refs, held))]
    for copy in copies:
        copy.start()
    for copy in copies:
        copy.wait()


def shape(*dims):
    return jax.ShapeDtypeStruct(dims, f32)


def limit(megabytes):
    return pltpu.CompilerParams(vmem_limit_bytes=megabytes << 20)


def cost(flops, size):
    return pl.CostEstimate(flops=flops, bytes_accessed=size, transcendentals=0)


def divisor(number, most):
    return max(c for c in range(1, min(number, most) + 1) if number % c == 0)


def power_of_two(number):
    return number & (number - 1) == 0


def partner(index, step, count):
    return index ^ step if power_of_two(count) else (index + step) % count


def source_of(index, step, count):
    return index ^ step if power_of_two(count) else (index - step) % count


def line_order(outer):
    return [0, *range(outer // 2, outer), *range(1, outer // 2)]


def particles_kernel(inner, outer, *refs):
    given, messages, held, sems = refs[:4], refs[4 : 4 + outer], refs[4 + outer : -1], refs[-1]
    fetch(given, held, sems)
    pos, strength, radius, points = held
    tiles = pos.shape[1] // LANES
    angles = points.shape[2]
    src = lax.axis_index("src")
    core = radius[...] * radius[...]
    for step, message in zip(line_order(outer), messages):
        plane = partner(src // inner, step, outer) * inner + src % inner
        for k in range(tiles):
            part = slice(k * LANES, (k + 1) * LANES)
            message[k, 0:3, :] = pos[:, part]
            message[k, 3:6, :] = strength[:, part]
            message[k, 6:7, :] = core[:, part]
            message[k, 7:8, :] = jnp.zeros((1, LANES), f32)
        message[tiles] = jnp.zeros((ROWS, LANES), f32)
        for m in range(3):
            message[tiles, m : m + 1, 0:angles] = points[m, pl.ds(plane, 1), :]


def edges_kernel(vort, swirl, diff, source, target, after, message, own, own_source, own_target, sems):
    angles = vort.shape[2]
    blocks = source.shape[2]
    total = angles * lax.axis_size("tgt")
    fetch(
        (vort.at[0], swirl, diff, source, target),
        (own.at[0:3], own.at[3:4], own.at[4:5], own_source, own_target),
        sems,
    )
    half = ROWS // 2
    for c in range(5):
        message[c, :, 0:angles] = jnp.transpose(own[c])[0:ROWS, :]
        message[c, :, angles:LANES] = jnp.zeros((ROWS, LANES - angles), f32)
        message[6 + c, 0:half, :] = own[c, 0:half]
        message[6 + c, half:ROWS, :] = own[c, angles - half : angles]
    message[5] = jnp.full((ROWS, LANES), -1.0, f32)
    q = own_source[0]
    row = (q // angles) * total + lax.axis_index("tgt") * angles + q % angles
    message[5, 0:1, 0:blocks] = row.astype(f32)
    message[5, 1:2, 0:blocks] = own_target[0].astype(f32)


def still_kernel(ways, *refs):
    messages = refs[:ways]
    own, source, after, grid, picks, inner_cells, index, placed = refs[ways:]
    angles = own.shape[1]
    height = angles + ROWS
    blocks = source.shape[2]
    me = lax.axis_index("tgt")
    for step, message in enumerate(messages):
        placed[source_of(me, step, ways)] = message[...]

    for c in range(5):
        inner_cells[c] = jnp.concatenate(
            [placed[t, c, :, 0:angles] for t in range(ways)], axis=1
        )

    shaped = index.shape
    name = (me * blocks + lax.broadcasted_iota(jnp.int32, shaped, 0)).astype(f32)
    lane = lax.broadcasted_iota(jnp.int32, shaped, 1).astype(f32)
    row = jnp.full(shaped, -1.0, f32)
    slot = jnp.zeros(shaped, f32)
    for step, message in enumerate(messages):
        match = message[5, 1:2, :] == name
        row = jnp.maximum(row, jnp.where(match, message[5, 0:1, :], -1.0))
        slot = jnp.maximum(slot, jnp.where(match, lane + float(step * picks.shape[0]), 0.0))
    row = jnp.max(row, axis=1, keepdims=True)
    slot = jnp.max(slot, axis=1, keepdims=True)
    index[...] = jnp.where(lane < 1.0, row, slot).astype(jnp.int32)

    upper = lax.broadcasted_iota(jnp.int32, (ROWS, LANES), 0) < ROWS // 2
    east = lax.rem(me + 1, ways)
    west = lax.rem(me + ways - 1, ways)
    cells = [
        jnp.concatenate(
            [own[c], jnp.where(upper, placed[east, 6 + c], placed[west, 6 + c])], axis=0
        )
        for c in range(5)
    ]
    field, local_swirl, local_diff = cells[0:3], cells[3], cells[4]
    lane = lax.broadcasted_iota(jnp.int32, (height, LANES), 1)
    for counter in range(SUBSTEPS):
        transport = 0.5 * (local_swirl + swirl_gain * field[2])
        renewed = []
        for m in range(3):
            center = field[m]
            eastern = pltpu.roll(center, height - 1, 0)
            western = pltpu.roll(center, 1, 0)
            outward = jnp.where(lane == LANES - 1, 0.0, pltpu.roll(center, LANES - 1, 1))
            inward = jnp.where(lane == 0, 0.0, pltpu.roll(center, 1, 1))
            renewed.append(
                center
                + local_diff * (eastern + western + outward + inward - 4.0 * center)
                - transport * (eastern - western)
            )
        field = renewed
    for m in range(3):
        grid[m] = field[m][0:angles]
    picks[...] = jnp.zeros(picks.shape, f32)
    for i in range(blocks):
        q = source[0, 0, i]
        picks[i : i + 1, :] = grid[q // angles, pl.ds(q % angles, 1), :]


def join_kernel(ways, outer, *refs):
    messages, (after, particles, columns, tiled) = refs[:outer], refs[outer:]
    tiles = messages[0].shape[0] - 1
    angles = columns.shape[1] // ways
    me = lax.axis_index("tgt")
    order = line_order(outer)
    for i, message in enumerate(messages):
        for k in range(tiles):
            particles[i * tiles + k] = message[k]
    tiled[...] = jnp.zeros(tiled.shape, f32)
    for step in range(ways):
        place = source_of(me, step, ways)
        tiled[pl.ds(pl.multiple_of(place * ROWS, ROWS), ROWS), :] = messages[order.index(step)][tiles]
    turned = jnp.transpose(tiled[...])
    for t in range(ways):
        for m in range(3):
            lane = t * ROWS + m
            columns[m, t * angles : (t + 1) * angles, :] = jnp.broadcast_to(
                turned[0:angles, lane : lane + 1], (angles, LANES)
            )


def pairs_kernel(scale, particles, columns, *refs):
    before, (result, sums) = refs[:-2], refs[-2:]
    spread = len(before) > 0
    tiles = particles.shape[0]
    angles = columns.shape[1]
    together = divisor(angles // ROWS, GROUP_SET)
    unroll = divisor(tiles, 12)

    def one_set(index, unused):
        base = index * (together * ROWS)
        rows = [pl.ds(pl.multiple_of(base + i * ROWS, ROWS), ROWS) for i in range(together)]
        targets = [[columns[m, r, :] for m in range(3)] for r in rows]

        def absorb(step, carried):
            carried = list(carried)
            for u in range(unroll):
                px, py, pz, sx, sy, sz, cc = [
                    particles[step * unroll + u, r : r + 1, :] for r in range(7)
                ]
                for i, (tx, ty, tz) in enumerate(targets):
                    dx = tx - px
                    dy = ty - py
                    dz = tz - pz
                    inverse = lax.rsqrt(dx * dx + dy * dy + (dz * dz + cc))
                    weight = inverse * inverse * inverse
                    dx = dx * weight
                    dy = dy * weight
                    dz = dz * weight
                    carried[3 * i] += sy * dz - sz * dy
                    carried[3 * i + 1] += sz * dx - sx * dz
                    carried[3 * i + 2] += sx * dy - sy * dx
            return tuple(carried)

        zero = jnp.zeros((ROWS, LANES), f32)
        carried = (zero,) * (3 * together)
        if tiles == unroll:
            carried = absorb(0, carried)
        else:
            carried = lax.fori_loop(0, tiles // unroll, absorb, carried)
        for i, r in enumerate(rows):
            for m in range(3):
                sums[m, r, :] = carried[3 * i + m]
        return unused

    lax.fori_loop(0, angles // (together * ROWS), one_set, 0)
    result[...] = jnp.zeros(result.shape, f32)
    parts = angles // LANES
    if spread:
        result[parts * ROWS :, :] = before[1][...]
    ones = jnp.full((ROWS, LANES), scale, f32)
    for m in range(3):
        total = lax.dot_general(
            ones, sums[m], (((1,), (1,)), ((), ())),
            precision=lax.Precision.HIGHEST, preferred_element_type=f32,
        )[0:1]
        for k in range(parts):
            row = slice(k * ROWS + m, k * ROWS + m + 1)
            value = total[:, k * LANES : (k + 1) * LANES]
            result[row, :] = value + before[0][row, :] if spread else value


def wall_kernel(ways, *refs):
    partials = refs[:ways]
    (still, inner_cells, strength, index, wall, grid, new_strength,
     fixed, picked, rows, sem) = refs[ways:]
    angles = grid.shape[2]
    total = angles * ways
    parts = total // LANES
    slots = picked.shape[0] // ways
    me = lax.axis_index("tgt")
    copy = pltpu.make_async_copy(index, rows, sem)
    copy.start()
    for step, partial in enumerate(partials):
        picked[step * slots : (step + 1) * slots, :] = partial[parts * ROWS :, :]
    speed = partials[0][0 : parts * ROWS, :]
    for partial in partials[1:]:
        speed = speed + partial[0 : parts * ROWS, :]
    speed = jnp.concatenate([speed[k * ROWS : (k + 1) * ROWS] for k in range(parts)], axis=1)
    own = pltpu.roll(speed, total - me * angles, 1)
    for m in range(3):
        wall[m] = own[m : m + 1, 0:angles]

    first = lax.broadcasted_iota(jnp.int32, (ROWS, total), 0) == 0
    field = [inner_cells[m] for m in range(3)]
    local_swirl = inner_cells[3]
    local_diff = inner_cells[4]
    for counter in range(SUBSTEPS):
        transport = 0.5 * (local_swirl + swirl_gain * field[2])
        renewed = []
        for m in range(3):
            center = field[m]
            eastern = pltpu.roll(center, total - 1, 1)
            western = pltpu.roll(center, 1, 1)
            outward = pltpu.roll(center, ROWS - 1, 0)
            inward = jnp.where(first, speed[m : m + 1, :], pltpu.roll(center, 1, 0))
            renewed.append(
                center
                + local_diff * (eastern + western + outward + inward - 4.0 * center)
                - transport * (eastern - western)
            )
        field = renewed
    stacked = jnp.concatenate(field + [jnp.zeros((LANES - 3 * ROWS, total), f32)], axis=0)
    for k in range(parts):
        turned = jnp.transpose(stacked[:, k * LANES : (k + 1) * LANES])
        for m in range(3):
            place = m * total + k * LANES
            fixed[place : place + LANES, :] = turned if m == 0 else pltpu.roll(
                turned, LANES - m * ROWS, 1
            )
    near = lax.broadcasted_iota(jnp.int32, (angles, LANES), 1) < SUBSTEPS
    for m in range(3):
        place = pl.multiple_of(m * total + me * angles, ROWS)
        grid[0, m] = jnp.where(near, fixed[pl.ds(place, angles), :], still[m])
    near = lax.broadcasted_iota(jnp.int32, (1, LANES), 1) < SUBSTEPS
    pieces = strength.shape[1] // LANES
    copy.wait()
    for b in range(3 * pieces):
        q = rows[b, 0]
        c, part = b // pieces, slice((b % pieces) * LANES, (b % pieces + 1) * LANES)
        row = jnp.where(
            near, fixed[pl.ds(jnp.maximum(q, 0), 1), :], picked[pl.ds(rows[b, 1], 1), :]
        )
        new_strength[c : c + 1, part] = jnp.where(q >= 0, row, strength[c : c + 1, part])


def send(block, pairs):
    return lax.ppermute(block, ("src", "tgt"), pairs)


def on_device(
    particle_position,
    particle_strength,
    core_radius,
    boundary_points,
    vorticity,
    swirl,
    diffusivity,
    intersection_source,
    intersection_target,
):
    sources = lax.axis_size("src")
    ways = lax.axis_size("tgt")
    planes, comps, angles, radial = vorticity.shape
    per_device = particle_position.shape[1]
    tiles = per_device // LANES
    blocks = intersection_source.shape[2]
    inner = 2 if sources % 2 == 0 else 1
    outer = sources // inner
    total = angles * ways
    scale = 1.6 / (4.0 * math.pi * math.sqrt(per_device * ways * sources))

    def pairs(move):
        found = []
        for s in range(sources):
            for t in range(ways):
                o, i, u = move(s // inner, s % inner, t)
                found.append((s * ways + t, (o * inner + i) * ways + u))
        return found

    def over_tgt(block, step):
        return send(block, pairs(lambda o, i, t: (o, i, partner(t, step, ways))))

    messages = pl.pallas_call(
        functools.partial(particles_kernel, inner, outer),
        out_shape=(shape(tiles + 1, ROWS, LANES),) * outer,
        in_specs=[hbm()] * 4,
        out_specs=(vmem(),) * outer,
        scratch_shapes=[
            pltpu.VMEM(particle_position.shape, f32),
            pltpu.VMEM(particle_strength.shape, f32),
            pltpu.VMEM(core_radius.shape, f32),
            pltpu.VMEM(boundary_points.shape, f32),
            pltpu.SemaphoreType.DMA((4,)),
        ],
        compiler_params=limit(4),
        name="particles",
    )(*stay(particle_position, particle_strength, core_radius, boundary_points))
    line = [messages[0]] + [
        send(
            message,
            pairs(lambda o, i, t: (partner(o, k, outer), i, partner(t, k % ways, ways))),
        )
        for k, message in zip(line_order(outer)[1:], messages[1:])
    ]

    edges, own = pl.pallas_call(
        edges_kernel,
        out_shape=(shape(11, ROWS, LANES), shape(5, angles, LANES)),
        in_specs=[hbm()] * 5 + [vmem()],
        out_specs=(vmem(), vmem()),
        scratch_shapes=[
            pltpu.VMEM(intersection_source.shape, jnp.int32),
            pltpu.VMEM(intersection_target.shape, jnp.int32),
            pltpu.SemaphoreType.DMA((5,)),
        ],
        compiler_params=limit(4),
        name="edges",
    )(
        *stay(vorticity, swirl, diffusivity, intersection_source, intersection_target),
        line[1],
    )
    around = [edges] + [over_tgt(edges, k) for k in range(1, ways)]

    near, columns = pl.pallas_call(
        functools.partial(join_kernel, ways, outer),
        out_shape=(shape(outer * tiles, ROWS, LANES), shape(3, total, LANES)),
        in_specs=[vmem()] * (outer + 1),
        out_specs=(vmem(), vmem()),
        scratch_shapes=[pltpu.VMEM((LANES, LANES), f32)],
        compiler_params=limit(8),
        name="join",
    )(*line, edges)

    def induced(particles, *before):
        rows = total // LANES * ROWS
        return pl.pallas_call(
            functools.partial(pairs_kernel, scale),
            out_shape=shape(rows + (before[1].shape[0] if before else 0), LANES),
            in_specs=[vmem()] * (2 + len(before)),
            out_specs=vmem(),
            scratch_shapes=[pltpu.VMEM((3, total, LANES), f32)],
            compiler_params=limit(12),
            cost_estimate=cost(1 << 31, 1 << 10),
            name="pairs",
        )(particles, columns, *before)

    near_sum = induced(near)
    far = send(near, pairs(lambda o, i, t: (o, inner - 1 - i, t)))
    slots = 16 * ((blocks + 15) // 16)
    still, picks, inner_cells, index = pl.pallas_call(
        functools.partial(still_kernel, ways),
        out_shape=(
            shape(3, angles, LANES),
            shape(slots, LANES),
            shape(5, ROWS, total),
            jax.ShapeDtypeStruct((slots, LANES), jnp.int32),
        ),
        in_specs=[vmem()] * (ways + 1) + [smem(), vmem()],
        out_specs=(vmem(),) * 4,
        scratch_shapes=[pltpu.VMEM((ways,) + edges.shape, f32)],
        compiler_params=limit(8),
        name="still",
    )(*around, own, intersection_source, near_sum)
    partial_sum = induced(far, near_sum, picks)
    partials = [partial_sum] + [over_tgt(partial_sum, k) for k in range(1, ways)]

    wall, grid, new_strength = pl.pallas_call(
        functools.partial(wall_kernel, ways),
        out_shape=(shape(3, planes, angles), shape(*vorticity.shape), shape(3, per_device)),
        in_specs=[vmem()] * (ways + 4),
        out_specs=(vmem(),) * 3,
        scratch_shapes=[
            pltpu.VMEM((3 * total, LANES), f32),
            pltpu.VMEM((slots * ways, LANES), f32),
            pltpu.SMEM((slots, LANES), jnp.int32),
            pltpu.SemaphoreType.DMA,
        ],
        compiler_params=limit(16),
        name="wall",
    )(*partials, still, inner_cells, particle_strength, index)
    return (wall, grid, new_strength)


def solution(mesh):
    in_specs = (
        P(None, ("src", "tgt")),
        P(None, ("src", "tgt")),
        P(None, ("src", "tgt")),
        P(None, None, "tgt"),
        P("src", None, "tgt", None),
        P("src", "tgt", None),
        P("src", "tgt", None),
        P("src", "tgt", None),
        P("src", "tgt", None),
    )
    out_specs = (P(None, "src", "tgt"), P("src", None, "tgt", None), P(None, ("src", "tgt")))
    return jax.shard_map(
        on_device, mesh=mesh, in_specs=in_specs, out_specs=out_specs, check_vma=False
    )
```

```python
import functools
import math

import jax
import jax.numpy as jnp
from jax import lax
from jax.experimental import pallas as pl
from jax.experimental.pallas import tpu as pltpu
from jax.sharding import PartitionSpec as P

SUBSTEPS = 3
LANES = 128
ROWS = 8
TOGETHER = 2
SETS = 4
swirl_gain = 0.2
f32 = jnp.float32


def vmem():
    return pl.BlockSpec(memory_space=pltpu.VMEM)


def smem():
    return pl.BlockSpec(memory_space=pltpu.SMEM)


def hbm():
    return pl.BlockSpec(memory_space=pltpu.HBM)


def stay(*arrays):
    return [pltpu.with_memory_space_constraint(a, pltpu.HBM) for a in arrays]


def shape(*dims):
    return jax.ShapeDtypeStruct(dims, f32)


def limit(megabytes):
    return pltpu.CompilerParams(vmem_limit_bytes=megabytes << 20)


def cost(flops, size):
    return pl.CostEstimate(flops=flops, bytes_accessed=size, transcendentals=0)


def divisor(number, most):
    return max(c for c in range(1, min(number, most) + 1) if number % c == 0)


def power_of_two(number):
    return number & (number - 1) == 0


def partner(index, step, count):
    return index ^ step if power_of_two(count) else (index + step) % count


def source_of(index, step, count):
    return index ^ step if power_of_two(count) else (index - step) % count


def line_order(outer):
    return [0, *range(outer // 2, outer), *range(1, outer // 2)]


def turn(step, ways):
    return {1: 2, 2: 1}.get(step % ways, step % ways)


def particles_kernel(inner, outer, *refs):
    given, messages = refs[:9], refs[9 : 9 + outer]
    own, lists, held, sems = refs[9 + outer], refs[10 + outer : 12 + outer], refs[12 + outer : -1], refs[-1]
    targets = (*held, own.at[0:3], own.at[3:4], own.at[4:5], *lists)
    sources = (*given[0:4], given[4].at[0], *given[5:9])
    copies = [
        pltpu.make_async_copy(a, b, sems.at[i]) for i, (a, b) in enumerate(zip(sources, targets))
    ]
    for copy in copies:
        copy.start()
    for copy in copies[0:4]:
        copy.wait()
    pos, strength, radius, points = held
    tiles = pos.shape[1] // LANES
    angles = points.shape[2]
    src = lax.axis_index("src")
    core = radius[...] * radius[...]
    for step, message in zip(line_order(outer), messages):
        plane = partner(src // inner, step, outer) * inner + src % inner
        for k in range(tiles):
            part = slice(k * LANES, (k + 1) * LANES)
            message[k, 0:3, :] = pos[:, part]
            message[k, 3:6, :] = strength[:, part]
            message[k, 6:7, :] = core[:, part]
            message[k, 7:8, :] = jnp.zeros((1, LANES), f32)
        for m in range(3):
            message[m, 7:8, 0:angles] = points[m, pl.ds(plane, 1), :]
    for copy in copies[4:]:
        copy.wait()


def edges_kernel(own, own_source, own_target, after, message):
    angles = own.shape[1]
    blocks = own_source.shape[2]
    total = angles * lax.axis_size("tgt")
    half = ROWS // 2
    for c in range(5):
        message[c, :, 0:angles] = jnp.transpose(own[c])[0:ROWS, :]
        message[c, :, angles:LANES] = jnp.zeros((ROWS, LANES - angles), f32)
        message[6 + c, 0:half, :] = own[c, 0:half]
        message[6 + c, half:ROWS, :] = own[c, angles - half : angles]
    message[5] = jnp.full((ROWS, LANES), -1.0, f32)
    q = own_source[0]
    row = (q // angles) * total + lax.axis_index("tgt") * angles + q % angles
    message[5, 0:1, 0:blocks] = row.astype(f32)
    message[5, 1:2, 0:blocks] = own_target[0].astype(f32)


def still_kernel(ways, *refs):
    messages = refs[:ways]
    own, lists, after, grid, picks, inner_cells, index, placed, source, sem = refs[ways:]
    copy = pltpu.make_async_copy(lists, source, sem)
    copy.start()
    angles = own.shape[1]
    height = angles + ROWS
    blocks = lists.shape[2]
    me = lax.axis_index("tgt")
    for step, message in enumerate(messages):
        placed[source_of(me, step, ways)] = message[...]

    for c in range(5):
        inner_cells[c] = jnp.concatenate(
            [placed[t, c, :, 0:angles] for t in range(ways)], axis=1
        )

    shaped = index.shape
    name = (me * blocks + lax.broadcasted_iota(jnp.int32, shaped, 0)).astype(f32)
    lane = lax.broadcasted_iota(jnp.int32, shaped, 1).astype(f32)
    row = jnp.full(shaped, -1.0, f32)
    slot = jnp.zeros(shaped, f32)
    for step, message in enumerate(messages):
        match = message[5, 1:2, :] == name
        row = jnp.maximum(row, jnp.where(match, message[5, 0:1, :], -1.0))
        slot = jnp.maximum(slot, jnp.where(match, lane + float(step * picks.shape[0]), 0.0))
    row = jnp.max(row, axis=1, keepdims=True)
    slot = jnp.max(slot, axis=1, keepdims=True)
    index[...] = jnp.where(lane < 1.0, row, slot).astype(jnp.int32)

    upper = lax.broadcasted_iota(jnp.int32, (ROWS, LANES), 0) < ROWS // 2
    east = lax.rem(me + 1, ways)
    west = lax.rem(me + ways - 1, ways)
    cells = [
        jnp.concatenate(
            [own[c], jnp.where(upper, placed[east, 6 + c], placed[west, 6 + c])], axis=0
        )
        for c in range(5)
    ]
    field, local_swirl, local_diff = cells[0:3], cells[3], cells[4]
    lane = lax.broadcasted_iota(jnp.int32, (height, LANES), 1)
    for counter in range(SUBSTEPS):
        transport = 0.5 * (local_swirl + swirl_gain * field[2])
        renewed = []
        for m in range(3):
            center = field[m]
            eastern = pltpu.roll(center, height - 1, 0)
            western = pltpu.roll(center, 1, 0)
            outward = jnp.where(lane == LANES - 1, 0.0, pltpu.roll(center, LANES - 1, 1))
            inward = jnp.where(lane == 0, 0.0, pltpu.roll(center, 1, 1))
            renewed.append(
                center
                + local_diff * (eastern + western + outward + inward - 4.0 * center)
                - transport * (eastern - western)
            )
        field = renewed
    for m in range(3):
        grid[m] = field[m][0:angles]
    picks[...] = jnp.zeros(picks.shape, f32)
    copy.wait()
    for i in range(blocks):
        q = source[0, 0, i]
        picks[i : i + 1, :] = grid[q // angles, pl.ds(q % angles, 1), :]


def join_kernel(outer, *refs):
    messages, (after, particles) = refs[:outer], refs[outer:]
    tiles = messages[0].shape[0]
    for i, message in enumerate(messages):
        particles[i * tiles : (i + 1) * tiles] = message[...]


def columns_kernel(ways, outer, particles, columns, tiled):
    tiles = particles.shape[0] // outer
    angles = columns.shape[1] // ways
    order = line_order(outer)
    me = lax.axis_index("tgt")
    tiled[...] = jnp.zeros(tiled.shape, f32)
    for step in range(ways):
        place = source_of(me, turn(step, ways), ways)
        first = order.index(step) * tiles
        for m in range(3):
            tiled[pl.ds(place * ROWS + m, 1), :] = particles[first + m, 7:8, :]
    turned = jnp.transpose(tiled[...])
    for t in range(ways):
        for m in range(3):
            lane = t * ROWS + m
            columns[m, t * angles : (t + 1) * angles, :] = jnp.broadcast_to(
                turned[0:angles, lane : lane + 1], (angles, LANES)
            )


def pairs_kernel(scale, particles, columns, result, crossed, sums):
    tiles = particles.shape[0]
    angles = columns.shape[1]
    parts = angles // LANES
    together = divisor(angles // ROWS, TOGETHER)
    sets = divisor(angles // ROWS // together, SETS)
    unroll = divisor(tiles, 12)
    for k in range(tiles):
        px, py, pz, sx, sy, sz = [particles[k, r : r + 1, :] for r in range(6)]
        crossed[k, 0:1, :] = sy * pz - sz * py
        crossed[k, 1:2, :] = sz * px - sx * pz
        crossed[k, 2:3, :] = sx * py - sy * px
    sums[...] = jnp.zeros(sums.shape, f32)
    diagonal = lax.broadcasted_iota(jnp.int32, (ROWS, LANES), 1) - lax.broadcasted_iota(
        jnp.int32, (ROWS, LANES), 0
    )

    def one_set(group):
        rows = [
            pl.ds(pl.multiple_of((group + i) * ROWS, ROWS), ROWS) for i in range(together)
        ]
        targets = [[columns[m, r, :] for m in range(3)] for r in rows]

        def absorb(step, carried):
            carried = list(carried)
            for u in range(unroll):
                tile = step * unroll + u
                px, py, pz, sx, sy, sz, cc = [particles[tile, r : r + 1, :] for r in range(7)]
                qx, qy, qz = [crossed[tile, r : r + 1, :] for r in range(3)]
                for i, (tx, ty, tz) in enumerate(targets):
                    dx = tx - px
                    dy = ty - py
                    dz = tz - pz
                    inverse = lax.rsqrt(dx * dx + dy * dy + (dz * dz + cc))
                    weight = inverse * inverse * inverse
                    for r, along in enumerate((sx, sy, sz, qx, qy, qz)):
                        carried[6 * i + r] += weight * along
            return tuple(carried)

        carried = (jnp.zeros((ROWS, LANES), f32),) * (6 * together)
        if tiles == unroll:
            carried = absorb(0, carried)
        else:
            carried = lax.fori_loop(0, tiles // unroll, absorb, carried)
        for i, (tx, ty, tz) in enumerate(targets):
            ax, ay, az, bx, by, bz = carried[6 * i : 6 * i + 6]
            speed = (ay * tz - az * ty - bx, az * tx - ax * tz - by, ax * ty - ay * tx - bz)
            here = (group + i) * ROWS
            mask = diagonal == here % LANES
            for m in range(3):
                value = jnp.sum(speed[m], axis=1, keepdims=True)
                sums[m * parts + here // LANES] += jnp.where(mask, value, 0.0)

    def some_sets(index, unused):
        for i in range(sets):
            one_set((index * sets + i) * together)
        return unused

    lax.fori_loop(0, angles // (sets * together * ROWS), some_sets, 0)
    for r in range(3 * parts):
        result[r : r + 1, :] += scale * jnp.sum(sums[r], axis=0, keepdims=True)


def near_kernel(scale, ways, outer, particles, result, columns, tiled, *scratch):
    columns_kernel(ways, outer, particles, columns, tiled)
    result[...] = jnp.zeros(result.shape, f32)
    pairs_kernel(scale, particles, columns, result, *scratch)


def far_kernel(scale, particles, columns, near_sum, picks, result, *scratch):
    rows = 3 * columns.shape[1] // LANES
    result[...] = jnp.zeros(result.shape, f32)
    result[0:rows, :] = near_sum[0:rows, :]
    result[rows : rows + picks.shape[0], :] = picks[...]
    pairs_kernel(scale, particles, columns, result, *scratch)


def wall_kernel(ways, *refs):
    partials = refs[:ways]
    (still, inner_cells, strength, index, wall, grid, new_strength,
     fixed, picked, rows, sem) = refs[ways:]
    angles = grid.shape[2]
    total = angles * ways
    parts = total // LANES
    rows_of = 3 * parts
    slots = picked.shape[0] // ways
    me = lax.axis_index("tgt")
    copy = pltpu.make_async_copy(index, rows, sem)
    copy.start()
    for step, partial in enumerate(partials):
        picked[step * slots : (step + 1) * slots, :] = partial[rows_of : rows_of + slots, :]
    added = partials[0][0:rows_of, :]
    for partial in partials[1:]:
        added = added + partial[0:rows_of, :]
    speed = [
        jnp.concatenate([added[r : r + 1] for r in range(m * parts, (m + 1) * parts)], axis=1)
        for m in range(3)
    ]
    stacked = jnp.concatenate(speed + [jnp.zeros((ROWS - 3, total), f32)], axis=0)
    own = pltpu.roll(stacked, total - me * angles, 1)
    for m in range(3):
        wall[m] = own[m : m + 1, 0:angles]

    first = lax.broadcasted_iota(jnp.int32, (ROWS, total), 0) == 0
    field = [inner_cells[m] for m in range(3)]
    local_swirl = inner_cells[3]
    local_diff = inner_cells[4]
    for counter in range(SUBSTEPS):
        transport = 0.5 * (local_swirl + swirl_gain * field[2])
        renewed = []
        for m in range(3):
            center = field[m]
            eastern = pltpu.roll(center, total - 1, 1)
            western = pltpu.roll(center, 1, 1)
            outward = pltpu.roll(center, ROWS - 1, 0)
            inward = jnp.where(first, speed[m], pltpu.roll(center, 1, 0))
            renewed.append(
                center
                + local_diff * (eastern + western + outward + inward - 4.0 * center)
                - transport * (eastern - western)
            )
        field = renewed
    stacked = jnp.concatenate(field + [jnp.zeros((LANES - 3 * ROWS, total), f32)], axis=0)
    for k in range(parts):
        turned = jnp.transpose(stacked[:, k * LANES : (k + 1) * LANES])
        for m in range(3):
            place = m * total + k * LANES
            fixed[place : place + LANES, :] = turned if m == 0 else pltpu.roll(
                turned, LANES - m * ROWS, 1
            )
    near = lax.broadcasted_iota(jnp.int32, (angles, LANES), 1) < SUBSTEPS
    for m in range(3):
        place = pl.multiple_of(m * total + me * angles, ROWS)
        grid[0, m] = jnp.where(near, fixed[pl.ds(place, angles), :], still[m])
    near = lax.broadcasted_iota(jnp.int32, (1, LANES), 1) < SUBSTEPS
    pieces = strength.shape[1] // LANES
    copy.wait()
    for b in range(3 * pieces):
        q = rows[b, 0]
        c, part = b // pieces, slice((b % pieces) * LANES, (b % pieces + 1) * LANES)
        row = jnp.where(
            near, fixed[pl.ds(jnp.maximum(q, 0), 1), :], picked[pl.ds(rows[b, 1], 1), :]
        )
        new_strength[c : c + 1, part] = jnp.where(q >= 0, row, strength[c : c + 1, part])


def send(block, pairs):
    return lax.ppermute(block, ("src", "tgt"), pairs)


def on_device(
    particle_position,
    particle_strength,
    core_radius,
    boundary_points,
    vorticity,
    swirl,
    diffusivity,
    intersection_source,
    intersection_target,
):
    sources = lax.axis_size("src")
    ways = lax.axis_size("tgt")
    planes, comps, angles, radial = vorticity.shape
    per_device = particle_position.shape[1]
    tiles = per_device // LANES
    blocks = intersection_source.shape[2]
    inner = 2 if sources % 2 == 0 else 1
    outer = sources // inner
    total = angles * ways
    scale = 1.6 / (4.0 * math.pi * math.sqrt(per_device * ways * sources))

    def pairs(move):
        found = []
        for s in range(sources):
            for t in range(ways):
                o, i, u = move(s // inner, s % inner, t)
                found.append((s * ways + t, (o * inner + i) * ways + u))
        return found

    def over_tgt(block, step):
        return send(block, pairs(lambda o, i, t: (o, i, partner(t, step, ways))))

    given = (
        particle_position, particle_strength, core_radius, boundary_points,
        vorticity, swirl, diffusivity, intersection_source, intersection_target,
    )
    *messages, own, source, target = pl.pallas_call(
        functools.partial(particles_kernel, inner, outer),
        out_shape=(shape(tiles, ROWS, LANES),) * outer + (
            shape(5, angles, LANES),
            jax.ShapeDtypeStruct(intersection_source.shape, jnp.int32),
            jax.ShapeDtypeStruct(intersection_target.shape, jnp.int32),
        ),
        in_specs=[hbm()] * 9,
        out_specs=(vmem(),) * (outer + 3),
        scratch_shapes=[pltpu.VMEM(a.shape, f32) for a in given[0:4]]
        + [pltpu.SemaphoreType.DMA((9,))],
        compiler_params=limit(4),
        name="particles",
    )(*stay(*given))
    line = [messages[0]] + [
        send(
            message,
            pairs(lambda o, i, t: (partner(o, k, outer), i, partner(t, turn(k, ways), ways))),
        )
        for k, message in zip(line_order(outer)[1:], messages[1:])
    ]

    edges = pl.pallas_call(
        edges_kernel,
        out_shape=shape(11, ROWS, LANES),
        in_specs=[vmem()] * 4,
        out_specs=vmem(),
        compiler_params=limit(4),
        name="edges",
    )(own, source, target, line[1])
    around = [edges] + [over_tgt(edges, k) for k in range(1, ways)]

    near = pl.pallas_call(
        functools.partial(join_kernel, outer),
        out_shape=shape(outer * tiles, ROWS, LANES),
        in_specs=[vmem()] * (outer + 1),
        out_specs=vmem(),
        compiler_params=limit(8),
        name="join",
    )(*line, edges)
    far = send(near, pairs(lambda o, i, t: (o, inner - 1 - i, t)))

    rows = 3 * total // LANES
    slots = blocks
    scratch = [
        pltpu.VMEM((outer * tiles, ROWS, LANES), f32),
        pltpu.VMEM((rows, ROWS, LANES), f32),
    ]
    near_sum, columns = pl.pallas_call(
        functools.partial(near_kernel, scale, ways, outer),
        out_shape=(shape(-(-rows // ROWS) * ROWS, LANES), shape(3, total, LANES)),
        in_specs=[vmem()],
        out_specs=(vmem(), vmem()),
        scratch_shapes=[pltpu.VMEM((LANES, LANES), f32)] + scratch,
        compiler_params=limit(12),
        cost_estimate=cost(1 << 31, 1 << 10),
        name="near",
    )(near)
    still, picks, inner_cells, index = pl.pallas_call(
        functools.partial(still_kernel, ways),
        out_shape=(
            shape(3, angles, LANES),
            shape(slots, LANES),
            shape(5, ROWS, total),
            jax.ShapeDtypeStruct((16 * ((blocks + 15) // 16), LANES), jnp.int32),
        ),
        in_specs=[vmem()] * (ways + 3),
        out_specs=(vmem(),) * 4,
        scratch_shapes=[
            pltpu.VMEM((ways,) + edges.shape, f32),
            pltpu.SMEM(source.shape, jnp.int32),
            pltpu.SemaphoreType.DMA,
        ],
        compiler_params=limit(8),
        name="still",
    )(*around, own, source, near_sum)
    partial_sum = pl.pallas_call(
        functools.partial(far_kernel, scale),
        out_shape=shape(-(-(rows + blocks) // ROWS) * ROWS, LANES),
        in_specs=[vmem()] * 4,
        out_specs=vmem(),
        scratch_shapes=scratch,
        compiler_params=limit(12),
        cost_estimate=cost(1 << 31, 1 << 10),
        name="far",
    )(far, columns, near_sum, picks)
    partials = [partial_sum] + [over_tgt(partial_sum, k) for k in range(1, ways)]

    wall, grid, new_strength = pl.pallas_call(
        functools.partial(wall_kernel, ways),
        out_shape=(shape(3, planes, angles), shape(*vorticity.shape), shape(3, per_device)),
        in_specs=[vmem()] * (ways + 4),
        out_specs=(vmem(),) * 3,
        scratch_shapes=[
            pltpu.VMEM((3 * total, LANES), f32),
            pltpu.VMEM((slots * ways, LANES), f32),
            pltpu.SMEM(index.shape, jnp.int32),
            pltpu.SemaphoreType.DMA,
        ],
        compiler_params=limit(16),
        name="wall",
    )(*partials, still, inner_cells, particle_strength, index)
    return (wall, grid, new_strength)


def solution(mesh):
    in_specs = (
        P(None, ("src", "tgt")),
        P(None, ("src", "tgt")),
        P(None, ("src", "tgt")),
        P(None, None, "tgt"),
        P("src", None, "tgt", None),
        P("src", "tgt", None),
        P("src", "tgt", None),
        P("src", "tgt", None),
        P("src", "tgt", None),
    )
    out_specs = (P(None, "src", "tgt"), P("src", None, "tgt", None), P(None, ("src", "tgt")))
    return jax.shard_map(
        on_device, mesh=mesh, in_specs=in_specs, out_specs=out_specs, check_vma=False
    )
```

```python
import functools
import math

import jax
import jax.numpy as jnp
from jax import lax
from jax.experimental import pallas as pl
from jax.experimental.pallas import tpu as pltpu
from jax.sharding import PartitionSpec as P

SUBSTEPS = 3
LANES = 128
ROWS = 8
DEEP = 256
CHANNELS = 32
swirl_gain = 0.2
f32 = jnp.float32
bf16 = jnp.bfloat16


def vmem():
    return pl.BlockSpec(memory_space=pltpu.VMEM)


def smem():
    return pl.BlockSpec(memory_space=pltpu.SMEM)


def hbm():
    return pl.BlockSpec(memory_space=pltpu.HBM)


def stay(*arrays):
    return [pltpu.with_memory_space_constraint(a, pltpu.HBM) for a in arrays]


def shape(*dims):
    return jax.ShapeDtypeStruct(dims, f32)


def limit(megabytes):
    return pltpu.CompilerParams(vmem_limit_bytes=megabytes << 20)


def cost(flops, size):
    return pl.CostEstimate(flops=flops, bytes_accessed=size, transcendentals=0)


def divisor(number, most):
    return max(c for c in range(1, min(number, most) + 1) if number % c == 0)


def power_of_two(number):
    return number & (number - 1) == 0


def partner(index, step, count):
    return index ^ step if power_of_two(count) else (index + step) % count


def source_of(index, step, count):
    return index ^ step if power_of_two(count) else (index - step) % count


def line_order(outer):
    return [0, *range(outer // 2, outer), *range(1, outer // 2)]


def tgt_order(ways):
    return [0, *reversed(range(1, ways))]


def turn(step, ways):
    return {1: 2, 2: 3, 3: 1}.get(step % ways, step % ways)


def particles_kernel(inner, outer, *refs):
    given, messages = refs[:9], refs[9 : 9 + outer]
    own, lists, held, sems = refs[9 + outer], refs[10 + outer : 12 + outer], refs[12 + outer : -1], refs[-1]
    targets = (*held, own.at[0:3], own.at[3:4], own.at[4:5], *lists)
    sources = (*given[0:4], given[4].at[0], *given[5:9])
    copies = [
        pltpu.make_async_copy(a, b, sems.at[i]) for i, (a, b) in enumerate(zip(sources, targets))
    ]
    for copy in copies:
        copy.start()
    for copy in copies[0:4]:
        copy.wait()
    pos, strength, radius, points = held
    tiles = pos.shape[1] // LANES
    angles = points.shape[2]
    src = lax.axis_index("src")
    core = radius[...] * radius[...]
    for step, message in zip(line_order(outer), messages):
        plane = partner(src // inner, step, outer) * inner + src % inner
        for k in range(tiles):
            part = slice(k * LANES, (k + 1) * LANES)
            message[k, 0:3, :] = pos[:, part]
            message[k, 3:6, :] = strength[:, part]
            message[k, 6:7, :] = core[:, part]
            message[k, 7:8, :] = jnp.zeros((1, LANES), f32)
        for m in range(3):
            message[m, 7:8, 0:angles] = points[m, pl.ds(plane, 1), :]
    for copy in copies[4:]:
        copy.wait()


def edges_kernel(own, own_source, own_target, after, message):
    angles = own.shape[1]
    blocks = own_source.shape[2]
    total = angles * lax.axis_size("tgt")
    half = ROWS // 2
    for c in range(5):
        message[c, :, 0:angles] = jnp.transpose(own[c])[0:ROWS, :]
        message[c, :, angles:LANES] = jnp.zeros((ROWS, LANES - angles), f32)
        message[6 + c, 0:half, :] = own[c, 0:half]
        message[6 + c, half:ROWS, :] = own[c, angles - half : angles]
    message[5] = jnp.full((ROWS, LANES), -1.0, f32)
    q = own_source[0]
    row = (q // angles) * total + lax.axis_index("tgt") * angles + q % angles
    message[5, 0:1, 0:blocks] = row.astype(f32)
    message[5, 1:2, 0:blocks] = own_target[0].astype(f32)


def still_kernel(ways, *refs):
    messages = refs[:ways]
    own, lists, after, grid, picks, inner_cells, index, placed, source, sem = refs[ways:]
    copy = pltpu.make_async_copy(lists, source, sem)
    copy.start()
    angles = own.shape[1]
    height = angles + ROWS
    blocks = lists.shape[2]
    me = lax.axis_index("tgt")
    for step, message in zip(tgt_order(ways), messages):
        placed[source_of(me, step, ways)] = message[...]

    for c in range(5):
        inner_cells[c] = jnp.concatenate(
            [placed[t, c, :, 0:angles] for t in range(ways)], axis=1
        )

    shaped = index.shape
    name = (me * blocks + lax.broadcasted_iota(jnp.int32, shaped, 0)).astype(f32)
    lane = lax.broadcasted_iota(jnp.int32, shaped, 1).astype(f32)
    row = jnp.full(shaped, -1.0, f32)
    slot = jnp.zeros(shaped, f32)
    for step, message in enumerate(messages):
        match = message[5, 1:2, :] == name
        row = jnp.maximum(row, jnp.where(match, message[5, 0:1, :], -1.0))
        slot = jnp.maximum(slot, jnp.where(match, lane + float(step * picks.shape[0]), 0.0))
    row = jnp.max(row, axis=1, keepdims=True)
    slot = jnp.max(slot, axis=1, keepdims=True)
    index[...] = jnp.where(lane < 1.0, row, slot).astype(jnp.int32)

    upper = lax.broadcasted_iota(jnp.int32, (ROWS, LANES), 0) < ROWS // 2
    east = lax.rem(me + 1, ways)
    west = lax.rem(me + ways - 1, ways)
    cells = [
        jnp.concatenate(
            [own[c], jnp.where(upper, placed[east, 6 + c], placed[west, 6 + c])], axis=0
        )
        for c in range(5)
    ]
    field, local_swirl, local_diff = cells[0:3], cells[3], cells[4]
    lane = lax.broadcasted_iota(jnp.int32, (height, LANES), 1)
    for counter in range(SUBSTEPS):
        transport = 0.5 * (local_swirl + swirl_gain * field[2])
        renewed = []
        for m in range(3):
            center = field[m]
            eastern = pltpu.roll(center, height - 1, 0)
            western = pltpu.roll(center, 1, 0)
            outward = jnp.where(lane == LANES - 1, 0.0, pltpu.roll(center, LANES - 1, 1))
            inward = jnp.where(lane == 0, 0.0, pltpu.roll(center, 1, 1))
            renewed.append(
                center
                + local_diff * (eastern + western + outward + inward - 4.0 * center)
                - transport * (eastern - western)
            )
        field = renewed
    for m in range(3):
        grid[m] = field[m][0:angles]
    picks[...] = jnp.zeros(picks.shape, f32)
    copy.wait()
    for i in range(blocks):
        q = source[0, 0, i]
        picks[i : i + 1, :] = grid[q // angles, pl.ds(q % angles, 1), :]


def join_kernel(outer, *refs):
    messages, (after, particles) = refs[:outer], refs[outer:]
    tiles = messages[0].shape[0]
    for i, message in enumerate(messages):
        particles[i * tiles : (i + 1) * tiles] = message[...]


def columns_kernel(ways, outer, particles, columns, along, tiled):
    tiles = particles.shape[0] // outer
    angles = columns.shape[1] // ways
    order = line_order(outer)
    me = lax.axis_index("tgt")
    tiled[...] = jnp.zeros(tiled.shape, f32)
    for step in range(ways):
        place = source_of(me, turn(step, ways), ways)
        first = order.index(step) * tiles
        for m in range(3):
            tiled[pl.ds(place * ROWS + m, 1), :] = particles[first + m, 7:8, :]
    turned = jnp.transpose(tiled[...])
    for t in range(ways):
        for m in range(3):
            lane = t * ROWS + m
            columns[m, t * angles : (t + 1) * angles, :] = jnp.broadcast_to(
                turned[0:angles, lane : lane + 1], (angles, LANES)
            )
    along[...] = jnp.concatenate(
        [tiled[t * ROWS : (t + 1) * ROWS, 0:angles] for t in range(ways)], axis=1
    )


def three_parts(value):
    high = value.astype(bf16)
    rest = value - high.astype(f32)
    middle = rest.astype(bf16)
    return high, middle, (rest - middle.astype(f32)).astype(bf16)


def pairs_kernel(scale, particles, columns, along, result, channels, weights):
    angles = columns.shape[1]
    parts = angles // LANES
    tall = min(angles, 2 * LANES)
    wide = DEEP // LANES
    steps = particles.shape[0] // wide
    for k in range(particles.shape[0]):
        px, py, pz, sx, sy, sz = [particles[k, r : r + 1, :] for r in range(6)]
        moved = jnp.concatenate(
            [sx, sy, sz, sy * pz - sz * py, sz * px - sx * pz, sx * py - sy * px]
            + [jnp.zeros((2, LANES), f32)],
            axis=0,
        )
        pieces = [p.astype(f32) for p in three_parts(moved)]
        stacked = jnp.concatenate(pieces + [jnp.zeros((CHANNELS - 24, LANES), f32)], axis=0)
        for third in range(3):
            start = third * DEEP + (k % wide) * LANES
            channels[k // wide, :, start : start + LANES] = stacked.astype(bf16)

    for block in range(angles // tall):

        def absorb(step, buffer, total):
            for low in range(0, tall, 16):
                rows = slice(block * tall + low, block * tall + low + 16)
                tx, ty, tz = [columns[m, rows, :] for m in range(3)]
                for half in range(wide):
                    tile = step * wide + half
                    px, py, pz = [particles[tile, r : r + 1, :] for r in range(3)]
                    dx = tx - px
                    dy = ty - py
                    dz = tz - pz
                    inverse = lax.rsqrt(dx * dx + dy * dy + (dz * dz + particles[tile, 6:7, :]))
                    for third, piece in enumerate(three_parts(inverse * inverse * inverse)):
                        start = third * DEEP + half * LANES
                        weights[buffer, low : low + 16, start : start + LANES] = piece
            return total + lax.dot_general(
                weights[buffer], channels[step], (((1,), (1,)), ((), ())),
                preferred_element_type=f32,
            )

        total = jnp.zeros((tall, CHANNELS), f32)
        if steps <= 8:
            for step in range(steps):
                total = absorb(step, step % 2, total)
        else:
            total = lax.fori_loop(0, steps, lambda step, t: absorb(step, 0, t), total)
        total = jnp.transpose(total)
        ax, ay, az, bx, by, bz = [
            total[r : r + 1] + total[8 + r : 9 + r] + total[16 + r : 17 + r] for r in range(6)
        ]
        tx, ty, tz = [along[m : m + 1, block * tall : (block + 1) * tall] for m in range(3)]
        speed = (ay * tz - az * ty - bx, az * tx - ax * tz - by, ax * ty - ay * tx - bz)
        for m in range(3):
            for k in range(tall // LANES):
                r = m * parts + block * (tall // LANES) + k
                result[r : r + 1, :] += scale * speed[m][:, k * LANES : (k + 1) * LANES]


def near_kernel(scale, ways, outer, particles, result, columns, along, tiled, *scratch):
    columns_kernel(ways, outer, particles, columns, along, tiled)
    result[...] = jnp.zeros(result.shape, f32)
    pairs_kernel(scale, particles, columns, along, result, *scratch)


def far_kernel(scale, particles, columns, along, near_sum, picks, result, *scratch):
    rows = 3 * columns.shape[1] // LANES
    result[...] = jnp.zeros(result.shape, f32)
    result[0:rows, :] = near_sum[0:rows, :]
    result[rows : rows + picks.shape[0], :] = picks[...]
    pairs_kernel(scale, particles, columns, along, result, *scratch)


def wall_kernel(ways, *refs):
    partials = refs[:ways]
    (still, inner_cells, strength, index, wall, grid, new_strength,
     fixed, picked, rows, sem) = refs[ways:]
    angles = grid.shape[2]
    total = angles * ways
    parts = total // LANES
    rows_of = 3 * parts
    slots = picked.shape[0] // ways
    me = lax.axis_index("tgt")
    copy = pltpu.make_async_copy(index, rows, sem)
    copy.start()
    for step, partial in enumerate(partials):
        picked[step * slots : (step + 1) * slots, :] = partial[rows_of : rows_of + slots, :]
    added = partials[0][0:rows_of, :]
    for partial in partials[1:]:
        added = added + partial[0:rows_of, :]
    speed = [
        jnp.concatenate([added[r : r + 1] for r in range(m * parts, (m + 1) * parts)], axis=1)
        for m in range(3)
    ]
    stacked = jnp.concatenate(speed + [jnp.zeros((ROWS - 3, total), f32)], axis=0)
    own = pltpu.roll(stacked, total - me * angles, 1)
    for m in range(3):
        wall[m] = own[m : m + 1, 0:angles]

    first = lax.broadcasted_iota(jnp.int32, (ROWS, total), 0) == 0
    field = [inner_cells[m] for m in range(3)]
    local_swirl = inner_cells[3]
    local_diff = inner_cells[4]
    for counter in range(SUBSTEPS):
        transport = 0.5 * (local_swirl + swirl_gain * field[2])
        renewed = []
        for m in range(3):
            center = field[m]
            eastern = pltpu.roll(center, total - 1, 1)
            western = pltpu.roll(center, 1, 1)
            outward = pltpu.roll(center, ROWS - 1, 0)
            inward = jnp.where(first, speed[m], pltpu.roll(center, 1, 0))
            renewed.append(
                center
                + local_diff * (eastern + western + outward + inward - 4.0 * center)
                - transport * (eastern - western)
            )
        field = renewed
    stacked = jnp.concatenate(field + [jnp.zeros((LANES - 3 * ROWS, total), f32)], axis=0)
    for k in range(parts):
        turned = jnp.transpose(stacked[:, k * LANES : (k + 1) * LANES])
        for m in range(3):
            place = m * total + k * LANES
            fixed[place : place + LANES, :] = turned if m == 0 else pltpu.roll(
                turned, LANES - m * ROWS, 1
            )
    near = lax.broadcasted_iota(jnp.int32, (angles, LANES), 1) < SUBSTEPS
    for m in range(3):
        place = pl.multiple_of(m * total + me * angles, ROWS)
        grid[0, m] = jnp.where(near, fixed[pl.ds(place, angles), :], still[m])
    near = lax.broadcasted_iota(jnp.int32, (1, LANES), 1) < SUBSTEPS
    pieces = strength.shape[1] // LANES
    copy.wait()
    for b in range(3 * pieces):
        q = rows[b, 0]
        c, part = b // pieces, slice((b % pieces) * LANES, (b % pieces + 1) * LANES)
        row = jnp.where(
            near, fixed[pl.ds(jnp.maximum(q, 0), 1), :], picked[pl.ds(rows[b, 1], 1), :]
        )
        new_strength[c : c + 1, part] = jnp.where(q >= 0, row, strength[c : c + 1, part])


def send(block, pairs):
    return lax.ppermute(block, ("src", "tgt"), pairs)


def on_device(
    particle_position,
    particle_strength,
    core_radius,
    boundary_points,
    vorticity,
    swirl,
    diffusivity,
    intersection_source,
    intersection_target,
):
    sources = lax.axis_size("src")
    ways = lax.axis_size("tgt")
    planes, comps, angles, radial = vorticity.shape
    per_device = particle_position.shape[1]
    tiles = per_device // LANES
    blocks = intersection_source.shape[2]
    inner = 2 if sources % 2 == 0 else 1
    outer = sources // inner
    total = angles * ways
    scale = 1.6 / (4.0 * math.pi * math.sqrt(per_device * ways * sources))

    def pairs(move):
        found = []
        for s in range(sources):
            for t in range(ways):
                o, i, u = move(s // inner, s % inner, t)
                found.append((s * ways + t, (o * inner + i) * ways + u))
        return found

    def over_tgt(block, step):
        return send(block, pairs(lambda o, i, t: (o, i, partner(t, step, ways))))

    given = (
        particle_position, particle_strength, core_radius, boundary_points,
        vorticity, swirl, diffusivity, intersection_source, intersection_target,
    )
    *messages, own, source, target = pl.pallas_call(
        functools.partial(particles_kernel, inner, outer),
        out_shape=(shape(tiles, ROWS, LANES),) * outer + (
            shape(5, angles, LANES),
            jax.ShapeDtypeStruct(intersection_source.shape, jnp.int32),
            jax.ShapeDtypeStruct(intersection_target.shape, jnp.int32),
        ),
        in_specs=[hbm()] * 9,
        out_specs=(vmem(),) * (outer + 3),
        scratch_shapes=[pltpu.VMEM(a.shape, f32) for a in given[0:4]]
        + [pltpu.SemaphoreType.DMA((9,))],
        compiler_params=limit(4),
        name="particles",
    )(*stay(*given))
    line = [messages[0]] + [
        send(
            message,
            pairs(lambda o, i, t: (partner(o, k, outer), i, partner(t, turn(k, ways), ways))),
        )
        for k, message in zip(line_order(outer)[1:], messages[1:])
    ]

    edges = pl.pallas_call(
        edges_kernel,
        out_shape=shape(11, ROWS, LANES),
        in_specs=[vmem()] * 4,
        out_specs=vmem(),
        compiler_params=limit(4),
        name="edges",
    )(own, source, target, line[1])
    steps = tgt_order(ways)
    around = [edges] + [over_tgt(edges, k) for k in steps[1:]]

    near = pl.pallas_call(
        functools.partial(join_kernel, outer),
        out_shape=shape(outer * tiles, ROWS, LANES),
        in_specs=[vmem()] * (outer + 1),
        out_specs=vmem(),
        compiler_params=limit(8),
        name="join",
    )(*line, edges)
    far = send(near, pairs(lambda o, i, t: (o, inner - 1 - i, t)))

    rows = 3 * total // LANES
    slots = blocks
    scratch = [
        pltpu.VMEM((outer * tiles * LANES // DEEP, CHANNELS, 3 * DEEP), bf16),
        pltpu.VMEM((2, min(total, 2 * LANES), 3 * DEEP), bf16),
    ]
    near_sum, columns, along = pl.pallas_call(
        functools.partial(near_kernel, scale, ways, outer),
        out_shape=(
            shape(-(-rows // ROWS) * ROWS, LANES),
            shape(3, total, LANES),
            shape(ROWS, total),
        ),
        in_specs=[vmem()],
        out_specs=(vmem(),) * 3,
        scratch_shapes=[pltpu.VMEM((LANES, LANES), f32)] + scratch,
        compiler_params=limit(12),
        cost_estimate=cost(1 << 31, 1 << 10),
        name="near",
    )(near)
    still, picks, inner_cells, index = pl.pallas_call(
        functools.partial(still_kernel, ways),
        out_shape=(
            shape(3, angles, LANES),
            shape(slots, LANES),
            shape(5, ROWS, total),
            jax.ShapeDtypeStruct((16 * ((blocks + 15) // 16), LANES), jnp.int32),
        ),
        in_specs=[vmem()] * (ways + 3),
        out_specs=(vmem(),) * 4,
        scratch_shapes=[
            pltpu.VMEM((ways,) + edges.shape, f32),
            pltpu.SMEM(source.shape, jnp.int32),
            pltpu.SemaphoreType.DMA,
        ],
        compiler_params=limit(8),
        name="still",
    )(*around, own, source, near_sum)
    partial_sum = pl.pallas_call(
        functools.partial(far_kernel, scale),
        out_shape=shape(-(-(rows + blocks) // ROWS) * ROWS, LANES),
        in_specs=[vmem()] * 5,
        out_specs=vmem(),
        scratch_shapes=scratch,
        compiler_params=limit(12),
        cost_estimate=cost(1 << 31, 1 << 10),
        name="far",
    )(far, columns, along, near_sum, picks)
    partials = [partial_sum] + [over_tgt(partial_sum, k) for k in steps[1:]]

    wall, grid, new_strength = pl.pallas_call(
        functools.partial(wall_kernel, ways),
        out_shape=(shape(3, planes, angles), shape(*vorticity.shape), shape(3, per_device)),
        in_specs=[vmem()] * (ways + 4),
        out_specs=(vmem(),) * 3,
        scratch_shapes=[
            pltpu.VMEM((3 * total, LANES), f32),
            pltpu.VMEM((slots * ways, LANES), f32),
            pltpu.SMEM(index.shape, jnp.int32),
            pltpu.SemaphoreType.DMA,
        ],
        compiler_params=limit(16),
        name="wall",
    )(*partials, still, inner_cells, particle_strength, index)
    return (wall, grid, new_strength)


def solution(mesh):
    in_specs = (
        P(None, ("src", "tgt")),
        P(None, ("src", "tgt")),
        P(None, ("src", "tgt")),
        P(None, None, "tgt"),
        P("src", None, "tgt", None),
        P("src", "tgt", None),
        P("src", "tgt", None),
        P("src", "tgt", None),
        P("src", "tgt", None),
    )
    out_specs = (P(None, "src", "tgt"), P("src", None, "tgt", None), P(None, ("src", "tgt")))
    return jax.shard_map(
        on_device, mesh=mesh, in_specs=in_specs, out_specs=out_specs, check_vma=False
    )
```

```python
import functools
import math

import jax
import jax.numpy as jnp
from jax import lax
from jax.experimental import pallas as pl
from jax.experimental.pallas import tpu as pltpu
from jax.sharding import PartitionSpec as P

SUBSTEPS = 3
LANES = 128
ROWS = 8
TOGETHER = 2
TALL = 64
TERMS = 48
swirl_gain = 0.2
f32 = jnp.float32
bf16 = jnp.bfloat16


def vmem():
    return pl.BlockSpec(memory_space=pltpu.VMEM)


def smem():
    return pl.BlockSpec(memory_space=pltpu.SMEM)


def hbm():
    return pl.BlockSpec(memory_space=pltpu.HBM)


def stay(*arrays):
    return [pltpu.with_memory_space_constraint(a, pltpu.HBM) for a in arrays]


def shape(*dims):
    return jax.ShapeDtypeStruct(dims, f32)


def limit(megabytes):
    return pltpu.CompilerParams(vmem_limit_bytes=megabytes << 20)


def cost(flops, size):
    return pl.CostEstimate(flops=flops, bytes_accessed=size, transcendentals=0)


def divisor(number, most):
    return max(c for c in range(1, min(number, most) + 1) if number % c == 0)


def power_of_two(number):
    return number & (number - 1) == 0


def partner(index, step, count):
    return index ^ step if power_of_two(count) else (index + step) % count


def source_of(index, step, count):
    return index ^ step if power_of_two(count) else (index - step) % count


def line_order(outer):
    return [0, *range(outer // 2, outer), *range(1, outer // 2)]


def tgt_order(ways):
    return [0, *reversed(range(1, ways))]


def turn(step, ways):
    return {1: 2, 2: 3, 3: 1}.get(step % ways, step % ways)


def particles_kernel(inner, outer, *refs):
    given, messages = refs[:9], refs[9 : 9 + outer]
    own, lists, held, sems = refs[9 + outer], refs[10 + outer : 12 + outer], refs[12 + outer : -1], refs[-1]
    targets = (*held, own.at[0:3], own.at[3:4], own.at[4:5], *lists)
    sources = (*given[0:4], given[4].at[0], *given[5:9])
    copies = [
        pltpu.make_async_copy(a, b, sems.at[i]) for i, (a, b) in enumerate(zip(sources, targets))
    ]
    for copy in copies:
        copy.start()
    for copy in copies[0:4]:
        copy.wait()
    pos, strength, radius, points = held
    tiles = pos.shape[1] // LANES
    angles = points.shape[2]
    src = lax.axis_index("src")
    core = radius[...] * radius[...]
    for step, message in zip(line_order(outer), messages):
        plane = partner(src // inner, step, outer) * inner + src % inner
        for k in range(tiles):
            part = slice(k * LANES, (k + 1) * LANES)
            message[k, 0:3, :] = pos[:, part]
            message[k, 3:6, :] = strength[:, part]
            message[k, 6:7, :] = core[:, part]
            message[k, 7:8, :] = jnp.zeros((1, LANES), f32)
        for m in range(3):
            message[m, 7:8, 0:angles] = points[m, pl.ds(plane, 1), :]
    for copy in copies[4:]:
        copy.wait()


def edges_kernel(own, own_source, own_target, after, message):
    angles = own.shape[1]
    blocks = own_source.shape[2]
    total = angles * lax.axis_size("tgt")
    half = ROWS // 2
    for c in range(5):
        message[c, :, 0:angles] = jnp.transpose(own[c])[0:ROWS, :]
        message[c, :, angles:LANES] = jnp.zeros((ROWS, LANES - angles), f32)
        message[6 + c, 0:half, :] = own[c, 0:half]
        message[6 + c, half:ROWS, :] = own[c, angles - half : angles]
    message[5] = jnp.full((ROWS, LANES), -1.0, f32)
    q = own_source[0]
    row = (q // angles) * total + lax.axis_index("tgt") * angles + q % angles
    message[5, 0:1, 0:blocks] = row.astype(f32)
    message[5, 1:2, 0:blocks] = own_target[0].astype(f32)


def still_kernel(ways, *refs):
    messages = refs[:ways]
    own, lists, after, grid, picks, inner_cells, index, placed, source, sem = refs[ways:]
    copy = pltpu.make_async_copy(lists, source, sem)
    copy.start()
    angles = own.shape[1]
    height = angles + ROWS
    blocks = lists.shape[2]
    me = lax.axis_index("tgt")
    for step, message in zip(tgt_order(ways), messages):
        placed[source_of(me, step, ways)] = message[...]

    for c in range(5):
        inner_cells[c] = jnp.concatenate(
            [placed[t, c, :, 0:angles] for t in range(ways)], axis=1
        )

    shaped = index.shape
    name = (me * blocks + lax.broadcasted_iota(jnp.int32, shaped, 0)).astype(f32)
    lane = lax.broadcasted_iota(jnp.int32, shaped, 1).astype(f32)
    row = jnp.full(shaped, -1.0, f32)
    slot = jnp.zeros(shaped, f32)
    for step, message in enumerate(messages):
        match = message[5, 1:2, :] == name
        row = jnp.maximum(row, jnp.where(match, message[5, 0:1, :], -1.0))
        slot = jnp.maximum(slot, jnp.where(match, lane + float(step * picks.shape[0]), 0.0))
    row = jnp.max(row, axis=1, keepdims=True)
    slot = jnp.max(slot, axis=1, keepdims=True)
    index[...] = jnp.where(lane < 1.0, row, slot).astype(jnp.int32)

    upper = lax.broadcasted_iota(jnp.int32, (ROWS, LANES), 0) < ROWS // 2
    east = lax.rem(me + 1, ways)
    west = lax.rem(me + ways - 1, ways)
    cells = [
        jnp.concatenate(
            [own[c], jnp.where(upper, placed[east, 6 + c], placed[west, 6 + c])], axis=0
        )
        for c in range(5)
    ]
    field, local_swirl, local_diff = cells[0:3], cells[3], cells[4]
    lane = lax.broadcasted_iota(jnp.int32, (height, LANES), 1)
    for counter in range(SUBSTEPS):
        transport = 0.5 * (local_swirl + swirl_gain * field[2])
        renewed = []
        for m in range(3):
            center = field[m]
            eastern = pltpu.roll(center, height - 1, 0)
            western = pltpu.roll(center, 1, 0)
            outward = jnp.where(lane == LANES - 1, 0.0, pltpu.roll(center, LANES - 1, 1))
            inward = jnp.where(lane == 0, 0.0, pltpu.roll(center, 1, 1))
            renewed.append(
                center
                + local_diff * (eastern + western + outward + inward - 4.0 * center)
                - transport * (eastern - western)
            )
        field = renewed
    for m in range(3):
        grid[m] = field[m][0:angles]
    picks[...] = jnp.zeros(picks.shape, f32)
    copy.wait()
    for i in range(blocks):
        q = source[0, 0, i]
        picks[i : i + 1, :] = grid[q // angles, pl.ds(q % angles, 1), :]


def join_kernel(outer, *refs):
    messages, (after, particles) = refs[:outer], refs[outer:]
    tiles = messages[0].shape[0]
    for i, message in enumerate(messages):
        particles[i * tiles : (i + 1) * tiles] = message[...]


def three_parts(value):
    high = value.astype(bf16).astype(f32)
    rest = value - high
    middle = rest.astype(bf16).astype(f32)
    return high, middle, rest - middle


def middle_of(planes):
    here = lax.axis_index("src").astype(f32)
    return 0.5, 0.5, (here + 0.5) * (1.0 / planes)


def points_kernel(ways, outer, particles, along, terms, tiled):
    tiles = particles.shape[0] // outer
    angles = along.shape[1] // ways
    order = line_order(outer)
    me = lax.axis_index("tgt")
    for step in range(ways):
        place = source_of(me, turn(step, ways), ways)
        first = order.index(step) * tiles
        for m in range(3):
            tiled[pl.ds(place * ROWS + m, 1), :] = particles[first + m, 7:8, :]
    middle = middle_of(outer * 2)
    x, y, z = [
        jnp.concatenate(
            [tiled[t * ROWS + m : t * ROWS + m + 1, 0:angles] for t in range(ways)], axis=1
        )
        - middle[m]
        for m in range(3)
    ]
    nothing = jnp.zeros((3, x.shape[1]), f32)
    along[...] = jnp.concatenate([x, y, z, nothing, nothing[0:2]], axis=0)
    vector = jnp.concatenate(
        [-2.0 * x, -2.0 * y, -2.0 * z, jnp.ones_like(x), x * x + y * y + z * z, nothing], axis=0
    )
    high, middle, low = three_parts(vector)
    terms[...] = jnp.transpose(
        jnp.concatenate([high, middle, low, high, middle, high], axis=0)
    ).astype(bf16)


def pairs_kernel(scale, planes, particles, along, terms, result, crossed, others, sums):
    tiles = particles.shape[0]
    angles = along.shape[1]
    parts = angles // LANES
    tall = min(angles, TALL)
    unroll = divisor(tiles, 12)
    middle = middle_of(planes)
    one = jnp.ones((1, LANES), f32)
    nothing = jnp.zeros((3, LANES), f32)
    for k in range(tiles):
        px, py, pz = [particles[k, r : r + 1, :] - middle[r] for r in range(3)]
        sx, sy, sz, cc = [particles[k, r : r + 1, :] for r in range(3, 7)]
        crossed[k, 0:1, :] = sy * pz - sz * py
        crossed[k, 1:2, :] = sz * px - sx * pz
        crossed[k, 2:3, :] = sx * py - sy * px
        vector = jnp.concatenate(
            [px, py, pz, px * px + py * py + (pz * pz + cc), one, nothing], axis=0
        )
        high, middling, low = three_parts(vector)
        others[k // unroll, :, (k % unroll) * LANES : (k % unroll + 1) * LANES] = jnp.concatenate(
            [high, high, high, middling, middling, low], axis=0
        ).astype(bf16)
    sums[...] = jnp.zeros(sums.shape, f32)
    diagonal = lax.broadcasted_iota(jnp.int32, (ROWS, LANES), 1) - lax.broadcasted_iota(
        jnp.int32, (ROWS, LANES), 0
    )
    together = TOGETHER

    def one_block(base, unused):
        def absorb(step, carried):
            distance = jnp.dot(
                terms[pl.ds(pl.multiple_of(base, tall), tall), :], others[step],
                preferred_element_type=f32,
            )
            renewed = []
            for start in range(0, tall // ROWS, together):
                held = list(carried[6 * start : 6 * (start + together)])
                for u in range(unroll):
                    tile = step * unroll + u
                    along_sums = [particles[tile, r : r + 1, :] for r in range(3, 6)]
                    along_sums += [crossed[tile, r : r + 1, :] for r in range(3)]
                    for i in range(together):
                        low = (start + i) * ROWS
                        inverse = lax.rsqrt(
                            distance[low : low + ROWS, u * LANES : (u + 1) * LANES]
                        )
                        weight = inverse * inverse * inverse
                        for r in range(6):
                            held[6 * i + r] += weight * along_sums[r]
                renewed += held
            return tuple(renewed)

        carried = (jnp.zeros((ROWS, LANES), f32),) * (6 * (tall // ROWS))
        if tiles == unroll:
            carried = absorb(0, carried)
        else:
            carried = lax.fori_loop(0, tiles // unroll, absorb, carried)
        for i in range(tall // ROWS):
            here = base + i * ROWS
            mask = diagonal == here % LANES
            for r in range(6):
                value = jnp.sum(carried[6 * i + r], axis=1, keepdims=True)
                sums[r * parts + here // LANES] += jnp.where(mask, value, 0.0)
        return unused

    if angles // tall <= 4:
        for block in range(angles // tall):
            one_block(block * tall, 0)
    else:
        lax.fori_loop(0, angles // tall, lambda i, c: one_block(i * tall, c), 0)
    for k in range(parts):
        ax, ay, az, bx, by, bz = [
            jnp.sum(sums[r * parts + k], axis=0, keepdims=True) for r in range(6)
        ]
        tx, ty, tz = [along[m : m + 1, k * LANES : (k + 1) * LANES] for m in range(3)]
        speed = (ay * tz - az * ty - bx, az * tx - ax * tz - by, ax * ty - ay * tx - bz)
        for m in range(3):
            result[m * parts + k : m * parts + k + 1, :] += scale * speed[m]


def near_kernel(scale, ways, outer, particles, result, along, terms, tiled, *scratch):
    points_kernel(ways, outer, particles, along, terms, tiled)
    result[...] = jnp.zeros(result.shape, f32)
    pairs_kernel(scale, outer * 2, particles, along, terms, result, *scratch)


def far_kernel(scale, outer, particles, along, terms, near_sum, picks, result, *scratch):
    rows = 3 * along.shape[1] // LANES
    result[...] = jnp.zeros(result.shape, f32)
    result[0:rows, :] = near_sum[0:rows, :]
    result[rows : rows + picks.shape[0], :] = picks[...]
    pairs_kernel(scale, outer * 2, particles, along, terms, result, *scratch)


def wall_kernel(ways, *refs):
    partials = refs[:ways]
    (still, inner_cells, strength, index, wall, grid, new_strength,
     fixed, picked, rows, sem) = refs[ways:]
    angles = grid.shape[2]
    total = angles * ways
    parts = total // LANES
    rows_of = 3 * parts
    slots = picked.shape[0] // ways
    me = lax.axis_index("tgt")
    copy = pltpu.make_async_copy(index, rows, sem)
    copy.start()
    for step, partial in enumerate(partials):
        picked[step * slots : (step + 1) * slots, :] = partial[rows_of : rows_of + slots, :]
    added = partials[0][0:rows_of, :]
    for partial in partials[1:]:
        added = added + partial[0:rows_of, :]
    speed = [
        jnp.concatenate([added[r : r + 1] for r in range(m * parts, (m + 1) * parts)], axis=1)
        for m in range(3)
    ]
    stacked = jnp.concatenate(speed + [jnp.zeros((ROWS - 3, total), f32)], axis=0)
    own = pltpu.roll(stacked, total - me * angles, 1)
    for m in range(3):
        wall[m] = own[m : m + 1, 0:angles]

    first = lax.broadcasted_iota(jnp.int32, (ROWS, total), 0) == 0
    field = [inner_cells[m] for m in range(3)]
    local_swirl = inner_cells[3]
    local_diff = inner_cells[4]
    for counter in range(SUBSTEPS):
        transport = 0.5 * (local_swirl + swirl_gain * field[2])
        renewed = []
        for m in range(3):
            center = field[m]
            eastern = pltpu.roll(center, total - 1, 1)
            western = pltpu.roll(center, 1, 1)
            outward = pltpu.roll(center, ROWS - 1, 0)
            inward = jnp.where(first, speed[m], pltpu.roll(center, 1, 0))
            renewed.append(
                center
                + local_diff * (eastern + western + outward + inward - 4.0 * center)
                - transport * (eastern - western)
            )
        field = renewed
    stacked = jnp.concatenate(field + [jnp.zeros((LANES - 3 * ROWS, total), f32)], axis=0)
    for k in range(parts):
        turned = jnp.transpose(stacked[:, k * LANES : (k + 1) * LANES])
        for m in range(3):
            place = m * total + k * LANES
            fixed[place : place + LANES, :] = turned if m == 0 else pltpu.roll(
                turned, LANES - m * ROWS, 1
            )
    near = lax.broadcasted_iota(jnp.int32, (angles, LANES), 1) < SUBSTEPS
    for m in range(3):
        place = pl.multiple_of(m * total + me * angles, ROWS)
        grid[0, m] = jnp.where(near, fixed[pl.ds(place, angles), :], still[m])
    near = lax.broadcasted_iota(jnp.int32, (1, LANES), 1) < SUBSTEPS
    pieces = strength.shape[1] // LANES
    copy.wait()
    for b in range(3 * pieces):
        q = rows[b, 0]
        c, part = b // pieces, slice((b % pieces) * LANES, (b % pieces + 1) * LANES)
        row = jnp.where(
            near, fixed[pl.ds(jnp.maximum(q, 0), 1), :], picked[pl.ds(rows[b, 1], 1), :]
        )
        new_strength[c : c + 1, part] = jnp.where(q >= 0, row, strength[c : c + 1, part])


def send(block, pairs):
    return lax.ppermute(block, ("src", "tgt"), pairs)


def on_device(
    particle_position,
    particle_strength,
    core_radius,
    boundary_points,
    vorticity,
    swirl,
    diffusivity,
    intersection_source,
    intersection_target,
):
    sources = lax.axis_size("src")
    ways = lax.axis_size("tgt")
    planes, comps, angles, radial = vorticity.shape
    per_device = particle_position.shape[1]
    tiles = per_device // LANES
    blocks = intersection_source.shape[2]
    inner = 2 if sources % 2 == 0 else 1
    outer = sources // inner
    total = angles * ways
    scale = 1.6 / (4.0 * math.pi * math.sqrt(per_device * ways * sources))

    def pairs(move):
        found = []
        for s in range(sources):
            for t in range(ways):
                o, i, u = move(s // inner, s % inner, t)
                found.append((s * ways + t, (o * inner + i) * ways + u))
        return found

    def over_tgt(block, step):
        return send(block, pairs(lambda o, i, t: (o, i, partner(t, step, ways))))

    given = (
        particle_position, particle_strength, core_radius, boundary_points,
        vorticity, swirl, diffusivity, intersection_source, intersection_target,
    )
    *messages, own, source, target = pl.pallas_call(
        functools.partial(particles_kernel, inner, outer),
        out_shape=(shape(tiles, ROWS, LANES),) * outer + (
            shape(5, angles, LANES),
            jax.ShapeDtypeStruct(intersection_source.shape, jnp.int32),
            jax.ShapeDtypeStruct(intersection_target.shape, jnp.int32),
        ),
        in_specs=[hbm()] * 9,
        out_specs=(vmem(),) * (outer + 3),
        scratch_shapes=[pltpu.VMEM(a.shape, f32) for a in given[0:4]]
        + [pltpu.SemaphoreType.DMA((9,))],
        compiler_params=limit(4),
        name="particles",
    )(*stay(*given))
    line = [messages[0]] + [
        send(
            message,
            pairs(lambda o, i, t: (partner(o, k, outer), i, partner(t, turn(k, ways), ways))),
        )
        for k, message in zip(line_order(outer)[1:], messages[1:])
    ]

    edges = pl.pallas_call(
        edges_kernel,
        out_shape=shape(11, ROWS, LANES),
        in_specs=[vmem()] * 4,
        out_specs=vmem(),
        compiler_params=limit(4),
        name="edges",
    )(own, source, target, line[1])
    steps = tgt_order(ways)
    around = [edges] + [over_tgt(edges, k) for k in steps[1:]]

    near = pl.pallas_call(
        functools.partial(join_kernel, outer),
        out_shape=shape(outer * tiles, ROWS, LANES),
        in_specs=[vmem()] * (outer + 1),
        out_specs=vmem(),
        compiler_params=limit(8),
        name="join",
    )(*line, edges)
    far = send(near, pairs(lambda o, i, t: (o, inner - 1 - i, t)))

    rows = 3 * total // LANES
    slots = blocks
    unroll = divisor(outer * tiles, 12)
    scratch = [
        pltpu.VMEM((outer * tiles, ROWS, LANES), f32),
        pltpu.VMEM((outer * tiles // unroll, TERMS, unroll * LANES), bf16),
        pltpu.VMEM((6 * total // LANES, ROWS, LANES), f32),
    ]
    near_sum, along, terms = pl.pallas_call(
        functools.partial(near_kernel, scale, ways, outer),
        out_shape=(
            shape(-(-rows // ROWS) * ROWS, LANES),
            shape(ROWS, total),
            jax.ShapeDtypeStruct((total, TERMS), bf16),
        ),
        in_specs=[vmem()],
        out_specs=(vmem(),) * 3,
        scratch_shapes=[pltpu.VMEM((ways * ROWS, LANES), f32)] + scratch,
        compiler_params=limit(12),
        cost_estimate=cost(1 << 31, 1 << 10),
        name="near",
    )(near)
    still, picks, inner_cells, index = pl.pallas_call(
        functools.partial(still_kernel, ways),
        out_shape=(
            shape(3, angles, LANES),
            shape(slots, LANES),
            shape(5, ROWS, total),
            jax.ShapeDtypeStruct((16 * ((blocks + 15) // 16), LANES), jnp.int32),
        ),
        in_specs=[vmem()] * (ways + 3),
        out_specs=(vmem(),) * 4,
        scratch_shapes=[
            pltpu.VMEM((ways,) + edges.shape, f32),
            pltpu.SMEM(source.shape, jnp.int32),
            pltpu.SemaphoreType.DMA,
        ],
        compiler_params=limit(8),
        name="still",
    )(*around, own, source, near_sum)
    partial_sum = pl.pallas_call(
        functools.partial(far_kernel, scale, outer),
        out_shape=shape(-(-(rows + blocks) // ROWS) * ROWS, LANES),
        in_specs=[vmem()] * 5,
        out_specs=vmem(),
        scratch_shapes=scratch,
        compiler_params=limit(12),
        cost_estimate=cost(1 << 31, 1 << 10),
        name="far",
    )(far, along, terms, near_sum, picks)
    partials = [partial_sum] + [over_tgt(partial_sum, k) for k in steps[1:]]

    wall, grid, new_strength = pl.pallas_call(
        functools.partial(wall_kernel, ways),
        out_shape=(shape(3, planes, angles), shape(*vorticity.shape), shape(3, per_device)),
        in_specs=[vmem()] * (ways + 4),
        out_specs=(vmem(),) * 3,
        scratch_shapes=[
            pltpu.VMEM((3 * total, LANES), f32),
            pltpu.VMEM((slots * ways, LANES), f32),
            pltpu.SMEM(index.shape, jnp.int32),
            pltpu.SemaphoreType.DMA,
        ],
        compiler_params=limit(16),
        name="wall",
    )(*partials, still, inner_cells, particle_strength, index)
    return (wall, grid, new_strength)


def solution(mesh):
    in_specs = (
        P(None, ("src", "tgt")),
        P(None, ("src", "tgt")),
        P(None, ("src", "tgt")),
        P(None, None, "tgt"),
        P("src", None, "tgt", None),
        P("src", "tgt", None),
        P("src", "tgt", None),
        P("src", "tgt", None),
        P("src", "tgt", None),
    )
    out_specs = (P(None, "src", "tgt"), P("src", None, "tgt", None), P(None, ("src", "tgt")))
    return jax.shard_map(
        on_device, mesh=mesh, in_specs=in_specs, out_specs=out_specs, check_vma=False
    )
```

```python
import functools
import math

import jax
import jax.numpy as jnp
from jax import lax
from jax.experimental import pallas as pl
from jax.experimental.pallas import tpu as pltpu
from jax.sharding import PartitionSpec as P

SUBSTEPS = 3
LANES = 128
ROWS = 8
TOGETHER = 2
TALL = 64
TERMS = 48
swirl_gain = 0.2
f32 = jnp.float32
bf16 = jnp.bfloat16


def vmem():
    return pl.BlockSpec(memory_space=pltpu.VMEM)


def smem():
    return pl.BlockSpec(memory_space=pltpu.SMEM)


def hbm():
    return pl.BlockSpec(memory_space=pltpu.HBM)


def stay(*arrays):
    return [pltpu.with_memory_space_constraint(a, pltpu.HBM) for a in arrays]


def shape(*dims):
    return jax.ShapeDtypeStruct(dims, f32)


def limit(megabytes):
    return pltpu.CompilerParams(vmem_limit_bytes=megabytes << 20)


def cost(flops, size):
    return pl.CostEstimate(flops=flops, bytes_accessed=size, transcendentals=0)


def divisor(number, most):
    return max(c for c in range(1, min(number, most) + 1) if number % c == 0)


def power_of_two(number):
    return number & (number - 1) == 0


def partner(index, step, count):
    return index ^ step if power_of_two(count) else (index + step) % count


def source_of(index, step, count):
    return index ^ step if power_of_two(count) else (index - step) % count


def line_order(outer):
    return [0, *range(outer // 2, outer), *range(1, outer // 2)]


def tgt_order(ways):
    return [0, *reversed(range(1, ways))]


def turn(step, ways):
    return {1: 2, 2: 3, 3: 1}.get(step % ways, step % ways)


def particles_kernel(inner, outer, *refs):
    given, messages = refs[:9], refs[9 : 9 + outer]
    own, lists, held, sems = refs[9 + outer], refs[10 + outer : 12 + outer], refs[12 + outer : -1], refs[-1]
    targets = (*held, own.at[0:3], own.at[3:4], own.at[4:5], *lists)
    sources = (*given[0:4], given[4].at[0], *given[5:9])
    copies = [
        pltpu.make_async_copy(a, b, sems.at[i]) for i, (a, b) in enumerate(zip(sources, targets))
    ]
    for copy in copies:
        copy.start()
    for copy in copies[0:4]:
        copy.wait()
    pos, strength, radius, points = held
    tiles = pos.shape[1] // LANES
    angles = points.shape[2]
    src = lax.axis_index("src")
    core = radius[...] * radius[...]
    for step, message in zip(line_order(outer), messages):
        there = partner(src // inner, step, outer) * inner
        planes = (there + src % inner, there + inner - 1 - src % inner)
        for k in range(tiles):
            part = slice(k * LANES, (k + 1) * LANES)
            message[k, 0:3, :] = pos[:, part]
            message[k, 3:6, :] = strength[:, part]
            message[k, 6:7, :] = core[:, part]
            message[k, 7:8, :] = jnp.zeros((1, LANES), f32)
        for m in range(3):
            for i, plane in enumerate(planes):
                message[m, 7:8, i * angles : (i + 1) * angles] = points[m, pl.ds(plane, 1), :]
    for copy in copies[4:]:
        copy.wait()


def edges_kernel(own, own_source, own_target, message):
    angles = own.shape[1]
    blocks = own_source.shape[2]
    total = angles * lax.axis_size("tgt")
    half = ROWS // 2
    for c in range(5):
        message[c, :, 0:angles] = jnp.transpose(own[c])[0:ROWS, :]
        message[c, :, angles:LANES] = jnp.zeros((ROWS, LANES - angles), f32)
        message[6 + c, 0:half, :] = own[c, 0:half]
        message[6 + c, half:ROWS, :] = own[c, angles - half : angles]
    message[5] = jnp.full((ROWS, LANES), -1.0, f32)
    q = own_source[0]
    row = (q // angles) * total + lax.axis_index("tgt") * angles + q % angles
    message[5, 0:1, 0:blocks] = row.astype(f32)
    message[5, 1:2, 0:blocks] = own_target[0].astype(f32)


def still_kernel(ways, *refs):
    messages = refs[:ways]
    own, lists, after, grid, picks, inner_cells, index, placed, source, sem = refs[ways:]
    copy = pltpu.make_async_copy(lists, source, sem)
    copy.start()
    angles = own.shape[1]
    height = angles + ROWS
    blocks = lists.shape[2]
    me = lax.axis_index("tgt")
    for step, message in zip(tgt_order(ways), messages):
        placed[source_of(me, step, ways)] = message[...]

    for c in range(5):
        inner_cells[c] = jnp.concatenate(
            [placed[t, c, :, 0:angles] for t in range(ways)], axis=1
        )

    shaped = index.shape
    name = (me * blocks + lax.broadcasted_iota(jnp.int32, shaped, 0)).astype(f32)
    lane = lax.broadcasted_iota(jnp.int32, shaped, 1).astype(f32)
    row = jnp.full(shaped, -1.0, f32)
    slot = jnp.zeros(shaped, f32)
    for step, message in enumerate(messages):
        match = message[5, 1:2, :] == name
        row = jnp.maximum(row, jnp.where(match, message[5, 0:1, :], -1.0))
        slot = jnp.maximum(slot, jnp.where(match, lane + float(step * picks.shape[0]), 0.0))
    row = jnp.max(row, axis=1, keepdims=True)
    slot = jnp.max(slot, axis=1, keepdims=True)
    index[...] = jnp.where(lane < 1.0, row, slot).astype(jnp.int32)

    upper = lax.broadcasted_iota(jnp.int32, (ROWS, LANES), 0) < ROWS // 2
    east = lax.rem(me + 1, ways)
    west = lax.rem(me + ways - 1, ways)
    cells = [
        jnp.concatenate(
            [own[c], jnp.where(upper, placed[east, 6 + c], placed[west, 6 + c])], axis=0
        )
        for c in range(5)
    ]
    field, local_swirl, local_diff = cells[0:3], cells[3], cells[4]
    lane = lax.broadcasted_iota(jnp.int32, (height, LANES), 1)
    for counter in range(SUBSTEPS):
        transport = 0.5 * (local_swirl + swirl_gain * field[2])
        renewed = []
        for m in range(3):
            center = field[m]
            eastern = pltpu.roll(center, height - 1, 0)
            western = pltpu.roll(center, 1, 0)
            outward = jnp.where(lane == LANES - 1, 0.0, pltpu.roll(center, LANES - 1, 1))
            inward = jnp.where(lane == 0, 0.0, pltpu.roll(center, 1, 1))
            renewed.append(
                center
                + local_diff * (eastern + western + outward + inward - 4.0 * center)
                - transport * (eastern - western)
            )
        field = renewed
    for m in range(3):
        grid[m] = field[m][0:angles]
    picks[...] = jnp.zeros(picks.shape, f32)
    copy.wait()
    for i in range(blocks):
        q = source[0, 0, i]
        picks[i : i + 1, :] = grid[q // angles, pl.ds(q % angles, 1), :]


def three_parts(value):
    high = value.astype(bf16).astype(f32)
    rest = value - high
    middle = rest.astype(bf16).astype(f32)
    return high, middle, rest - middle


def middle_of(outer, inner):
    here = (lax.axis_index("src") // inner).astype(f32)
    return 0.5, 0.5, (here + 0.5) * (1.0 / outer)


def points_kernel(ways, middle, messages, lane, along, terms, tiled):
    angles = along.shape[1] // ways
    order = line_order(len(messages))
    me = lax.axis_index("tgt")
    for step in range(ways):
        place = source_of(me, turn(step, ways), ways)
        message = messages[order.index(step)]
        for m in range(3):
            tiled[pl.ds(place * ROWS + m, 1), :] = message[m, 7:8, :]
    x, y, z = [
        jnp.concatenate(
            [
                tiled[t * ROWS + m : t * ROWS + m + 1, lane : lane + angles]
                for t in range(ways)
            ],
            axis=1,
        )
        - middle[m]
        for m in range(3)
    ]
    nothing = jnp.zeros((3, x.shape[1]), f32)
    along[...] = jnp.concatenate([x, y, z, nothing, nothing[0:2]], axis=0)
    vector = jnp.concatenate(
        [-2.0 * x, -2.0 * y, -2.0 * z, jnp.ones_like(x), x * x + y * y + z * z, nothing], axis=0
    )
    high, middling, low = three_parts(vector)
    terms[...] = jnp.transpose(
        jnp.concatenate([high, middling, low, high, middling, high], axis=0)
    ).astype(bf16)


def moments_kernel(middle, messages, moments, others):
    tiles = messages[0].shape[0]
    unroll = others.shape[2] // LANES
    one = jnp.ones((1, LANES), f32)
    nothing = jnp.zeros((3, LANES), f32)
    for k in range(moments.shape[0]):
        message = messages[k // tiles]
        px, py, pz = [message[k % tiles, r : r + 1, :] - middle[r] for r in range(3)]
        sx, sy, sz, cc = [message[k % tiles, r : r + 1, :] for r in range(3, 7)]
        moments[k] = jnp.concatenate(
            [sx, sy, sz, sy * pz - sz * py, sz * px - sx * pz, sx * py - sy * px, nothing[0:2]],
            axis=0,
        )
        vector = jnp.concatenate(
            [px, py, pz, px * px + py * py + (pz * pz + cc), one, nothing], axis=0
        )
        high, middling, low = three_parts(vector)
        others[k // unroll, :, (k % unroll) * LANES : (k % unroll + 1) * LANES] = jnp.concatenate(
            [high, high, high, middling, middling, low], axis=0
        ).astype(bf16)


def pairs_kernel(scale, moments, others, along, terms, result, sums):
    tiles = moments.shape[0]
    angles = along.shape[1]
    parts = angles // LANES
    tall = min(angles, TALL)
    unroll = others.shape[2] // LANES
    sums[...] = jnp.zeros(sums.shape, f32)
    diagonal = lax.broadcasted_iota(jnp.int32, (ROWS, LANES), 1) - lax.broadcasted_iota(
        jnp.int32, (ROWS, LANES), 0
    )
    together = TOGETHER

    def one_block(base, unused):
        def absorb(step, carried):
            distance = jnp.dot(
                terms[pl.ds(pl.multiple_of(base, tall), tall), :], others[step],
                preferred_element_type=f32,
            )
            renewed = []
            for start in range(0, tall // ROWS, together):
                held = list(carried[6 * start : 6 * (start + together)])
                for u in range(unroll):
                    tile = step * unroll + u
                    summed = [moments[tile, r : r + 1, :] for r in range(6)]
                    for i in range(together):
                        low = (start + i) * ROWS
                        inverse = lax.rsqrt(
                            distance[low : low + ROWS, u * LANES : (u + 1) * LANES]
                        )
                        weight = inverse * inverse * inverse
                        for r in range(6):
                            held[6 * i + r] += weight * summed[r]
                renewed += held
            return tuple(renewed)

        carried = (jnp.zeros((ROWS, LANES), f32),) * (6 * (tall // ROWS))
        if tiles == unroll:
            carried = absorb(0, carried)
        else:
            carried = lax.fori_loop(0, tiles // unroll, absorb, carried)
        for i in range(tall // ROWS):
            here = base + i * ROWS
            mask = diagonal == here % LANES
            for r in range(6):
                value = jnp.sum(carried[6 * i + r], axis=1, keepdims=True)
                sums[r * parts + here // LANES] += jnp.where(mask, value, 0.0)
        return unused

    if angles // tall <= 4:
        for block in range(angles // tall):
            one_block(block * tall, 0)
    else:
        lax.fori_loop(0, angles // tall, lambda i, c: one_block(i * tall, c), 0)
    for k in range(parts):
        ax, ay, az, bx, by, bz = [
            jnp.sum(sums[r * parts + k], axis=0, keepdims=True) for r in range(6)
        ]
        tx, ty, tz = [along[m : m + 1, k * LANES : (k + 1) * LANES] for m in range(3)]
        speed = (ay * tz - az * ty - bx, az * tx - ax * tz - by, ax * ty - ay * tx - bz)
        for m in range(3):
            result[m * parts + k : m * parts + k + 1, :] = scale * speed[m]


def partner_kernel(scale, ways, outer, inner, *refs):
    messages, (after, result, moments, others, along, terms) = refs[:outer], refs[outer : outer + 6]
    tiled, sums, there_along, there_terms = refs[outer + 6 :]
    middle = middle_of(outer, inner)
    angles = along.shape[1] // ways
    points_kernel(ways, middle, messages, angles, there_along, there_terms, tiled)
    moments_kernel(middle, messages, moments, others)
    points_kernel(ways, middle, messages, 0, along, terms, tiled)
    pairs_kernel(scale, moments, others, there_along, there_terms, result, sums)


def merge_kernel(rows, own, arrived, picks, result):
    result[...] = jnp.zeros(result.shape, f32)
    result[0:rows, :] = own[0:rows, :] + arrived[0:rows, :]
    result[rows : rows + picks.shape[0], :] = picks[...]


def wall_kernel(ways, *refs):
    partials = refs[:ways]
    (still, inner_cells, strength, index, wall, grid, new_strength,
     fixed, picked, rows, sem) = refs[ways:]
    angles = grid.shape[2]
    total = angles * ways
    parts = total // LANES
    rows_of = 3 * parts
    slots = picked.shape[0] // ways
    me = lax.axis_index("tgt")
    copy = pltpu.make_async_copy(index, rows, sem)
    copy.start()
    for step, partial in enumerate(partials):
        picked[step * slots : (step + 1) * slots, :] = partial[rows_of : rows_of + slots, :]
    added = partials[0][0:rows_of, :]
    for partial in partials[1:]:
        added = added + partial[0:rows_of, :]
    speed = [
        jnp.concatenate([added[r : r + 1] for r in range(m * parts, (m + 1) * parts)], axis=1)
        for m in range(3)
    ]
    stacked = jnp.concatenate(speed + [jnp.zeros((ROWS - 3, total), f32)], axis=0)
    own = pltpu.roll(stacked, total - me * angles, 1)
    for m in range(3):
        wall[m] = own[m : m + 1, 0:angles]

    first = lax.broadcasted_iota(jnp.int32, (ROWS, total), 0) == 0
    field = [inner_cells[m] for m in range(3)]
    local_swirl = inner_cells[3]
    local_diff = inner_cells[4]
    for counter in range(SUBSTEPS):
        transport = 0.5 * (local_swirl + swirl_gain * field[2])
        renewed = []
        for m in range(3):
            center = field[m]
            eastern = pltpu.roll(center, total - 1, 1)
            western = pltpu.roll(center, 1, 1)
            outward = pltpu.roll(center, ROWS - 1, 0)
            inward = jnp.where(first, speed[m], pltpu.roll(center, 1, 0))
            renewed.append(
                center
                + local_diff * (eastern + western + outward + inward - 4.0 * center)
                - transport * (eastern - western)
            )
        field = renewed
    stacked = jnp.concatenate(field + [jnp.zeros((LANES - 3 * ROWS, total), f32)], axis=0)
    for k in range(parts):
        turned = jnp.transpose(stacked[:, k * LANES : (k + 1) * LANES])
        for m in range(3):
            place = m * total + k * LANES
            fixed[place : place + LANES, :] = turned if m == 0 else pltpu.roll(
                turned, LANES - m * ROWS, 1
            )
    near = lax.broadcasted_iota(jnp.int32, (angles, LANES), 1) < SUBSTEPS
    for m in range(3):
        place = pl.multiple_of(m * total + me * angles, ROWS)
        grid[0, m] = jnp.where(near, fixed[pl.ds(place, angles), :], still[m])
    near = lax.broadcasted_iota(jnp.int32, (1, LANES), 1) < SUBSTEPS
    pieces = strength.shape[1] // LANES
    copy.wait()
    for b in range(3 * pieces):
        q = rows[b, 0]
        c, part = b // pieces, slice((b % pieces) * LANES, (b % pieces + 1) * LANES)
        row = jnp.where(
            near, fixed[pl.ds(jnp.maximum(q, 0), 1), :], picked[pl.ds(rows[b, 1], 1), :]
        )
        new_strength[c : c + 1, part] = jnp.where(q >= 0, row, strength[c : c + 1, part])


def send(block, pairs):
    return lax.ppermute(block, ("src", "tgt"), pairs)


def on_device(
    particle_position,
    particle_strength,
    core_radius,
    boundary_points,
    vorticity,
    swirl,
    diffusivity,
    intersection_source,
    intersection_target,
):
    sources = lax.axis_size("src")
    ways = lax.axis_size("tgt")
    planes, comps, angles, radial = vorticity.shape
    per_device = particle_position.shape[1]
    tiles = per_device // LANES
    blocks = intersection_source.shape[2]
    inner = 2 if sources % 2 == 0 else 1
    outer = sources // inner
    total = angles * ways
    scale = 1.6 / (4.0 * math.pi * math.sqrt(per_device * ways * sources))

    def pairs(move):
        found = []
        for s in range(sources):
            for t in range(ways):
                o, i, u = move(s // inner, s % inner, t)
                found.append((s * ways + t, (o * inner + i) * ways + u))
        return found

    def over_tgt(block, step):
        return send(block, pairs(lambda o, i, t: (o, i, partner(t, step, ways))))

    given = (
        particle_position, particle_strength, core_radius, boundary_points,
        vorticity, swirl, diffusivity, intersection_source, intersection_target,
    )
    *messages, own, source, target = pl.pallas_call(
        functools.partial(particles_kernel, inner, outer),
        out_shape=(shape(tiles, ROWS, LANES),) * outer + (
            shape(5, angles, LANES),
            jax.ShapeDtypeStruct(intersection_source.shape, jnp.int32),
            jax.ShapeDtypeStruct(intersection_target.shape, jnp.int32),
        ),
        in_specs=[hbm()] * 9,
        out_specs=(vmem(),) * (outer + 3),
        scratch_shapes=[pltpu.VMEM(a.shape, f32) for a in given[0:4]]
        + [pltpu.SemaphoreType.DMA((9,))],
        compiler_params=limit(4),
        name="particles",
    )(*stay(*given))
    line = [messages[0]] + [
        send(
            message,
            pairs(lambda o, i, t: (partner(o, k, outer), i, partner(t, turn(k, ways), ways))),
        )
        for k, message in zip(line_order(outer)[1:], messages[1:])
    ]

    edges = pl.pallas_call(
        edges_kernel,
        out_shape=shape(11, ROWS, LANES),
        in_specs=[vmem()] * 3,
        out_specs=vmem(),
        compiler_params=limit(4),
        cost_estimate=cost(1 << 31, 1 << 10),
        name="edges",
    )(own, source, target)
    steps = tgt_order(ways)
    around = [edges] + [over_tgt(edges, k) for k in steps[1:]]

    rows = 3 * total // LANES
    slots = blocks
    count = outer * tiles
    unroll = divisor(count, 12)
    sums_of_tile = pltpu.VMEM((6 * total // LANES, ROWS, LANES), f32)
    sums_shape = shape(-(-rows // ROWS) * ROWS, LANES)
    terms_shape = jax.ShapeDtypeStruct((total, TERMS), bf16)
    for_partner, moments, others, along, terms = pl.pallas_call(
        functools.partial(partner_kernel, scale, ways, outer, inner),
        out_shape=(
            sums_shape,
            shape(count, ROWS, LANES),
            jax.ShapeDtypeStruct((count // unroll, TERMS, unroll * LANES), bf16),
            shape(ROWS, total),
            terms_shape,
        ),
        in_specs=[vmem()] * (outer + 1),
        out_specs=(vmem(),) * 5,
        scratch_shapes=[
            pltpu.VMEM((ways * ROWS, LANES), f32),
            sums_of_tile,
            pltpu.VMEM((ROWS, total), f32),
            pltpu.VMEM(terms_shape.shape, bf16),
        ],
        compiler_params=limit(12),
        cost_estimate=cost(1 << 31, 1 << 10),
        name="partner",
    )(*line, edges)
    arrived = send(for_partner, pairs(lambda o, i, t: (o, inner - 1 - i, t)))
    own_sum = pl.pallas_call(
        functools.partial(pairs_kernel, scale),
        out_shape=sums_shape,
        in_specs=[vmem()] * 4,
        out_specs=vmem(),
        scratch_shapes=[sums_of_tile],
        compiler_params=limit(12),
        cost_estimate=cost(1 << 31, 1 << 10),
        name="own",
    )(moments, others, along, terms)
    still, picks, inner_cells, index = pl.pallas_call(
        functools.partial(still_kernel, ways),
        out_shape=(
            shape(3, angles, LANES),
            shape(slots, LANES),
            shape(5, ROWS, total),
            jax.ShapeDtypeStruct((16 * ((blocks + 15) // 16), LANES), jnp.int32),
        ),
        in_specs=[vmem()] * (ways + 3),
        out_specs=(vmem(),) * 4,
        scratch_shapes=[
            pltpu.VMEM((ways,) + edges.shape, f32),
            pltpu.SMEM(source.shape, jnp.int32),
            pltpu.SemaphoreType.DMA,
        ],
        compiler_params=limit(8),
        name="still",
    )(*around, own, source, own_sum)
    partial_sum = pl.pallas_call(
        functools.partial(merge_kernel, rows),
        out_shape=shape(-(-(rows + blocks) // ROWS) * ROWS, LANES),
        in_specs=[vmem()] * 3,
        out_specs=vmem(),
        compiler_params=limit(4),
        name="merge",
    )(own_sum, arrived, picks)
    partials = [partial_sum] + [over_tgt(partial_sum, k) for k in steps[1:]]

    wall, grid, new_strength = pl.pallas_call(
        functools.partial(wall_kernel, ways),
        out_shape=(shape(3, planes, angles), shape(*vorticity.shape), shape(3, per_device)),
        in_specs=[vmem()] * (ways + 4),
        out_specs=(vmem(),) * 3,
        scratch_shapes=[
            pltpu.VMEM((3 * total, LANES), f32),
            pltpu.VMEM((slots * ways, LANES), f32),
            pltpu.SMEM(index.shape, jnp.int32),
            pltpu.SemaphoreType.DMA,
        ],
        compiler_params=limit(16),
        name="wall",
    )(*partials, still, inner_cells, particle_strength, index)
    return (wall, grid, new_strength)


def solution(mesh):
    in_specs = (
        P(None, ("src", "tgt")),
        P(None, ("src", "tgt")),
        P(None, ("src", "tgt")),
        P(None, None, "tgt"),
        P("src", None, "tgt", None),
        P("src", "tgt", None),
        P("src", "tgt", None),
        P("src", "tgt", None),
        P("src", "tgt", None),
    )
    out_specs = (P(None, "src", "tgt"), P("src", None, "tgt", None), P(None, ("src", "tgt")))
    return jax.shard_map(
        on_device, mesh=mesh, in_specs=in_specs, out_specs=out_specs, check_vma=False
    )
```

```python
import functools
import math

import jax
import jax.numpy as jnp
from jax import lax
from jax.experimental import pallas as pl
from jax.experimental.pallas import tpu as pltpu
from jax.sharding import PartitionSpec as P

SUBSTEPS = 3
LANES = 128
ROWS = 8
TOGETHER = 2
TERMS = 48
UNROLLED = 4
swirl_gain = 0.2
f32 = jnp.float32
bf16 = jnp.bfloat16


def vmem():
    return pl.BlockSpec(memory_space=pltpu.VMEM)


def smem():
    return pl.BlockSpec(memory_space=pltpu.SMEM)


def hbm():
    return pl.BlockSpec(memory_space=pltpu.HBM)


def stay(*arrays):
    return [pltpu.with_memory_space_constraint(a, pltpu.HBM) for a in arrays]


def shape(*dims):
    return jax.ShapeDtypeStruct(dims, f32)


def limit(megabytes):
    return pltpu.CompilerParams(vmem_limit_bytes=megabytes << 20)


def cost(flops, size):
    return pl.CostEstimate(flops=flops, bytes_accessed=size, transcendentals=0)


def divisor(number, most):
    return max(c for c in range(1, min(number, most) + 1) if number % c == 0)


def power_of_two(number):
    return number & (number - 1) == 0


def partner(index, step, count):
    return index ^ step if power_of_two(count) else (index + step) % count


def source_of(index, step, count):
    return index ^ step if power_of_two(count) else (index - step) % count


def line_order(outer):
    return [0, *range(outer // 2, outer), *range(1, outer // 2)]


def tgt_order(ways):
    return [0, *reversed(range(1, ways))]


def turn(step, ways):
    return {1: 2, 2: 3, 3: 1}.get(step % ways, step % ways)


def particles_kernel(inner, outer, *refs):
    given, messages = refs[:9], refs[9 : 9 + outer]
    own, lists, held, sems = refs[9 + outer], refs[10 + outer : 12 + outer], refs[12 + outer : -1], refs[-1]
    targets = (*held, own.at[0:3], own.at[3:4], own.at[4:5], *lists)
    sources = (*given[0:4], given[4].at[0], *given[5:9])
    copies = [
        pltpu.make_async_copy(a, b, sems.at[i]) for i, (a, b) in enumerate(zip(sources, targets))
    ]
    for copy in copies:
        copy.start()
    for copy in copies[0:4]:
        copy.wait()
    pos, strength, radius, points = held
    tiles = pos.shape[1] // LANES
    angles = points.shape[2]
    src = lax.axis_index("src")
    core = radius[...] * radius[...]
    for step, message in zip(line_order(outer), messages):
        there = partner(src // inner, step, outer) * inner
        planes = (there + src % inner, there + inner - 1 - src % inner)
        for k in range(tiles):
            part = slice(k * LANES, (k + 1) * LANES)
            message[k, 0:3, :] = pos[:, part]
            message[k, 3:6, :] = strength[:, part]
            message[k, 6:7, :] = core[:, part]
            message[k, 7:8, :] = jnp.zeros((1, LANES), f32)
        for m in range(3):
            for i, plane in enumerate(planes):
                message[m, 7:8, i * angles : (i + 1) * angles] = points[m, pl.ds(plane, 1), :]
    for copy in copies[4:]:
        copy.wait()


def edges_kernel(own, own_source, own_target, message):
    angles = own.shape[1]
    blocks = own_source.shape[2]
    total = angles * lax.axis_size("tgt")
    half = ROWS // 2
    for c in range(5):
        message[c, :, 0:angles] = jnp.transpose(own[c])[0:ROWS, :]
        message[c, :, angles:LANES] = jnp.zeros((ROWS, LANES - angles), f32)
        message[6 + c, 0:half, :] = own[c, 0:half]
        message[6 + c, half:ROWS, :] = own[c, angles - half : angles]
    message[5] = jnp.full((ROWS, LANES), -1.0, f32)
    q = own_source[0]
    row = (q // angles) * total + lax.axis_index("tgt") * angles + q % angles
    message[5, 0:1, 0:blocks] = row.astype(f32)
    message[5, 1:2, 0:blocks] = own_target[0].astype(f32)


def still_kernel(ways, *refs):
    messages = refs[:ways]
    own, lists, after, grid, picks, inner_cells, index, placed, source, sem = refs[ways:]
    copy = pltpu.make_async_copy(lists, source, sem)
    copy.start()
    angles = own.shape[1]
    height = angles + ROWS
    blocks = lists.shape[2]
    me = lax.axis_index("tgt")
    for step, message in zip(tgt_order(ways), messages):
        placed[source_of(me, step, ways)] = message[...]

    for c in range(5):
        inner_cells[c] = jnp.concatenate(
            [placed[t, c, :, 0:angles] for t in range(ways)], axis=1
        )

    shaped = index.shape
    name = (me * blocks + lax.broadcasted_iota(jnp.int32, shaped, 0)).astype(f32)
    lane = lax.broadcasted_iota(jnp.int32, shaped, 1).astype(f32)
    row = jnp.full(shaped, -1.0, f32)
    slot = jnp.zeros(shaped, f32)
    for step, message in enumerate(messages):
        match = message[5, 1:2, :] == name
        row = jnp.maximum(row, jnp.where(match, message[5, 0:1, :], -1.0))
        slot = jnp.maximum(slot, jnp.where(match, lane + float(step * picks.shape[0]), 0.0))
    row = jnp.max(row, axis=1, keepdims=True)
    slot = jnp.max(slot, axis=1, keepdims=True)
    index[...] = jnp.where(lane < 1.0, row, slot).astype(jnp.int32)

    upper = lax.broadcasted_iota(jnp.int32, (ROWS, LANES), 0) < ROWS // 2
    east = lax.rem(me + 1, ways)
    west = lax.rem(me + ways - 1, ways)
    cells = [
        jnp.concatenate(
            [own[c], jnp.where(upper, placed[east, 6 + c], placed[west, 6 + c])], axis=0
        )
        for c in range(5)
    ]
    field, local_swirl, local_diff = cells[0:3], cells[3], cells[4]
    lane = lax.broadcasted_iota(jnp.int32, (height, LANES), 1)
    for counter in range(SUBSTEPS):
        transport = 0.5 * (local_swirl + swirl_gain * field[2])
        renewed = []
        for m in range(3):
            center = field[m]
            eastern = pltpu.roll(center, height - 1, 0)
            western = pltpu.roll(center, 1, 0)
            outward = jnp.where(lane == LANES - 1, 0.0, pltpu.roll(center, LANES - 1, 1))
            inward = jnp.where(lane == 0, 0.0, pltpu.roll(center, 1, 1))
            renewed.append(
                center
                + local_diff * (eastern + western + outward + inward - 4.0 * center)
                - transport * (eastern - western)
            )
        field = renewed
    for m in range(3):
        grid[m] = field[m][0:angles]
    picks[...] = jnp.zeros(picks.shape, f32)
    copy.wait()
    for i in range(blocks):
        q = source[0, 0, i]
        picks[i : i + 1, :] = grid[q // angles, pl.ds(q % angles, 1), :]


def three_parts(value):
    high = value.astype(bf16).astype(f32)
    rest = value - high
    middle = rest.astype(bf16).astype(f32)
    return high, middle, rest - middle


def middle_of(outer, inner):
    here = (lax.axis_index("src") // inner).astype(f32)
    return 0.5, 0.5, (here + 0.5) * (1.0 / outer)


def point_terms(message, lane, angles, middle):
    x, y, z = [message[m, 7:8, lane : lane + angles] - middle[m] for m in range(3)]
    nothing = jnp.zeros((3, angles), f32)
    vector = jnp.concatenate(
        [-2.0 * x, -2.0 * y, -2.0 * z, jnp.ones_like(x), x * x + y * y + z * z, nothing], axis=0
    )
    high, middling, low = three_parts(vector)
    terms = jnp.transpose(jnp.concatenate([high, middling, low, high, middling, high], axis=0))
    return jnp.concatenate([x, y, z, nothing, nothing[0:2]], axis=0), terms.astype(bf16)


def tile_terms(message, middle, moments, others):
    one = jnp.ones((1, LANES), f32)
    nothing = jnp.zeros((3, LANES), f32)
    for k in range(message.shape[0]):
        px, py, pz = [message[k, r : r + 1, :] - middle[r] for r in range(3)]
        sx, sy, sz, cc = [message[k, r : r + 1, :] for r in range(3, 7)]
        moments[k] = jnp.concatenate(
            [sx, sy, sz, sy * pz - sz * py, sz * px - sx * pz, sx * py - sy * px, nothing[0:2]],
            axis=0,
        )
        vector = jnp.concatenate(
            [px, py, pz, px * px + py * py + (pz * pz + cc), one, nothing], axis=0
        )
        high, middling, low = three_parts(vector)
        others[:, k * LANES : (k + 1) * LANES] = jnp.concatenate(
            [high, high, high, middling, middling, low], axis=0
        ).astype(bf16)


def quarter(terms, blocks):
    tall = terms.shape[0]
    diagonal = lax.broadcasted_iota(jnp.int32, (ROWS, LANES), 1) - lax.broadcasted_iota(
        jnp.int32, (ROWS, LANES), 0
    )
    distances = [
        jnp.dot(terms, others[...], preferred_element_type=f32) for moments, others in blocks
    ]
    rows = [jnp.zeros((ROWS, LANES), f32)] * 6
    for start in range(0, tall // ROWS, TOGETHER):
        held = [jnp.zeros((ROWS, LANES), f32)] * (6 * TOGETHER)
        for distance, (moments, others) in zip(distances, blocks):
            for k in range(moments.shape[0]):
                summed = [moments[k, r : r + 1, :] for r in range(6)]
                for i in range(TOGETHER):
                    low = (start + i) * ROWS
                    inverse = lax.rsqrt(distance[low : low + ROWS, k * LANES : (k + 1) * LANES])
                    weight = inverse * inverse * inverse
                    for r in range(6):
                        held[6 * i + r] += weight * summed[r]
        for i in range(TOGETHER):
            mask = diagonal == (start + i) * ROWS
            for r in range(6):
                value = jnp.sum(held[6 * i + r], axis=1, keepdims=True)
                rows[r] = rows[r] + jnp.where(mask, value, 0.0)
    return rows


def repeat(count, body, carried):
    if count <= UNROLLED:
        for i in range(count):
            carried = body(i, carried)
        return carried
    return lax.fori_loop(0, count, body, carried)


def quarter_speed(scale, along, terms, blocks):
    if isinstance(blocks, list):
        rows = quarter(terms, blocks)
    else:
        moments, others = blocks
        count = others.shape[0]
        if count <= UNROLLED:
            rows = quarter(terms, [(moments.at[i], others.at[i]) for i in range(count)])
        else:

            def add(i, rows):
                more = quarter(terms, [(moments.at[i], others.at[i])])
                return tuple(a + b for a, b in zip(rows, more))

            rows = lax.fori_loop(0, count, add, (jnp.zeros((ROWS, LANES), f32),) * 6)
    angles = terms.shape[0]
    ax, ay, az, bx, by, bz = [jnp.sum(r, axis=0, keepdims=True) for r in rows]
    tx, ty, tz = [
        jnp.concatenate([along[m : m + 1, :], jnp.zeros((1, LANES - angles), f32)], axis=1)
        for m in range(3)
    ]
    return jnp.concatenate(
        [
            scale * (ay * tz - az * ty - bx),
            scale * (az * tx - ax * tz - by),
            scale * (ax * ty - ay * tx - bz),
            jnp.zeros((ROWS - 3, LANES), f32),
        ],
        axis=0,
    )


def place_quarters(outer, ways, angles, speeds, result):
    per = LANES // angles
    parts = ways // per
    me = lax.axis_index("tgt")
    for i, step in enumerate(line_order(outer)):
        if step < ways:
            place = source_of(me, turn(step, ways), ways)
            moved = pltpu.roll(speeds[i], (place % per) * angles, 1)
            for m in range(3):
                result[pl.ds(m * parts + place // per, 1), :] += moved[m : m + 1, :]


def early_kernel(scale, ways, outer, inner, *refs):
    messages, (after, speeds, moments, others, along, terms) = refs[: outer - 1], refs[outer - 1 :]
    middle = middle_of(outer, inner)
    angles = along.shape[2]
    for i, message in enumerate(messages):
        tile_terms(message, middle, moments.at[i], others.at[i])
        along[i], terms[i] = point_terms(message, angles, angles, middle)

    def one(i, unused):
        speeds[i] = quarter_speed(scale, along.at[i], terms[i], (moments, others))
        return unused

    repeat(outer - 1, one, 0)


def late_kernel(scale, ways, outer, inner, *refs):
    (message, before, moments, others, along, terms, result, last_moments, last_others, speeds) = refs
    middle = middle_of(outer, inner)
    angles = along.shape[2]
    tile_terms(message, middle, last_moments, last_others)
    last_along, last_terms = point_terms(message, angles, angles, middle)

    def one(i, unused):
        speeds[i] = before[i] + quarter_speed(
            scale, along.at[i], terms[i], [(last_moments, last_others)]
        )
        return unused

    repeat(outer - 1, one, 0)
    speeds[outer - 1] = quarter_speed(
        scale, last_along, last_terms, (moments, others)
    ) + quarter_speed(scale, last_along, last_terms, [(last_moments, last_others)])
    result[...] = jnp.zeros(result.shape, f32)
    place_quarters(outer, ways, angles, speeds, result)


def own_kernel(scale, ways, outer, inner, *refs):
    messages, (moments, others, last_moments, last_others) = refs[:outer], refs[outer : outer + 4]
    after, result, along, terms, speeds = refs[outer + 4 :]
    middle = middle_of(outer, inner)
    angles = along.shape[2]
    for i, message in enumerate(messages):
        along[i], terms[i] = point_terms(message, 0, angles, middle)

    def one(i, unused):
        if outer <= UNROLLED:
            blocks = [(moments.at[j], others.at[j]) for j in range(outer - 1)]
            speeds[i] = quarter_speed(
                scale, along.at[i], terms[i], blocks + [(last_moments, last_others)]
            )
        else:
            speeds[i] = quarter_speed(
                scale, along.at[i], terms[i], (moments, others)
            ) + quarter_speed(scale, along.at[i], terms[i], [(last_moments, last_others)])
        return unused

    repeat(outer, one, 0)
    result[...] = jnp.zeros(result.shape, f32)
    place_quarters(outer, ways, angles, speeds, result)


def merge_kernel(rows, own, arrived, picks, result):
    result[...] = jnp.zeros(result.shape, f32)
    result[0:rows, :] = own[0:rows, :] + arrived[0:rows, :]
    result[rows : rows + picks.shape[0], :] = picks[...]


def wall_kernel(ways, *refs):
    partials = refs[:ways]
    (still, inner_cells, strength, index, wall, grid, new_strength,
     fixed, picked, rows, sem) = refs[ways:]
    angles = grid.shape[2]
    total = angles * ways
    parts = total // LANES
    rows_of = 3 * parts
    slots = picked.shape[0] // ways
    me = lax.axis_index("tgt")
    copy = pltpu.make_async_copy(index, rows, sem)
    copy.start()
    for step, partial in enumerate(partials):
        picked[step * slots : (step + 1) * slots, :] = partial[rows_of : rows_of + slots, :]
    added = partials[0][0:rows_of, :]
    for partial in partials[1:]:
        added = added + partial[0:rows_of, :]
    speed = [
        jnp.concatenate([added[r : r + 1] for r in range(m * parts, (m + 1) * parts)], axis=1)
        for m in range(3)
    ]
    stacked = jnp.concatenate(speed + [jnp.zeros((ROWS - 3, total), f32)], axis=0)
    own = pltpu.roll(stacked, total - me * angles, 1)
    for m in range(3):
        wall[m] = own[m : m + 1, 0:angles]

    first = lax.broadcasted_iota(jnp.int32, (ROWS, total), 0) == 0
    field = [inner_cells[m] for m in range(3)]
    local_swirl = inner_cells[3]
    local_diff = inner_cells[4]
    for counter in range(SUBSTEPS):
        transport = 0.5 * (local_swirl + swirl_gain * field[2])
        renewed = []
        for m in range(3):
            center = field[m]
            eastern = pltpu.roll(center, total - 1, 1)
            western = pltpu.roll(center, 1, 1)
            outward = pltpu.roll(center, ROWS - 1, 0)
            inward = jnp.where(first, speed[m], pltpu.roll(center, 1, 0))
            renewed.append(
                center
                + local_diff * (eastern + western + outward + inward - 4.0 * center)
                - transport * (eastern - western)
            )
        field = renewed
    fixed[:, 0 : 3 * ROWS] = jnp.transpose(jnp.concatenate(field, axis=0))
    near = lax.broadcasted_iota(jnp.int32, (angles, LANES), 1) < SUBSTEPS
    mine = fixed[pl.ds(pl.multiple_of(me * angles, ROWS), angles), :]
    for m in range(3):
        moved = mine if m == 0 else pltpu.roll(mine, LANES - m * ROWS, 1)
        grid[0, m] = jnp.where(near, moved, still[m])
    near = lax.broadcasted_iota(jnp.int32, (1, LANES), 1) < SUBSTEPS
    pieces = strength.shape[1] // LANES
    copy.wait()
    for b in range(3 * pieces):
        q = rows[b, 0]
        c, part = b // pieces, slice((b % pieces) * LANES, (b % pieces + 1) * LANES)
        there = jnp.maximum(q, 0)
        row = pltpu.roll(
            fixed[pl.ds(there % total, 1), :], (LANES - there // total * ROWS) % LANES, 1
        )
        row = jnp.where(near, row, picked[pl.ds(rows[b, 1], 1), :])
        new_strength[c : c + 1, part] = jnp.where(q >= 0, row, strength[c : c + 1, part])


def send(block, pairs):
    return lax.ppermute(block, ("src", "tgt"), pairs)


def on_device(
    particle_position,
    particle_strength,
    core_radius,
    boundary_points,
    vorticity,
    swirl,
    diffusivity,
    intersection_source,
    intersection_target,
):
    sources = lax.axis_size("src")
    ways = lax.axis_size("tgt")
    planes, comps, angles, radial = vorticity.shape
    per_device = particle_position.shape[1]
    tiles = per_device // LANES
    blocks = intersection_source.shape[2]
    inner = 2 if sources % 2 == 0 else 1
    outer = sources // inner
    total = angles * ways
    scale = 1.6 / (4.0 * math.pi * math.sqrt(per_device * ways * sources))

    def pairs(move):
        found = []
        for s in range(sources):
            for t in range(ways):
                o, i, u = move(s // inner, s % inner, t)
                found.append((s * ways + t, (o * inner + i) * ways + u))
        return found

    def over_tgt(block, step):
        return send(block, pairs(lambda o, i, t: (o, i, partner(t, step, ways))))

    given = (
        particle_position, particle_strength, core_radius, boundary_points,
        vorticity, swirl, diffusivity, intersection_source, intersection_target,
    )
    *messages, own, source, target = pl.pallas_call(
        functools.partial(particles_kernel, inner, outer),
        out_shape=(shape(tiles, ROWS, LANES),) * outer + (
            shape(5, angles, LANES),
            jax.ShapeDtypeStruct(intersection_source.shape, jnp.int32),
            jax.ShapeDtypeStruct(intersection_target.shape, jnp.int32),
        ),
        in_specs=[hbm()] * 9,
        out_specs=(vmem(),) * (outer + 3),
        scratch_shapes=[pltpu.VMEM(a.shape, f32) for a in given[0:4]]
        + [pltpu.SemaphoreType.DMA((9,))],
        compiler_params=limit(4),
        name="particles",
    )(*stay(*given))
    line = [messages[0]] + [
        send(
            message,
            pairs(lambda o, i, t: (partner(o, k, outer), i, partner(t, turn(k, ways), ways))),
        )
        for k, message in zip(line_order(outer)[1:], messages[1:])
    ]

    edges = pl.pallas_call(
        edges_kernel,
        out_shape=shape(11, ROWS, LANES),
        in_specs=[vmem()] * 3,
        out_specs=vmem(),
        compiler_params=limit(4),
        cost_estimate=cost(1 << 31, 1 << 10),
        name="edges",
    )(own, source, target)
    steps = tgt_order(ways)
    around = [edges] + [over_tgt(edges, k) for k in steps[1:]]

    rows = 3 * total // LANES
    slots = blocks
    sums_shape = shape(-(-rows // ROWS) * ROWS, LANES)
    along_shape = (ROWS, angles)
    terms_shape = (angles, TERMS)
    others_shape = (TERMS, per_device)
    early = outer - 1
    before, *held = pl.pallas_call(
        functools.partial(early_kernel, scale, ways, outer, inner),
        out_shape=(
            shape(early, ROWS, LANES),
            shape(early, tiles, ROWS, LANES),
            jax.ShapeDtypeStruct((early, *others_shape), bf16),
            shape(early, *along_shape),
            jax.ShapeDtypeStruct((early, *terms_shape), bf16),
        ),
        in_specs=[vmem()] * outer,
        out_specs=(vmem(),) * 5,
        compiler_params=limit(12),
        cost_estimate=cost(1 << 10, 1 << 10),
        name="early",
    )(*line[:-1], edges)
    for_partner, last_moments, last_others = pl.pallas_call(
        functools.partial(late_kernel, scale, ways, outer, inner),
        out_shape=(
            sums_shape,
            shape(tiles, ROWS, LANES),
            jax.ShapeDtypeStruct(others_shape, bf16),
        ),
        in_specs=[vmem()] * 6,
        out_specs=(vmem(),) * 3,
        scratch_shapes=[pltpu.VMEM((outer, ROWS, LANES), f32)],
        compiler_params=limit(12),
        cost_estimate=cost(1 << 30, 1 << 10),
        name="late",
    )(line[-1], before, *held)
    arrived = send(for_partner, pairs(lambda o, i, t: (o, inner - 1 - i, t)))
    own_sum = pl.pallas_call(
        functools.partial(own_kernel, scale, ways, outer, inner),
        out_shape=sums_shape,
        in_specs=[vmem()] * (outer + 5),
        out_specs=vmem(),
        scratch_shapes=[
            pltpu.VMEM((outer, *along_shape), f32),
            pltpu.VMEM((outer, *terms_shape), bf16),
            pltpu.VMEM((outer, ROWS, LANES), f32),
        ],
        compiler_params=limit(12),
        cost_estimate=cost(1 << 31, 1 << 10),
        name="own",
    )(*line, held[0], held[1], last_moments, last_others, for_partner)
    still, picks, inner_cells, index = pl.pallas_call(
        functools.partial(still_kernel, ways),
        out_shape=(
            shape(3, angles, LANES),
            shape(slots, LANES),
            shape(5, ROWS, total),
            jax.ShapeDtypeStruct((16 * ((blocks + 15) // 16), LANES), jnp.int32),
        ),
        in_specs=[vmem()] * (ways + 3),
        out_specs=(vmem(),) * 4,
        scratch_shapes=[
            pltpu.VMEM((ways,) + edges.shape, f32),
            pltpu.SMEM(source.shape, jnp.int32),
            pltpu.SemaphoreType.DMA,
        ],
        compiler_params=limit(8),
        name="still",
    )(*around, own, source, own_sum)
    partial_sum = pl.pallas_call(
        functools.partial(merge_kernel, rows),
        out_shape=shape(-(-(rows + blocks) // ROWS) * ROWS, LANES),
        in_specs=[vmem()] * 3,
        out_specs=vmem(),
        compiler_params=limit(4),
        name="merge",
    )(own_sum, arrived, picks)
    partials = [partial_sum] + [over_tgt(partial_sum, k) for k in steps[1:]]

    wall, grid, new_strength = pl.pallas_call(
        functools.partial(wall_kernel, ways),
        out_shape=(shape(3, planes, angles), shape(*vorticity.shape), shape(3, per_device)),
        in_specs=[vmem()] * (ways + 4),
        out_specs=(vmem(),) * 3,
        scratch_shapes=[
            pltpu.VMEM((total, LANES), f32),
            pltpu.VMEM((slots * ways, LANES), f32),
            pltpu.SMEM(index.shape, jnp.int32),
            pltpu.SemaphoreType.DMA,
        ],
        compiler_params=limit(16),
        name="wall",
    )(*partials, still, inner_cells, particle_strength, index)
    return (wall, grid, new_strength)


def solution(mesh):
    in_specs = (
        P(None, ("src", "tgt")),
        P(None, ("src", "tgt")),
        P(None, ("src", "tgt")),
        P(None, None, "tgt"),
        P("src", None, "tgt", None),
        P("src", "tgt", None),
        P("src", "tgt", None),
        P("src", "tgt", None),
        P("src", "tgt", None),
    )
    out_specs = (P(None, "src", "tgt"), P("src", None, "tgt", None), P(None, ("src", "tgt")))
    return jax.shard_map(
        on_device, mesh=mesh, in_specs=in_specs, out_specs=out_specs, check_vma=False
    )
```

```python
import functools
import math

import jax
import jax.numpy as jnp
from jax import lax
from jax.experimental import pallas as pl
from jax.experimental.pallas import tpu as pltpu
from jax.sharding import PartitionSpec as P

SUBSTEPS = 3
LANES = 128
ROWS = 8
TOGETHER = 2
TERMS = 48
UNROLLED = 4
swirl_gain = 0.2
f32 = jnp.float32
bf16 = jnp.bfloat16


def vmem():
    return pl.BlockSpec(memory_space=pltpu.VMEM)


def smem():
    return pl.BlockSpec(memory_space=pltpu.SMEM)


def hbm():
    return pl.BlockSpec(memory_space=pltpu.HBM)


def stay(*arrays):
    return [pltpu.with_memory_space_constraint(a, pltpu.HBM) for a in arrays]


def shape(*dims):
    return jax.ShapeDtypeStruct(dims, f32)


def limit(megabytes):
    return pltpu.CompilerParams(vmem_limit_bytes=megabytes << 20)


def cost(flops, size):
    return pl.CostEstimate(flops=flops, bytes_accessed=size, transcendentals=0)


def divisor(number, most):
    return max(c for c in range(1, min(number, most) + 1) if number % c == 0)


def power_of_two(number):
    return number & (number - 1) == 0


def partner(index, step, count):
    return index ^ step if power_of_two(count) else (index + step) % count


def source_of(index, step, count):
    return index ^ step if power_of_two(count) else (index - step) % count


def line_order(outer):
    return [0, *range(outer // 2, outer), *range(1, outer // 2)]


def tgt_order(ways):
    return [0, *reversed(range(1, ways))]


def turn(step, ways):
    return {1: 2, 2: 3, 3: 1}.get(step % ways, step % ways)


def particles_kernel(inner, outer, *refs):
    given, messages = refs[:9], refs[9 : 9 + outer]
    own, lists, held, sems = refs[9 + outer], refs[10 + outer : 12 + outer], refs[12 + outer : -1], refs[-1]
    targets = (*held, own.at[0:3], own.at[3:4], own.at[4:5], *lists)
    sources = (*given[0:4], given[4].at[0], *given[5:9])
    copies = [
        pltpu.make_async_copy(a, b, sems.at[i]) for i, (a, b) in enumerate(zip(sources, targets))
    ]
    for copy in copies:
        copy.start()
    for copy in copies[0:4]:
        copy.wait()
    pos, strength, radius, points = held
    tiles = pos.shape[1] // LANES
    angles = points.shape[2]
    src = lax.axis_index("src")
    core = radius[...] * radius[...]
    for step, message in zip(line_order(outer), messages):
        there = partner(src // inner, step, outer) * inner
        planes = (there + src % inner, there + inner - 1 - src % inner)
        for k in range(tiles):
            part = slice(k * LANES, (k + 1) * LANES)
            message[k, 0:3, :] = pos[:, part]
            message[k, 3:6, :] = strength[:, part]
            message[k, 6:7, :] = core[:, part]
            message[k, 7:8, :] = jnp.zeros((1, LANES), f32)
        for m in range(3):
            for i, plane in enumerate(planes):
                message[m, 7:8, i * angles : (i + 1) * angles] = points[m, pl.ds(plane, 1), :]
    for copy in copies[4:]:
        copy.wait()


def edges_kernel(own, own_source, own_target, message):
    angles = own.shape[1]
    blocks = own_source.shape[2]
    total = angles * lax.axis_size("tgt")
    half = ROWS // 2
    for c in range(5):
        message[c, :, 0:angles] = jnp.transpose(own[c])[0:ROWS, :]
        message[c, :, angles:LANES] = jnp.zeros((ROWS, LANES - angles), f32)
        message[6 + c, 0:half, :] = own[c, 0:half]
        message[6 + c, half:ROWS, :] = own[c, angles - half : angles]
    message[5] = jnp.full((ROWS, LANES), -1.0, f32)
    q = own_source[0]
    row = (q // angles) * total + lax.axis_index("tgt") * angles + q % angles
    message[5, 0:1, 0:blocks] = row.astype(f32)
    message[5, 1:2, 0:blocks] = own_target[0].astype(f32)


def still_kernel(ways, *refs):
    messages = refs[:ways]
    own, lists, after, grid, picks, inner_cells, index, component, placed, source, sem = refs[ways:]
    copy = pltpu.make_async_copy(lists, source, sem)
    copy.start()
    angles = own.shape[1]
    height = angles + ROWS
    blocks = lists.shape[2]
    me = lax.axis_index("tgt")
    for step, message in zip(tgt_order(ways), messages):
        placed[source_of(me, step, ways)] = message[...]

    for c in range(5):
        inner_cells[c] = jnp.concatenate(
            [placed[t, c, :, 0:angles] for t in range(ways)], axis=1
        )

    shaped = index.shape
    name = (me * blocks + lax.broadcasted_iota(jnp.int32, shaped, 0)).astype(f32)
    lane = lax.broadcasted_iota(jnp.int32, shaped, 1).astype(f32)
    row = jnp.full(shaped, -1.0, f32)
    slot = jnp.zeros(shaped, f32)
    for step, message in enumerate(messages):
        match = message[5, 1:2, :] == name
        row = jnp.maximum(row, jnp.where(match, message[5, 0:1, :], -1.0))
        slot = jnp.maximum(slot, jnp.where(match, lane + float(step * picks.shape[0]), 0.0))
    row = jnp.max(row, axis=1, keepdims=True)
    slot = jnp.max(slot, axis=1, keepdims=True)
    total = angles * ways
    comp = jnp.where(row >= 0.0, 0.0, -1.0)
    for m in range(1, 3):
        comp = jnp.where(row >= float(m * total), float(m), comp)
    angle = row - jnp.maximum(comp, 0.0) * float(total)
    index[...] = jnp.where(lane < 1.0, jnp.maximum(angle, 0.0), slot).astype(jnp.int32)
    component[...] = jnp.broadcast_to(comp, shaped)

    upper = lax.broadcasted_iota(jnp.int32, (ROWS, LANES), 0) < ROWS // 2
    east = lax.rem(me + 1, ways)
    west = lax.rem(me + ways - 1, ways)
    cells = [
        jnp.concatenate(
            [own[c], jnp.where(upper, placed[east, 6 + c], placed[west, 6 + c])], axis=0
        )
        for c in range(5)
    ]
    field, local_swirl, local_diff = cells[0:3], cells[3], cells[4]
    lane = lax.broadcasted_iota(jnp.int32, (height, LANES), 1)
    for counter in range(SUBSTEPS):
        transport = 0.5 * (local_swirl + swirl_gain * field[2])
        renewed = []
        for m in range(3):
            center = field[m]
            eastern = pltpu.roll(center, height - 1, 0)
            western = pltpu.roll(center, 1, 0)
            outward = jnp.where(lane == LANES - 1, 0.0, pltpu.roll(center, LANES - 1, 1))
            inward = jnp.where(lane == 0, 0.0, pltpu.roll(center, 1, 1))
            renewed.append(
                center
                + local_diff * (eastern + western + outward + inward - 4.0 * center)
                - transport * (eastern - western)
            )
        field = renewed
    for m in range(3):
        grid[m] = field[m][0:angles]
    picks[...] = jnp.zeros(picks.shape, f32)
    copy.wait()
    for i in range(blocks):
        q = source[0, 0, i]
        picks[i : i + 1, :] = grid[q // angles, pl.ds(q % angles, 1), :]


def three_parts(value):
    high = value.astype(bf16).astype(f32)
    rest = value - high
    middle = rest.astype(bf16).astype(f32)
    return high, middle, rest - middle


def middle_of(outer, inner):
    here = (lax.axis_index("src") // inner).astype(f32)
    return 0.5, 0.5, (here + 0.5) * (1.0 / outer)


def point_terms(message, lane, angles, middle):
    x, y, z = [message[m, 7:8, lane : lane + angles] - middle[m] for m in range(3)]
    nothing = jnp.zeros((3, angles), f32)
    vector = jnp.concatenate(
        [-2.0 * x, -2.0 * y, -2.0 * z, jnp.ones_like(x), x * x + y * y + z * z, nothing], axis=0
    )
    high, middling, low = three_parts(vector)
    terms = jnp.transpose(jnp.concatenate([high, middling, low, high, middling, high], axis=0))
    return jnp.concatenate([x, y, z, nothing, nothing[0:2]], axis=0), terms.astype(bf16)


def tile_terms(message, middle, moments, others):
    one = jnp.ones((1, LANES), f32)
    nothing = jnp.zeros((3, LANES), f32)
    for k in range(message.shape[0]):
        px, py, pz = [message[k, r : r + 1, :] - middle[r] for r in range(3)]
        sx, sy, sz, cc = [message[k, r : r + 1, :] for r in range(3, 7)]
        moments[k] = jnp.concatenate(
            [sx, sy, sz, sy * pz - sz * py, sz * px - sx * pz, sx * py - sy * px, nothing[0:2]],
            axis=0,
        )
        vector = jnp.concatenate(
            [px, py, pz, px * px + py * py + (pz * pz + cc), one, nothing], axis=0
        )
        high, middling, low = three_parts(vector)
        others[:, k * LANES : (k + 1) * LANES] = jnp.concatenate(
            [high, high, high, middling, middling, low], axis=0
        ).astype(bf16)


def quarter(terms, blocks):
    tall = terms.shape[0]
    diagonal = lax.broadcasted_iota(jnp.int32, (ROWS, LANES), 1) - lax.broadcasted_iota(
        jnp.int32, (ROWS, LANES), 0
    )
    distances = [
        jnp.dot(terms, others[...], preferred_element_type=f32) for moments, others in blocks
    ]
    rows = [jnp.zeros((ROWS, LANES), f32)] * 6
    for start in range(0, tall // ROWS, TOGETHER):
        held = [jnp.zeros((ROWS, LANES), f32)] * (6 * TOGETHER)
        for distance, (moments, others) in zip(distances, blocks):
            for k in range(moments.shape[0]):
                summed = [moments[k, r : r + 1, :] for r in range(6)]
                for i in range(TOGETHER):
                    low = (start + i) * ROWS
                    inverse = lax.rsqrt(distance[low : low + ROWS, k * LANES : (k + 1) * LANES])
                    weight = inverse * inverse * inverse
                    for r in range(6):
                        held[6 * i + r] += weight * summed[r]
        for i in range(TOGETHER):
            mask = diagonal == (start + i) * ROWS
            for r in range(6):
                value = jnp.sum(held[6 * i + r], axis=1, keepdims=True)
                rows[r] = rows[r] + jnp.where(mask, value, 0.0)
    return rows


def repeat(count, body, carried):
    if count <= UNROLLED:
        for i in range(count):
            carried = body(i, carried)
        return carried
    return lax.fori_loop(0, count, body, carried)


def quarter_speed(scale, along, terms, blocks):
    if isinstance(blocks, list):
        rows = quarter(terms, blocks)
    else:
        moments, others = blocks
        count = others.shape[0]
        if count <= UNROLLED:
            rows = quarter(terms, [(moments.at[i], others.at[i]) for i in range(count)])
        else:

            def add(i, rows):
                more = quarter(terms, [(moments.at[i], others.at[i])])
                return tuple(a + b for a, b in zip(rows, more))

            rows = lax.fori_loop(0, count, add, (jnp.zeros((ROWS, LANES), f32),) * 6)
    angles = terms.shape[0]
    ax, ay, az, bx, by, bz = [jnp.sum(r, axis=0, keepdims=True) for r in rows]
    tx, ty, tz = [
        jnp.concatenate([along[m : m + 1, :], jnp.zeros((1, LANES - angles), f32)], axis=1)
        for m in range(3)
    ]
    return jnp.concatenate(
        [
            scale * (ay * tz - az * ty - bx),
            scale * (az * tx - ax * tz - by),
            scale * (ax * ty - ay * tx - bz),
            jnp.zeros((ROWS - 3, LANES), f32),
        ],
        axis=0,
    )


def place_quarters(outer, ways, angles, speeds, result):
    per = LANES // angles
    parts = ways // per
    me = lax.axis_index("tgt")
    for i, step in enumerate(line_order(outer)):
        if step < ways:
            place = source_of(me, turn(step, ways), ways)
            moved = speeds[i]
            for step in range(1, per):
                moved = jnp.where(
                    place % per == step, pltpu.roll(speeds[i], step * angles, 1), moved
                )
            for m in range(3):
                result[pl.ds(m * parts + place // per, 1), :] += moved[m : m + 1, :]


def early_kernel(scale, ways, outer, inner, *refs):
    messages, (after, speeds, moments, others, along, terms) = refs[: outer - 1], refs[outer - 1 :]
    middle = middle_of(outer, inner)
    angles = along.shape[2]
    for i, message in enumerate(messages):
        tile_terms(message, middle, moments.at[i], others.at[i])
        along[i], terms[i] = point_terms(message, angles, angles, middle)

    def one(i, unused):
        speeds[i] = quarter_speed(scale, along.at[i], terms[i], (moments, others))
        return unused

    repeat(outer - 1, one, 0)


def late_kernel(scale, ways, outer, inner, *refs):
    (message, before, moments, others, along, terms, result, last_moments, last_others, speeds) = refs
    middle = middle_of(outer, inner)
    angles = along.shape[2]
    tile_terms(message, middle, last_moments, last_others)
    last_along, last_terms = point_terms(message, angles, angles, middle)

    def one(i, unused):
        speeds[i] = before[i] + quarter_speed(
            scale, along.at[i], terms[i], [(last_moments, last_others)]
        )
        return unused

    repeat(outer - 1, one, 0)
    speeds[outer - 1] = quarter_speed(
        scale, last_along, last_terms, (moments, others)
    ) + quarter_speed(scale, last_along, last_terms, [(last_moments, last_others)])
    result[...] = jnp.zeros(result.shape, f32)
    place_quarters(outer, ways, angles, speeds, result)


def own_kernel(scale, ways, outer, inner, *refs):
    messages, (moments, others, last_moments, last_others) = refs[:outer], refs[outer : outer + 4]
    after, result, along, terms, speeds = refs[outer + 4 :]
    middle = middle_of(outer, inner)
    angles = along.shape[2]
    for i, message in enumerate(messages):
        along[i], terms[i] = point_terms(message, 0, angles, middle)

    def one(i, unused):
        if outer <= UNROLLED:
            blocks = [(moments.at[j], others.at[j]) for j in range(outer - 1)]
            speeds[i] = quarter_speed(
                scale, along.at[i], terms[i], blocks + [(last_moments, last_others)]
            )
        else:
            speeds[i] = quarter_speed(
                scale, along.at[i], terms[i], (moments, others)
            ) + quarter_speed(scale, along.at[i], terms[i], [(last_moments, last_others)])
        return unused

    repeat(outer, one, 0)
    result[...] = jnp.zeros(result.shape, f32)
    place_quarters(outer, ways, angles, speeds, result)


def merge_kernel(rows, own, arrived, picks, result):
    result[...] = jnp.zeros(result.shape, f32)
    result[0:rows, :] = own[0:rows, :] + arrived[0:rows, :]
    result[rows : rows + picks.shape[0], :] = picks[...]


def wall_kernel(ways, *refs):
    partials = refs[:ways]
    (still, inner_cells, strength, index, component, wall, grid, new_strength,
     fixed, found, picked, rows, sem) = refs[ways:]
    angles = grid.shape[2]
    total = angles * ways
    parts = total // LANES
    rows_of = 3 * parts
    slots = picked.shape[0] // ways
    me = lax.axis_index("tgt")
    copy = pltpu.make_async_copy(index, rows, sem)
    copy.start()
    for step, partial in enumerate(partials):
        picked[step * slots : (step + 1) * slots, :] = partial[rows_of : rows_of + slots, :]
    added = partials[0][0:rows_of, :]
    for partial in partials[1:]:
        added = added + partial[0:rows_of, :]
    speed = [
        jnp.concatenate([added[r : r + 1] for r in range(m * parts, (m + 1) * parts)], axis=1)
        for m in range(3)
    ]
    for m in range(3):
        own = speed[m][:, 0:angles]
        for t in range(1, ways):
            own = jnp.where(me == t, speed[m][:, t * angles : (t + 1) * angles], own)
        wall[m] = own

    first = lax.broadcasted_iota(jnp.int32, (ROWS, total), 0) == 0
    field = [inner_cells[m] for m in range(3)]
    local_swirl = inner_cells[3]
    local_diff = inner_cells[4]
    for counter in range(SUBSTEPS):
        transport = 0.5 * (local_swirl + swirl_gain * field[2])
        renewed = []
        for m in range(3):
            center = field[m]
            eastern = pltpu.roll(center, total - 1, 1)
            western = pltpu.roll(center, 1, 1)
            outward = pltpu.roll(center, ROWS - 1, 0)
            inward = jnp.where(first, speed[m], pltpu.roll(center, 1, 0))
            renewed.append(
                center
                + local_diff * (eastern + western + outward + inward - 4.0 * center)
                - transport * (eastern - western)
            )
        field = renewed
    stacked = jnp.concatenate(field + [jnp.zeros((LANES - 3 * ROWS, total), f32)], axis=0)
    for k in range(parts):
        part = slice(k * LANES, (k + 1) * LANES)
        fixed[part, :] = jnp.transpose(stacked[:, part])
    near = lax.broadcasted_iota(jnp.int32, (angles, LANES), 1) < SUBSTEPS
    mine = fixed[pl.ds(pl.multiple_of(me * angles, ROWS), angles), :]
    for m in range(3):
        moved = mine if m == 0 else pltpu.roll(mine, LANES - m * ROWS, 1)
        grid[0, m] = jnp.where(near, moved, still[m])
    pieces = strength.shape[1] // LANES
    copy.wait()
    found[...] = jnp.zeros(found.shape, f32)
    for b in range(3 * pieces):
        found[0, b : b + 1, :] = fixed[pl.ds(rows[b, 0], 1), :]
        found[1, b : b + 1, :] = picked[pl.ds(rows[b, 1], 1), :]
    comp = component[...]
    row = found[0]
    for m in range(1, 3):
        row = jnp.where(comp == float(m), pltpu.roll(found[0], LANES - m * ROWS, 1), row)
    near = lax.broadcasted_iota(jnp.int32, comp.shape, 1) < SUBSTEPS
    row = jnp.where(near, row, found[1])
    for b in range(3 * pieces):
        c, part = b // pieces, slice((b % pieces) * LANES, (b % pieces + 1) * LANES)
        new_strength[c : c + 1, part] = jnp.where(
            comp[b : b + 1] >= 0.0, row[b : b + 1], strength[c : c + 1, part]
        )


def send(block, pairs):
    return lax.ppermute(block, ("src", "tgt"), pairs)


def on_device(
    particle_position,
    particle_strength,
    core_radius,
    boundary_points,
    vorticity,
    swirl,
    diffusivity,
    intersection_source,
    intersection_target,
):
    sources = lax.axis_size("src")
    ways = lax.axis_size("tgt")
    planes, comps, angles, radial = vorticity.shape
    per_device = particle_position.shape[1]
    tiles = per_device // LANES
    blocks = intersection_source.shape[2]
    inner = 2 if sources % 2 == 0 else 1
    outer = sources // inner
    total = angles * ways
    scale = 1.6 / (4.0 * math.pi * math.sqrt(per_device * ways * sources))

    def pairs(move):
        found = []
        for s in range(sources):
            for t in range(ways):
                o, i, u = move(s // inner, s % inner, t)
                found.append((s * ways + t, (o * inner + i) * ways + u))
        return found

    def over_tgt(block, step):
        return send(block, pairs(lambda o, i, t: (o, i, partner(t, step, ways))))

    given = (
        particle_position, particle_strength, core_radius, boundary_points,
        vorticity, swirl, diffusivity, intersection_source, intersection_target,
    )
    *messages, own, source, target = pl.pallas_call(
        functools.partial(particles_kernel, inner, outer),
        out_shape=(shape(tiles, ROWS, LANES),) * outer + (
            shape(5, angles, LANES),
            jax.ShapeDtypeStruct(intersection_source.shape, jnp.int32),
            jax.ShapeDtypeStruct(intersection_target.shape, jnp.int32),
        ),
        in_specs=[hbm()] * 9,
        out_specs=(vmem(),) * (outer + 3),
        scratch_shapes=[pltpu.VMEM(a.shape, f32) for a in given[0:4]]
        + [pltpu.SemaphoreType.DMA((9,))],
        compiler_params=limit(4),
        name="particles",
    )(*stay(*given))
    line = [messages[0]] + [
        send(
            message,
            pairs(lambda o, i, t: (partner(o, k, outer), i, partner(t, turn(k, ways), ways))),
        )
        for k, message in zip(line_order(outer)[1:], messages[1:])
    ]

    edges = pl.pallas_call(
        edges_kernel,
        out_shape=shape(11, ROWS, LANES),
        in_specs=[vmem()] * 3,
        out_specs=vmem(),
        compiler_params=limit(4),
        cost_estimate=cost(1 << 31, 1 << 10),
        name="edges",
    )(own, source, target)
    steps = tgt_order(ways)
    around = [edges] + [over_tgt(edges, k) for k in steps[1:]]

    rows = 3 * total // LANES
    slots = blocks
    sums_shape = shape(-(-rows // ROWS) * ROWS, LANES)
    along_shape = (ROWS, angles)
    terms_shape = (angles, TERMS)
    others_shape = (TERMS, per_device)
    early = outer - 1
    before, *held = pl.pallas_call(
        functools.partial(early_kernel, scale, ways, outer, inner),
        out_shape=(
            shape(early, ROWS, LANES),
            shape(early, tiles, ROWS, LANES),
            jax.ShapeDtypeStruct((early, *others_shape), bf16),
            shape(early, *along_shape),
            jax.ShapeDtypeStruct((early, *terms_shape), bf16),
        ),
        in_specs=[vmem()] * outer,
        out_specs=(vmem(),) * 5,
        compiler_params=limit(12),
        cost_estimate=cost(1 << 10, 1 << 10),
        name="early",
    )(*line[:-1], edges)
    for_partner, last_moments, last_others = pl.pallas_call(
        functools.partial(late_kernel, scale, ways, outer, inner),
        out_shape=(
            sums_shape,
            shape(tiles, ROWS, LANES),
            jax.ShapeDtypeStruct(others_shape, bf16),
        ),
        in_specs=[vmem()] * 6,
        out_specs=(vmem(),) * 3,
        scratch_shapes=[pltpu.VMEM((outer, ROWS, LANES), f32)],
        compiler_params=limit(12),
        cost_estimate=cost(1 << 30, 1 << 10),
        name="late",
    )(line[-1], before, *held)
    arrived = send(for_partner, pairs(lambda o, i, t: (o, inner - 1 - i, t)))
    own_sum = pl.pallas_call(
        functools.partial(own_kernel, scale, ways, outer, inner),
        out_shape=sums_shape,
        in_specs=[vmem()] * (outer + 5),
        out_specs=vmem(),
        scratch_shapes=[
            pltpu.VMEM((outer, *along_shape), f32),
            pltpu.VMEM((outer, *terms_shape), bf16),
            pltpu.VMEM((outer, ROWS, LANES), f32),
        ],
        compiler_params=limit(12),
        cost_estimate=cost(1 << 31, 1 << 10),
        name="own",
    )(*line, held[0], held[1], last_moments, last_others, for_partner)
    still, picks, inner_cells, index, component = pl.pallas_call(
        functools.partial(still_kernel, ways),
        out_shape=(
            shape(3, angles, LANES),
            shape(slots, LANES),
            shape(5, ROWS, total),
            jax.ShapeDtypeStruct((16 * ((blocks + 15) // 16), LANES), jnp.int32),
            shape(16 * ((blocks + 15) // 16), LANES),
        ),
        in_specs=[vmem()] * (ways + 3),
        out_specs=(vmem(),) * 5,
        scratch_shapes=[
            pltpu.VMEM((ways,) + edges.shape, f32),
            pltpu.SMEM(source.shape, jnp.int32),
            pltpu.SemaphoreType.DMA,
        ],
        compiler_params=limit(8),
        name="still",
    )(*around, own, source, own_sum)
    partial_sum = pl.pallas_call(
        functools.partial(merge_kernel, rows),
        out_shape=shape(-(-(rows + blocks) // ROWS) * ROWS, LANES),
        in_specs=[vmem()] * 3,
        out_specs=vmem(),
        compiler_params=limit(4),
        name="merge",
    )(own_sum, arrived, picks)
    partials = [partial_sum] + [over_tgt(partial_sum, k) for k in steps[1:]]

    wall, grid, new_strength = pl.pallas_call(
        functools.partial(wall_kernel, ways),
        out_shape=(shape(3, planes, angles), shape(*vorticity.shape), shape(3, per_device)),
        in_specs=[vmem()] * (ways + 5),
        out_specs=(vmem(),) * 3,
        scratch_shapes=[
            pltpu.VMEM((total, LANES), f32),
            pltpu.VMEM((2, *component.shape), f32),
            pltpu.VMEM((slots * ways, LANES), f32),
            pltpu.SMEM(index.shape, jnp.int32),
            pltpu.SemaphoreType.DMA,
        ],
        compiler_params=limit(16),
        name="wall",
    )(*partials, still, inner_cells, particle_strength, index, component)
    return (wall, grid, new_strength)


def solution(mesh):
    in_specs = (
        P(None, ("src", "tgt")),
        P(None, ("src", "tgt")),
        P(None, ("src", "tgt")),
        P(None, None, "tgt"),
        P("src", None, "tgt", None),
        P("src", "tgt", None),
        P("src", "tgt", None),
        P("src", "tgt", None),
        P("src", "tgt", None),
    )
    out_specs = (P(None, "src", "tgt"), P("src", None, "tgt", None), P(None, ("src", "tgt")))
    return jax.shard_map(
        on_device, mesh=mesh, in_specs=in_specs, out_specs=out_specs, check_vma=False
    )
```

```python
import functools
import math

import jax
import jax.numpy as jnp
from jax import lax
from jax.experimental import pallas as pl
from jax.experimental.pallas import tpu as pltpu
from jax.sharding import PartitionSpec as P

SUBSTEPS = 3
LANES = 128
ROWS = 8
TOGETHER = 2
TERMS = 48
UNROLLED = 4
swirl_gain = 0.2
f32 = jnp.float32
bf16 = jnp.bfloat16


def vmem():
    return pl.BlockSpec(memory_space=pltpu.VMEM)


def smem():
    return pl.BlockSpec(memory_space=pltpu.SMEM)


def hbm():
    return pl.BlockSpec(memory_space=pltpu.HBM)


def stay(*arrays):
    return [pltpu.with_memory_space_constraint(a, pltpu.HBM) for a in arrays]


def shape(*dims):
    return jax.ShapeDtypeStruct(dims, f32)


def limit(megabytes):
    return pltpu.CompilerParams(vmem_limit_bytes=megabytes << 20)


def cost(flops, size):
    return pl.CostEstimate(flops=flops, bytes_accessed=size, transcendentals=0)


def divisor(number, most):
    return max(c for c in range(1, min(number, most) + 1) if number % c == 0)


def power_of_two(number):
    return number & (number - 1) == 0


def partner(index, step, count):
    return index ^ step if power_of_two(count) else (index + step) % count


def source_of(index, step, count):
    return index ^ step if power_of_two(count) else (index - step) % count


def line_order(outer):
    return [0, *range(outer // 2, outer), *range(1, outer // 2)]


def tgt_order(ways):
    return [0, *reversed(range(1, ways))]


def turn(step, ways):
    return {1: 2, 2: 3, 3: 1}.get(step % ways, step % ways)


def particles_kernel(inner, outer, *refs):
    given, messages = refs[:9], refs[9 : 9 + outer]
    own, lists, held, sems = refs[9 + outer], refs[10 + outer : 12 + outer], refs[12 + outer : -1], refs[-1]
    vort, swirl, diff = given[4:7]
    targets = (*held, *[own.at[c] for c in range(5)], *lists)
    sources = (*given[0:4], *[vort.at[0, m] for m in range(3)], swirl.at[0], diff.at[0], *given[7:9])
    copies = [
        pltpu.make_async_copy(a, b, sems.at[i]) for i, (a, b) in enumerate(zip(sources, targets))
    ]
    for copy in copies:
        copy.start()
    for copy in copies[0:4]:
        copy.wait()
    pos, strength, radius, points = held
    tiles = pos.shape[1] // LANES
    angles = points.shape[2]
    src = lax.axis_index("src")
    core = radius[...] * radius[...]
    for step, message in zip(line_order(outer), messages):
        there = partner(src // inner, step, outer) * inner
        planes = (there + src % inner, there + inner - 1 - src % inner)
        for k in range(tiles):
            part = slice(k * LANES, (k + 1) * LANES)
            message[k, 0:3, :] = pos[:, part]
            message[k, 3:6, :] = strength[:, part]
            message[k, 6:7, :] = core[:, part]
            message[k, 7:8, :] = jnp.zeros((1, LANES), f32)
        for m in range(3):
            for i, plane in enumerate(planes):
                message[m, 7:8, i * angles : (i + 1) * angles] = points[m, pl.ds(plane, 1), :]
    for copy in copies[4:]:
        copy.wait()


def edges_kernel(own, own_source, own_target, message):
    angles = own.shape[1]
    blocks = own_source.shape[2]
    total = angles * lax.axis_size("tgt")
    half = ROWS // 2
    for c in range(5):
        message[c, :, 0:angles] = jnp.transpose(own[c])[0:ROWS, :]
        message[c, :, angles:LANES] = jnp.zeros((ROWS, LANES - angles), f32)
        message[6 + c, 0:half, :] = own[c, 0:half]
        message[6 + c, half:ROWS, :] = own[c, angles - half : angles]
    message[5] = jnp.full((ROWS, LANES), -1.0, f32)
    q = own_source[0]
    row = (q // angles) * total + lax.axis_index("tgt") * angles + q % angles
    message[5, 0:1, 0:blocks] = row.astype(f32)
    message[5, 1:2, 0:blocks] = own_target[0].astype(f32)


def still_kernel(ways, *refs):
    messages = refs[:ways]
    own, lists, after, grid, picks, inner_cells, index, placed, source, sem = refs[ways:]
    copy = pltpu.make_async_copy(lists, source, sem)
    copy.start()
    angles = own.shape[1]
    height = angles + ROWS
    blocks = lists.shape[2]
    me = lax.axis_index("tgt")
    for step, message in zip(tgt_order(ways), messages):
        placed[source_of(me, step, ways)] = message[...]

    for c in range(5):
        inner_cells[c] = jnp.concatenate(
            [placed[t, c, :, 0:angles] for t in range(ways)], axis=1
        )

    shaped = index.shape
    name = (me * blocks + lax.broadcasted_iota(jnp.int32, shaped, 0)).astype(f32)
    lane = lax.broadcasted_iota(jnp.int32, shaped, 1).astype(f32)
    row = jnp.full(shaped, -1.0, f32)
    slot = jnp.zeros(shaped, f32)
    for step, message in enumerate(messages):
        match = message[5, 1:2, :] == name
        row = jnp.maximum(row, jnp.where(match, message[5, 0:1, :], -1.0))
        slot = jnp.maximum(slot, jnp.where(match, lane + float(step * picks.shape[0]), 0.0))
    row = jnp.max(row, axis=1, keepdims=True)
    slot = jnp.max(slot, axis=1, keepdims=True)
    index[...] = jnp.where(lane < 1.0, row, slot).astype(jnp.int32)

    upper = lax.broadcasted_iota(jnp.int32, (ROWS, LANES), 0) < ROWS // 2
    east = lax.rem(me + 1, ways)
    west = lax.rem(me + ways - 1, ways)
    cells = [
        jnp.concatenate(
            [own[c], jnp.where(upper, placed[east, 6 + c], placed[west, 6 + c])], axis=0
        )
        for c in range(5)
    ]
    field, local_swirl, local_diff = cells[0:3], cells[3], cells[4]
    lane = lax.broadcasted_iota(jnp.int32, (height, LANES), 1)
    for counter in range(SUBSTEPS):
        transport = 0.5 * (local_swirl + swirl_gain * field[2])
        renewed = []
        for m in range(3):
            center = field[m]
            eastern = pltpu.roll(center, height - 1, 0)
            western = pltpu.roll(center, 1, 0)
            outward = jnp.where(lane == LANES - 1, 0.0, pltpu.roll(center, LANES - 1, 1))
            inward = jnp.where(lane == 0, 0.0, pltpu.roll(center, 1, 1))
            renewed.append(
                center
                + local_diff * (eastern + western + outward + inward - 4.0 * center)
                - transport * (eastern - western)
            )
        field = renewed
    for m in range(3):
        grid[m] = field[m][0:angles]
    picks[...] = jnp.zeros(picks.shape, f32)
    copy.wait()
    for i in range(blocks):
        q = source[0, 0, i]
        picks[i : i + 1, :] = grid[q // angles, pl.ds(q % angles, 1), :]


def three_parts(value):
    high = value.astype(bf16).astype(f32)
    rest = value - high
    middle = rest.astype(bf16).astype(f32)
    return high, middle, rest - middle


def middle_of(outer, inner):
    here = (lax.axis_index("src") // inner).astype(f32)
    return 0.5, 0.5, (here + 0.5) * (1.0 / outer)


def point_terms(message, lane, angles, middle):
    x, y, z = [message[m, 7:8, lane : lane + angles] - middle[m] for m in range(3)]
    nothing = jnp.zeros((3, angles), f32)
    vector = jnp.concatenate(
        [-2.0 * x, -2.0 * y, -2.0 * z, jnp.ones_like(x), x * x + y * y + z * z, nothing], axis=0
    )
    high, middling, low = three_parts(vector)
    terms = jnp.transpose(jnp.concatenate([high, middling, low, high, middling, high], axis=0))
    return jnp.concatenate([x, y, z, nothing, nothing[0:2]], axis=0), terms.astype(bf16)


def tile_terms(message, middle, moments, others):
    one = jnp.ones((1, LANES), f32)
    nothing = jnp.zeros((3, LANES), f32)
    for k in range(message.shape[0]):
        px, py, pz = [message[k, r : r + 1, :] - middle[r] for r in range(3)]
        sx, sy, sz, cc = [message[k, r : r + 1, :] for r in range(3, 7)]
        moments[k] = jnp.concatenate(
            [sx, sy, sz, sy * pz - sz * py, sz * px - sx * pz, sx * py - sy * px, nothing[0:2]],
            axis=0,
        )
        vector = jnp.concatenate(
            [px, py, pz, px * px + py * py + (pz * pz + cc), one, nothing], axis=0
        )
        high, middling, low = three_parts(vector)
        others[:, k * LANES : (k + 1) * LANES] = jnp.concatenate(
            [high, high, high, middling, middling, low], axis=0
        ).astype(bf16)


def quarter(terms, blocks):
    tall = terms.shape[0]
    diagonal = lax.broadcasted_iota(jnp.int32, (ROWS, LANES), 1) - lax.broadcasted_iota(
        jnp.int32, (ROWS, LANES), 0
    )
    distances = [
        jnp.dot(terms, others[...], preferred_element_type=f32) for moments, others in blocks
    ]
    rows = [jnp.zeros((ROWS, LANES), f32)] * 6
    for start in range(0, tall // ROWS, TOGETHER):
        held = [jnp.zeros((ROWS, LANES), f32)] * (6 * TOGETHER)
        for distance, (moments, others) in zip(distances, blocks):
            for k in range(moments.shape[0]):
                summed = [moments[k, r : r + 1, :] for r in range(6)]
                for i in range(TOGETHER):
                    low = (start + i) * ROWS
                    inverse = lax.rsqrt(distance[low : low + ROWS, k * LANES : (k + 1) * LANES])
                    weight = inverse * inverse * inverse
                    for r in range(6):
                        held[6 * i + r] += weight * summed[r]
        for i in range(TOGETHER):
            mask = diagonal == (start + i) * ROWS
            for r in range(6):
                value = jnp.sum(held[6 * i + r], axis=1, keepdims=True)
                rows[r] = rows[r] + jnp.where(mask, value, 0.0)
    return rows


def repeat(count, body, carried):
    if count <= UNROLLED:
        for i in range(count):
            carried = body(i, carried)
        return carried
    return lax.fori_loop(0, count, body, carried)


def quarter_speed(scale, along, terms, blocks):
    if isinstance(blocks, list):
        rows = quarter(terms, blocks)
    else:
        moments, others = blocks
        count = others.shape[0]
        if count <= UNROLLED:
            rows = quarter(terms, [(moments.at[i], others.at[i]) for i in range(count)])
        else:

            def add(i, rows):
                more = quarter(terms, [(moments.at[i], others.at[i])])
                return tuple(a + b for a, b in zip(rows, more))

            rows = lax.fori_loop(0, count, add, (jnp.zeros((ROWS, LANES), f32),) * 6)
    angles = terms.shape[0]
    ax, ay, az, bx, by, bz = [jnp.sum(r, axis=0, keepdims=True) for r in rows]
    tx, ty, tz = [
        jnp.concatenate([along[m : m + 1, :], jnp.zeros((1, LANES - angles), f32)], axis=1)
        for m in range(3)
    ]
    return jnp.concatenate(
        [
            scale * (ay * tz - az * ty - bx),
            scale * (az * tx - ax * tz - by),
            scale * (ax * ty - ay * tx - bz),
            jnp.zeros((ROWS - 3, LANES), f32),
        ],
        axis=0,
    )


def place_quarters(outer, ways, angles, speeds, result):
    per = LANES // angles
    parts = ways // per
    me = lax.axis_index("tgt")
    for i, step in enumerate(line_order(outer)):
        if step < ways:
            place = source_of(me, turn(step, ways), ways)
            moved = speeds[i]
            for step in range(1, per):
                moved = jnp.where(
                    place % per == step, pltpu.roll(speeds[i], step * angles, 1), moved
                )
            for m in range(3):
                result[pl.ds(m * parts + place // per, 1), :] += moved[m : m + 1, :]


def early_kernel(scale, ways, outer, inner, *refs):
    messages, (after, speeds, moments, others, along, terms) = refs[: outer - 1], refs[outer - 1 :]
    middle = middle_of(outer, inner)
    angles = along.shape[2]
    for i, message in enumerate(messages):
        tile_terms(message, middle, moments.at[i], others.at[i])
        along[i], terms[i] = point_terms(message, angles, angles, middle)

    def one(i, unused):
        speeds[i] = quarter_speed(scale, along.at[i], terms[i], (moments, others))
        return unused

    repeat(outer - 1, one, 0)


def late_kernel(scale, ways, outer, inner, *refs):
    (message, before, moments, others, along, terms, result, last_moments, last_others, speeds) = refs
    middle = middle_of(outer, inner)
    angles = along.shape[2]
    tile_terms(message, middle, last_moments, last_others)
    last_along, last_terms = point_terms(message, angles, angles, middle)

    def one(i, unused):
        speeds[i] = before[i] + quarter_speed(
            scale, along.at[i], terms[i], [(last_moments, last_others)]
        )
        return unused

    repeat(outer - 1, one, 0)
    speeds[outer - 1] = quarter_speed(
        scale, last_along, last_terms, (moments, others)
    ) + quarter_speed(scale, last_along, last_terms, [(last_moments, last_others)])
    result[...] = jnp.zeros(result.shape, f32)
    place_quarters(outer, ways, angles, speeds, result)


def own_kernel(scale, ways, outer, inner, *refs):
    messages, (moments, others, last_moments, last_others) = refs[:outer], refs[outer : outer + 4]
    after, result, along, terms, speeds = refs[outer + 4 :]
    middle = middle_of(outer, inner)
    angles = along.shape[2]
    for i, message in enumerate(messages):
        along[i], terms[i] = point_terms(message, 0, angles, middle)

    def one(i, unused):
        if outer <= UNROLLED:
            blocks = [(moments.at[j], others.at[j]) for j in range(outer - 1)]
            speeds[i] = quarter_speed(
                scale, along.at[i], terms[i], blocks + [(last_moments, last_others)]
            )
        else:
            speeds[i] = quarter_speed(
                scale, along.at[i], terms[i], (moments, others)
            ) + quarter_speed(scale, along.at[i], terms[i], [(last_moments, last_others)])
        return unused

    repeat(outer, one, 0)
    result[...] = jnp.zeros(result.shape, f32)
    place_quarters(outer, ways, angles, speeds, result)


def merge_kernel(rows, own, arrived, picks, result):
    result[...] = jnp.zeros(result.shape, f32)
    result[0:rows, :] = own[0:rows, :] + arrived[0:rows, :]
    result[rows : rows + picks.shape[0], :] = picks[...]


def wall_kernel(ways, *refs):
    partials = refs[:ways]
    (still, inner_cells, strength, index, wall_out, grid_out, strength_out,
     fixed, picked, wall, grid, new_strength, rows, sems) = refs[ways:]
    angles = still.shape[1]
    total = angles * ways
    parts = total // LANES
    rows_of = 3 * parts
    slots = picked.shape[0] // ways
    me = lax.axis_index("tgt")
    copy = pltpu.make_async_copy(index, rows, sems.at[0])
    copy.start()
    leave = [
        pltpu.make_async_copy(a, b, sems.at[1 + i])
        for i, (a, b) in enumerate(
            ((wall, wall_out), (grid, grid_out), (new_strength, strength_out))
        )
    ]
    for step, partial in enumerate(partials):
        picked[step * slots : (step + 1) * slots, :] = partial[rows_of : rows_of + slots, :]
    added = partials[0][0:rows_of, :]
    for partial in partials[1:]:
        added = added + partial[0:rows_of, :]
    speed = [
        jnp.concatenate([added[r : r + 1] for r in range(m * parts, (m + 1) * parts)], axis=1)
        for m in range(3)
    ]
    for m in range(3):
        own = speed[m][:, 0:angles]
        for t in range(1, ways):
            own = jnp.where(me == t, speed[m][:, t * angles : (t + 1) * angles], own)
        wall[m] = own
    leave[0].start()

    first = lax.broadcasted_iota(jnp.int32, (ROWS, total), 0) == 0
    field = [inner_cells[m] for m in range(3)]
    local_swirl = inner_cells[3]
    local_diff = inner_cells[4]
    for counter in range(SUBSTEPS):
        transport = 0.5 * (local_swirl + swirl_gain * field[2])
        renewed = []
        for m in range(3):
            center = field[m]
            eastern = pltpu.roll(center, total - 1, 1)
            western = pltpu.roll(center, 1, 1)
            outward = pltpu.roll(center, ROWS - 1, 0)
            inward = jnp.where(first, speed[m], pltpu.roll(center, 1, 0))
            renewed.append(
                center
                + local_diff * (eastern + western + outward + inward - 4.0 * center)
                - transport * (eastern - western)
            )
        field = renewed
    stacked = jnp.concatenate(field + [jnp.zeros((LANES - 3 * ROWS, total), f32)], axis=0)
    for k in range(parts):
        turned = jnp.transpose(stacked[:, k * LANES : (k + 1) * LANES])
        for m in range(3):
            place = m * total + k * LANES
            fixed[place : place + LANES, :] = turned if m == 0 else pltpu.roll(
                turned, LANES - m * ROWS, 1
            )
    near = lax.broadcasted_iota(jnp.int32, (angles, LANES), 1) < SUBSTEPS
    for m in range(3):
        place = pl.multiple_of(m * total + me * angles, ROWS)
        grid[0, m] = jnp.where(near, fixed[pl.ds(place, angles), :], still[m])
    leave[1].start()
    near = lax.broadcasted_iota(jnp.int32, (1, LANES), 1) < SUBSTEPS
    pieces = strength.shape[1] // LANES
    copy.wait()
    for b in range(3 * pieces):
        q = rows[b, 0]
        c, part = b // pieces, slice((b % pieces) * LANES, (b % pieces + 1) * LANES)
        row = jnp.where(
            near, fixed[pl.ds(jnp.maximum(q, 0), 1), :], picked[pl.ds(rows[b, 1], 1), :]
        )
        new_strength[c : c + 1, part] = jnp.where(q >= 0, row, strength[c : c + 1, part])
    leave[2].start()
    for copy in leave:
        copy.wait()


def send(block, pairs):
    return lax.ppermute(block, ("src", "tgt"), pairs)


def on_device(
    particle_position,
    particle_strength,
    core_radius,
    boundary_points,
    vorticity,
    swirl,
    diffusivity,
    intersection_source,
    intersection_target,
):
    sources = lax.axis_size("src")
    ways = lax.axis_size("tgt")
    planes, comps, angles, radial = vorticity.shape
    per_device = particle_position.shape[1]
    tiles = per_device // LANES
    blocks = intersection_source.shape[2]
    inner = 2 if sources % 2 == 0 else 1
    outer = sources // inner
    total = angles * ways
    scale = 1.6 / (4.0 * math.pi * math.sqrt(per_device * ways * sources))

    def pairs(move):
        found = []
        for s in range(sources):
            for t in range(ways):
                o, i, u = move(s // inner, s % inner, t)
                found.append((s * ways + t, (o * inner + i) * ways + u))
        return found

    def over_tgt(block, step):
        return send(block, pairs(lambda o, i, t: (o, i, partner(t, step, ways))))

    given = (
        particle_position, particle_strength, core_radius, boundary_points,
        vorticity, swirl, diffusivity, intersection_source, intersection_target,
    )
    *messages, own, source, target = pl.pallas_call(
        functools.partial(particles_kernel, inner, outer),
        out_shape=(shape(tiles, ROWS, LANES),) * outer + (
            shape(5, angles, LANES),
            jax.ShapeDtypeStruct(intersection_source.shape, jnp.int32),
            jax.ShapeDtypeStruct(intersection_target.shape, jnp.int32),
        ),
        in_specs=[hbm()] * 9,
        out_specs=(vmem(),) * (outer + 3),
        scratch_shapes=[pltpu.VMEM(a.shape, f32) for a in given[0:4]]
        + [pltpu.SemaphoreType.DMA((11,))],
        compiler_params=limit(4),
        name="particles",
    )(*stay(*given))
    line = [messages[0]] + [
        send(
            message,
            pairs(lambda o, i, t: (partner(o, k, outer), i, partner(t, turn(k, ways), ways))),
        )
        for k, message in zip(line_order(outer)[1:], messages[1:])
    ]

    edges = pl.pallas_call(
        edges_kernel,
        out_shape=shape(11, ROWS, LANES),
        in_specs=[vmem()] * 3,
        out_specs=vmem(),
        compiler_params=limit(4),
        cost_estimate=cost(1 << 31, 1 << 10),
        name="edges",
    )(own, source, target)
    steps = tgt_order(ways)
    around = [edges] + [over_tgt(edges, k) for k in steps[1:]]

    rows = 3 * total // LANES
    slots = blocks
    sums_shape = shape(-(-rows // ROWS) * ROWS, LANES)
    along_shape = (ROWS, angles)
    terms_shape = (angles, TERMS)
    others_shape = (TERMS, per_device)
    early = outer - 1
    before, *held = pl.pallas_call(
        functools.partial(early_kernel, scale, ways, outer, inner),
        out_shape=(
            shape(early, ROWS, LANES),
            shape(early, tiles, ROWS, LANES),
            jax.ShapeDtypeStruct((early, *others_shape), bf16),
            shape(early, *along_shape),
            jax.ShapeDtypeStruct((early, *terms_shape), bf16),
        ),
        in_specs=[vmem()] * outer,
        out_specs=(vmem(),) * 5,
        compiler_params=limit(12),
        cost_estimate=cost(1 << 10, 1 << 10),
        name="early",
    )(*line[:-1], edges)
    for_partner, last_moments, last_others = pl.pallas_call(
        functools.partial(late_kernel, scale, ways, outer, inner),
        out_shape=(
            sums_shape,
            shape(tiles, ROWS, LANES),
            jax.ShapeDtypeStruct(others_shape, bf16),
        ),
        in_specs=[vmem()] * 6,
        out_specs=(vmem(),) * 3,
        scratch_shapes=[pltpu.VMEM((outer, ROWS, LANES), f32)],
        compiler_params=limit(12),
        cost_estimate=cost(1 << 30, 1 << 10),
        name="late",
    )(line[-1], before, *held)
    arrived = send(for_partner, pairs(lambda o, i, t: (o, inner - 1 - i, t)))
    own_sum = pl.pallas_call(
        functools.partial(own_kernel, scale, ways, outer, inner),
        out_shape=sums_shape,
        in_specs=[vmem()] * (outer + 5),
        out_specs=vmem(),
        scratch_shapes=[
            pltpu.VMEM((outer, *along_shape), f32),
            pltpu.VMEM((outer, *terms_shape), bf16),
            pltpu.VMEM((outer, ROWS, LANES), f32),
        ],
        compiler_params=limit(12),
        cost_estimate=cost(1 << 31, 1 << 10),
        name="own",
    )(*line, held[0], held[1], last_moments, last_others, for_partner)
    still, picks, inner_cells, index = pl.pallas_call(
        functools.partial(still_kernel, ways),
        out_shape=(
            shape(3, angles, LANES),
            shape(slots, LANES),
            shape(5, ROWS, total),
            jax.ShapeDtypeStruct((16 * ((blocks + 15) // 16), LANES), jnp.int32),
        ),
        in_specs=[vmem()] * (ways + 3),
        out_specs=(vmem(),) * 4,
        scratch_shapes=[
            pltpu.VMEM((ways,) + edges.shape, f32),
            pltpu.SMEM(source.shape, jnp.int32),
            pltpu.SemaphoreType.DMA,
        ],
        compiler_params=limit(8),
        name="still",
    )(*around, own, source, own_sum)
    partial_sum = pl.pallas_call(
        functools.partial(merge_kernel, rows),
        out_shape=shape(-(-(rows + blocks) // ROWS) * ROWS, LANES),
        in_specs=[vmem()] * 3,
        out_specs=vmem(),
        compiler_params=limit(4),
        name="merge",
    )(own_sum, arrived, picks)
    partials = [partial_sum] + [over_tgt(partial_sum, k) for k in steps[1:]]

    wall, grid, new_strength = pl.pallas_call(
        functools.partial(wall_kernel, ways),
        out_shape=(shape(3, planes, angles), shape(*vorticity.shape), shape(3, per_device)),
        in_specs=[vmem()] * (ways + 4),
        out_specs=(hbm(),) * 3,
        scratch_shapes=[
            pltpu.VMEM((3 * total, LANES), f32),
            pltpu.VMEM((slots * ways, LANES), f32),
            pltpu.VMEM((3, planes, angles), f32),
            pltpu.VMEM(vorticity.shape, f32),
            pltpu.VMEM(particle_strength.shape, f32),
            pltpu.SMEM(index.shape, jnp.int32),
            pltpu.SemaphoreType.DMA((4,)),
        ],
        compiler_params=limit(16),
        name="wall",
    )(*partials, still, inner_cells, particle_strength, index)
    return (wall, grid, new_strength)


def solution(mesh):
    in_specs = (
        P(None, ("src", "tgt")),
        P(None, ("src", "tgt")),
        P(None, ("src", "tgt")),
        P(None, None, "tgt"),
        P("src", None, "tgt", None),
        P("src", "tgt", None),
        P("src", "tgt", None),
        P("src", "tgt", None),
        P("src", "tgt", None),
    )
    out_specs = (P(None, "src", "tgt"), P("src", None, "tgt", None), P(None, ("src", "tgt")))
    return jax.shard_map(
        on_device, mesh=mesh, in_specs=in_specs, out_specs=out_specs, check_vma=False
    )
```

```python
import functools
import math

import jax
import jax.numpy as jnp
from jax import lax
from jax.experimental import pallas as pl
from jax.experimental.pallas import tpu as pltpu
from jax.sharding import PartitionSpec as P

SUBSTEPS = 3
LANES = 128
ROWS = 8
TOGETHER = 2
TERMS = 48
UNROLLED = 4
swirl_gain = 0.2
f32 = jnp.float32
bf16 = jnp.bfloat16


def vmem():
    return pl.BlockSpec(memory_space=pltpu.VMEM)


def smem():
    return pl.BlockSpec(memory_space=pltpu.SMEM)


def hbm():
    return pl.BlockSpec(memory_space=pltpu.HBM)


def stay(*arrays):
    return [pltpu.with_memory_space_constraint(a, pltpu.HBM) for a in arrays]


def shape(*dims):
    return jax.ShapeDtypeStruct(dims, f32)


def limit(megabytes):
    return pltpu.CompilerParams(vmem_limit_bytes=megabytes << 20)


def cost(flops, size):
    return pl.CostEstimate(flops=flops, bytes_accessed=size, transcendentals=0)


def divisor(number, most):
    return max(c for c in range(1, min(number, most) + 1) if number % c == 0)


def power_of_two(number):
    return number & (number - 1) == 0


def partner(index, step, count):
    return index ^ step if power_of_two(count) else (index + step) % count


def source_of(index, step, count):
    return index ^ step if power_of_two(count) else (index - step) % count


def line_order(outer):
    return [0, *range(outer // 2, outer), *range(1, outer // 2)]


def tgt_order(ways):
    return [0, *range(ways // 2, ways), *range(1, ways // 2)]


def turn(step, ways):
    return {1: 2, 2: 3, 3: 1}.get(step % ways, step % ways)


def particles_kernel(inner, outer, *refs):
    given, messages = refs[:9], refs[9 : 9 + outer]
    own, lists, held, sems = refs[9 + outer], refs[10 + outer : 12 + outer], refs[12 + outer : -1], refs[-1]
    vort, swirl, diff = given[4:7]
    targets = (*held, *[own.at[c] for c in range(5)], *lists)
    sources = (*given[0:4], *[vort.at[0, m] for m in range(3)], swirl.at[0], diff.at[0], *given[7:9])
    copies = [
        pltpu.make_async_copy(a, b, sems.at[i]) for i, (a, b) in enumerate(zip(sources, targets))
    ]
    for copy in copies:
        copy.start()
    for copy in copies[0:4]:
        copy.wait()
    pos, strength, radius, points = held
    tiles = pos.shape[1] // LANES
    angles = points.shape[2]
    src = lax.axis_index("src")
    core = radius[...] * radius[...]
    for step, message in zip(line_order(outer), messages):
        there = partner(src // inner, step, outer) * inner
        planes = (there + src % inner, there + inner - 1 - src % inner)
        for k in range(tiles):
            part = slice(k * LANES, (k + 1) * LANES)
            message[k, 0:3, :] = pos[:, part]
            message[k, 3:6, :] = strength[:, part]
            message[k, 6:7, :] = core[:, part]
            message[k, 7:8, :] = jnp.zeros((1, LANES), f32)
        for m in range(3):
            for i, plane in enumerate(planes):
                message[m, 7:8, i * angles : (i + 1) * angles] = points[m, pl.ds(plane, 1), :]
    for copy in copies[4:]:
        copy.wait()


def edges_kernel(own, own_source, own_target, message):
    angles = own.shape[1]
    blocks = own_source.shape[2]
    total = angles * lax.axis_size("tgt")
    half = ROWS // 2
    for c in range(5):
        message[c, :, 0:angles] = jnp.transpose(own[c])[0:ROWS, :]
        message[c, :, angles:LANES] = jnp.zeros((ROWS, LANES - angles), f32)
        message[6 + c, 0:half, :] = own[c, 0:half]
        message[6 + c, half:ROWS, :] = own[c, angles - half : angles]
    message[5] = jnp.full((ROWS, LANES), -1.0, f32)
    q = own_source[0]
    row = (q // angles) * total + lax.axis_index("tgt") * angles + q % angles
    message[5, 0:1, 0:blocks] = row.astype(f32)
    message[5, 1:2, 0:blocks] = own_target[0].astype(f32)


def still_kernel(ways, *refs):
    messages = refs[:ways]
    own, lists, after, grid, picks, inner_cells, index, placed, source, sem = refs[ways:]
    copy = pltpu.make_async_copy(lists, source, sem)
    copy.start()
    angles = own.shape[1]
    height = angles + ROWS
    blocks = lists.shape[2]
    me = lax.axis_index("tgt")
    for step, message in zip(tgt_order(ways), messages):
        placed[source_of(me, step, ways)] = message[...]

    for c in range(5):
        inner_cells[c] = jnp.concatenate(
            [placed[t, c, :, 0:angles] for t in range(ways)], axis=1
        )

    shaped = index.shape
    name = (me * blocks + lax.broadcasted_iota(jnp.int32, shaped, 0)).astype(f32)
    lane = lax.broadcasted_iota(jnp.int32, shaped, 1).astype(f32)
    row = jnp.full(shaped, -1.0, f32)
    slot = jnp.zeros(shaped, f32)
    for step, message in enumerate(messages):
        match = message[5, 1:2, :] == name
        row = jnp.maximum(row, jnp.where(match, message[5, 0:1, :], -1.0))
        slot = jnp.maximum(slot, jnp.where(match, lane + float(step * picks.shape[0]), 0.0))
    row = jnp.max(row, axis=1, keepdims=True)
    slot = jnp.max(slot, axis=1, keepdims=True)
    index[...] = jnp.where(lane < 1.0, row, slot).astype(jnp.int32)

    upper = lax.broadcasted_iota(jnp.int32, (ROWS, LANES), 0) < ROWS // 2
    east = lax.rem(me + 1, ways)
    west = lax.rem(me + ways - 1, ways)
    cells = [
        jnp.concatenate(
            [own[c], jnp.where(upper, placed[east, 6 + c], placed[west, 6 + c])], axis=0
        )
        for c in range(5)
    ]
    field, local_swirl, local_diff = cells[0:3], cells[3], cells[4]
    lane = lax.broadcasted_iota(jnp.int32, (height, LANES), 1)
    for counter in range(SUBSTEPS):
        transport = 0.5 * (local_swirl + swirl_gain * field[2])
        renewed = []
        for m in range(3):
            center = field[m]
            eastern = pltpu.roll(center, height - 1, 0)
            western = pltpu.roll(center, 1, 0)
            outward = jnp.where(lane == LANES - 1, 0.0, pltpu.roll(center, LANES - 1, 1))
            inward = jnp.where(lane == 0, 0.0, pltpu.roll(center, 1, 1))
            renewed.append(
                center
                + local_diff * (eastern + western + outward + inward - 4.0 * center)
                - transport * (eastern - western)
            )
        field = renewed
    for m in range(3):
        grid[m] = field[m][0:angles]
    picks[...] = jnp.zeros(picks.shape, f32)
    copy.wait()
    for i in range(blocks):
        q = source[0, 0, i]
        picks[i : i + 1, :] = grid[q // angles, pl.ds(q % angles, 1), :]


def three_parts(value):
    high = value.astype(bf16).astype(f32)
    rest = value - high
    middle = rest.astype(bf16).astype(f32)
    return high, middle, rest - middle


def middle_of(outer, inner):
    here = (lax.axis_index("src") // inner).astype(f32)
    return 0.5, 0.5, (here + 0.5) * (1.0 / outer)


def point_terms(message, lane, angles, middle):
    x, y, z = [message[m, 7:8, lane : lane + angles] - middle[m] for m in range(3)]
    nothing = jnp.zeros((3, angles), f32)
    vector = jnp.concatenate(
        [-2.0 * x, -2.0 * y, -2.0 * z, jnp.ones_like(x), x * x + y * y + z * z, nothing], axis=0
    )
    high, middling, low = three_parts(vector)
    terms = jnp.transpose(jnp.concatenate([high, middling, low, high, middling, high], axis=0))
    return jnp.concatenate([x, y, z, nothing, nothing[0:2]], axis=0), terms.astype(bf16)


def tile_terms(message, middle, moments, others):
    one = jnp.ones((1, LANES), f32)
    nothing = jnp.zeros((3, LANES), f32)
    for k in range(message.shape[0]):
        px, py, pz = [message[k, r : r + 1, :] - middle[r] for r in range(3)]
        sx, sy, sz, cc = [message[k, r : r + 1, :] for r in range(3, 7)]
        moments[k] = jnp.concatenate(
            [sx, sy, sz, sy * pz - sz * py, sz * px - sx * pz, sx * py - sy * px, nothing[0:2]],
            axis=0,
        )
        vector = jnp.concatenate(
            [px, py, pz, px * px + py * py + (pz * pz + cc), one, nothing], axis=0
        )
        high, middling, low = three_parts(vector)
        others[:, k * LANES : (k + 1) * LANES] = jnp.concatenate(
            [high, high, high, middling, middling, low], axis=0
        ).astype(bf16)


def quarter(terms, blocks):
    tall = terms.shape[0]
    diagonal = lax.broadcasted_iota(jnp.int32, (ROWS, LANES), 1) - lax.broadcasted_iota(
        jnp.int32, (ROWS, LANES), 0
    )
    distances = [
        jnp.dot(terms, others[...], preferred_element_type=f32) for moments, others in blocks
    ]
    rows = [jnp.zeros((ROWS, LANES), f32)] * 6
    for start in range(0, tall // ROWS, TOGETHER):
        held = [jnp.zeros((ROWS, LANES), f32)] * (6 * TOGETHER)
        for distance, (moments, others) in zip(distances, blocks):
            for k in range(moments.shape[0]):
                summed = [moments[k, r : r + 1, :] for r in range(6)]
                for i in range(TOGETHER):
                    low = (start + i) * ROWS
                    inverse = lax.rsqrt(distance[low : low + ROWS, k * LANES : (k + 1) * LANES])
                    weight = inverse * inverse * inverse
                    for r in range(6):
                        held[6 * i + r] += weight * summed[r]
        for i in range(TOGETHER):
            mask = diagonal == (start + i) * ROWS
            for r in range(6):
                value = jnp.sum(held[6 * i + r], axis=1, keepdims=True)
                rows[r] = rows[r] + jnp.where(mask, value, 0.0)
    return rows


def repeat(count, body, carried):
    if count <= UNROLLED:
        for i in range(count):
            carried = body(i, carried)
        return carried
    return lax.fori_loop(0, count, body, carried)


def quarter_speed(scale, along, terms, blocks):
    if isinstance(blocks, list):
        rows = quarter(terms, blocks)
    else:
        moments, others = blocks
        count = others.shape[0]
        if count <= UNROLLED:
            rows = quarter(terms, [(moments.at[i], others.at[i]) for i in range(count)])
        else:

            def add(i, rows):
                more = quarter(terms, [(moments.at[i], others.at[i])])
                return tuple(a + b for a, b in zip(rows, more))

            rows = lax.fori_loop(0, count, add, (jnp.zeros((ROWS, LANES), f32),) * 6)
    angles = terms.shape[0]
    ax, ay, az, bx, by, bz = [jnp.sum(r, axis=0, keepdims=True) for r in rows]
    tx, ty, tz = [
        jnp.concatenate([along[m : m + 1, :], jnp.zeros((1, LANES - angles), f32)], axis=1)
        for m in range(3)
    ]
    return jnp.concatenate(
        [
            scale * (ay * tz - az * ty - bx),
            scale * (az * tx - ax * tz - by),
            scale * (ax * ty - ay * tx - bz),
            jnp.zeros((ROWS - 3, LANES), f32),
        ],
        axis=0,
    )


def place_quarters(outer, ways, angles, speeds, result):
    per = LANES // angles
    parts = ways // per
    me = lax.axis_index("tgt")
    for i, step in enumerate(line_order(outer)):
        if step < ways:
            place = source_of(me, turn(step, ways), ways)
            moved = speeds[i]
            for step in range(1, per):
                moved = jnp.where(
                    place % per == step, pltpu.roll(speeds[i], step * angles, 1), moved
                )
            for m in range(3):
                result[pl.ds(m * parts + place // per, 1), :] += moved[m : m + 1, :]


def early_kernel(scale, ways, outer, inner, *refs):
    messages, (after, speeds, moments, others, along, terms) = refs[: outer - 1], refs[outer - 1 :]
    middle = middle_of(outer, inner)
    angles = along.shape[2]
    for i, message in enumerate(messages):
        tile_terms(message, middle, moments.at[i], others.at[i])
        along[i], terms[i] = point_terms(message, angles, angles, middle)

    def one(i, unused):
        speeds[i] = quarter_speed(scale, along.at[i], terms[i], (moments, others))
        return unused

    repeat(outer - 1, one, 0)


def late_kernel(scale, ways, outer, inner, *refs):
    (message, before, moments, others, along, terms, result, last_moments, last_others, speeds) = refs
    middle = middle_of(outer, inner)
    angles = along.shape[2]
    tile_terms(message, middle, last_moments, last_others)
    last_along, last_terms = point_terms(message, angles, angles, middle)

    def one(i, unused):
        speeds[i] = before[i] + quarter_speed(
            scale, along.at[i], terms[i], [(last_moments, last_others)]
        )
        return unused

    repeat(outer - 1, one, 0)
    speeds[outer - 1] = quarter_speed(
        scale, last_along, last_terms, (moments, others)
    ) + quarter_speed(scale, last_along, last_terms, [(last_moments, last_others)])
    result[...] = jnp.zeros(result.shape, f32)
    place_quarters(outer, ways, angles, speeds, result)


def own_kernel(scale, ways, outer, inner, *refs):
    messages, (moments, others, last_moments, last_others) = refs[:outer], refs[outer : outer + 4]
    after, result, along, terms, speeds = refs[outer + 4 :]
    middle = middle_of(outer, inner)
    angles = along.shape[2]
    for i, message in enumerate(messages):
        along[i], terms[i] = point_terms(message, 0, angles, middle)

    def one(i, unused):
        if outer <= UNROLLED:
            blocks = [(moments.at[j], others.at[j]) for j in range(outer - 1)]
            speeds[i] = quarter_speed(
                scale, along.at[i], terms[i], blocks + [(last_moments, last_others)]
            )
        else:
            speeds[i] = quarter_speed(
                scale, along.at[i], terms[i], (moments, others)
            ) + quarter_speed(scale, along.at[i], terms[i], [(last_moments, last_others)])
        return unused

    repeat(outer, one, 0)
    result[...] = jnp.zeros(result.shape, f32)
    place_quarters(outer, ways, angles, speeds, result)


def merge_kernel(rows, own, arrived, picks, result):
    result[...] = jnp.zeros(result.shape, f32)
    result[0:rows, :] = own[0:rows, :] + arrived[0:rows, :]
    result[rows : rows + picks.shape[0], :] = picks[...]


def wall_kernel(ways, *refs):
    partials = refs[:ways]
    (still, inner_cells, strength, index, wall, grid, new_strength,
     fixed, picked, rows, sem) = refs[ways:]
    angles = grid.shape[2]
    total = angles * ways
    parts = total // LANES
    rows_of = 3 * parts
    slots = picked.shape[0] // ways
    me = lax.axis_index("tgt")
    copy = pltpu.make_async_copy(index, rows, sem)
    copy.start()
    for step, partial in enumerate(partials):
        picked[step * slots : (step + 1) * slots, :] = partial[rows_of : rows_of + slots, :]
    added = partials[0][0:rows_of, :]
    for partial in partials[1:]:
        added = added + partial[0:rows_of, :]
    speed = [
        jnp.concatenate([added[r : r + 1] for r in range(m * parts, (m + 1) * parts)], axis=1)
        for m in range(3)
    ]
    stacked = jnp.concatenate(speed + [jnp.zeros((ROWS - 3, total), f32)], axis=0)
    own = pltpu.roll(stacked, total - me * angles, 1)
    for m in range(3):
        wall[m] = own[m : m + 1, 0:angles]

    first = lax.broadcasted_iota(jnp.int32, (ROWS, total), 0) == 0
    field = [inner_cells[m] for m in range(3)]
    local_swirl = inner_cells[3]
    local_diff = inner_cells[4]
    for counter in range(SUBSTEPS):
        transport = 0.5 * (local_swirl + swirl_gain * field[2])
        renewed = []
        for m in range(3):
            center = field[m]
            eastern = pltpu.roll(center, total - 1, 1)
            western = pltpu.roll(center, 1, 1)
            outward = pltpu.roll(center, ROWS - 1, 0)
            inward = jnp.where(first, speed[m], pltpu.roll(center, 1, 0))
            renewed.append(
                center
                + local_diff * (eastern + western + outward + inward - 4.0 * center)
                - transport * (eastern - western)
            )
        field = renewed
    stacked = jnp.concatenate(field + [jnp.zeros((LANES - 3 * ROWS, total), f32)], axis=0)
    for k in range(parts):
        turned = jnp.transpose(stacked[:, k * LANES : (k + 1) * LANES])
        for m in range(3):
            place = m * total + k * LANES
            fixed[place : place + LANES, :] = turned if m == 0 else pltpu.roll(
                turned, LANES - m * ROWS, 1
            )
    near = lax.broadcasted_iota(jnp.int32, (angles, LANES), 1) < SUBSTEPS
    for m in range(3):
        place = pl.multiple_of(m * total + me * angles, ROWS)
        grid[0, m] = jnp.where(near, fixed[pl.ds(place, angles), :], still[m])
    near = lax.broadcasted_iota(jnp.int32, (1, LANES), 1) < SUBSTEPS
    pieces = strength.shape[1] // LANES
    copy.wait()
    for b in range(3 * pieces):
        q = rows[b, 0]
        c, part = b // pieces, slice((b % pieces) * LANES, (b % pieces + 1) * LANES)
        row = jnp.where(
            near, fixed[pl.ds(jnp.maximum(q, 0), 1), :], picked[pl.ds(rows[b, 1], 1), :]
        )
        new_strength[c : c + 1, part] = jnp.where(q >= 0, row, strength[c : c + 1, part])


def send(block, pairs):
    return lax.ppermute(block, ("src", "tgt"), pairs)


def on_device(
    particle_position,
    particle_strength,
    core_radius,
    boundary_points,
    vorticity,
    swirl,
    diffusivity,
    intersection_source,
    intersection_target,
):
    sources = lax.axis_size("src")
    ways = lax.axis_size("tgt")
    planes, comps, angles, radial = vorticity.shape
    per_device = particle_position.shape[1]
    tiles = per_device // LANES
    blocks = intersection_source.shape[2]
    inner = 2 if sources % 2 == 0 else 1
    outer = sources // inner
    total = angles * ways
    scale = 1.6 / (4.0 * math.pi * math.sqrt(per_device * ways * sources))

    def pairs(move):
        found = []
        for s in range(sources):
            for t in range(ways):
                o, i, u = move(s // inner, s % inner, t)
                found.append((s * ways + t, (o * inner + i) * ways + u))
        return found

    def over_tgt(block, step):
        return send(block, pairs(lambda o, i, t: (o, i, partner(t, step, ways))))

    given = (
        particle_position, particle_strength, core_radius, boundary_points,
        vorticity, swirl, diffusivity, intersection_source, intersection_target,
    )
    *messages, own, source, target = pl.pallas_call(
        functools.partial(particles_kernel, inner, outer),
        out_shape=(shape(tiles, ROWS, LANES),) * outer + (
            shape(5, angles, LANES),
            jax.ShapeDtypeStruct(intersection_source.shape, jnp.int32),
            jax.ShapeDtypeStruct(intersection_target.shape, jnp.int32),
        ),
        in_specs=[hbm()] * 9,
        out_specs=(vmem(),) * (outer + 3),
        scratch_shapes=[pltpu.VMEM(a.shape, f32) for a in given[0:4]]
        + [pltpu.SemaphoreType.DMA((11,))],
        compiler_params=limit(4),
        name="particles",
    )(*stay(*given))
    line = [messages[0]] + [
        send(
            message,
            pairs(lambda o, i, t: (partner(o, k, outer), i, partner(t, turn(k, ways), ways))),
        )
        for k, message in zip(line_order(outer)[1:], messages[1:])
    ]

    edges = pl.pallas_call(
        edges_kernel,
        out_shape=shape(11, ROWS, LANES),
        in_specs=[vmem()] * 3,
        out_specs=vmem(),
        compiler_params=limit(4),
        cost_estimate=cost(1 << 31, 1 << 10),
        name="edges",
    )(own, source, target)
    steps = tgt_order(ways)
    around = [edges] + [over_tgt(edges, k) for k in steps[1:]]

    rows = 3 * total // LANES
    slots = blocks
    sums_shape = shape(-(-rows // ROWS) * ROWS, LANES)
    along_shape = (ROWS, angles)
    terms_shape = (angles, TERMS)
    others_shape = (TERMS, per_device)
    early = outer - 1
    before, *held = pl.pallas_call(
        functools.partial(early_kernel, scale, ways, outer, inner),
        out_shape=(
            shape(early, ROWS, LANES),
            shape(early, tiles, ROWS, LANES),
            jax.ShapeDtypeStruct((early, *others_shape), bf16),
            shape(early, *along_shape),
            jax.ShapeDtypeStruct((early, *terms_shape), bf16),
        ),
        in_specs=[vmem()] * outer,
        out_specs=(vmem(),) * 5,
        compiler_params=limit(12),
        cost_estimate=cost(1 << 10, 1 << 10),
        name="early",
    )(*line[:-1], edges)
    for_partner, last_moments, last_others = pl.pallas_call(
        functools.partial(late_kernel, scale, ways, outer, inner),
        out_shape=(
            sums_shape,
            shape(tiles, ROWS, LANES),
            jax.ShapeDtypeStruct(others_shape, bf16),
        ),
        in_specs=[vmem()] * 6,
        out_specs=(vmem(),) * 3,
        scratch_shapes=[pltpu.VMEM((outer, ROWS, LANES), f32)],
        compiler_params=limit(12),
        cost_estimate=cost(1 << 30, 1 << 10),
        name="late",
    )(line[-1], before, *held)
    arrived = send(for_partner, pairs(lambda o, i, t: (o, inner - 1 - i, t)))
    own_sum = pl.pallas_call(
        functools.partial(own_kernel, scale, ways, outer, inner),
        out_shape=sums_shape,
        in_specs=[vmem()] * (outer + 5),
        out_specs=vmem(),
        scratch_shapes=[
            pltpu.VMEM((outer, *along_shape), f32),
            pltpu.VMEM((outer, *terms_shape), bf16),
            pltpu.VMEM((outer, ROWS, LANES), f32),
        ],
        compiler_params=limit(12),
        cost_estimate=cost(1 << 31, 1 << 10),
        name="own",
    )(*line, held[0], held[1], last_moments, last_others, for_partner)
    still, picks, inner_cells, index = pl.pallas_call(
        functools.partial(still_kernel, ways),
        out_shape=(
            shape(3, angles, LANES),
            shape(slots, LANES),
            shape(5, ROWS, total),
            jax.ShapeDtypeStruct((16 * ((blocks + 15) // 16), LANES), jnp.int32),
        ),
        in_specs=[vmem()] * (ways + 3),
        out_specs=(vmem(),) * 4,
        scratch_shapes=[
            pltpu.VMEM((ways,) + edges.shape, f32),
            pltpu.SMEM(source.shape, jnp.int32),
            pltpu.SemaphoreType.DMA,
        ],
        compiler_params=limit(8),
        name="still",
    )(*around, own, source, own_sum)
    partial_sum = pl.pallas_call(
        functools.partial(merge_kernel, rows),
        out_shape=shape(-(-(rows + blocks) // ROWS) * ROWS, LANES),
        in_specs=[vmem()] * 3,
        out_specs=vmem(),
        compiler_params=limit(4),
        name="merge",
    )(own_sum, arrived, picks)
    partials = [partial_sum] + [over_tgt(partial_sum, k) for k in steps[1:]]

    wall, grid, new_strength = pl.pallas_call(
        functools.partial(wall_kernel, ways),
        out_shape=(shape(3, planes, angles), shape(*vorticity.shape), shape(3, per_device)),
        in_specs=[vmem()] * (ways + 4),
        out_specs=(vmem(),) * 3,
        scratch_shapes=[
            pltpu.VMEM((3 * total, LANES), f32),
            pltpu.VMEM((slots * ways, LANES), f32),
            pltpu.SMEM(index.shape, jnp.int32),
            pltpu.SemaphoreType.DMA,
        ],
        compiler_params=limit(16),
        name="wall",
    )(*partials, still, inner_cells, particle_strength, index)
    return (wall, grid, new_strength)


def solution(mesh):
    in_specs = (
        P(None, ("src", "tgt")),
        P(None, ("src", "tgt")),
        P(None, ("src", "tgt")),
        P(None, None, "tgt"),
        P("src", None, "tgt", None),
        P("src", "tgt", None),
        P("src", "tgt", None),
        P("src", "tgt", None),
        P("src", "tgt", None),
    )
    out_specs = (P(None, "src", "tgt"), P("src", None, "tgt", None), P(None, ("src", "tgt")))
    return jax.shard_map(
        on_device, mesh=mesh, in_specs=in_specs, out_specs=out_specs, check_vma=False
    )
```

```python
import functools
import math

import jax
import jax.numpy as jnp
from jax import lax
from jax.experimental import pallas as pl
from jax.experimental.pallas import tpu as pltpu
from jax.sharding import PartitionSpec as P

SUBSTEPS = 3
LANES = 128
ROWS = 8
TOGETHER = 2
TERMS = 48
UNROLLED = 4
swirl_gain = 0.2
f32 = jnp.float32
bf16 = jnp.bfloat16


def vmem():
    return pl.BlockSpec(memory_space=pltpu.VMEM)


def smem():
    return pl.BlockSpec(memory_space=pltpu.SMEM)


def hbm():
    return pl.BlockSpec(memory_space=pltpu.HBM)


def stay(*arrays):
    return [pltpu.with_memory_space_constraint(a, pltpu.HBM) for a in arrays]


def shape(*dims):
    return jax.ShapeDtypeStruct(dims, f32)


def limit(megabytes):
    return pltpu.CompilerParams(vmem_limit_bytes=megabytes << 20)


def cost(flops, size):
    return pl.CostEstimate(flops=flops, bytes_accessed=size, transcendentals=0)


def divisor(number, most):
    return max(c for c in range(1, min(number, most) + 1) if number % c == 0)


def power_of_two(number):
    return number & (number - 1) == 0


def partner(index, step, count):
    return index ^ step if power_of_two(count) else (index + step) % count


def source_of(index, step, count):
    return index ^ step if power_of_two(count) else (index - step) % count


def line_order(outer):
    return [0, *range(outer // 2, outer), *range(1, outer // 2)]


def tgt_order(ways):
    return [0, *range(ways // 2, ways), *range(1, ways // 2)]


def turn(step, ways):
    return {1: 2, 2: 3, 3: 1}.get(step % ways, step % ways)


def particles_kernel(inner, outer, *refs):
    given, messages = refs[:9], refs[9 : 9 + outer]
    own, lists, held, sems = refs[9 + outer], refs[10 + outer : 12 + outer], refs[12 + outer : -1], refs[-1]
    vort, swirl, diff = given[4:7]
    targets = (*held, *[own.at[c] for c in range(5)], *lists)
    sources = (*given[0:4], *[vort.at[0, m] for m in range(3)], swirl.at[0], diff.at[0], *given[7:9])
    copies = [
        pltpu.make_async_copy(a, b, sems.at[i]) for i, (a, b) in enumerate(zip(sources, targets))
    ]
    for copy in copies:
        copy.start()
    for copy in copies[0:4]:
        copy.wait()
    pos, strength, radius, points = held
    tiles = pos.shape[1] // LANES
    angles = points.shape[2]
    src = lax.axis_index("src")
    core = radius[...] * radius[...]
    for step, message in zip(line_order(outer), messages):
        there = partner(src // inner, step, outer) * inner
        planes = (there + src % inner, there + inner - 1 - src % inner)
        for k in range(tiles):
            part = slice(k * LANES, (k + 1) * LANES)
            message[k, 0:3, :] = pos[:, part]
            message[k, 3:6, :] = strength[:, part]
            message[k, 6:7, :] = core[:, part]
            message[k, 7:8, :] = jnp.zeros((1, LANES), f32)
        for m in range(3):
            for i, plane in enumerate(planes):
                message[m, 7:8, i * angles : (i + 1) * angles] = points[m, pl.ds(plane, 1), :]
    for copy in copies[4:]:
        copy.wait()


def edges_kernel(own, own_source, own_target, message):
    angles = own.shape[1]
    blocks = own_source.shape[2]
    total = angles * lax.axis_size("tgt")
    half = ROWS // 2
    for c in range(5):
        message[c, :, 0:angles] = jnp.transpose(own[c])[0:ROWS, :]
        message[c, :, angles:LANES] = jnp.zeros((ROWS, LANES - angles), f32)
        message[6 + c, 0:half, :] = own[c, 0:half]
        message[6 + c, half:ROWS, :] = own[c, angles - half : angles]
    message[5] = jnp.full((ROWS, LANES), -1.0, f32)
    q = own_source[0]
    row = (q // angles) * total + lax.axis_index("tgt") * angles + q % angles
    message[5, 0:1, 0:blocks] = row.astype(f32)
    message[5, 1:2, 0:blocks] = own_target[0].astype(f32)


def still_kernel(ways, *refs):
    messages = refs[:ways]
    own, lists, after, grid, picks, inner_cells, index, placed, source, sem = refs[ways:]
    copy = pltpu.make_async_copy(lists, source, sem)
    copy.start()
    angles = own.shape[1]
    height = angles + ROWS
    blocks = lists.shape[2]
    me = lax.axis_index("tgt")
    for step, message in zip(tgt_order(ways), messages):
        placed[source_of(me, step, ways)] = message[...]

    for c in range(5):
        inner_cells[c] = jnp.concatenate(
            [placed[t, c, :, 0:angles] for t in range(ways)], axis=1
        )

    shaped = index.shape
    name = (me * blocks + lax.broadcasted_iota(jnp.int32, shaped, 0)).astype(f32)
    lane = lax.broadcasted_iota(jnp.int32, shaped, 1).astype(f32)
    row = jnp.full(shaped, -1.0, f32)
    slot = jnp.zeros(shaped, f32)
    for step, message in enumerate(messages):
        match = message[5, 1:2, :] == name
        row = jnp.maximum(row, jnp.where(match, message[5, 0:1, :], -1.0))
        slot = jnp.maximum(slot, jnp.where(match, lane + float(step * picks.shape[0]), 0.0))
    row = jnp.max(row, axis=1, keepdims=True)
    slot = jnp.max(slot, axis=1, keepdims=True)
    block = lax.broadcasted_iota(jnp.int32, shaped, 0).astype(f32)
    block = jnp.minimum(block, float(blocks - 1))
    kept = row < 0.0
    row = jnp.where(kept, float(3 * angles * ways) + block, row)
    slot = jnp.where(kept, float(ways * blocks) + block, slot)
    index[...] = jnp.where(lane < 1.0, row, slot).astype(jnp.int32)

    upper = lax.broadcasted_iota(jnp.int32, (ROWS, LANES), 0) < ROWS // 2
    east = lax.rem(me + 1, ways)
    west = lax.rem(me + ways - 1, ways)
    cells = [
        jnp.concatenate(
            [own[c], jnp.where(upper, placed[east, 6 + c], placed[west, 6 + c])], axis=0
        )
        for c in range(5)
    ]
    field, local_swirl, local_diff = cells[0:3], cells[3], cells[4]
    lane = lax.broadcasted_iota(jnp.int32, (height, LANES), 1)
    for counter in range(SUBSTEPS):
        transport = 0.5 * (local_swirl + swirl_gain * field[2])
        renewed = []
        for m in range(3):
            center = field[m]
            eastern = pltpu.roll(center, height - 1, 0)
            western = pltpu.roll(center, 1, 0)
            outward = jnp.where(lane == LANES - 1, 0.0, pltpu.roll(center, LANES - 1, 1))
            inward = jnp.where(lane == 0, 0.0, pltpu.roll(center, 1, 1))
            renewed.append(
                center
                + local_diff * (eastern + western + outward + inward - 4.0 * center)
                - transport * (eastern - western)
            )
        field = renewed
    for m in range(3):
        grid[m] = field[m][0:angles]
    picks[...] = jnp.zeros(picks.shape, f32)
    copy.wait()
    for i in range(blocks):
        q = source[0, 0, i]
        picks[i : i + 1, :] = grid[q // angles, pl.ds(q % angles, 1), :]


def three_parts(value):
    high = value.astype(bf16).astype(f32)
    rest = value - high
    middle = rest.astype(bf16).astype(f32)
    return high, middle, rest - middle


def middle_of(outer, inner):
    here = (lax.axis_index("src") // inner).astype(f32)
    return 0.5, 0.5, (here + 0.5) * (1.0 / outer)


def point_terms(message, lane, angles, middle):
    x, y, z = [message[m, 7:8, lane : lane + angles] - middle[m] for m in range(3)]
    nothing = jnp.zeros((3, angles), f32)
    vector = jnp.concatenate(
        [-2.0 * x, -2.0 * y, -2.0 * z, jnp.ones_like(x), x * x + y * y + z * z, nothing], axis=0
    )
    high, middling, low = three_parts(vector)
    terms = jnp.transpose(jnp.concatenate([high, middling, low, high, middling, high], axis=0))
    return jnp.concatenate([x, y, z, nothing, nothing[0:2]], axis=0), terms.astype(bf16)


def tile_terms(message, middle, moments, others):
    one = jnp.ones((1, LANES), f32)
    nothing = jnp.zeros((3, LANES), f32)
    for k in range(message.shape[0]):
        px, py, pz = [message[k, r : r + 1, :] - middle[r] for r in range(3)]
        sx, sy, sz, cc = [message[k, r : r + 1, :] for r in range(3, 7)]
        moments[k] = jnp.concatenate(
            [sx, sy, sz, sy * pz - sz * py, sz * px - sx * pz, sx * py - sy * px, nothing[0:2]],
            axis=0,
        )
        vector = jnp.concatenate(
            [px, py, pz, px * px + py * py + (pz * pz + cc), one, nothing], axis=0
        )
        high, middling, low = three_parts(vector)
        others[:, k * LANES : (k + 1) * LANES] = jnp.concatenate(
            [high, high, high, middling, middling, low], axis=0
        ).astype(bf16)


def quarter(terms, blocks):
    tall = terms.shape[0]
    diagonal = lax.broadcasted_iota(jnp.int32, (ROWS, LANES), 1) - lax.broadcasted_iota(
        jnp.int32, (ROWS, LANES), 0
    )
    distances = [
        jnp.dot(terms, others[...], preferred_element_type=f32) for moments, others in blocks
    ]
    rows = [jnp.zeros((ROWS, LANES), f32)] * 6
    for start in range(0, tall // ROWS, TOGETHER):
        held = [jnp.zeros((ROWS, LANES), f32)] * (6 * TOGETHER)
        for distance, (moments, others) in zip(distances, blocks):
            for k in range(moments.shape[0]):
                summed = [moments[k, r : r + 1, :] for r in range(6)]
                for i in range(TOGETHER):
                    low = (start + i) * ROWS
                    inverse = lax.rsqrt(distance[low : low + ROWS, k * LANES : (k + 1) * LANES])
                    weight = inverse * inverse * inverse
                    for r in range(6):
                        held[6 * i + r] += weight * summed[r]
        for i in range(TOGETHER):
            mask = diagonal == (start + i) * ROWS
            for r in range(6):
                value = jnp.sum(held[6 * i + r], axis=1, keepdims=True)
                rows[r] = rows[r] + jnp.where(mask, value, 0.0)
    return rows


def repeat(count, body, carried):
    if count <= UNROLLED:
        for i in range(count):
            carried = body(i, carried)
        return carried
    return lax.fori_loop(0, count, body, carried)


def quarter_speed(scale, along, terms, blocks):
    if isinstance(blocks, list):
        rows = quarter(terms, blocks)
    else:
        moments, others = blocks
        count = others.shape[0]
        if count <= UNROLLED:
            rows = quarter(terms, [(moments.at[i], others.at[i]) for i in range(count)])
        else:

            def add(i, rows):
                more = quarter(terms, [(moments.at[i], others.at[i])])
                return tuple(a + b for a, b in zip(rows, more))

            rows = lax.fori_loop(0, count, add, (jnp.zeros((ROWS, LANES), f32),) * 6)
    angles = terms.shape[0]
    ax, ay, az, bx, by, bz = [jnp.sum(r, axis=0, keepdims=True) for r in rows]
    tx, ty, tz = [
        jnp.concatenate([along[m : m + 1, :], jnp.zeros((1, LANES - angles), f32)], axis=1)
        for m in range(3)
    ]
    return jnp.concatenate(
        [
            scale * (ay * tz - az * ty - bx),
            scale * (az * tx - ax * tz - by),
            scale * (ax * ty - ay * tx - bz),
            jnp.zeros((ROWS - 3, LANES), f32),
        ],
        axis=0,
    )


def place_quarters(outer, ways, angles, speeds, placed, result):
    per = LANES // angles
    me = lax.axis_index("tgt")
    for i, step in enumerate(line_order(outer)):
        if step < ways:
            placed[source_of(me, turn(step, ways), ways)] = speeds[i]
    result[...] = jnp.zeros(result.shape, f32)
    for k in range(ways // per):
        block = placed[k * per]
        for i in range(1, per):
            block = block + pltpu.roll(placed[k * per + i], i * angles, 1)
        result[3 * k : 3 * k + 3, :] = block[0:3]


def early_kernel(scale, ways, outer, inner, *refs):
    messages, (after, speeds, moments, others, along, terms) = refs[: outer - 1], refs[outer - 1 :]
    middle = middle_of(outer, inner)
    angles = along.shape[2]
    for i, message in enumerate(messages):
        tile_terms(message, middle, moments.at[i], others.at[i])
        along[i], terms[i] = point_terms(message, angles, angles, middle)

    def one(i, unused):
        speeds[i] = quarter_speed(scale, along.at[i], terms[i], (moments, others))
        return unused

    repeat(outer - 1, one, 0)


def late_kernel(scale, ways, outer, inner, *refs):
    message, before, moments, others, along, terms = refs[:6]
    result, last_moments, last_others, speeds, placed = refs[6:]
    middle = middle_of(outer, inner)
    angles = along.shape[2]
    tile_terms(message, middle, last_moments, last_others)
    last_along, last_terms = point_terms(message, angles, angles, middle)

    def one(i, unused):
        speeds[i] = before[i] + quarter_speed(
            scale, along.at[i], terms[i], [(last_moments, last_others)]
        )
        return unused

    repeat(outer - 1, one, 0)
    speeds[outer - 1] = quarter_speed(
        scale, last_along, last_terms, (moments, others)
    ) + quarter_speed(scale, last_along, last_terms, [(last_moments, last_others)])
    place_quarters(outer, ways, angles, speeds, placed, result)


def own_kernel(scale, ways, outer, inner, *refs):
    messages, (moments, others, last_moments, last_others) = refs[:outer], refs[outer : outer + 4]
    after, result, along, terms, speeds, placed = refs[outer + 4 :]
    middle = middle_of(outer, inner)
    angles = along.shape[2]
    for i, message in enumerate(messages):
        along[i], terms[i] = point_terms(message, 0, angles, middle)

    def one(i, unused):
        if outer <= UNROLLED:
            blocks = [(moments.at[j], others.at[j]) for j in range(outer - 1)]
            speeds[i] = quarter_speed(
                scale, along.at[i], terms[i], blocks + [(last_moments, last_others)]
            )
        else:
            speeds[i] = quarter_speed(
                scale, along.at[i], terms[i], (moments, others)
            ) + quarter_speed(scale, along.at[i], terms[i], [(last_moments, last_others)])
        return unused

    repeat(outer, one, 0)
    place_quarters(outer, ways, angles, speeds, placed, result)


def merge_kernel(rows, own, arrived, picks, result):
    result[...] = jnp.zeros(result.shape, f32)
    result[0:rows, :] = own[0:rows, :] + arrived[0:rows, :]
    result[rows : rows + picks.shape[0], :] = picks[...]


def wall_kernel(ways, *refs):
    partials = refs[:ways]
    (still, inner_cells, strength, index, wall, grid, new_strength,
     fixed, picked, halves, rows, sem) = refs[ways:]
    angles = grid.shape[2]
    total = angles * ways
    parts = total // LANES
    per = LANES // angles
    rows_of = 3 * parts
    pieces = strength.shape[1] // LANES
    slots = 3 * pieces
    me = lax.axis_index("tgt")
    copy = pltpu.make_async_copy(index, rows, sem)
    copy.start()
    places = [
        (b, b // pieces, slice((b % pieces) * LANES, (b % pieces + 1) * LANES))
        for b in range(3 * pieces)
    ]
    for step, partial in enumerate(partials):
        picked[step * slots : (step + 1) * slots, :] = partial[rows_of : rows_of + slots, :]
    for b, c, part in places:
        picked[ways * slots + b : ways * slots + b + 1, :] = strength[c : c + 1, part]
        fixed[3 * total + b : 3 * total + b + 1, :] = strength[c : c + 1, part]
    added = partials[0][0:rows_of, :]
    for partial in partials[1:]:
        added = added + partial[0:rows_of, :]
    speed = [
        jnp.concatenate([added[3 * k + m : 3 * k + m + 1] for k in range(parts)], axis=1)
        for m in range(3)
    ]
    for i in range(per):
        moved = added if i == 0 else pltpu.roll(added, LANES - i * angles, 1)
        for k in range(parts):
            halves[k * per + i, 0:3, :] = moved[3 * k : 3 * k + 3]
    for m in range(3):
        wall[m] = halves[me, m : m + 1, 0:angles]

    first = lax.broadcasted_iota(jnp.int32, (ROWS, total), 0) == 0
    field = [inner_cells[m] for m in range(3)]
    local_swirl = inner_cells[3]
    local_diff = inner_cells[4]
    for counter in range(SUBSTEPS):
        transport = 0.5 * (local_swirl + swirl_gain * field[2])
        renewed = []
        for m in range(3):
            center = field[m]
            eastern = pltpu.roll(center, total - 1, 1)
            western = pltpu.roll(center, 1, 1)
            outward = pltpu.roll(center, ROWS - 1, 0)
            inward = jnp.where(first, speed[m], pltpu.roll(center, 1, 0))
            renewed.append(
                center
                + local_diff * (eastern + western + outward + inward - 4.0 * center)
                - transport * (eastern - western)
            )
        field = renewed
    stacked = jnp.concatenate(field + [jnp.zeros((LANES - 3 * ROWS, total), f32)], axis=0)
    for k in range(parts):
        turned = jnp.transpose(stacked[:, k * LANES : (k + 1) * LANES])
        for m in range(3):
            place = m * total + k * LANES
            fixed[place : place + LANES, :] = turned if m == 0 else pltpu.roll(
                turned, LANES - m * ROWS, 1
            )
    near = lax.broadcasted_iota(jnp.int32, (angles, LANES), 1) < SUBSTEPS
    for m in range(3):
        place = pl.multiple_of(m * total + me * angles, ROWS)
        grid[0, m] = jnp.where(near, fixed[pl.ds(place, angles), :], still[m])
    near = lax.broadcasted_iota(jnp.int32, (1, LANES), 1) < SUBSTEPS
    copy.wait()
    for b, c, part in places:
        new_strength[c : c + 1, part] = jnp.where(
            near, fixed[pl.ds(rows[b, 0], 1), :], picked[pl.ds(rows[b, 1], 1), :]
        )


def send(block, pairs):
    return lax.ppermute(block, ("src", "tgt"), pairs)


def on_device(
    particle_position,
    particle_strength,
    core_radius,
    boundary_points,
    vorticity,
    swirl,
    diffusivity,
    intersection_source,
    intersection_target,
):
    sources = lax.axis_size("src")
    ways = lax.axis_size("tgt")
    planes, comps, angles, radial = vorticity.shape
    per_device = particle_position.shape[1]
    tiles = per_device // LANES
    blocks = intersection_source.shape[2]
    inner = 2 if sources % 2 == 0 else 1
    outer = sources // inner
    total = angles * ways
    scale = 1.6 / (4.0 * math.pi * math.sqrt(per_device * ways * sources))

    def pairs(move):
        found = []
        for s in range(sources):
            for t in range(ways):
                o, i, u = move(s // inner, s % inner, t)
                found.append((s * ways + t, (o * inner + i) * ways + u))
        return found

    def over_tgt(block, step):
        return send(block, pairs(lambda o, i, t: (o, i, partner(t, step, ways))))

    given = (
        particle_position, particle_strength, core_radius, boundary_points,
        vorticity, swirl, diffusivity, intersection_source, intersection_target,
    )
    *messages, own, source, target = pl.pallas_call(
        functools.partial(particles_kernel, inner, outer),
        out_shape=(shape(tiles, ROWS, LANES),) * outer + (
            shape(5, angles, LANES),
            jax.ShapeDtypeStruct(intersection_source.shape, jnp.int32),
            jax.ShapeDtypeStruct(intersection_target.shape, jnp.int32),
        ),
        in_specs=[hbm()] * 9,
        out_specs=(vmem(),) * (outer + 3),
        scratch_shapes=[pltpu.VMEM(a.shape, f32) for a in given[0:4]]
        + [pltpu.SemaphoreType.DMA((11,))],
        compiler_params=limit(4),
        name="particles",
    )(*stay(*given))
    line = [messages[0]] + [
        send(
            message,
            pairs(lambda o, i, t: (partner(o, k, outer), i, partner(t, turn(k, ways), ways))),
        )
        for k, message in zip(line_order(outer)[1:], messages[1:])
    ]

    edges = pl.pallas_call(
        edges_kernel,
        out_shape=shape(11, ROWS, LANES),
        in_specs=[vmem()] * 3,
        out_specs=vmem(),
        compiler_params=limit(4),
        cost_estimate=cost(1 << 31, 1 << 10),
        name="edges",
    )(own, source, target)
    steps = tgt_order(ways)
    around = [edges] + [over_tgt(edges, k) for k in steps[1:]]

    rows = 3 * total // LANES
    slots = blocks
    sums_shape = shape(-(-rows // ROWS) * ROWS, LANES)
    along_shape = (ROWS, angles)
    terms_shape = (angles, TERMS)
    others_shape = (TERMS, per_device)
    early = outer - 1
    before, *held = pl.pallas_call(
        functools.partial(early_kernel, scale, ways, outer, inner),
        out_shape=(
            shape(early, ROWS, LANES),
            shape(early, tiles, ROWS, LANES),
            jax.ShapeDtypeStruct((early, *others_shape), bf16),
            shape(early, *along_shape),
            jax.ShapeDtypeStruct((early, *terms_shape), bf16),
        ),
        in_specs=[vmem()] * outer,
        out_specs=(vmem(),) * 5,
        compiler_params=limit(12),
        cost_estimate=cost(1 << 10, 1 << 10),
        name="early",
    )(*line[:-1], edges)
    for_partner, last_moments, last_others = pl.pallas_call(
        functools.partial(late_kernel, scale, ways, outer, inner),
        out_shape=(
            sums_shape,
            shape(tiles, ROWS, LANES),
            jax.ShapeDtypeStruct(others_shape, bf16),
        ),
        in_specs=[vmem()] * 6,
        out_specs=(vmem(),) * 3,
        scratch_shapes=[
            pltpu.VMEM((outer, ROWS, LANES), f32),
            pltpu.VMEM((ways, ROWS, LANES), f32),
        ],
        compiler_params=limit(12),
        cost_estimate=cost(1 << 30, 1 << 10),
        name="late",
    )(line[-1], before, *held)
    arrived = send(for_partner, pairs(lambda o, i, t: (o, inner - 1 - i, t)))
    own_sum = pl.pallas_call(
        functools.partial(own_kernel, scale, ways, outer, inner),
        out_shape=sums_shape,
        in_specs=[vmem()] * (outer + 5),
        out_specs=vmem(),
        scratch_shapes=[
            pltpu.VMEM((outer, *along_shape), f32),
            pltpu.VMEM((outer, *terms_shape), bf16),
            pltpu.VMEM((outer, ROWS, LANES), f32),
            pltpu.VMEM((ways, ROWS, LANES), f32),
        ],
        compiler_params=limit(12),
        cost_estimate=cost(1 << 31, 1 << 10),
        name="own",
    )(*line, held[0], held[1], last_moments, last_others, for_partner)
    still, picks, inner_cells, index = pl.pallas_call(
        functools.partial(still_kernel, ways),
        out_shape=(
            shape(3, angles, LANES),
            shape(slots, LANES),
            shape(5, ROWS, total),
            jax.ShapeDtypeStruct((16 * ((blocks + 15) // 16), LANES), jnp.int32),
        ),
        in_specs=[vmem()] * (ways + 3),
        out_specs=(vmem(),) * 4,
        scratch_shapes=[
            pltpu.VMEM((ways,) + edges.shape, f32),
            pltpu.SMEM(source.shape, jnp.int32),
            pltpu.SemaphoreType.DMA,
        ],
        compiler_params=limit(8),
        name="still",
    )(*around, own, source, own_sum)
    partial_sum = pl.pallas_call(
        functools.partial(merge_kernel, rows),
        out_shape=shape(-(-(rows + blocks) // ROWS) * ROWS, LANES),
        in_specs=[vmem()] * 3,
        out_specs=vmem(),
        compiler_params=limit(4),
        name="merge",
    )(own_sum, arrived, picks)
    partials = [partial_sum] + [over_tgt(partial_sum, k) for k in steps[1:]]

    wall, grid, new_strength = pl.pallas_call(
        functools.partial(wall_kernel, ways),
        out_shape=(shape(3, planes, angles), shape(*vorticity.shape), shape(3, per_device)),
        in_specs=[vmem()] * (ways + 4),
        out_specs=(vmem(),) * 3,
        scratch_shapes=[
            pltpu.VMEM((3 * total + slots, LANES), f32),
            pltpu.VMEM((slots * ways + slots, LANES), f32),
            pltpu.VMEM((ways, ROWS, LANES), f32),
            pltpu.SMEM(index.shape, jnp.int32),
            pltpu.SemaphoreType.DMA,
        ],
        compiler_params=limit(16),
        name="wall",
    )(*partials, still, inner_cells, particle_strength, index)
    return (wall, grid, new_strength)


def solution(mesh):
    in_specs = (
        P(None, ("src", "tgt")),
        P(None, ("src", "tgt")),
        P(None, ("src", "tgt")),
        P(None, None, "tgt"),
        P("src", None, "tgt", None),
        P("src", "tgt", None),
        P("src", "tgt", None),
        P("src", "tgt", None),
        P("src", "tgt", None),
    )
    out_specs = (P(None, "src", "tgt"), P("src", None, "tgt", None), P(None, ("src", "tgt")))
    return jax.shard_map(
        on_device, mesh=mesh, in_specs=in_specs, out_specs=out_specs, check_vma=False
    )
```

```python
import functools
import math

import jax
import jax.numpy as jnp
from jax import lax
from jax.experimental import pallas as pl
from jax.experimental.pallas import tpu as pltpu
from jax.sharding import PartitionSpec as P

SUBSTEPS = 3
LANES = 128
ROWS = 8
TOGETHER = 2
TERMS = 48
UNROLLED = 4
swirl_gain = 0.2
f32 = jnp.float32
bf16 = jnp.bfloat16


def vmem():
    return pl.BlockSpec(memory_space=pltpu.VMEM)


def smem():
    return pl.BlockSpec(memory_space=pltpu.SMEM)


def hbm():
    return pl.BlockSpec(memory_space=pltpu.HBM)


def stay(*arrays):
    return [pltpu.with_memory_space_constraint(a, pltpu.HBM) for a in arrays]


def shape(*dims):
    return jax.ShapeDtypeStruct(dims, f32)


def limit(megabytes):
    return pltpu.CompilerParams(vmem_limit_bytes=megabytes << 20)


def cost(flops, size):
    return pl.CostEstimate(flops=flops, bytes_accessed=size, transcendentals=0)


def divisor(number, most):
    return max(c for c in range(1, min(number, most) + 1) if number % c == 0)


def power_of_two(number):
    return number & (number - 1) == 0


def partner(index, step, count):
    return index ^ step if power_of_two(count) else (index + step) % count


def source_of(index, step, count):
    return index ^ step if power_of_two(count) else (index - step) % count


def line_order(outer):
    return [0, *range(1, outer // 2), *reversed(range(outer // 2, outer))]


def tgt_order(ways):
    return [0, *range(ways // 2, ways), *range(1, ways // 2)]


def turn(step, ways):
    return {1: 2, 2: 3, 3: 1}.get(step % ways, step % ways)


def particles_kernel(inner, outer, *refs):
    given, messages = refs[:9], refs[9 : 9 + outer]
    own, lists, held, sems = refs[9 + outer], refs[10 + outer : 12 + outer], refs[12 + outer : -1], refs[-1]
    vort, swirl, diff = given[4:7]
    targets = (*held, *[own.at[c] for c in range(5)], *lists)
    sources = (*given[0:4], *[vort.at[0, m] for m in range(3)], swirl.at[0], diff.at[0], *given[7:9])
    copies = [
        pltpu.make_async_copy(a, b, sems.at[i]) for i, (a, b) in enumerate(zip(sources, targets))
    ]
    for copy in copies:
        copy.start()
    for copy in copies[0:4]:
        copy.wait()
    pos, strength, radius, points = held
    tiles = pos.shape[1] // LANES
    angles = points.shape[2]
    src = lax.axis_index("src")
    core = radius[...] * radius[...]
    parts = [slice(k * LANES, (k + 1) * LANES) for k in range(tiles)]
    bare = [
        jnp.concatenate(
            [pos[:, part], strength[:, part], core[:, part], jnp.zeros((1, LANES), f32)], axis=0
        )
        for part in parts
    ]
    last = lax.broadcasted_iota(jnp.int32, (ROWS, LANES), 0) == ROWS - 1
    for step, message in zip(line_order(outer), messages):
        there = partner(src // inner, step, outer) * inner
        planes = (there + src % inner, there + inner - 1 - src % inner)
        for k in range(tiles):
            if k < 3:
                both = [points[k, pl.ds(plane, 1), :] for plane in planes]
                both.append(jnp.zeros((1, LANES - 2 * angles), f32))
                both = [p for p in both if p.shape[1]]
                message[k] = jnp.where(last, jnp.concatenate(both, axis=1), bare[k])
            else:
                message[k] = bare[k]
    for copy in copies[4:]:
        copy.wait()


def edges_kernel(own, own_source, own_target, message):
    angles = own.shape[1]
    blocks = own_source.shape[2]
    total = angles * lax.axis_size("tgt")
    half = ROWS // 2
    for c in range(5):
        message[c, :, 0:angles] = jnp.transpose(own[c])[0:ROWS, :]
        message[c, :, angles:LANES] = jnp.zeros((ROWS, LANES - angles), f32)
        message[6 + c, 0:half, :] = own[c, 0:half]
        message[6 + c, half:ROWS, :] = own[c, angles - half : angles]
    message[5] = jnp.full((ROWS, LANES), -1.0, f32)
    q = own_source[0]
    row = (q // angles) * total + lax.axis_index("tgt") * angles + q % angles
    message[5, 0:1, 0:blocks] = row.astype(f32)
    message[5, 1:2, 0:blocks] = own_target[0].astype(f32)


def inner_step(field, local_swirl, local_diff, speed, first):
    total = field[0].shape[1]
    transport = 0.5 * (local_swirl + swirl_gain * field[2])
    renewed = []
    for m in range(3):
        center = field[m]
        eastern = pltpu.roll(center, total - 1, 1)
        western = pltpu.roll(center, 1, 1)
        outward = pltpu.roll(center, ROWS - 1, 0)
        inward = jnp.where(first, speed[m], pltpu.roll(center, 1, 0))
        renewed.append(
            center
            + local_diff * (eastern + western + outward + inward - 4.0 * center)
            - transport * (eastern - western)
        )
    return renewed


def still_kernel(ways, *refs):
    messages = refs[:ways]
    own, lists, after, grid, picks, inner_cells, index, placed, source, sem = refs[ways:]
    copy = pltpu.make_async_copy(lists, source, sem)
    copy.start()
    angles = own.shape[1]
    height = angles + ROWS
    blocks = lists.shape[2]
    me = lax.axis_index("tgt")
    for step, message in zip(tgt_order(ways), messages):
        placed[source_of(me, step, ways)] = message[...]

    cells = [
        jnp.concatenate([placed[t, c, :, 0:angles] for t in range(ways)], axis=1)
        for c in range(5)
    ]
    first = lax.broadcasted_iota(jnp.int32, cells[0].shape, 0) == 0
    for m, center in enumerate(inner_step(cells[0:3], cells[3], cells[4], [0.0] * 3, first)):
        inner_cells[m] = center
    inner_cells[3] = cells[3]
    inner_cells[4] = cells[4]

    shaped = index.shape
    name = (me * blocks + lax.broadcasted_iota(jnp.int32, shaped, 0)).astype(f32)
    lane = lax.broadcasted_iota(jnp.int32, shaped, 1).astype(f32)
    row = jnp.full(shaped, -1.0, f32)
    slot = jnp.zeros(shaped, f32)
    for step, message in enumerate(messages):
        match = message[5, 1:2, :] == name
        row = jnp.maximum(row, jnp.where(match, message[5, 0:1, :], -1.0))
        slot = jnp.maximum(slot, jnp.where(match, lane + float(step * picks.shape[0]), 0.0))
    row = jnp.max(row, axis=1, keepdims=True)
    slot = jnp.max(slot, axis=1, keepdims=True)
    block = lax.broadcasted_iota(jnp.int32, shaped, 0).astype(f32)
    block = jnp.minimum(block, float(blocks - 1))
    kept = row < 0.0
    row = jnp.where(kept, float(3 * angles * ways) + block, row)
    slot = jnp.where(kept, float(ways * blocks) + block, slot)
    index[...] = jnp.where(lane < 1.0, row, slot).astype(jnp.int32)

    upper = lax.broadcasted_iota(jnp.int32, (ROWS, LANES), 0) < ROWS // 2
    east = lax.rem(me + 1, ways)
    west = lax.rem(me + ways - 1, ways)
    cells = [
        jnp.concatenate(
            [own[c], jnp.where(upper, placed[east, 6 + c], placed[west, 6 + c])], axis=0
        )
        for c in range(5)
    ]
    field, local_swirl, local_diff = cells[0:3], cells[3], cells[4]
    lane = lax.broadcasted_iota(jnp.int32, (height, LANES), 1)
    for counter in range(SUBSTEPS):
        transport = 0.5 * (local_swirl + swirl_gain * field[2])
        renewed = []
        for m in range(3):
            center = field[m]
            eastern = pltpu.roll(center, height - 1, 0)
            western = pltpu.roll(center, 1, 0)
            outward = jnp.where(lane == LANES - 1, 0.0, pltpu.roll(center, LANES - 1, 1))
            inward = jnp.where(lane == 0, 0.0, pltpu.roll(center, 1, 1))
            renewed.append(
                center
                + local_diff * (eastern + western + outward + inward - 4.0 * center)
                - transport * (eastern - western)
            )
        field = renewed
    for m in range(3):
        grid[m] = field[m][0:angles]
    picks[...] = jnp.zeros(picks.shape, f32)
    copy.wait()
    for i in range(blocks):
        q = source[0, 0, i]
        picks[i : i + 1, :] = grid[q // angles, pl.ds(q % angles, 1), :]


def three_parts(value):
    high = value.astype(bf16).astype(f32)
    rest = value - high
    middle = rest.astype(bf16).astype(f32)
    return high, middle, rest - middle


def middle_of(outer, inner):
    here = (lax.axis_index("src") // inner).astype(f32)
    return 0.5, 0.5, (here + 0.5) * (1.0 / outer)


def point_terms(message, lane, angles, middle):
    x, y, z = [message[m, 7:8, lane : lane + angles] - middle[m] for m in range(3)]
    nothing = jnp.zeros((3, angles), f32)
    vector = jnp.concatenate(
        [-2.0 * x, -2.0 * y, -2.0 * z, jnp.ones_like(x), x * x + y * y + z * z, nothing], axis=0
    )
    high, middling, low = three_parts(vector)
    terms = jnp.transpose(jnp.concatenate([high, middling, low, high, middling, high], axis=0))
    return jnp.concatenate([x, y, z, nothing, nothing[0:2]], axis=0), terms.astype(bf16)


def tile_terms(message, middle, moments, others):
    one = jnp.ones((1, LANES), f32)
    nothing = jnp.zeros((3, LANES), f32)
    for k in range(message.shape[0]):
        px, py, pz = [message[k, r : r + 1, :] - middle[r] for r in range(3)]
        sx, sy, sz, cc = [message[k, r : r + 1, :] for r in range(3, 7)]
        moments[k] = jnp.concatenate(
            [sx, sy, sz, sy * pz - sz * py, sz * px - sx * pz, sx * py - sy * px, nothing[0:2]],
            axis=0,
        )
        vector = jnp.concatenate(
            [px, py, pz, px * px + py * py + (pz * pz + cc), one, nothing], axis=0
        )
        high, middling, low = three_parts(vector)
        others[:, k * LANES : (k + 1) * LANES] = jnp.concatenate(
            [high, high, high, middling, middling, low], axis=0
        ).astype(bf16)


def quarter(terms, blocks):
    tall = terms.shape[0]
    diagonal = lax.broadcasted_iota(jnp.int32, (ROWS, LANES), 1) - lax.broadcasted_iota(
        jnp.int32, (ROWS, LANES), 0
    )
    distances = [
        jnp.dot(terms, others[...], preferred_element_type=f32) for moments, others in blocks
    ]
    rows = [jnp.zeros((ROWS, LANES), f32)] * 6
    for start in range(0, tall // ROWS, TOGETHER):
        held = [jnp.zeros((ROWS, LANES), f32)] * (6 * TOGETHER)
        for distance, (moments, others) in zip(distances, blocks):
            for k in range(moments.shape[0]):
                summed = [moments[k, r : r + 1, :] for r in range(6)]
                for i in range(TOGETHER):
                    low = (start + i) * ROWS
                    inverse = lax.rsqrt(distance[low : low + ROWS, k * LANES : (k + 1) * LANES])
                    weight = inverse * inverse * inverse
                    for r in range(6):
                        held[6 * i + r] += weight * summed[r]
        for i in range(TOGETHER):
            mask = diagonal == (start + i) * ROWS
            for r in range(6):
                value = jnp.sum(held[6 * i + r], axis=1, keepdims=True)
                rows[r] = rows[r] + jnp.where(mask, value, 0.0)
    return rows


def repeat(count, body, carried):
    if count <= UNROLLED:
        for i in range(count):
            carried = body(i, carried)
        return carried
    return lax.fori_loop(0, count, body, carried)


def quarter_speed(scale, along, terms, blocks):
    if isinstance(blocks, list):
        rows = quarter(terms, blocks)
    else:
        moments, others = blocks
        count = others.shape[0]
        if count <= UNROLLED:
            rows = quarter(terms, [(moments.at[i], others.at[i]) for i in range(count)])
        else:

            def add(i, rows):
                more = quarter(terms, [(moments.at[i], others.at[i])])
                return tuple(a + b for a, b in zip(rows, more))

            rows = lax.fori_loop(0, count, add, (jnp.zeros((ROWS, LANES), f32),) * 6)
    angles = terms.shape[0]
    ax, ay, az, bx, by, bz = [jnp.sum(r, axis=0, keepdims=True) for r in rows]
    tx, ty, tz = [
        jnp.concatenate([along[m : m + 1, :], jnp.zeros((1, LANES - angles), f32)], axis=1)
        for m in range(3)
    ]
    return jnp.concatenate(
        [
            scale * (ay * tz - az * ty - bx),
            scale * (az * tx - ax * tz - by),
            scale * (ax * ty - ay * tx - bz),
            jnp.zeros((ROWS - 3, LANES), f32),
        ],
        axis=0,
    )


def place_quarters(outer, ways, angles, speeds, placed, result):
    per = LANES // angles
    me = lax.axis_index("tgt")
    for i, step in enumerate(line_order(outer)):
        if step < ways:
            placed[source_of(me, turn(step, ways), ways)] = speeds[i]
    result[...] = jnp.zeros(result.shape, f32)
    for k in range(ways // per):
        block = placed[k * per]
        for i in range(1, per):
            block = block + pltpu.roll(placed[k * per + i], i * angles, 1)
        result[3 * k : 3 * k + 3, :] = block[0:3]


def early_kernel(scale, ways, outer, inner, *refs):
    messages, (after, speeds, moments, others, along, terms) = refs[: outer - 1], refs[outer - 1 :]
    middle = middle_of(outer, inner)
    angles = along.shape[2]
    for i, message in enumerate(messages):
        tile_terms(message, middle, moments.at[i], others.at[i])
        along[i], terms[i] = point_terms(message, angles, angles, middle)

    def one(i, unused):
        speeds[i] = quarter_speed(scale, along.at[i], terms[i], (moments, others))
        return unused

    repeat(outer - 1, one, 0)


def late_kernel(scale, ways, outer, inner, *refs):
    message, before, moments, others, along, terms = refs[:6]
    result, last_moments, last_others, speeds, placed = refs[6:]
    middle = middle_of(outer, inner)
    angles = along.shape[2]
    tile_terms(message, middle, last_moments, last_others)
    last_along, last_terms = point_terms(message, angles, angles, middle)

    def one(i, unused):
        speeds[i] = before[i] + quarter_speed(
            scale, along.at[i], terms[i], [(last_moments, last_others)]
        )
        return unused

    repeat(outer - 1, one, 0)
    speeds[outer - 1] = quarter_speed(
        scale, last_along, last_terms, (moments, others)
    ) + quarter_speed(scale, last_along, last_terms, [(last_moments, last_others)])
    place_quarters(outer, ways, angles, speeds, placed, result)


def own_kernel(scale, ways, outer, inner, *refs):
    messages, (moments, others, last_moments, last_others) = refs[:outer], refs[outer : outer + 4]
    after, result, along, terms, speeds, placed = refs[outer + 4 :]
    middle = middle_of(outer, inner)
    angles = along.shape[2]
    for i, message in enumerate(messages):
        along[i], terms[i] = point_terms(message, 0, angles, middle)

    def one(i, unused):
        if outer <= UNROLLED:
            blocks = [(moments.at[j], others.at[j]) for j in range(outer - 1)]
            speeds[i] = quarter_speed(
                scale, along.at[i], terms[i], blocks + [(last_moments, last_others)]
            )
        else:
            speeds[i] = quarter_speed(
                scale, along.at[i], terms[i], (moments, others)
            ) + quarter_speed(scale, along.at[i], terms[i], [(last_moments, last_others)])
        return unused

    repeat(outer, one, 0)
    place_quarters(outer, ways, angles, speeds, placed, result)


def merge_kernel(rows, own, arrived, picks, result):
    result[...] = jnp.zeros(result.shape, f32)
    result[0:rows, :] = own[0:rows, :] + arrived[0:rows, :]
    result[rows : rows + picks.shape[0], :] = picks[...]


def wall_kernel(ways, *refs):
    partials = refs[:ways]
    (still, inner_cells, strength, index, wall, grid, new_strength,
     fixed, picked, halves, rows, sem) = refs[ways:]
    angles = grid.shape[2]
    total = angles * ways
    parts = total // LANES
    per = LANES // angles
    rows_of = 3 * parts
    pieces = strength.shape[1] // LANES
    slots = 3 * pieces
    me = lax.axis_index("tgt")
    copy = pltpu.make_async_copy(index, rows, sem)
    copy.start()
    places = [
        (b, b // pieces, slice((b % pieces) * LANES, (b % pieces + 1) * LANES))
        for b in range(3 * pieces)
    ]
    for step, partial in enumerate(partials):
        picked[step * slots : (step + 1) * slots, :] = partial[rows_of : rows_of + slots, :]
    for b, c, part in places:
        picked[ways * slots + b : ways * slots + b + 1, :] = strength[c : c + 1, part]
        fixed[3 * total + b : 3 * total + b + 1, :] = strength[c : c + 1, part]
    added = partials[0][0:rows_of, :]
    for partial in partials[1:]:
        added = added + partial[0:rows_of, :]
    speed = [
        jnp.concatenate([added[3 * k + m : 3 * k + m + 1] for k in range(parts)], axis=1)
        for m in range(3)
    ]
    for i in range(per):
        moved = added if i == 0 else pltpu.roll(added, LANES - i * angles, 1)
        for k in range(parts):
            halves[k * per + i, 0:3, :] = moved[3 * k : 3 * k + 3]
    for m in range(3):
        wall[m] = halves[me, m : m + 1, 0:angles]

    first = lax.broadcasted_iota(jnp.int32, (ROWS, total), 0) == 0
    local_swirl = inner_cells[3]
    local_diff = inner_cells[4]
    gain = jnp.where(first, local_diff, 0.0)
    field = [inner_cells[m] + gain * speed[m] for m in range(3)]
    for counter in range(1, SUBSTEPS):
        field = inner_step(field, local_swirl, local_diff, speed, first)
    stacked = jnp.concatenate(field + [jnp.zeros((LANES - 3 * ROWS, total), f32)], axis=0)
    for k in range(parts):
        turned = jnp.transpose(stacked[:, k * LANES : (k + 1) * LANES])
        for m in range(3):
            place = m * total + k * LANES
            fixed[place : place + LANES, :] = turned if m == 0 else pltpu.roll(
                turned, LANES - m * ROWS, 1
            )
    near = lax.broadcasted_iota(jnp.int32, (angles, LANES), 1) < SUBSTEPS
    for m in range(3):
        place = pl.multiple_of(m * total + me * angles, ROWS)
        grid[0, m] = jnp.where(near, fixed[pl.ds(place, angles), :], still[m])
    near = lax.broadcasted_iota(jnp.int32, (1, LANES), 1) < SUBSTEPS
    copy.wait()
    for b, c, part in places:
        new_strength[c : c + 1, part] = jnp.where(
            near, fixed[pl.ds(rows[b, 0], 1), :], picked[pl.ds(rows[b, 1], 1), :]
        )


def send(block, pairs):
    return lax.ppermute(block, ("src", "tgt"), pairs)


def on_device(
    particle_position,
    particle_strength,
    core_radius,
    boundary_points,
    vorticity,
    swirl,
    diffusivity,
    intersection_source,
    intersection_target,
):
    sources = lax.axis_size("src")
    ways = lax.axis_size("tgt")
    planes, comps, angles, radial = vorticity.shape
    per_device = particle_position.shape[1]
    tiles = per_device // LANES
    blocks = intersection_source.shape[2]
    inner = 2 if sources % 2 == 0 else 1
    outer = sources // inner
    total = angles * ways
    scale = 1.6 / (4.0 * math.pi * math.sqrt(per_device * ways * sources))

    def pairs(move):
        found = []
        for s in range(sources):
            for t in range(ways):
                o, i, u = move(s // inner, s % inner, t)
                found.append((s * ways + t, (o * inner + i) * ways + u))
        return found

    def over_tgt(block, step):
        return send(block, pairs(lambda o, i, t: (o, i, partner(t, step, ways))))

    given = (
        particle_position, particle_strength, core_radius, boundary_points,
        vorticity, swirl, diffusivity, intersection_source, intersection_target,
    )
    *messages, own, source, target = pl.pallas_call(
        functools.partial(particles_kernel, inner, outer),
        out_shape=(shape(tiles, ROWS, LANES),) * outer + (
            shape(5, angles, LANES),
            jax.ShapeDtypeStruct(intersection_source.shape, jnp.int32),
            jax.ShapeDtypeStruct(intersection_target.shape, jnp.int32),
        ),
        in_specs=[hbm()] * 9,
        out_specs=(vmem(),) * (outer + 3),
        scratch_shapes=[pltpu.VMEM(a.shape, f32) for a in given[0:4]]
        + [pltpu.SemaphoreType.DMA((11,))],
        compiler_params=limit(4),
        name="particles",
    )(*stay(*given))
    line = [messages[0]] + [
        send(
            message,
            pairs(lambda o, i, t: (partner(o, k, outer), i, partner(t, turn(k, ways), ways))),
        )
        for k, message in zip(line_order(outer)[1:], messages[1:])
    ]

    edges = pl.pallas_call(
        edges_kernel,
        out_shape=shape(11, ROWS, LANES),
        in_specs=[vmem()] * 3,
        out_specs=vmem(),
        compiler_params=limit(4),
        cost_estimate=cost(1 << 31, 1 << 10),
        name="edges",
    )(own, source, target)
    steps = tgt_order(ways)
    around = [edges] + [over_tgt(edges, k) for k in steps[1:]]

    rows = 3 * total // LANES
    slots = blocks
    sums_shape = shape(-(-rows // ROWS) * ROWS, LANES)
    along_shape = (ROWS, angles)
    terms_shape = (angles, TERMS)
    others_shape = (TERMS, per_device)
    early = outer - 1
    before, *held = pl.pallas_call(
        functools.partial(early_kernel, scale, ways, outer, inner),
        out_shape=(
            shape(early, ROWS, LANES),
            shape(early, tiles, ROWS, LANES),
            jax.ShapeDtypeStruct((early, *others_shape), bf16),
            shape(early, *along_shape),
            jax.ShapeDtypeStruct((early, *terms_shape), bf16),
        ),
        in_specs=[vmem()] * outer,
        out_specs=(vmem(),) * 5,
        compiler_params=limit(12),
        cost_estimate=cost(1 << 10, 1 << 10),
        name="early",
    )(*line[:-1], edges)
    for_partner, last_moments, last_others = pl.pallas_call(
        functools.partial(late_kernel, scale, ways, outer, inner),
        out_shape=(
            sums_shape,
            shape(tiles, ROWS, LANES),
            jax.ShapeDtypeStruct(others_shape, bf16),
        ),
        in_specs=[vmem()] * 6,
        out_specs=(vmem(),) * 3,
        scratch_shapes=[
            pltpu.VMEM((outer, ROWS, LANES), f32),
            pltpu.VMEM((ways, ROWS, LANES), f32),
        ],
        compiler_params=limit(12),
        cost_estimate=cost(1 << 30, 1 << 10),
        name="late",
    )(line[-1], before, *held)
    arrived = send(for_partner, pairs(lambda o, i, t: (o, inner - 1 - i, t)))
    own_sum = pl.pallas_call(
        functools.partial(own_kernel, scale, ways, outer, inner),
        out_shape=sums_shape,
        in_specs=[vmem()] * (outer + 5),
        out_specs=vmem(),
        scratch_shapes=[
            pltpu.VMEM((outer, *along_shape), f32),
            pltpu.VMEM((outer, *terms_shape), bf16),
            pltpu.VMEM((outer, ROWS, LANES), f32),
            pltpu.VMEM((ways, ROWS, LANES), f32),
        ],
        compiler_params=limit(12),
        cost_estimate=cost(1 << 31, 1 << 10),
        name="own",
    )(*line, held[0], held[1], last_moments, last_others, for_partner)
    still, picks, inner_cells, index = pl.pallas_call(
        functools.partial(still_kernel, ways),
        out_shape=(
            shape(3, angles, LANES),
            shape(slots, LANES),
            shape(5, ROWS, total),
            jax.ShapeDtypeStruct((16 * ((blocks + 15) // 16), LANES), jnp.int32),
        ),
        in_specs=[vmem()] * (ways + 3),
        out_specs=(vmem(),) * 4,
        scratch_shapes=[
            pltpu.VMEM((ways,) + edges.shape, f32),
            pltpu.SMEM(source.shape, jnp.int32),
            pltpu.SemaphoreType.DMA,
        ],
        compiler_params=limit(8),
        name="still",
    )(*around, own, source, own_sum)
    partial_sum = pl.pallas_call(
        functools.partial(merge_kernel, rows),
        out_shape=shape(-(-(rows + blocks) // ROWS) * ROWS, LANES),
        in_specs=[vmem()] * 3,
        out_specs=vmem(),
        compiler_params=limit(4),
        name="merge",
    )(own_sum, arrived, picks)
    partials = [partial_sum] + [over_tgt(partial_sum, k) for k in steps[1:]]

    wall, grid, new_strength = pl.pallas_call(
        functools.partial(wall_kernel, ways),
        out_shape=(shape(3, planes, angles), shape(*vorticity.shape), shape(3, per_device)),
        in_specs=[vmem()] * (ways + 4),
        out_specs=(vmem(),) * 3,
        scratch_shapes=[
            pltpu.VMEM((3 * total + slots, LANES), f32),
            pltpu.VMEM((slots * ways + slots, LANES), f32),
            pltpu.VMEM((ways, ROWS, LANES), f32),
            pltpu.SMEM(index.shape, jnp.int32),
            pltpu.SemaphoreType.DMA,
        ],
        compiler_params=limit(16),
        name="wall",
    )(*partials, still, inner_cells, particle_strength, index)
    return (wall, grid, new_strength)


def solution(mesh):
    in_specs = (
        P(None, ("src", "tgt")),
        P(None, ("src", "tgt")),
        P(None, ("src", "tgt")),
        P(None, None, "tgt"),
        P("src", None, "tgt", None),
        P("src", "tgt", None),
        P("src", "tgt", None),
        P("src", "tgt", None),
        P("src", "tgt", None),
    )
    out_specs = (P(None, "src", "tgt"), P("src", None, "tgt", None), P(None, ("src", "tgt")))
    return jax.shard_map(
        on_device, mesh=mesh, in_specs=in_specs, out_specs=out_specs, check_vma=False
    )
```

```python
import functools
import math

import jax
import jax.numpy as jnp
from jax import lax
from jax.experimental import pallas as pl
from jax.experimental.pallas import tpu as pltpu
from jax.sharding import PartitionSpec as P

SUBSTEPS = 3
LANES = 128
ROWS = 8
TOGETHER = 2
TERMS = 48
UNROLLED = 4
swirl_gain = 0.2
f32 = jnp.float32
bf16 = jnp.bfloat16


def vmem():
    return pl.BlockSpec(memory_space=pltpu.VMEM)


def smem():
    return pl.BlockSpec(memory_space=pltpu.SMEM)


def hbm():
    return pl.BlockSpec(memory_space=pltpu.HBM)


def stay(*arrays):
    return [pltpu.with_memory_space_constraint(a, pltpu.HBM) for a in arrays]


def shape(*dims):
    return jax.ShapeDtypeStruct(dims, f32)


def limit(megabytes):
    return pltpu.CompilerParams(vmem_limit_bytes=megabytes << 20)


def cost(flops, size):
    return pl.CostEstimate(flops=flops, bytes_accessed=size, transcendentals=0)


def divisor(number, most):
    return max(c for c in range(1, min(number, most) + 1) if number % c == 0)


def power_of_two(number):
    return number & (number - 1) == 0


def partner(index, step, count):
    return index ^ step if power_of_two(count) else (index + step) % count


def source_of(index, step, count):
    return index ^ step if power_of_two(count) else (index - step) % count


def line_order(outer):
    return [0, *range(1, outer // 2), *reversed(range(outer // 2, outer))]


def tgt_order(ways):
    return [0, *range(ways // 2, ways), *range(1, ways // 2)]


def turn(step, ways):
    return {1: 2, 2: 3, 3: 1}.get(step % ways, step % ways)


def particles_kernel(inner, outer, *refs):
    given, messages = refs[:9], refs[9 : 9 + outer]
    own, lists, held, sems = refs[9 + outer], refs[10 + outer : 12 + outer], refs[12 + outer : -1], refs[-1]
    vort, swirl, diff = given[4:7]
    targets = (*held, *[own.at[c] for c in range(5)], *lists)
    sources = (*given[0:4], *[vort.at[0, m] for m in range(3)], swirl.at[0], diff.at[0], *given[7:9])
    copies = [
        pltpu.make_async_copy(a, b, sems.at[i]) for i, (a, b) in enumerate(zip(sources, targets))
    ]
    for copy in copies:
        copy.start()
    for copy in copies[0:4]:
        copy.wait()
    pos, strength, radius, points = held
    tiles = pos.shape[1] // LANES
    angles = points.shape[2]
    src = lax.axis_index("src")
    core = radius[...] * radius[...]
    parts = [slice(k * LANES, (k + 1) * LANES) for k in range(tiles)]
    bare = [
        jnp.concatenate(
            [pos[:, part], strength[:, part], core[:, part], jnp.zeros((1, LANES), f32)], axis=0
        )
        for part in parts
    ]
    last = lax.broadcasted_iota(jnp.int32, (ROWS, LANES), 0) == ROWS - 1
    for step, message in zip(line_order(outer), messages):
        there = partner(src // inner, step, outer) * inner
        planes = (there + src % inner, there + inner - 1 - src % inner)
        for k in range(tiles):
            if k < 3:
                both = [points[k, pl.ds(plane, 1), :] for plane in planes]
                both.append(jnp.zeros((1, LANES - 2 * angles), f32))
                both = [p for p in both if p.shape[1]]
                message[k] = jnp.where(last, jnp.concatenate(both, axis=1), bare[k])
            else:
                message[k] = bare[k]
    for copy in copies[4:]:
        copy.wait()


def edges_kernel(own, own_source, own_target, message):
    angles = own.shape[1]
    blocks = own_source.shape[2]
    total = angles * lax.axis_size("tgt")
    half = ROWS // 2
    for c in range(5):
        message[c, :, 0:angles] = jnp.transpose(own[c])[0:ROWS, :]
        message[c, :, angles:LANES] = jnp.zeros((ROWS, LANES - angles), f32)
        message[6 + c, 0:half, :] = own[c, 0:half]
        message[6 + c, half:ROWS, :] = own[c, angles - half : angles]
    message[5] = jnp.full((ROWS, LANES), -1.0, f32)
    q = own_source[0]
    row = (q // angles) * total + lax.axis_index("tgt") * angles + q % angles
    message[5, 0:1, 0:blocks] = row.astype(f32)
    message[5, 1:2, 0:blocks] = own_target[0].astype(f32)


def inner_step(field, local_swirl, local_diff, speed, first):
    total = field[0].shape[1]
    transport = 0.5 * (local_swirl + swirl_gain * field[2])
    renewed = []
    for m in range(3):
        center = field[m]
        eastern = pltpu.roll(center, total - 1, 1)
        western = pltpu.roll(center, 1, 1)
        outward = pltpu.roll(center, ROWS - 1, 0)
        inward = jnp.where(first, speed[m], pltpu.roll(center, 1, 0))
        renewed.append(
            center
            + local_diff * (eastern + western + outward + inward - 4.0 * center)
            - transport * (eastern - western)
        )
    return renewed


def still_kernel(ways, *refs):
    messages = refs[:ways]
    own, lists, after, grid, picks, inner_cells, index, placed, source, sem = refs[ways:]
    copy = pltpu.make_async_copy(lists, source, sem)
    copy.start()
    angles = own.shape[1]
    height = angles + ROWS
    blocks = lists.shape[2]
    me = lax.axis_index("tgt")
    for step, message in zip(tgt_order(ways), messages):
        placed[source_of(me, step, ways)] = message[...]

    cells = [
        jnp.concatenate([placed[t, c, :, 0:angles] for t in range(ways)], axis=1)
        for c in range(5)
    ]
    first = lax.broadcasted_iota(jnp.int32, cells[0].shape, 0) == 0
    for m, center in enumerate(inner_step(cells[0:3], cells[3], cells[4], [0.0] * 3, first)):
        inner_cells[m] = center
    inner_cells[3] = cells[3]
    inner_cells[4] = cells[4]

    shaped = (16 * ((blocks + 15) // 16), LANES)
    name = (me * blocks + lax.broadcasted_iota(jnp.int32, shaped, 0)).astype(f32)
    lane = lax.broadcasted_iota(jnp.int32, shaped, 1).astype(f32)
    row = jnp.full(shaped, -1.0, f32)
    slot = jnp.zeros(shaped, f32)
    for step, message in enumerate(messages):
        match = message[5, 1:2, :] == name
        row = jnp.maximum(row, jnp.where(match, message[5, 0:1, :], -1.0))
        slot = jnp.maximum(slot, jnp.where(match, lane + float(step * picks.shape[0]), 0.0))
    row = jnp.max(row, axis=1, keepdims=True)
    slot = jnp.max(slot, axis=1, keepdims=True)
    block = lax.broadcasted_iota(jnp.int32, shaped, 0).astype(f32)
    kept = row < 0.0
    row = jnp.where(kept, float(3 * angles * ways) + block, row)
    slot = jnp.where(kept, float(ways * blocks) + block, slot)
    half = LANES // 2
    across = jnp.where(lane == block, row, 0.0) + jnp.where(lane == block + float(half), slot, 0.0)
    index[...] = jnp.sum(across, axis=0, keepdims=True).astype(jnp.int32)

    upper = lax.broadcasted_iota(jnp.int32, (ROWS, LANES), 0) < ROWS // 2
    east = lax.rem(me + 1, ways)
    west = lax.rem(me + ways - 1, ways)
    cells = [
        jnp.concatenate(
            [own[c], jnp.where(upper, placed[east, 6 + c], placed[west, 6 + c])], axis=0
        )
        for c in range(5)
    ]
    field, local_swirl, local_diff = cells[0:3], cells[3], cells[4]
    lane = lax.broadcasted_iota(jnp.int32, (height, LANES), 1)
    for counter in range(SUBSTEPS):
        transport = 0.5 * (local_swirl + swirl_gain * field[2])
        renewed = []
        for m in range(3):
            center = field[m]
            eastern = pltpu.roll(center, height - 1, 0)
            western = pltpu.roll(center, 1, 0)
            outward = jnp.where(lane == LANES - 1, 0.0, pltpu.roll(center, LANES - 1, 1))
            inward = jnp.where(lane == 0, 0.0, pltpu.roll(center, 1, 1))
            renewed.append(
                center
                + local_diff * (eastern + western + outward + inward - 4.0 * center)
                - transport * (eastern - western)
            )
        field = renewed
    for m in range(3):
        grid[m] = field[m][0:angles]
    picks[...] = jnp.zeros(picks.shape, f32)
    copy.wait()
    for i in range(blocks):
        q = source[0, 0, i]
        picks[i : i + 1, :] = grid[q // angles, pl.ds(q % angles, 1), :]


def three_parts(value):
    high = value.astype(bf16).astype(f32)
    rest = value - high
    middle = rest.astype(bf16).astype(f32)
    return high, middle, rest - middle


def middle_of(outer, inner):
    here = (lax.axis_index("src") // inner).astype(f32)
    return 0.5, 0.5, (here + 0.5) * (1.0 / outer)


def point_terms(message, lane, angles, middle):
    x, y, z = [message[m, 7:8, lane : lane + angles] - middle[m] for m in range(3)]
    nothing = jnp.zeros((3, angles), f32)
    vector = jnp.concatenate(
        [-2.0 * x, -2.0 * y, -2.0 * z, jnp.ones_like(x), x * x + y * y + z * z, nothing], axis=0
    )
    high, middling, low = three_parts(vector)
    terms = jnp.transpose(jnp.concatenate([high, middling, low, high, middling, high], axis=0))
    return jnp.concatenate([x, y, z, nothing, nothing[0:2]], axis=0), terms.astype(bf16)


def tile_terms(message, middle, moments, others):
    one = jnp.ones((1, LANES), f32)
    nothing = jnp.zeros((3, LANES), f32)
    for k in range(message.shape[0]):
        px, py, pz = [message[k, r : r + 1, :] - middle[r] for r in range(3)]
        sx, sy, sz, cc = [message[k, r : r + 1, :] for r in range(3, 7)]
        moments[k] = jnp.concatenate(
            [sx, sy, sz, sy * pz - sz * py, sz * px - sx * pz, sx * py - sy * px, nothing[0:2]],
            axis=0,
        )
        vector = jnp.concatenate(
            [px, py, pz, px * px + py * py + (pz * pz + cc), one, nothing], axis=0
        )
        high, middling, low = three_parts(vector)
        others[:, k * LANES : (k + 1) * LANES] = jnp.concatenate(
            [high, high, high, middling, middling, low], axis=0
        ).astype(bf16)


def quarter(terms, blocks):
    tall = terms.shape[0]
    diagonal = lax.broadcasted_iota(jnp.int32, (ROWS, LANES), 1) - lax.broadcasted_iota(
        jnp.int32, (ROWS, LANES), 0
    )
    distances = [
        jnp.dot(terms, others[...], preferred_element_type=f32) for moments, others in blocks
    ]
    rows = [jnp.zeros((ROWS, LANES), f32)] * 6
    for start in range(0, tall // ROWS, TOGETHER):
        held = [jnp.zeros((ROWS, LANES), f32)] * (6 * TOGETHER)
        for distance, (moments, others) in zip(distances, blocks):
            for k in range(moments.shape[0]):
                summed = [moments[k, r : r + 1, :] for r in range(6)]
                for i in range(TOGETHER):
                    low = (start + i) * ROWS
                    inverse = lax.rsqrt(distance[low : low + ROWS, k * LANES : (k + 1) * LANES])
                    weight = inverse * inverse * inverse
                    for r in range(6):
                        held[6 * i + r] += weight * summed[r]
        for i in range(TOGETHER):
            mask = diagonal == (start + i) * ROWS
            for r in range(6):
                value = jnp.sum(held[6 * i + r], axis=1, keepdims=True)
                rows[r] = rows[r] + jnp.where(mask, value, 0.0)
    return rows


def repeat(count, body, carried):
    if count <= UNROLLED:
        for i in range(count):
            carried = body(i, carried)
        return carried
    return lax.fori_loop(0, count, body, carried)


def quarter_speed(scale, along, terms, blocks):
    if isinstance(blocks, list):
        rows = quarter(terms, blocks)
    else:
        moments, others = blocks
        count = others.shape[0]
        if count <= UNROLLED:
            rows = quarter(terms, [(moments.at[i], others.at[i]) for i in range(count)])
        else:

            def add(i, rows):
                more = quarter(terms, [(moments.at[i], others.at[i])])
                return tuple(a + b for a, b in zip(rows, more))

            rows = lax.fori_loop(0, count, add, (jnp.zeros((ROWS, LANES), f32),) * 6)
    angles = terms.shape[0]
    ax, ay, az, bx, by, bz = [jnp.sum(r, axis=0, keepdims=True) for r in rows]
    tx, ty, tz = [
        jnp.concatenate([along[m : m + 1, :], jnp.zeros((1, LANES - angles), f32)], axis=1)
        for m in range(3)
    ]
    return jnp.concatenate(
        [
            scale * (ay * tz - az * ty - bx),
            scale * (az * tx - ax * tz - by),
            scale * (ax * ty - ay * tx - bz),
            jnp.zeros((ROWS - 3, LANES), f32),
        ],
        axis=0,
    )


def place_quarters(outer, ways, angles, speeds, placed, result):
    per = LANES // angles
    me = lax.axis_index("tgt")
    for i, step in enumerate(line_order(outer)):
        if step < ways:
            placed[source_of(me, turn(step, ways), ways)] = speeds[i]
    result[...] = jnp.zeros(result.shape, f32)
    for k in range(ways // per):
        block = placed[k * per]
        for i in range(1, per):
            block = block + pltpu.roll(placed[k * per + i], i * angles, 1)
        result[3 * k : 3 * k + 3, :] = block[0:3]


def early_kernel(scale, ways, outer, inner, *refs):
    messages, (after, speeds, moments, others, along, terms) = refs[: outer - 1], refs[outer - 1 :]
    middle = middle_of(outer, inner)
    angles = along.shape[2]
    for i, message in enumerate(messages):
        tile_terms(message, middle, moments.at[i], others.at[i])
        along[i], terms[i] = point_terms(message, angles, angles, middle)

    def one(i, unused):
        speeds[i] = quarter_speed(scale, along.at[i], terms[i], (moments, others))
        return unused

    repeat(outer - 1, one, 0)


def late_kernel(scale, ways, outer, inner, *refs):
    message, before, moments, others, along, terms = refs[:6]
    result, last_moments, last_others, speeds, placed = refs[6:]
    middle = middle_of(outer, inner)
    angles = along.shape[2]
    tile_terms(message, middle, last_moments, last_others)
    last_along, last_terms = point_terms(message, angles, angles, middle)

    def one(i, unused):
        speeds[i] = before[i] + quarter_speed(
            scale, along.at[i], terms[i], [(last_moments, last_others)]
        )
        return unused

    repeat(outer - 1, one, 0)
    speeds[outer - 1] = quarter_speed(
        scale, last_along, last_terms, (moments, others)
    ) + quarter_speed(scale, last_along, last_terms, [(last_moments, last_others)])
    place_quarters(outer, ways, angles, speeds, placed, result)


def own_kernel(scale, ways, outer, inner, *refs):
    messages, (moments, others, last_moments, last_others) = refs[:outer], refs[outer : outer + 4]
    after, result, along, terms, speeds, placed = refs[outer + 4 :]
    middle = middle_of(outer, inner)
    angles = along.shape[2]
    for i, message in enumerate(messages):
        along[i], terms[i] = point_terms(message, 0, angles, middle)

    def one(i, unused):
        if outer <= UNROLLED:
            blocks = [(moments.at[j], others.at[j]) for j in range(outer - 1)]
            speeds[i] = quarter_speed(
                scale, along.at[i], terms[i], blocks + [(last_moments, last_others)]
            )
        else:
            speeds[i] = quarter_speed(
                scale, along.at[i], terms[i], (moments, others)
            ) + quarter_speed(scale, along.at[i], terms[i], [(last_moments, last_others)])
        return unused

    repeat(outer, one, 0)
    place_quarters(outer, ways, angles, speeds, placed, result)


def merge_kernel(rows, own, arrived, picks, result):
    result[...] = jnp.zeros(result.shape, f32)
    result[0:rows, :] = own[0:rows, :] + arrived[0:rows, :]
    result[rows : rows + picks.shape[0], :] = picks[...]


def wall_kernel(ways, *refs):
    partials = refs[:ways]
    (still, inner_cells, strength, index, wall, grid, new_strength,
     fixed, picked, halves, rows, sem) = refs[ways:]
    angles = grid.shape[2]
    total = angles * ways
    parts = total // LANES
    per = LANES // angles
    rows_of = 3 * parts
    pieces = strength.shape[1] // LANES
    slots = 3 * pieces
    me = lax.axis_index("tgt")
    copy = pltpu.make_async_copy(index, rows, sem)
    copy.start()
    places = [
        (b, b // pieces, slice((b % pieces) * LANES, (b % pieces + 1) * LANES))
        for b in range(3 * pieces)
    ]
    for step, partial in enumerate(partials):
        picked[step * slots : (step + 1) * slots, :] = partial[rows_of : rows_of + slots, :]
    for b, c, part in places:
        picked[ways * slots + b : ways * slots + b + 1, :] = strength[c : c + 1, part]
        fixed[3 * total + b : 3 * total + b + 1, :] = strength[c : c + 1, part]
    added = partials[0][0:rows_of, :]
    for partial in partials[1:]:
        added = added + partial[0:rows_of, :]
    speed = [
        jnp.concatenate([added[3 * k + m : 3 * k + m + 1] for k in range(parts)], axis=1)
        for m in range(3)
    ]
    for i in range(per):
        moved = added if i == 0 else pltpu.roll(added, LANES - i * angles, 1)
        for k in range(parts):
            halves[k * per + i, 0:3, :] = moved[3 * k : 3 * k + 3]
    for m in range(3):
        wall[m] = halves[me, m : m + 1, 0:angles]

    first = lax.broadcasted_iota(jnp.int32, (ROWS, total), 0) == 0
    local_swirl = inner_cells[3]
    local_diff = inner_cells[4]
    gain = jnp.where(first, local_diff, 0.0)
    field = [inner_cells[m] + gain * speed[m] for m in range(3)]
    for counter in range(1, SUBSTEPS):
        field = inner_step(field, local_swirl, local_diff, speed, first)
    stacked = jnp.concatenate(field + [jnp.zeros((LANES - 3 * ROWS, total), f32)], axis=0)
    for k in range(parts):
        turned = jnp.transpose(stacked[:, k * LANES : (k + 1) * LANES])
        for m in range(3):
            place = m * total + k * LANES
            fixed[place : place + LANES, :] = turned if m == 0 else pltpu.roll(
                turned, LANES - m * ROWS, 1
            )
    near = lax.broadcasted_iota(jnp.int32, (angles, LANES), 1) < SUBSTEPS
    for m in range(3):
        place = pl.multiple_of(m * total + me * angles, ROWS)
        grid[0, m] = jnp.where(near, fixed[pl.ds(place, angles), :], still[m])
    near = lax.broadcasted_iota(jnp.int32, (1, LANES), 1) < SUBSTEPS
    copy.wait()
    for b, c, part in places:
        new_strength[c : c + 1, part] = jnp.where(
            near, fixed[pl.ds(rows[0, b], 1), :], picked[pl.ds(rows[0, LANES // 2 + b], 1), :]
        )


def send(block, pairs):
    return lax.ppermute(block, ("src", "tgt"), pairs)


def on_device(
    particle_position,
    particle_strength,
    core_radius,
    boundary_points,
    vorticity,
    swirl,
    diffusivity,
    intersection_source,
    intersection_target,
):
    sources = lax.axis_size("src")
    ways = lax.axis_size("tgt")
    planes, comps, angles, radial = vorticity.shape
    per_device = particle_position.shape[1]
    tiles = per_device // LANES
    blocks = intersection_source.shape[2]
    inner = 2 if sources % 2 == 0 else 1
    outer = sources // inner
    total = angles * ways
    scale = 1.6 / (4.0 * math.pi * math.sqrt(per_device * ways * sources))

    def pairs(move):
        found = []
        for s in range(sources):
            for t in range(ways):
                o, i, u = move(s // inner, s % inner, t)
                found.append((s * ways + t, (o * inner + i) * ways + u))
        return found

    def over_tgt(block, step):
        return send(block, pairs(lambda o, i, t: (o, i, partner(t, step, ways))))

    given = (
        particle_position, particle_strength, core_radius, boundary_points,
        vorticity, swirl, diffusivity, intersection_source, intersection_target,
    )
    *messages, own, source, target = pl.pallas_call(
        functools.partial(particles_kernel, inner, outer),
        out_shape=(shape(tiles, ROWS, LANES),) * outer + (
            shape(5, angles, LANES),
            jax.ShapeDtypeStruct(intersection_source.shape, jnp.int32),
            jax.ShapeDtypeStruct(intersection_target.shape, jnp.int32),
        ),
        in_specs=[hbm()] * 9,
        out_specs=(vmem(),) * (outer + 3),
        scratch_shapes=[pltpu.VMEM(a.shape, f32) for a in given[0:4]]
        + [pltpu.SemaphoreType.DMA((11,))],
        compiler_params=limit(4),
        name="particles",
    )(*stay(*given))
    line = [messages[0]] + [
        send(
            message,
            pairs(lambda o, i, t: (partner(o, k, outer), i, partner(t, turn(k, ways), ways))),
        )
        for k, message in zip(line_order(outer)[1:], messages[1:])
    ]

    edges = pl.pallas_call(
        edges_kernel,
        out_shape=shape(11, ROWS, LANES),
        in_specs=[vmem()] * 3,
        out_specs=vmem(),
        compiler_params=limit(4),
        cost_estimate=cost(1 << 31, 1 << 10),
        name="edges",
    )(own, source, target)
    steps = tgt_order(ways)
    around = [edges] + [over_tgt(edges, k) for k in steps[1:]]

    rows = 3 * total // LANES
    slots = blocks
    sums_shape = shape(-(-rows // ROWS) * ROWS, LANES)
    along_shape = (ROWS, angles)
    terms_shape = (angles, TERMS)
    others_shape = (TERMS, per_device)
    early = outer - 1
    before, *held = pl.pallas_call(
        functools.partial(early_kernel, scale, ways, outer, inner),
        out_shape=(
            shape(early, ROWS, LANES),
            shape(early, tiles, ROWS, LANES),
            jax.ShapeDtypeStruct((early, *others_shape), bf16),
            shape(early, *along_shape),
            jax.ShapeDtypeStruct((early, *terms_shape), bf16),
        ),
        in_specs=[vmem()] * outer,
        out_specs=(vmem(),) * 5,
        compiler_params=limit(12),
        cost_estimate=cost(1 << 10, 1 << 10),
        name="early",
    )(*line[:-1], edges)
    for_partner, last_moments, last_others = pl.pallas_call(
        functools.partial(late_kernel, scale, ways, outer, inner),
        out_shape=(
            sums_shape,
            shape(tiles, ROWS, LANES),
            jax.ShapeDtypeStruct(others_shape, bf16),
        ),
        in_specs=[vmem()] * 6,
        out_specs=(vmem(),) * 3,
        scratch_shapes=[
            pltpu.VMEM((outer, ROWS, LANES), f32),
            pltpu.VMEM((ways, ROWS, LANES), f32),
        ],
        compiler_params=limit(12),
        cost_estimate=cost(1 << 30, 1 << 10),
        name="late",
    )(line[-1], before, *held)
    arrived = send(for_partner, pairs(lambda o, i, t: (o, inner - 1 - i, t)))
    own_sum = pl.pallas_call(
        functools.partial(own_kernel, scale, ways, outer, inner),
        out_shape=sums_shape,
        in_specs=[vmem()] * (outer + 5),
        out_specs=vmem(),
        scratch_shapes=[
            pltpu.VMEM((outer, *along_shape), f32),
            pltpu.VMEM((outer, *terms_shape), bf16),
            pltpu.VMEM((outer, ROWS, LANES), f32),
            pltpu.VMEM((ways, ROWS, LANES), f32),
        ],
        compiler_params=limit(12),
        cost_estimate=cost(1 << 31, 1 << 10),
        name="own",
    )(*line, held[0], held[1], last_moments, last_others, for_partner)
    still, picks, inner_cells, index = pl.pallas_call(
        functools.partial(still_kernel, ways),
        out_shape=(
            shape(3, angles, LANES),
            shape(slots, LANES),
            shape(5, ROWS, total),
            jax.ShapeDtypeStruct((1, LANES), jnp.int32),
        ),
        in_specs=[vmem()] * (ways + 3),
        out_specs=(vmem(),) * 4,
        scratch_shapes=[
            pltpu.VMEM((ways,) + edges.shape, f32),
            pltpu.SMEM(source.shape, jnp.int32),
            pltpu.SemaphoreType.DMA,
        ],
        compiler_params=limit(8),
        name="still",
    )(*around, own, source, own_sum)
    partial_sum = pl.pallas_call(
        functools.partial(merge_kernel, rows),
        out_shape=shape(-(-(rows + blocks) // ROWS) * ROWS, LANES),
        in_specs=[vmem()] * 3,
        out_specs=vmem(),
        compiler_params=limit(4),
        name="merge",
    )(own_sum, arrived, picks)
    partials = [partial_sum] + [over_tgt(partial_sum, k) for k in steps[1:]]

    wall, grid, new_strength = pl.pallas_call(
        functools.partial(wall_kernel, ways),
        out_shape=(shape(3, planes, angles), shape(*vorticity.shape), shape(3, per_device)),
        in_specs=[vmem()] * (ways + 4),
        out_specs=(vmem(),) * 3,
        scratch_shapes=[
            pltpu.VMEM((3 * total + slots, LANES), f32),
            pltpu.VMEM((slots * ways + slots, LANES), f32),
            pltpu.VMEM((ways, ROWS, LANES), f32),
            pltpu.SMEM(index.shape, jnp.int32),
            pltpu.SemaphoreType.DMA,
        ],
        compiler_params=limit(16),
        name="wall",
    )(*partials, still, inner_cells, particle_strength, index)
    return (wall, grid, new_strength)


def solution(mesh):
    in_specs = (
        P(None, ("src", "tgt")),
        P(None, ("src", "tgt")),
        P(None, ("src", "tgt")),
        P(None, None, "tgt"),
        P("src", None, "tgt", None),
        P("src", "tgt", None),
        P("src", "tgt", None),
        P("src", "tgt", None),
        P("src", "tgt", None),
    )
    out_specs = (P(None, "src", "tgt"), P("src", None, "tgt", None), P(None, ("src", "tgt")))
    return jax.shard_map(
        on_device, mesh=mesh, in_specs=in_specs, out_specs=out_specs, check_vma=False
    )
```

```python
import functools
import math

import jax
import jax.numpy as jnp
from jax import lax
from jax.experimental import pallas as pl
from jax.experimental.pallas import tpu as pltpu
from jax.sharding import PartitionSpec as P

SUBSTEPS = 3
LANES = 128
ROWS = 8
TOGETHER = 2
TERMS = 48
UNROLLED = 4
swirl_gain = 0.2
f32 = jnp.float32
bf16 = jnp.bfloat16


def vmem():
    return pl.BlockSpec(memory_space=pltpu.VMEM)


def smem():
    return pl.BlockSpec(memory_space=pltpu.SMEM)


def hbm():
    return pl.BlockSpec(memory_space=pltpu.HBM)


def stay(*arrays):
    return [pltpu.with_memory_space_constraint(a, pltpu.HBM) for a in arrays]


def shape(*dims):
    return jax.ShapeDtypeStruct(dims, f32)


def limit(megabytes):
    return pltpu.CompilerParams(vmem_limit_bytes=megabytes << 20)


def cost(flops, size):
    return pl.CostEstimate(flops=flops, bytes_accessed=size, transcendentals=0)


def divisor(number, most):
    return max(c for c in range(1, min(number, most) + 1) if number % c == 0)


def power_of_two(number):
    return number & (number - 1) == 0


def partner(index, step, count):
    return index ^ step if power_of_two(count) else (index + step) % count


def source_of(index, step, count):
    return index ^ step if power_of_two(count) else (index - step) % count


def line_order(outer):
    return [0, *range(1, outer // 2), *reversed(range(outer // 2, outer))]


def tgt_order(ways):
    return [0, *range(ways // 2, ways), *range(1, ways // 2)]


def turn(step, ways):
    return {1: 2, 2: 3, 3: 1}.get(step % ways, step % ways)


def particles_kernel(inner, outer, *refs):
    given, messages = refs[:9], refs[9 : 9 + outer]
    own, lists, held, sems = refs[9 + outer], refs[10 + outer : 12 + outer], refs[12 + outer : -1], refs[-1]
    vort, swirl, diff = given[4:7]
    targets = (*held, *[own.at[c] for c in range(5)], *lists)
    sources = (*given[0:4], *[vort.at[0, m] for m in range(3)], swirl.at[0], diff.at[0], *given[7:9])
    copies = [
        pltpu.make_async_copy(a, b, sems.at[i]) for i, (a, b) in enumerate(zip(sources, targets))
    ]
    for copy in copies:
        copy.start()
    for copy in copies[0:4]:
        copy.wait()
    pos, strength, radius, points = held
    tiles = pos.shape[1] // LANES
    angles = points.shape[2]
    src = lax.axis_index("src")
    core = radius[...] * radius[...]
    parts = [slice(k * LANES, (k + 1) * LANES) for k in range(tiles)]
    bare = [
        jnp.concatenate(
            [pos[:, part], strength[:, part], core[:, part], jnp.zeros((1, LANES), f32)], axis=0
        )
        for part in parts
    ]
    last = lax.broadcasted_iota(jnp.int32, (ROWS, LANES), 0) == ROWS - 1
    for step, message in zip(line_order(outer), messages):
        there = partner(src // inner, step, outer) * inner
        planes = (there + src % inner, there + inner - 1 - src % inner)
        for k in range(tiles):
            if k < 3:
                both = [points[k, pl.ds(plane, 1), :] for plane in planes]
                both.append(jnp.zeros((1, LANES - 2 * angles), f32))
                both = [p for p in both if p.shape[1]]
                message[k] = jnp.where(last, jnp.concatenate(both, axis=1), bare[k])
            else:
                message[k] = bare[k]
    for copy in copies[4:]:
        copy.wait()


def edges_kernel(own, own_source, own_target, message):
    angles = own.shape[1]
    blocks = own_source.shape[2]
    total = angles * lax.axis_size("tgt")
    half = ROWS // 2
    for c in range(5):
        message[c, :, 0:angles] = jnp.transpose(own[c])[0:ROWS, :]
        message[c, :, angles:LANES] = jnp.zeros((ROWS, LANES - angles), f32)
        message[6 + c, 0:half, :] = own[c, 0:half]
        message[6 + c, half:ROWS, :] = own[c, angles - half : angles]
    message[5] = jnp.full((ROWS, LANES), -1.0, f32)
    q = own_source[0]
    row = (q // angles) * total + lax.axis_index("tgt") * angles + q % angles
    message[5, 0:1, 0:blocks] = row.astype(f32)
    message[5, 1:2, 0:blocks] = own_target[0].astype(f32)


def inner_step(field, local_swirl, local_diff, speed, first):
    total = field[0].shape[1]
    transport = 0.5 * (local_swirl + swirl_gain * field[2])
    renewed = []
    for m in range(3):
        center = field[m]
        eastern = pltpu.roll(center, total - 1, 1)
        western = pltpu.roll(center, 1, 1)
        outward = pltpu.roll(center, ROWS - 1, 0)
        inward = jnp.where(first, speed[m], pltpu.roll(center, 1, 0))
        renewed.append(
            center
            + local_diff * (eastern + western + outward + inward - 4.0 * center)
            - transport * (eastern - western)
        )
    return renewed


def still_kernel(ways, *refs):
    messages = refs[:ways]
    own, lists, after, grid, picks, placed, source, sem = refs[ways:]
    copy = pltpu.make_async_copy(lists, source, sem)
    copy.start()
    angles = own.shape[1]
    height = angles + ROWS
    blocks = lists.shape[2]
    me = lax.axis_index("tgt")
    for step, message in zip(tgt_order(ways), messages):
        placed[source_of(me, step, ways)] = message[6:11]

    upper = lax.broadcasted_iota(jnp.int32, (ROWS, LANES), 0) < ROWS // 2
    east = lax.rem(me + 1, ways)
    west = lax.rem(me + ways - 1, ways)
    cells = [
        jnp.concatenate(
            [own[c], jnp.where(upper, placed[east, c], placed[west, c])], axis=0
        )
        for c in range(5)
    ]
    field, local_swirl, local_diff = cells[0:3], cells[3], cells[4]
    lane = lax.broadcasted_iota(jnp.int32, (height, LANES), 1)
    for counter in range(SUBSTEPS):
        transport = 0.5 * (local_swirl + swirl_gain * field[2])
        renewed = []
        for m in range(3):
            center = field[m]
            eastern = pltpu.roll(center, height - 1, 0)
            western = pltpu.roll(center, 1, 0)
            outward = jnp.where(lane == LANES - 1, 0.0, pltpu.roll(center, LANES - 1, 1))
            inward = jnp.where(lane == 0, 0.0, pltpu.roll(center, 1, 1))
            renewed.append(
                center
                + local_diff * (eastern + western + outward + inward - 4.0 * center)
                - transport * (eastern - western)
            )
        field = renewed
    for m in range(3):
        grid[m] = field[m][0:angles]
    picks[...] = jnp.zeros(picks.shape, f32)
    copy.wait()
    for i in range(blocks):
        q = source[0, 0, i]
        picks[i : i + 1, :] = grid[q // angles, pl.ds(q % angles, 1), :]


def three_parts(value):
    high = value.astype(bf16).astype(f32)
    rest = value - high
    middle = rest.astype(bf16).astype(f32)
    return high, middle, rest - middle


def middle_of(outer, inner):
    here = (lax.axis_index("src") // inner).astype(f32)
    return 0.5, 0.5, (here + 0.5) * (1.0 / outer)


def point_terms(message, lane, angles, middle):
    x, y, z = [message[m, 7:8, lane : lane + angles] - middle[m] for m in range(3)]
    nothing = jnp.zeros((3, angles), f32)
    vector = jnp.concatenate(
        [-2.0 * x, -2.0 * y, -2.0 * z, jnp.ones_like(x), x * x + y * y + z * z, nothing], axis=0
    )
    high, middling, low = three_parts(vector)
    terms = jnp.transpose(jnp.concatenate([high, middling, low, high, middling, high], axis=0))
    return jnp.concatenate([x, y, z, nothing, nothing[0:2]], axis=0), terms.astype(bf16)


def tile_terms(message, middle, moments, others):
    one = jnp.ones((1, LANES), f32)
    nothing = jnp.zeros((3, LANES), f32)
    for k in range(message.shape[0]):
        px, py, pz = [message[k, r : r + 1, :] - middle[r] for r in range(3)]
        sx, sy, sz, cc = [message[k, r : r + 1, :] for r in range(3, 7)]
        moments[k] = jnp.concatenate(
            [sx, sy, sz, sy * pz - sz * py, sz * px - sx * pz, sx * py - sy * px, nothing[0:2]],
            axis=0,
        )
        vector = jnp.concatenate(
            [px, py, pz, px * px + py * py + (pz * pz + cc), one, nothing], axis=0
        )
        high, middling, low = three_parts(vector)
        others[:, k * LANES : (k + 1) * LANES] = jnp.concatenate(
            [high, high, high, middling, middling, low], axis=0
        ).astype(bf16)


def quarter(terms, blocks):
    tall = terms.shape[0]
    diagonal = lax.broadcasted_iota(jnp.int32, (ROWS, LANES), 1) - lax.broadcasted_iota(
        jnp.int32, (ROWS, LANES), 0
    )
    distances = [
        jnp.dot(terms, others[...], preferred_element_type=f32) for moments, others in blocks
    ]
    rows = [jnp.zeros((ROWS, LANES), f32)] * 6
    for start in range(0, tall // ROWS, TOGETHER):
        held = [jnp.zeros((ROWS, LANES), f32)] * (6 * TOGETHER)
        for distance, (moments, others) in zip(distances, blocks):
            for k in range(moments.shape[0]):
                summed = [moments[k, r : r + 1, :] for r in range(6)]
                for i in range(TOGETHER):
                    low = (start + i) * ROWS
                    inverse = lax.rsqrt(distance[low : low + ROWS, k * LANES : (k + 1) * LANES])
                    weight = inverse * inverse * inverse
                    for r in range(6):
                        held[6 * i + r] += weight * summed[r]
        for i in range(TOGETHER):
            mask = diagonal == (start + i) * ROWS
            for r in range(6):
                value = jnp.sum(held[6 * i + r], axis=1, keepdims=True)
                rows[r] = rows[r] + jnp.where(mask, value, 0.0)
    return rows


def repeat(count, body, carried):
    if count <= UNROLLED:
        for i in range(count):
            carried = body(i, carried)
        return carried
    return lax.fori_loop(0, count, body, carried)


def quarter_speed(scale, along, terms, blocks):
    if isinstance(blocks, list):
        rows = quarter(terms, blocks)
    else:
        moments, others = blocks
        count = others.shape[0]
        if count <= UNROLLED:
            rows = quarter(terms, [(moments.at[i], others.at[i]) for i in range(count)])
        else:

            def add(i, rows):
                more = quarter(terms, [(moments.at[i], others.at[i])])
                return tuple(a + b for a, b in zip(rows, more))

            rows = lax.fori_loop(0, count, add, (jnp.zeros((ROWS, LANES), f32),) * 6)
    angles = terms.shape[0]
    ax, ay, az, bx, by, bz = [jnp.sum(r, axis=0, keepdims=True) for r in rows]
    tx, ty, tz = [
        jnp.concatenate([along[m : m + 1, :], jnp.zeros((1, LANES - angles), f32)], axis=1)
        for m in range(3)
    ]
    return jnp.concatenate(
        [
            scale * (ay * tz - az * ty - bx),
            scale * (az * tx - ax * tz - by),
            scale * (ax * ty - ay * tx - bz),
            jnp.zeros((ROWS - 3, LANES), f32),
        ],
        axis=0,
    )


def place_quarters(outer, ways, angles, speeds, placed, result):
    per = LANES // angles
    me = lax.axis_index("tgt")
    for i, step in enumerate(line_order(outer)):
        if step < ways:
            placed[source_of(me, turn(step, ways), ways)] = speeds[i]
    result[...] = jnp.zeros(result.shape, f32)
    for k in range(ways // per):
        block = placed[k * per]
        for i in range(1, per):
            block = block + pltpu.roll(placed[k * per + i], i * angles, 1)
        result[3 * k : 3 * k + 3, :] = block[0:3]


def early_kernel(scale, ways, outer, inner, *refs):
    messages, (after, speeds, moments, others, along, terms) = refs[: outer - 1], refs[outer - 1 :]
    middle = middle_of(outer, inner)
    angles = along.shape[2]
    for i, message in enumerate(messages):
        tile_terms(message, middle, moments.at[i], others.at[i])
        along[i], terms[i] = point_terms(message, angles, angles, middle)

    def one(i, unused):
        speeds[i] = quarter_speed(scale, along.at[i], terms[i], (moments, others))
        return unused

    repeat(outer - 1, one, 0)


def late_kernel(scale, ways, outer, inner, *refs):
    message, before, moments, others, along, terms = refs[:6]
    result, last_moments, last_others, speeds, placed = refs[6:]
    middle = middle_of(outer, inner)
    angles = along.shape[2]
    tile_terms(message, middle, last_moments, last_others)
    last_along, last_terms = point_terms(message, angles, angles, middle)

    def one(i, unused):
        speeds[i] = before[i] + quarter_speed(
            scale, along.at[i], terms[i], [(last_moments, last_others)]
        )
        return unused

    repeat(outer - 1, one, 0)
    speeds[outer - 1] = quarter_speed(
        scale, last_along, last_terms, (moments, others)
    ) + quarter_speed(scale, last_along, last_terms, [(last_moments, last_others)])
    place_quarters(outer, ways, angles, speeds, placed, result)


def own_kernel(scale, ways, outer, inner, *refs):
    messages, (moments, others, last_moments, last_others) = refs[:outer], refs[outer : outer + 4]
    after, result, along, terms, speeds, placed = refs[outer + 4 :]
    middle = middle_of(outer, inner)
    angles = along.shape[2]
    for i, message in enumerate(messages):
        along[i], terms[i] = point_terms(message, 0, angles, middle)

    def one(i, unused):
        if outer <= UNROLLED:
            blocks = [(moments.at[j], others.at[j]) for j in range(outer - 1)]
            speeds[i] = quarter_speed(
                scale, along.at[i], terms[i], blocks + [(last_moments, last_others)]
            )
        else:
            speeds[i] = quarter_speed(
                scale, along.at[i], terms[i], (moments, others)
            ) + quarter_speed(scale, along.at[i], terms[i], [(last_moments, last_others)])
        return unused

    repeat(outer, one, 0)
    place_quarters(outer, ways, angles, speeds, placed, result)


def prepare_kernel(ways, angles, blocks, *refs):
    messages = refs[:ways]
    after, inner_cells, index, placed = refs[ways:]
    me = lax.axis_index("tgt")
    for step, message in zip(tgt_order(ways), messages):
        placed[source_of(me, step, ways)] = message[0:5]

    cells = [
        jnp.concatenate([placed[t, c, :, 0:angles] for t in range(ways)], axis=1)
        for c in range(5)
    ]
    first = lax.broadcasted_iota(jnp.int32, cells[0].shape, 0) == 0
    for m, center in enumerate(inner_step(cells[0:3], cells[3], cells[4], [0.0] * 3, first)):
        inner_cells[m] = center
    inner_cells[3] = cells[3]
    inner_cells[4] = cells[4]

    shaped = (16 * ((blocks + 15) // 16), LANES)
    name = (me * blocks + lax.broadcasted_iota(jnp.int32, shaped, 0)).astype(f32)
    lane = lax.broadcasted_iota(jnp.int32, shaped, 1).astype(f32)
    row = jnp.full(shaped, -1.0, f32)
    slot = jnp.zeros(shaped, f32)
    for step, message in enumerate(messages):
        match = message[5, 1:2, :] == name
        row = jnp.maximum(row, jnp.where(match, message[5, 0:1, :], -1.0))
        slot = jnp.maximum(slot, jnp.where(match, lane + float(step * blocks), 0.0))
    row = jnp.max(row, axis=1, keepdims=True)
    slot = jnp.max(slot, axis=1, keepdims=True)
    block = lax.broadcasted_iota(jnp.int32, shaped, 0).astype(f32)
    kept = row < 0.0
    row = jnp.where(kept, float(3 * angles * ways) + block, row)
    slot = jnp.where(kept, float(ways * blocks) + block, slot)
    half = LANES // 2
    across = jnp.where(lane == block, row, 0.0) + jnp.where(lane == block + float(half), slot, 0.0)
    index[...] = jnp.sum(across, axis=0, keepdims=True).astype(jnp.int32)


def merge_kernel(rows, own, arrived, picks, result):
    result[...] = jnp.zeros(result.shape, f32)
    result[0:rows, :] = own[0:rows, :] + arrived[0:rows, :]
    result[rows : rows + picks.shape[0], :] = picks[...]


def wall_kernel(ways, *refs):
    partials = refs[:ways]
    (still, inner_cells, strength, index, wall, grid, new_strength,
     fixed, picked, halves, rows, sem) = refs[ways:]
    angles = grid.shape[2]
    total = angles * ways
    parts = total // LANES
    per = LANES // angles
    rows_of = 3 * parts
    pieces = strength.shape[1] // LANES
    slots = 3 * pieces
    me = lax.axis_index("tgt")
    copy = pltpu.make_async_copy(index, rows, sem)
    copy.start()
    places = [
        (b, b // pieces, slice((b % pieces) * LANES, (b % pieces + 1) * LANES))
        for b in range(3 * pieces)
    ]
    for step, partial in enumerate(partials):
        picked[step * slots : (step + 1) * slots, :] = partial[rows_of : rows_of + slots, :]
    for b, c, part in places:
        picked[ways * slots + b : ways * slots + b + 1, :] = strength[c : c + 1, part]
        fixed[3 * total + b : 3 * total + b + 1, :] = strength[c : c + 1, part]
    added = partials[0][0:rows_of, :]
    for partial in partials[1:]:
        added = added + partial[0:rows_of, :]
    speed = [
        jnp.concatenate([added[3 * k + m : 3 * k + m + 1] for k in range(parts)], axis=1)
        for m in range(3)
    ]
    for i in range(per):
        moved = added if i == 0 else pltpu.roll(added, LANES - i * angles, 1)
        for k in range(parts):
            halves[k * per + i, 0:3, :] = moved[3 * k : 3 * k + 3]
    for m in range(3):
        wall[m] = halves[me, m : m + 1, 0:angles]

    first = lax.broadcasted_iota(jnp.int32, (ROWS, total), 0) == 0
    local_swirl = inner_cells[3]
    local_diff = inner_cells[4]
    gain = jnp.where(first, local_diff, 0.0)
    field = [inner_cells[m] + gain * speed[m] for m in range(3)]
    for counter in range(1, SUBSTEPS):
        field = inner_step(field, local_swirl, local_diff, speed, first)
    stacked = jnp.concatenate(field + [jnp.zeros((LANES - 3 * ROWS, total), f32)], axis=0)
    for k in range(parts):
        turned = jnp.transpose(stacked[:, k * LANES : (k + 1) * LANES])
        for m in range(3):
            place = m * total + k * LANES
            fixed[place : place + LANES, :] = turned if m == 0 else pltpu.roll(
                turned, LANES - m * ROWS, 1
            )
    near = lax.broadcasted_iota(jnp.int32, (angles, LANES), 1) < SUBSTEPS
    for m in range(3):
        place = pl.multiple_of(m * total + me * angles, ROWS)
        grid[0, m] = jnp.where(near, fixed[pl.ds(place, angles), :], still[m])
    near = lax.broadcasted_iota(jnp.int32, (1, LANES), 1) < SUBSTEPS
    copy.wait()
    for b, c, part in places:
        new_strength[c : c + 1, part] = jnp.where(
            near, fixed[pl.ds(rows[0, b], 1), :], picked[pl.ds(rows[0, LANES // 2 + b], 1), :]
        )


def send(block, pairs):
    return lax.ppermute(block, ("src", "tgt"), pairs)


def on_device(
    particle_position,
    particle_strength,
    core_radius,
    boundary_points,
    vorticity,
    swirl,
    diffusivity,
    intersection_source,
    intersection_target,
):
    sources = lax.axis_size("src")
    ways = lax.axis_size("tgt")
    planes, comps, angles, radial = vorticity.shape
    per_device = particle_position.shape[1]
    tiles = per_device // LANES
    blocks = intersection_source.shape[2]
    inner = 2 if sources % 2 == 0 else 1
    outer = sources // inner
    total = angles * ways
    scale = 1.6 / (4.0 * math.pi * math.sqrt(per_device * ways * sources))

    def pairs(move):
        found = []
        for s in range(sources):
            for t in range(ways):
                o, i, u = move(s // inner, s % inner, t)
                found.append((s * ways + t, (o * inner + i) * ways + u))
        return found

    def over_tgt(block, step):
        return send(block, pairs(lambda o, i, t: (o, i, partner(t, step, ways))))

    given = (
        particle_position, particle_strength, core_radius, boundary_points,
        vorticity, swirl, diffusivity, intersection_source, intersection_target,
    )
    *messages, own, source, target = pl.pallas_call(
        functools.partial(particles_kernel, inner, outer),
        out_shape=(shape(tiles, ROWS, LANES),) * outer + (
            shape(5, angles, LANES),
            jax.ShapeDtypeStruct(intersection_source.shape, jnp.int32),
            jax.ShapeDtypeStruct(intersection_target.shape, jnp.int32),
        ),
        in_specs=[hbm()] * 9,
        out_specs=(vmem(),) * (outer + 3),
        scratch_shapes=[pltpu.VMEM(a.shape, f32) for a in given[0:4]]
        + [pltpu.SemaphoreType.DMA((11,))],
        compiler_params=limit(4),
        name="particles",
    )(*stay(*given))
    line = [messages[0]] + [
        send(
            message,
            pairs(lambda o, i, t: (partner(o, k, outer), i, partner(t, turn(k, ways), ways))),
        )
        for k, message in zip(line_order(outer)[1:], messages[1:])
    ]

    edges = pl.pallas_call(
        edges_kernel,
        out_shape=shape(11, ROWS, LANES),
        in_specs=[vmem()] * 3,
        out_specs=vmem(),
        compiler_params=limit(4),
        cost_estimate=cost(1 << 31, 1 << 10),
        name="edges",
    )(own, source, target)
    steps = tgt_order(ways)
    around = [edges] + [over_tgt(edges, k) for k in steps[1:]]

    rows = 3 * total // LANES
    slots = blocks
    sums_shape = shape(-(-rows // ROWS) * ROWS, LANES)
    along_shape = (ROWS, angles)
    terms_shape = (angles, TERMS)
    others_shape = (TERMS, per_device)
    early = outer - 1
    before, *held = pl.pallas_call(
        functools.partial(early_kernel, scale, ways, outer, inner),
        out_shape=(
            shape(early, ROWS, LANES),
            shape(early, tiles, ROWS, LANES),
            jax.ShapeDtypeStruct((early, *others_shape), bf16),
            shape(early, *along_shape),
            jax.ShapeDtypeStruct((early, *terms_shape), bf16),
        ),
        in_specs=[vmem()] * outer,
        out_specs=(vmem(),) * 5,
        compiler_params=limit(12),
        cost_estimate=cost(1 << 10, 1 << 10),
        name="early",
    )(*line[:-1], edges)
    for_partner, last_moments, last_others = pl.pallas_call(
        functools.partial(late_kernel, scale, ways, outer, inner),
        out_shape=(
            sums_shape,
            shape(tiles, ROWS, LANES),
            jax.ShapeDtypeStruct(others_shape, bf16),
        ),
        in_specs=[vmem()] * 6,
        out_specs=(vmem(),) * 3,
        scratch_shapes=[
            pltpu.VMEM((outer, ROWS, LANES), f32),
            pltpu.VMEM((ways, ROWS, LANES), f32),
        ],
        compiler_params=limit(12),
        cost_estimate=cost(1 << 30, 1 << 10),
        name="late",
    )(line[-1], before, *held)
    arrived = send(
        for_partner, pairs(lambda o, i, t: (o, inner - 1 - i, t ^ 1 if ways % 2 == 0 else t))
    )
    own_sum = pl.pallas_call(
        functools.partial(own_kernel, scale, ways, outer, inner),
        out_shape=sums_shape,
        in_specs=[vmem()] * (outer + 5),
        out_specs=vmem(),
        scratch_shapes=[
            pltpu.VMEM((outer, *along_shape), f32),
            pltpu.VMEM((outer, *terms_shape), bf16),
            pltpu.VMEM((outer, ROWS, LANES), f32),
            pltpu.VMEM((ways, ROWS, LANES), f32),
        ],
        compiler_params=limit(12),
        cost_estimate=cost(1 << 31, 1 << 10),
        name="own",
    )(*line, held[0], held[1], last_moments, last_others, for_partner)
    still, picks = pl.pallas_call(
        functools.partial(still_kernel, ways),
        out_shape=(
            shape(3, angles, LANES),
            shape(slots, LANES),
        ),
        in_specs=[vmem()] * (ways + 3),
        out_specs=(vmem(),) * 2,
        scratch_shapes=[
            pltpu.VMEM((ways, 5, ROWS, LANES), f32),
            pltpu.SMEM(source.shape, jnp.int32),
            pltpu.SemaphoreType.DMA,
        ],
        compiler_params=limit(8),
        name="still",
    )(*around, own, source, own_sum)
    partial_sum = pl.pallas_call(
        functools.partial(merge_kernel, rows),
        out_shape=shape(-(-(rows + blocks) // ROWS) * ROWS, LANES),
        in_specs=[vmem()] * 3,
        out_specs=vmem(),
        compiler_params=limit(4),
        name="merge",
    )(own_sum, arrived, picks)
    inner_cells, index = pl.pallas_call(
        functools.partial(prepare_kernel, ways, angles, blocks),
        out_shape=(
            shape(5, ROWS, total),
            jax.ShapeDtypeStruct((1, LANES), jnp.int32),
        ),
        in_specs=[vmem()] * (ways + 1),
        out_specs=(vmem(),) * 2,
        scratch_shapes=[pltpu.VMEM((ways, 5, ROWS, LANES), f32)],
        compiler_params=limit(8),
        name="prepare",
    )(*around, partial_sum)
    partials = [partial_sum] + [over_tgt(partial_sum, k) for k in steps[1:]]

    wall, grid, new_strength = pl.pallas_call(
        functools.partial(wall_kernel, ways),
        out_shape=(shape(3, planes, angles), shape(*vorticity.shape), shape(3, per_device)),
        in_specs=[vmem()] * (ways + 4),
        out_specs=(vmem(),) * 3,
        scratch_shapes=[
            pltpu.VMEM((3 * total + slots, LANES), f32),
            pltpu.VMEM((slots * ways + slots, LANES), f32),
            pltpu.VMEM((ways, ROWS, LANES), f32),
            pltpu.SMEM(index.shape, jnp.int32),
            pltpu.SemaphoreType.DMA,
        ],
        compiler_params=limit(16),
        name="wall",
    )(*partials, still, inner_cells, particle_strength, index)
    return (wall, grid, new_strength)


def solution(mesh):
    in_specs = (
        P(None, ("src", "tgt")),
        P(None, ("src", "tgt")),
        P(None, ("src", "tgt")),
        P(None, None, "tgt"),
        P("src", None, "tgt", None),
        P("src", "tgt", None),
        P("src", "tgt", None),
        P("src", "tgt", None),
        P("src", "tgt", None),
    )
    out_specs = (P(None, "src", "tgt"), P("src", None, "tgt", None), P(None, ("src", "tgt")))
    return jax.shard_map(
        on_device, mesh=mesh, in_specs=in_specs, out_specs=out_specs, check_vma=False
    )
```

```python
import functools
import math

import jax
import jax.numpy as jnp
from jax import lax
from jax.experimental import pallas as pl
from jax.experimental.pallas import tpu as pltpu
from jax.sharding import PartitionSpec as P

SUBSTEPS = 3
LANES = 128
ROWS = 8
TOGETHER = 2
TERMS = 48
UNROLLED = 4
swirl_gain = 0.2
f32 = jnp.float32
bf16 = jnp.bfloat16


def vmem():
    return pl.BlockSpec(memory_space=pltpu.VMEM)


def smem():
    return pl.BlockSpec(memory_space=pltpu.SMEM)


def hbm():
    return pl.BlockSpec(memory_space=pltpu.HBM)


def stay(*arrays):
    return [pltpu.with_memory_space_constraint(a, pltpu.HBM) for a in arrays]


def shape(*dims):
    return jax.ShapeDtypeStruct(dims, f32)


def limit(megabytes):
    return pltpu.CompilerParams(vmem_limit_bytes=megabytes << 20)


def cost(flops, size):
    return pl.CostEstimate(flops=flops, bytes_accessed=size, transcendentals=0)


def divisor(number, most):
    return max(c for c in range(1, min(number, most) + 1) if number % c == 0)


def power_of_two(number):
    return number & (number - 1) == 0


def partner(index, step, count):
    return index ^ step if power_of_two(count) else (index + step) % count


def source_of(index, step, count):
    return index ^ step if power_of_two(count) else (index - step) % count


def line_order(outer):
    return [0, *range(outer // 2, outer), *range(1, outer // 2)]


def tgt_order(ways):
    return [0, *range(ways // 2, ways), *range(1, ways // 2)]


def turn(step, ways):
    return {1: 3, 3: 1}.get(step % ways, step % ways)


def particles_kernel(inner, outer, *refs):
    given, messages = refs[:9], refs[9 : 9 + outer]
    own, lists, held, sems = refs[9 + outer], refs[10 + outer : 12 + outer], refs[12 + outer : -1], refs[-1]
    vort, swirl, diff = given[4:7]
    targets = (*held, *[own.at[c] for c in range(5)], *lists)
    sources = (*given[0:4], *[vort.at[0, m] for m in range(3)], swirl.at[0], diff.at[0], *given[7:9])
    copies = [
        pltpu.make_async_copy(a, b, sems.at[i]) for i, (a, b) in enumerate(zip(sources, targets))
    ]
    for copy in copies:
        copy.start()
    for copy in copies[0:4]:
        copy.wait()
    pos, strength, radius, points = held
    tiles = pos.shape[1] // LANES
    angles = points.shape[2]
    src = lax.axis_index("src")
    core = radius[...] * radius[...]
    parts = [slice(k * LANES, (k + 1) * LANES) for k in range(tiles)]
    bare = [
        jnp.concatenate(
            [pos[:, part], strength[:, part], core[:, part], jnp.zeros((1, LANES), f32)], axis=0
        )
        for part in parts
    ]
    last = lax.broadcasted_iota(jnp.int32, (ROWS, LANES), 0) == ROWS - 1
    for step, message in zip(line_order(outer), messages):
        there = partner(src // inner, step, outer) * inner
        planes = (there + src % inner, there + inner - 1 - src % inner)
        for k in range(tiles):
            if k < 3:
                both = [points[k, pl.ds(plane, 1), :] for plane in planes]
                both.append(jnp.zeros((1, LANES - 2 * angles), f32))
                both = [p for p in both if p.shape[1]]
                message[k] = jnp.where(last, jnp.concatenate(both, axis=1), bare[k])
            else:
                message[k] = bare[k]
    for copy in copies[4:]:
        copy.wait()


def edges_kernel(own, own_source, own_target, message):
    angles = own.shape[1]
    blocks = own_source.shape[2]
    total = angles * lax.axis_size("tgt")
    half = ROWS // 2
    for c in range(5):
        message[c, :, 0:angles] = jnp.transpose(own[c])[0:ROWS, :]
        message[c, :, angles:LANES] = jnp.zeros((ROWS, LANES - angles), f32)
        message[6 + c, 0:half, :] = own[c, 0:half]
        message[6 + c, half:ROWS, :] = own[c, angles - half : angles]
    message[5] = jnp.full((ROWS, LANES), -1.0, f32)
    q = own_source[0]
    row = (q // angles) * total + lax.axis_index("tgt") * angles + q % angles
    message[5, 0:1, 0:blocks] = row.astype(f32)
    message[5, 1:2, 0:blocks] = own_target[0].astype(f32)


def inner_step(field, local_swirl, local_diff, speed, first):
    total = field[0].shape[1]
    transport = 0.5 * (local_swirl + swirl_gain * field[2])
    renewed = []
    for m in range(3):
        center = field[m]
        eastern = pltpu.roll(center, total - 1, 1)
        western = pltpu.roll(center, 1, 1)
        outward = pltpu.roll(center, ROWS - 1, 0)
        inward = jnp.where(first, speed[m], pltpu.roll(center, 1, 0))
        renewed.append(
            center
            + local_diff * (eastern + western + outward + inward - 4.0 * center)
            - transport * (eastern - western)
        )
    return renewed


def still_kernel(ways, *refs):
    messages = refs[:ways]
    own, lists, after, grid, picks, placed, source, sem = refs[ways:]
    copy = pltpu.make_async_copy(lists, source, sem)
    copy.start()
    angles = own.shape[1]
    height = angles + ROWS
    blocks = lists.shape[2]
    me = lax.axis_index("tgt")
    for step, message in zip(tgt_order(ways), messages):
        placed[source_of(me, step, ways)] = message[6:11]

    upper = lax.broadcasted_iota(jnp.int32, (ROWS, LANES), 0) < ROWS // 2
    east = lax.rem(me + 1, ways)
    west = lax.rem(me + ways - 1, ways)
    cells = [
        jnp.concatenate(
            [own[c], jnp.where(upper, placed[east, c], placed[west, c])], axis=0
        )
        for c in range(5)
    ]
    field, local_swirl, local_diff = cells[0:3], cells[3], cells[4]
    lane = lax.broadcasted_iota(jnp.int32, (height, LANES), 1)
    for counter in range(SUBSTEPS):
        transport = 0.5 * (local_swirl + swirl_gain * field[2])
        renewed = []
        for m in range(3):
            center = field[m]
            eastern = pltpu.roll(center, height - 1, 0)
            western = pltpu.roll(center, 1, 0)
            outward = jnp.where(lane == LANES - 1, 0.0, pltpu.roll(center, LANES - 1, 1))
            inward = jnp.where(lane == 0, 0.0, pltpu.roll(center, 1, 1))
            renewed.append(
                center
                + local_diff * (eastern + western + outward + inward - 4.0 * center)
                - transport * (eastern - western)
            )
        field = renewed
    for m in range(3):
        grid[m] = field[m][0:angles]
    picks[...] = jnp.zeros(picks.shape, f32)
    copy.wait()
    for i in range(blocks):
        q = source[0, 0, i]
        picks[i : i + 1, :] = grid[q // angles, pl.ds(q % angles, 1), :]


def three_parts(value):
    high = value.astype(bf16).astype(f32)
    rest = value - high
    middle = rest.astype(bf16).astype(f32)
    return high, middle, rest - middle


def middle_of(outer, inner):
    here = (lax.axis_index("src") // inner).astype(f32)
    return 0.5, 0.5, (here + 0.5) * (1.0 / outer)


def point_terms(message, lane, angles, middle):
    x, y, z = [message[m, 7:8, lane : lane + angles] - middle[m] for m in range(3)]
    nothing = jnp.zeros((3, angles), f32)
    vector = jnp.concatenate(
        [-2.0 * x, -2.0 * y, -2.0 * z, jnp.ones_like(x), x * x + y * y + z * z, nothing], axis=0
    )
    high, middling, low = three_parts(vector)
    terms = jnp.transpose(jnp.concatenate([high, middling, low, high, middling, high], axis=0))
    return jnp.concatenate([x, y, z, nothing, nothing[0:2]], axis=0), terms.astype(bf16)


def tile_terms(message, middle, moments, others):
    one = jnp.ones((1, LANES), f32)
    nothing = jnp.zeros((3, LANES), f32)
    for k in range(message.shape[0]):
        px, py, pz = [message[k, r : r + 1, :] - middle[r] for r in range(3)]
        sx, sy, sz, cc = [message[k, r : r + 1, :] for r in range(3, 7)]
        moments[k] = jnp.concatenate(
            [sx, sy, sz, sy * pz - sz * py, sz * px - sx * pz, sx * py - sy * px, nothing[0:2]],
            axis=0,
        )
        vector = jnp.concatenate(
            [px, py, pz, px * px + py * py + (pz * pz + cc), one, nothing], axis=0
        )
        high, middling, low = three_parts(vector)
        others[:, k * LANES : (k + 1) * LANES] = jnp.concatenate(
            [high, high, high, middling, middling, low], axis=0
        ).astype(bf16)


def quarter(terms, blocks):
    tall = terms.shape[0]
    diagonal = lax.broadcasted_iota(jnp.int32, (ROWS, LANES), 1) - lax.broadcasted_iota(
        jnp.int32, (ROWS, LANES), 0
    )
    distances = [
        jnp.dot(terms, others[...], preferred_element_type=f32) for moments, others in blocks
    ]
    rows = [jnp.zeros((ROWS, LANES), f32)] * 6
    for start in range(0, tall // ROWS, TOGETHER):
        held = [jnp.zeros((ROWS, LANES), f32)] * (6 * TOGETHER)
        for distance, (moments, others) in zip(distances, blocks):
            for k in range(moments.shape[0]):
                summed = [moments[k, r : r + 1, :] for r in range(6)]
                for i in range(TOGETHER):
                    low = (start + i) * ROWS
                    inverse = lax.rsqrt(distance[low : low + ROWS, k * LANES : (k + 1) * LANES])
                    weight = inverse * inverse * inverse
                    for r in range(6):
                        held[6 * i + r] += weight * summed[r]
        for i in range(TOGETHER):
            mask = diagonal == (start + i) * ROWS
            for r in range(6):
                value = jnp.sum(held[6 * i + r], axis=1, keepdims=True)
                rows[r] = rows[r] + jnp.where(mask, value, 0.0)
    return rows


def repeat(count, body, carried):
    if count <= UNROLLED:
        for i in range(count):
            carried = body(i, carried)
        return carried
    return lax.fori_loop(0, count, body, carried)


def quarter_speed(scale, along, terms, blocks):
    if isinstance(blocks, list):
        rows = quarter(terms, blocks)
    else:
        moments, others = blocks
        count = others.shape[0]
        if count <= UNROLLED:
            rows = quarter(terms, [(moments.at[i], others.at[i]) for i in range(count)])
        else:

            def add(i, rows):
                more = quarter(terms, [(moments.at[i], others.at[i])])
                return tuple(a + b for a, b in zip(rows, more))

            rows = lax.fori_loop(0, count, add, (jnp.zeros((ROWS, LANES), f32),) * 6)
    angles = terms.shape[0]
    ax, ay, az, bx, by, bz = [jnp.sum(r, axis=0, keepdims=True) for r in rows]
    tx, ty, tz = [
        jnp.concatenate([along[m : m + 1, :], jnp.zeros((1, LANES - angles), f32)], axis=1)
        for m in range(3)
    ]
    return jnp.concatenate(
        [
            scale * (ay * tz - az * ty - bx),
            scale * (az * tx - ax * tz - by),
            scale * (ax * ty - ay * tx - bz),
            jnp.zeros((ROWS - 3, LANES), f32),
        ],
        axis=0,
    )


def place_quarters(outer, ways, angles, speeds, placed, result):
    per = LANES // angles
    me = lax.axis_index("tgt")
    for i, step in enumerate(line_order(outer)):
        if step < ways:
            placed[source_of(me, turn(step, ways), ways)] = speeds[i]
    result[...] = jnp.zeros(result.shape, f32)
    for k in range(ways // per):
        block = placed[k * per]
        for i in range(1, per):
            block = block + pltpu.roll(placed[k * per + i], i * angles, 1)
        result[3 * k : 3 * k + 3, :] = block[0:3]


def early_kernel(scale, ways, outer, inner, *refs):
    messages, (after, speeds, moments, others, along, terms) = refs[: outer - 1], refs[outer - 1 :]
    middle = middle_of(outer, inner)
    angles = along.shape[2]
    for i, message in enumerate(messages):
        tile_terms(message, middle, moments.at[i], others.at[i])
        along[i], terms[i] = point_terms(message, angles, angles, middle)

    def one(i, unused):
        speeds[i] = quarter_speed(scale, along.at[i], terms[i], (moments, others))
        return unused

    repeat(outer - 1, one, 0)


def late_kernel(scale, ways, outer, inner, *refs):
    message, before, moments, others, along, terms = refs[:6]
    result, last_moments, last_others, speeds, placed = refs[6:]
    middle = middle_of(outer, inner)
    angles = along.shape[2]
    tile_terms(message, middle, last_moments, last_others)
    last_along, last_terms = point_terms(message, angles, angles, middle)

    def one(i, unused):
        speeds[i] = before[i] + quarter_speed(
            scale, along.at[i], terms[i], [(last_moments, last_others)]
        )
        return unused

    repeat(outer - 1, one, 0)
    speeds[outer - 1] = quarter_speed(
        scale, last_along, last_terms, (moments, others)
    ) + quarter_speed(scale, last_along, last_terms, [(last_moments, last_others)])
    place_quarters(outer, ways, angles, speeds, placed, result)


def own_kernel(scale, ways, outer, inner, *refs):
    messages, (moments, others, last_moments, last_others) = refs[:outer], refs[outer : outer + 4]
    after, result, along, terms, speeds, placed = refs[outer + 4 :]
    middle = middle_of(outer, inner)
    angles = along.shape[2]
    for i, message in enumerate(messages):
        along[i], terms[i] = point_terms(message, 0, angles, middle)

    def one(i, unused):
        if outer <= UNROLLED:
            blocks = [(moments.at[j], others.at[j]) for j in range(outer - 1)]
            speeds[i] = quarter_speed(
                scale, along.at[i], terms[i], blocks + [(last_moments, last_others)]
            )
        else:
            speeds[i] = quarter_speed(
                scale, along.at[i], terms[i], (moments, others)
            ) + quarter_speed(scale, along.at[i], terms[i], [(last_moments, last_others)])
        return unused

    repeat(outer, one, 0)
    place_quarters(outer, ways, angles, speeds, placed, result)


def prepare_kernel(ways, angles, blocks, *refs):
    messages = refs[:ways]
    after, inner_cells, index, placed = refs[ways:]
    me = lax.axis_index("tgt")
    for step, message in zip(tgt_order(ways), messages):
        placed[source_of(me, step, ways)] = message[0:5]

    cells = [
        jnp.concatenate([placed[t, c, :, 0:angles] for t in range(ways)], axis=1)
        for c in range(5)
    ]
    first = lax.broadcasted_iota(jnp.int32, cells[0].shape, 0) == 0
    for m, center in enumerate(inner_step(cells[0:3], cells[3], cells[4], [0.0] * 3, first)):
        inner_cells[m] = center
    inner_cells[3] = cells[3]
    inner_cells[4] = cells[4]

    shaped = (16 * ((blocks + 15) // 16), LANES)
    name = (me * blocks + lax.broadcasted_iota(jnp.int32, shaped, 0)).astype(f32)
    lane = lax.broadcasted_iota(jnp.int32, shaped, 1).astype(f32)
    row = jnp.full(shaped, -1.0, f32)
    slot = jnp.zeros(shaped, f32)
    for step, message in enumerate(messages):
        match = message[5, 1:2, :] == name
        row = jnp.maximum(row, jnp.where(match, message[5, 0:1, :], -1.0))
        slot = jnp.maximum(slot, jnp.where(match, lane + float(step * blocks), 0.0))
    row = jnp.max(row, axis=1, keepdims=True)
    slot = jnp.max(slot, axis=1, keepdims=True)
    block = lax.broadcasted_iota(jnp.int32, shaped, 0).astype(f32)
    kept = row < 0.0
    row = jnp.where(kept, float(3 * angles * ways) + block, row)
    slot = jnp.where(kept, float(ways * blocks) + block, slot)
    half = LANES // 2
    across = jnp.where(lane == block, row, 0.0) + jnp.where(lane == block + float(half), slot, 0.0)
    index[...] = jnp.sum(across, axis=0, keepdims=True).astype(jnp.int32)


def merge_kernel(rows, own, arrived, picks, result):
    result[...] = jnp.zeros(result.shape, f32)
    result[0:rows, :] = own[0:rows, :] + arrived[0:rows, :]
    result[rows : rows + picks.shape[0], :] = picks[...]


def wall_kernel(ways, *refs):
    partials = refs[:ways]
    still, inner_cells, strength, index, *leaving = refs[ways : ways + 7]
    fixed, picked, halves, wall, grid, new_strength, rows, sems = refs[ways + 7 :]
    leave = [
        pltpu.make_async_copy(a, b, sems.at[1 + i])
        for i, (a, b) in enumerate(zip((wall, grid, new_strength), leaving))
    ]
    angles = grid.shape[2]
    total = angles * ways
    parts = total // LANES
    per = LANES // angles
    rows_of = 3 * parts
    pieces = strength.shape[1] // LANES
    slots = 3 * pieces
    me = lax.axis_index("tgt")
    copy = pltpu.make_async_copy(index, rows, sems.at[0])
    copy.start()
    places = [
        (b, b // pieces, slice((b % pieces) * LANES, (b % pieces + 1) * LANES))
        for b in range(3 * pieces)
    ]
    for step, partial in enumerate(partials):
        picked[step * slots : (step + 1) * slots, :] = partial[rows_of : rows_of + slots, :]
    for b, c, part in places:
        picked[ways * slots + b : ways * slots + b + 1, :] = strength[c : c + 1, part]
        fixed[3 * total + b : 3 * total + b + 1, :] = strength[c : c + 1, part]
    added = partials[0][0:rows_of, :]
    for partial in partials[1:]:
        added = added + partial[0:rows_of, :]
    speed = [
        jnp.concatenate([added[3 * k + m : 3 * k + m + 1] for k in range(parts)], axis=1)
        for m in range(3)
    ]
    for i in range(per):
        moved = added if i == 0 else pltpu.roll(added, LANES - i * angles, 1)
        for k in range(parts):
            halves[k * per + i, 0:3, :] = moved[3 * k : 3 * k + 3]
    for m in range(3):
        wall[m] = halves[me, m : m + 1, 0:angles]
    leave[0].start()

    first = lax.broadcasted_iota(jnp.int32, (ROWS, total), 0) == 0
    local_swirl = inner_cells[3]
    local_diff = inner_cells[4]
    gain = jnp.where(first, local_diff, 0.0)
    field = [inner_cells[m] + gain * speed[m] for m in range(3)]
    for counter in range(1, SUBSTEPS):
        field = inner_step(field, local_swirl, local_diff, speed, first)
    stacked = jnp.concatenate(field + [jnp.zeros((LANES - 3 * ROWS, total), f32)], axis=0)
    for k in range(parts):
        turned = jnp.transpose(stacked[:, k * LANES : (k + 1) * LANES])
        for m in range(3):
            place = m * total + k * LANES
            fixed[place : place + LANES, :] = turned if m == 0 else pltpu.roll(
                turned, LANES - m * ROWS, 1
            )
    near = lax.broadcasted_iota(jnp.int32, (angles, LANES), 1) < SUBSTEPS
    for m in range(3):
        place = pl.multiple_of(m * total + me * angles, ROWS)
        grid[0, m] = jnp.where(near, fixed[pl.ds(place, angles), :], still[m])
    leave[1].start()
    near = lax.broadcasted_iota(jnp.int32, (1, LANES), 1) < SUBSTEPS
    copy.wait()
    for b, c, part in places:
        new_strength[c : c + 1, part] = jnp.where(
            near, fixed[pl.ds(rows[0, b], 1), :], picked[pl.ds(rows[0, LANES // 2 + b], 1), :]
        )
    leave[2].start()
    for copy in leave:
        copy.wait()


def send(block, pairs):
    return lax.ppermute(block, ("src", "tgt"), pairs)


def on_device(
    particle_position,
    particle_strength,
    core_radius,
    boundary_points,
    vorticity,
    swirl,
    diffusivity,
    intersection_source,
    intersection_target,
):
    sources = lax.axis_size("src")
    ways = lax.axis_size("tgt")
    planes, comps, angles, radial = vorticity.shape
    per_device = particle_position.shape[1]
    tiles = per_device // LANES
    blocks = intersection_source.shape[2]
    inner = 2 if sources % 2 == 0 else 1
    outer = sources // inner
    total = angles * ways
    scale = 1.6 / (4.0 * math.pi * math.sqrt(per_device * ways * sources))

    def pairs(move):
        found = []
        for s in range(sources):
            for t in range(ways):
                o, i, u = move(s // inner, s % inner, t)
                found.append((s * ways + t, (o * inner + i) * ways + u))
        return found

    def over_tgt(block, step):
        return send(block, pairs(lambda o, i, t: (o, i, partner(t, step, ways))))

    given = (
        particle_position, particle_strength, core_radius, boundary_points,
        vorticity, swirl, diffusivity, intersection_source, intersection_target,
    )
    *messages, own, source, target = pl.pallas_call(
        functools.partial(particles_kernel, inner, outer),
        out_shape=(shape(tiles, ROWS, LANES),) * outer + (
            shape(5, angles, LANES),
            jax.ShapeDtypeStruct(intersection_source.shape, jnp.int32),
            jax.ShapeDtypeStruct(intersection_target.shape, jnp.int32),
        ),
        in_specs=[hbm()] * 9,
        out_specs=(vmem(),) * (outer + 3),
        scratch_shapes=[pltpu.VMEM(a.shape, f32) for a in given[0:4]]
        + [pltpu.SemaphoreType.DMA((11,))],
        compiler_params=limit(4),
        name="particles",
    )(*stay(*given))
    line = [messages[0]] + [
        send(
            message,
            pairs(lambda o, i, t: (partner(o, k, outer), i, partner(t, turn(k, ways), ways))),
        )
        for k, message in zip(line_order(outer)[1:], messages[1:])
    ]

    edges = pl.pallas_call(
        edges_kernel,
        out_shape=shape(11, ROWS, LANES),
        in_specs=[vmem()] * 3,
        out_specs=vmem(),
        compiler_params=limit(4),
        cost_estimate=cost(1 << 31, 1 << 10),
        name="edges",
    )(own, source, target)
    steps = tgt_order(ways)
    around = [edges] + [over_tgt(edges, k) for k in steps[1:]]

    rows = 3 * total // LANES
    slots = blocks
    sums_shape = shape(-(-rows // ROWS) * ROWS, LANES)
    along_shape = (ROWS, angles)
    terms_shape = (angles, TERMS)
    others_shape = (TERMS, per_device)
    early = outer - 1
    before, *held = pl.pallas_call(
        functools.partial(early_kernel, scale, ways, outer, inner),
        out_shape=(
            shape(early, ROWS, LANES),
            shape(early, tiles, ROWS, LANES),
            jax.ShapeDtypeStruct((early, *others_shape), bf16),
            shape(early, *along_shape),
            jax.ShapeDtypeStruct((early, *terms_shape), bf16),
        ),
        in_specs=[vmem()] * outer,
        out_specs=(vmem(),) * 5,
        compiler_params=limit(12),
        cost_estimate=cost(1 << 10, 1 << 10),
        name="early",
    )(*line[:-1], edges)
    for_partner, last_moments, last_others = pl.pallas_call(
        functools.partial(late_kernel, scale, ways, outer, inner),
        out_shape=(
            sums_shape,
            shape(tiles, ROWS, LANES),
            jax.ShapeDtypeStruct(others_shape, bf16),
        ),
        in_specs=[vmem()] * 6,
        out_specs=(vmem(),) * 3,
        scratch_shapes=[
            pltpu.VMEM((outer, ROWS, LANES), f32),
            pltpu.VMEM((ways, ROWS, LANES), f32),
        ],
        compiler_params=limit(12),
        cost_estimate=cost(1 << 30, 1 << 10),
        name="late",
    )(line[-1], before, *held)
    arrived = send(
        for_partner, pairs(lambda o, i, t: (o, inner - 1 - i, t ^ 1 if ways % 2 == 0 else t))
    )
    own_sum = pl.pallas_call(
        functools.partial(own_kernel, scale, ways, outer, inner),
        out_shape=sums_shape,
        in_specs=[vmem()] * (outer + 5),
        out_specs=vmem(),
        scratch_shapes=[
            pltpu.VMEM((outer, *along_shape), f32),
            pltpu.VMEM((outer, *terms_shape), bf16),
            pltpu.VMEM((outer, ROWS, LANES), f32),
            pltpu.VMEM((ways, ROWS, LANES), f32),
        ],
        compiler_params=limit(12),
        cost_estimate=cost(1 << 31, 1 << 10),
        name="own",
    )(*line, held[0], held[1], last_moments, last_others, for_partner)
    still, picks = pl.pallas_call(
        functools.partial(still_kernel, ways),
        out_shape=(
            shape(3, angles, LANES),
            shape(slots, LANES),
        ),
        in_specs=[vmem()] * (ways + 3),
        out_specs=(vmem(),) * 2,
        scratch_shapes=[
            pltpu.VMEM((ways, 5, ROWS, LANES), f32),
            pltpu.SMEM(source.shape, jnp.int32),
            pltpu.SemaphoreType.DMA,
        ],
        compiler_params=limit(8),
        name="still",
    )(*around, own, source, own_sum)
    partial_sum = pl.pallas_call(
        functools.partial(merge_kernel, rows),
        out_shape=shape(-(-(rows + blocks) // ROWS) * ROWS, LANES),
        in_specs=[vmem()] * 3,
        out_specs=vmem(),
        compiler_params=limit(4),
        name="merge",
    )(own_sum, arrived, picks)
    inner_cells, index = pl.pallas_call(
        functools.partial(prepare_kernel, ways, angles, blocks),
        out_shape=(
            shape(5, ROWS, total),
            jax.ShapeDtypeStruct((1, LANES), jnp.int32),
        ),
        in_specs=[vmem()] * (ways + 1),
        out_specs=(vmem(),) * 2,
        scratch_shapes=[pltpu.VMEM((ways, 5, ROWS, LANES), f32)],
        compiler_params=limit(8),
        name="prepare",
    )(*around, partial_sum)
    partials = [partial_sum] + [over_tgt(partial_sum, k) for k in steps[1:]]

    wall, grid, new_strength = pl.pallas_call(
        functools.partial(wall_kernel, ways),
        out_shape=(shape(3, planes, angles), shape(*vorticity.shape), shape(3, per_device)),
        in_specs=[vmem()] * (ways + 4),
        out_specs=(hbm(),) * 3,
        scratch_shapes=[
            pltpu.VMEM((3 * total + slots, LANES), f32),
            pltpu.VMEM((slots * ways + slots, LANES), f32),
            pltpu.VMEM((ways, ROWS, LANES), f32),
            pltpu.VMEM((3, planes, angles), f32),
            pltpu.VMEM(vorticity.shape, f32),
            pltpu.VMEM(particle_strength.shape, f32),
            pltpu.SMEM(index.shape, jnp.int32),
            pltpu.SemaphoreType.DMA((4,)),
        ],
        compiler_params=limit(16),
        name="wall",
    )(*partials, still, inner_cells, particle_strength, index)
    return (wall, grid, new_strength)


def solution(mesh):
    in_specs = (
        P(None, ("src", "tgt")),
        P(None, ("src", "tgt")),
        P(None, ("src", "tgt")),
        P(None, None, "tgt"),
        P("src", None, "tgt", None),
        P("src", "tgt", None),
        P("src", "tgt", None),
        P("src", "tgt", None),
        P("src", "tgt", None),
    )
    out_specs = (P(None, "src", "tgt"), P("src", None, "tgt", None), P(None, ("src", "tgt")))
    return jax.shard_map(
        on_device, mesh=mesh, in_specs=in_specs, out_specs=out_specs, check_vma=False
    )
```

```python
import functools
import math

import jax
import jax.numpy as jnp
from jax import lax
from jax.experimental import pallas as pl
from jax.experimental.pallas import tpu as pltpu
from jax.sharding import PartitionSpec as P

SUBSTEPS = 3
LANES = 128
ROWS = 8
TOGETHER = 2
TERMS = 48
UNROLLED = 4
swirl_gain = 0.2
f32 = jnp.float32
bf16 = jnp.bfloat16


def vmem():
    return pl.BlockSpec(memory_space=pltpu.VMEM)


def smem():
    return pl.BlockSpec(memory_space=pltpu.SMEM)


def hbm():
    return pl.BlockSpec(memory_space=pltpu.HBM)


def stay(*arrays):
    return [pltpu.with_memory_space_constraint(a, pltpu.HBM) for a in arrays]


def shape(*dims):
    return jax.ShapeDtypeStruct(dims, f32)


def limit(megabytes):
    return pltpu.CompilerParams(vmem_limit_bytes=megabytes << 20)


def cost(flops, size):
    return pl.CostEstimate(flops=flops, bytes_accessed=size, transcendentals=0)


def divisor(number, most):
    return max(c for c in range(1, min(number, most) + 1) if number % c == 0)


def power_of_two(number):
    return number & (number - 1) == 0


def partner(index, step, count):
    return index ^ step if power_of_two(count) else (index + step) % count


def source_of(index, step, count):
    return index ^ step if power_of_two(count) else (index - step) % count


def line_order(outer):
    return [0, *range(outer // 2, outer), *range(1, outer // 2)]


def tgt_order(ways):
    return [0, *range(ways // 2, ways), *range(1, ways // 2)]


def turn(step, ways):
    return {1: 3, 3: 1}.get(step % ways, step % ways)


def particles_kernel(inner, outer, *refs):
    given, messages = refs[:9], refs[9 : 9 + outer]
    own, lists, held, sems = refs[9 + outer], refs[10 + outer : 12 + outer], refs[12 + outer : -1], refs[-1]
    vort, swirl, diff = given[4:7]
    targets = (*held, *[own.at[c] for c in range(5)], *lists)
    sources = (*given[0:4], *[vort.at[0, m] for m in range(3)], swirl.at[0], diff.at[0], *given[7:9])
    copies = [
        pltpu.make_async_copy(a, b, sems.at[i]) for i, (a, b) in enumerate(zip(sources, targets))
    ]
    for copy in copies:
        copy.start()
    for copy in copies[0:4]:
        copy.wait()
    pos, strength, radius, points = held
    tiles = pos.shape[1] // LANES
    angles = points.shape[2]
    src = lax.axis_index("src")
    core = radius[...] * radius[...]
    parts = [slice(k * LANES, (k + 1) * LANES) for k in range(tiles)]
    bare = [
        jnp.concatenate(
            [pos[:, part], strength[:, part], core[:, part], jnp.zeros((1, LANES), f32)], axis=0
        )
        for part in parts
    ]
    last = lax.broadcasted_iota(jnp.int32, (ROWS, LANES), 0) == ROWS - 1
    for step, message in zip(line_order(outer), messages):
        there = partner(src // inner, step, outer) * inner
        planes = (there + src % inner, there + inner - 1 - src % inner)
        for k in range(tiles):
            if k < 3:
                both = [points[k, pl.ds(plane, 1), :] for plane in planes]
                both.append(jnp.zeros((1, LANES - 2 * angles), f32))
                both = [p for p in both if p.shape[1]]
                message[k] = jnp.where(last, jnp.concatenate(both, axis=1), bare[k])
            else:
                message[k] = bare[k]
    for copy in copies[4:]:
        copy.wait()


def edges_kernel(own, own_source, own_target, message):
    angles = own.shape[1]
    blocks = own_source.shape[2]
    total = angles * lax.axis_size("tgt")
    half = ROWS // 2
    for c in range(5):
        message[c, :, 0:angles] = jnp.transpose(own[c])[0:ROWS, :]
        message[c, :, angles:LANES] = jnp.zeros((ROWS, LANES - angles), f32)
        message[6 + c, 0:half, :] = own[c, 0:half]
        message[6 + c, half:ROWS, :] = own[c, angles - half : angles]
    message[5] = jnp.full((ROWS, LANES), -1.0, f32)
    q = own_source[0]
    row = (q // angles) * total + lax.axis_index("tgt") * angles + q % angles
    message[5, 0:1, 0:blocks] = row.astype(f32)
    message[5, 1:2, 0:blocks] = own_target[0].astype(f32)


def inner_step(field, local_swirl, local_diff, speed, first):
    total = field[0].shape[1]
    transport = 0.5 * (local_swirl + swirl_gain * field[2])
    renewed = []
    for m in range(3):
        center = field[m]
        eastern = pltpu.roll(center, total - 1, 1)
        western = pltpu.roll(center, 1, 1)
        outward = pltpu.roll(center, ROWS - 1, 0)
        inward = jnp.where(first, speed[m], pltpu.roll(center, 1, 0))
        renewed.append(
            center
            + local_diff * (eastern + western + outward + inward - 4.0 * center)
            - transport * (eastern - western)
        )
    return renewed


def still_kernel(ways, *refs):
    messages = refs[:ways]
    own, lists, after, grid, picks, placed, source, sem = refs[ways:]
    copy = pltpu.make_async_copy(lists, source, sem)
    copy.start()
    angles = own.shape[1]
    height = angles + ROWS
    blocks = lists.shape[2]
    me = lax.axis_index("tgt")
    for step, message in zip(tgt_order(ways), messages):
        placed[source_of(me, step, ways)] = message[6:11]

    upper = lax.broadcasted_iota(jnp.int32, (ROWS, LANES), 0) < ROWS // 2
    east = lax.rem(me + 1, ways)
    west = lax.rem(me + ways - 1, ways)
    cells = [
        jnp.concatenate(
            [own[c], jnp.where(upper, placed[east, c], placed[west, c])], axis=0
        )
        for c in range(5)
    ]
    field, local_swirl, local_diff = cells[0:3], cells[3], cells[4]
    lane = lax.broadcasted_iota(jnp.int32, (height, LANES), 1)
    for counter in range(SUBSTEPS):
        transport = 0.5 * (local_swirl + swirl_gain * field[2])
        renewed = []
        for m in range(3):
            center = field[m]
            eastern = pltpu.roll(center, height - 1, 0)
            western = pltpu.roll(center, 1, 0)
            outward = jnp.where(lane == LANES - 1, 0.0, pltpu.roll(center, LANES - 1, 1))
            inward = jnp.where(lane == 0, 0.0, pltpu.roll(center, 1, 1))
            renewed.append(
                center
                + local_diff * (eastern + western + outward + inward - 4.0 * center)
                - transport * (eastern - western)
            )
        field = renewed
    for m in range(3):
        grid[m] = field[m][0:angles]
    picks[...] = jnp.zeros(picks.shape, f32)
    copy.wait()
    for i in range(blocks):
        q = source[0, 0, i]
        picks[i : i + 1, :] = grid[q // angles, pl.ds(q % angles, 1), :]


def three_parts(value):
    high = value.astype(bf16).astype(f32)
    rest = value - high
    middle = rest.astype(bf16).astype(f32)
    return high, middle, rest - middle


def middle_of(outer, inner):
    here = (lax.axis_index("src") // inner).astype(f32)
    return 0.5, 0.5, (here + 0.5) * (1.0 / outer)


def point_terms(message, lane, angles, middle):
    x, y, z = [message[m, 7:8, lane : lane + angles] - middle[m] for m in range(3)]
    nothing = jnp.zeros((3, angles), f32)
    vector = jnp.concatenate(
        [-2.0 * x, -2.0 * y, -2.0 * z, jnp.ones_like(x), x * x + y * y + z * z, nothing], axis=0
    )
    high, middling, low = three_parts(vector)
    terms = jnp.transpose(jnp.concatenate([high, middling, low, high, middling, high], axis=0))
    return jnp.concatenate([x, y, z, nothing, nothing[0:2]], axis=0), terms.astype(bf16)


def tile_terms(message, middle, moments, others):
    one = jnp.ones((1, LANES), f32)
    nothing = jnp.zeros((3, LANES), f32)
    for k in range(message.shape[0]):
        px, py, pz = [message[k, r : r + 1, :] - middle[r] for r in range(3)]
        sx, sy, sz, cc = [message[k, r : r + 1, :] for r in range(3, 7)]
        moments[k] = jnp.concatenate(
            [sx, sy, sz, sy * pz - sz * py, sz * px - sx * pz, sx * py - sy * px, nothing[0:2]],
            axis=0,
        )
        vector = jnp.concatenate(
            [px, py, pz, px * px + py * py + (pz * pz + cc), one, nothing], axis=0
        )
        high, middling, low = three_parts(vector)
        others[:, k * LANES : (k + 1) * LANES] = jnp.concatenate(
            [high, high, high, middling, middling, low], axis=0
        ).astype(bf16)


def quarter(terms, blocks):
    tall = terms.shape[0]
    diagonal = lax.broadcasted_iota(jnp.int32, (ROWS, LANES), 1) - lax.broadcasted_iota(
        jnp.int32, (ROWS, LANES), 0
    )
    distances = [
        jnp.dot(terms, others[...], preferred_element_type=f32) for moments, others in blocks
    ]
    rows = [jnp.zeros((ROWS, LANES), f32)] * 6
    for start in range(0, tall // ROWS, TOGETHER):
        held = [jnp.zeros((ROWS, LANES), f32)] * (6 * TOGETHER)
        for distance, (moments, others) in zip(distances, blocks):
            for k in range(moments.shape[0]):
                summed = [moments[k, r : r + 1, :] for r in range(6)]
                for i in range(TOGETHER):
                    low = (start + i) * ROWS
                    inverse = lax.rsqrt(distance[low : low + ROWS, k * LANES : (k + 1) * LANES])
                    weight = inverse * inverse * inverse
                    for r in range(6):
                        held[6 * i + r] += weight * summed[r]
        for i in range(TOGETHER):
            mask = diagonal == (start + i) * ROWS
            for r in range(6):
                value = jnp.sum(held[6 * i + r], axis=1, keepdims=True)
                rows[r] = rows[r] + jnp.where(mask, value, 0.0)
    return rows


def repeat(count, body, carried):
    if count <= UNROLLED:
        for i in range(count):
            carried = body(i, carried)
        return carried
    return lax.fori_loop(0, count, body, carried)


def quarter_speed(scale, along, terms, blocks):
    if isinstance(blocks, list):
        rows = quarter(terms, blocks)
    else:
        moments, others = blocks
        count = others.shape[0]
        if count <= UNROLLED:
            rows = quarter(terms, [(moments.at[i], others.at[i]) for i in range(count)])
        else:

            def add(i, rows):
                more = quarter(terms, [(moments.at[i], others.at[i])])
                return tuple(a + b for a, b in zip(rows, more))

            rows = lax.fori_loop(0, count, add, (jnp.zeros((ROWS, LANES), f32),) * 6)
    angles = terms.shape[0]
    ax, ay, az, bx, by, bz = [jnp.sum(r, axis=0, keepdims=True) for r in rows]
    tx, ty, tz = [
        jnp.concatenate([along[m : m + 1, :], jnp.zeros((1, LANES - angles), f32)], axis=1)
        for m in range(3)
    ]
    return jnp.concatenate(
        [
            scale * (ay * tz - az * ty - bx),
            scale * (az * tx - ax * tz - by),
            scale * (ax * ty - ay * tx - bz),
            jnp.zeros((ROWS - 3, LANES), f32),
        ],
        axis=0,
    )


def place_quarters(outer, ways, angles, speeds, placed, result):
    per = LANES // angles
    me = lax.axis_index("tgt")
    for i, step in enumerate(line_order(outer)):
        if step < ways:
            placed[source_of(me, turn(step, ways), ways)] = speeds[i]
    result[...] = jnp.zeros(result.shape, f32)
    for k in range(ways // per):
        block = placed[k * per]
        for i in range(1, per):
            block = block + pltpu.roll(placed[k * per + i], i * angles, 1)
        result[3 * k : 3 * k + 3, :] = block[0:3]


def early_kernel(scale, outer, inner, count, *refs):
    messages, (after, speeds, moments, others, along, terms) = refs[:count], refs[count:]
    middle = middle_of(outer, inner)
    angles = along.shape[2]
    for i, message in enumerate(messages):
        tile_terms(message, middle, moments.at[i], others.at[i])
        along[i], terms[i] = point_terms(message, angles, angles, middle)

    def one(i, unused):
        speeds[i] = quarter_speed(scale, along.at[i], terms[i], (moments, others))
        return unused

    repeat(count, one, 0)


def over_groups(scale, along, terms, groups, more):
    count = sum(others.shape[0] for moments, others, *rest in groups)
    if count <= UNROLLED:
        blocks = [
            (moments.at[i], others.at[i])
            for moments, others, *rest in groups
            for i in range(others.shape[0])
        ]
        return quarter_speed(scale, along, terms, blocks + more)
    total = quarter_speed(scale, along, terms, more)
    for moments, others, *rest in groups:
        total = total + quarter_speed(scale, along, terms, (moments, others))
    return total


def add_message(scale, middle, message, before, groups, moments, others, speeds):
    angles = groups[0][2].shape[2]
    tile_terms(message, middle, moments, others)
    along, terms = point_terms(message, angles, angles, middle)
    start = 0
    for there_moments, there_others, there_along, there_terms in groups:

        def one(i, unused, start=start, there_along=there_along, there_terms=there_terms):
            speeds[start + i] = before[start + i] + quarter_speed(
                scale, there_along.at[i], there_terms[i], [(moments, others)]
            )
            return unused

        repeat(there_others.shape[0], one, 0)
        start += there_others.shape[0]
    speeds[start] = over_groups(scale, along, terms, groups, [(moments, others)])
    return along, terms


def second_kernel(scale, outer, inner, *refs):
    message, before, *held, speeds, moments, others, along, terms = refs
    along[0], terms[0] = add_message(
        scale, middle_of(outer, inner), message, before, [held], moments.at[0], others.at[0], speeds
    )


def late_kernel(scale, ways, outer, inner, *refs):
    message, before = refs[:2]
    result, moments, others, speeds, placed = refs[10:]
    groups = [refs[2:6], refs[6:10]]
    add_message(scale, middle_of(outer, inner), message, before, groups, moments, others, speeds)
    place_quarters(outer, ways, groups[0][2].shape[2], speeds, placed, result)


def own_kernel(scale, ways, outer, inner, *refs):
    messages, held = refs[:outer], refs[outer : outer + 6]
    after, result, along, terms, speeds, placed = refs[outer + 6 :]
    groups, last = [held[0:2], held[2:4]], [tuple(held[4:6])]
    middle = middle_of(outer, inner)
    angles = along.shape[2]
    for i, message in enumerate(messages):
        along[i], terms[i] = point_terms(message, 0, angles, middle)

    def one(i, unused):
        speeds[i] = over_groups(scale, along.at[i], terms[i], groups, last)
        return unused

    repeat(outer, one, 0)
    place_quarters(outer, ways, angles, speeds, placed, result)


def prepare_kernel(ways, angles, blocks, *refs):
    messages = refs[:ways]
    after, inner_cells, index, placed = refs[ways:]
    me = lax.axis_index("tgt")
    for step, message in zip(tgt_order(ways), messages):
        placed[source_of(me, step, ways)] = message[0:5]

    cells = [
        jnp.concatenate([placed[t, c, :, 0:angles] for t in range(ways)], axis=1)
        for c in range(5)
    ]
    first = lax.broadcasted_iota(jnp.int32, cells[0].shape, 0) == 0
    for m, center in enumerate(inner_step(cells[0:3], cells[3], cells[4], [0.0] * 3, first)):
        inner_cells[m] = center
    inner_cells[3] = cells[3]
    inner_cells[4] = cells[4]

    shaped = (16 * ((blocks + 15) // 16), LANES)
    name = (me * blocks + lax.broadcasted_iota(jnp.int32, shaped, 0)).astype(f32)
    lane = lax.broadcasted_iota(jnp.int32, shaped, 1).astype(f32)
    row = jnp.full(shaped, -1.0, f32)
    slot = jnp.zeros(shaped, f32)
    for step, message in enumerate(messages):
        match = message[5, 1:2, :] == name
        row = jnp.maximum(row, jnp.where(match, message[5, 0:1, :], -1.0))
        slot = jnp.maximum(slot, jnp.where(match, lane + float(step * blocks), 0.0))
    row = jnp.max(row, axis=1, keepdims=True)
    slot = jnp.max(slot, axis=1, keepdims=True)
    block = lax.broadcasted_iota(jnp.int32, shaped, 0).astype(f32)
    kept = row < 0.0
    row = jnp.where(kept, float(3 * angles * ways) + block, row)
    slot = jnp.where(kept, float(ways * blocks) + block, slot)
    half = LANES // 2
    across = jnp.where(lane == block, row, 0.0) + jnp.where(lane == block + float(half), slot, 0.0)
    index[...] = jnp.sum(across, axis=0, keepdims=True).astype(jnp.int32)


def merge_kernel(rows, own, arrived, picks, result):
    result[...] = jnp.zeros(result.shape, f32)
    result[0:rows, :] = own[0:rows, :] + arrived[0:rows, :]
    result[rows : rows + picks.shape[0], :] = picks[...]


def wall_kernel(ways, *refs):
    partials = refs[:ways]
    (still, inner_cells, strength, index, wall, grid, new_strength,
     fixed, picked, halves, rows, sem) = refs[ways:]
    angles = grid.shape[2]
    total = angles * ways
    parts = total // LANES
    per = LANES // angles
    rows_of = 3 * parts
    pieces = strength.shape[1] // LANES
    slots = 3 * pieces
    me = lax.axis_index("tgt")
    copy = pltpu.make_async_copy(index, rows, sem)
    copy.start()
    places = [
        (b, b // pieces, slice((b % pieces) * LANES, (b % pieces + 1) * LANES))
        for b in range(3 * pieces)
    ]
    for step, partial in enumerate(partials):
        picked[step * slots : (step + 1) * slots, :] = partial[rows_of : rows_of + slots, :]
    for b, c, part in places:
        picked[ways * slots + b : ways * slots + b + 1, :] = strength[c : c + 1, part]
        fixed[3 * total + b : 3 * total + b + 1, :] = strength[c : c + 1, part]
    added = partials[0][0:rows_of, :]
    for partial in partials[1:]:
        added = added + partial[0:rows_of, :]
    speed = [
        jnp.concatenate([added[3 * k + m : 3 * k + m + 1] for k in range(parts)], axis=1)
        for m in range(3)
    ]
    for i in range(per):
        moved = added if i == 0 else pltpu.roll(added, LANES - i * angles, 1)
        for k in range(parts):
            halves[k * per + i, 0:3, :] = moved[3 * k : 3 * k + 3]
    for m in range(3):
        wall[m] = halves[me, m : m + 1, 0:angles]

    first = lax.broadcasted_iota(jnp.int32, (ROWS, total), 0) == 0
    local_swirl = inner_cells[3]
    local_diff = inner_cells[4]
    gain = jnp.where(first, local_diff, 0.0)
    field = [inner_cells[m] + gain * speed[m] for m in range(3)]
    for counter in range(1, SUBSTEPS):
        field = inner_step(field, local_swirl, local_diff, speed, first)
    stacked = jnp.concatenate(field + [jnp.zeros((LANES - 3 * ROWS, total), f32)], axis=0)
    for k in range(parts):
        turned = jnp.transpose(stacked[:, k * LANES : (k + 1) * LANES])
        for m in range(3):
            place = m * total + k * LANES
            fixed[place : place + LANES, :] = turned if m == 0 else pltpu.roll(
                turned, LANES - m * ROWS, 1
            )
    near = lax.broadcasted_iota(jnp.int32, (angles, LANES), 1) < SUBSTEPS
    for m in range(3):
        place = pl.multiple_of(m * total + me * angles, ROWS)
        grid[0, m] = jnp.where(near, fixed[pl.ds(place, angles), :], still[m])
    near = lax.broadcasted_iota(jnp.int32, (1, LANES), 1) < SUBSTEPS
    copy.wait()
    for b, c, part in places:
        new_strength[c : c + 1, part] = jnp.where(
            near, fixed[pl.ds(rows[0, b], 1), :], picked[pl.ds(rows[0, LANES // 2 + b], 1), :]
        )


def send(block, pairs):
    return lax.ppermute(block, ("src", "tgt"), pairs)


def on_device(
    particle_position,
    particle_strength,
    core_radius,
    boundary_points,
    vorticity,
    swirl,
    diffusivity,
    intersection_source,
    intersection_target,
):
    sources = lax.axis_size("src")
    ways = lax.axis_size("tgt")
    planes, comps, angles, radial = vorticity.shape
    per_device = particle_position.shape[1]
    tiles = per_device // LANES
    blocks = intersection_source.shape[2]
    inner = 2 if sources % 2 == 0 else 1
    outer = sources // inner
    total = angles * ways
    scale = 1.6 / (4.0 * math.pi * math.sqrt(per_device * ways * sources))

    def pairs(move):
        found = []
        for s in range(sources):
            for t in range(ways):
                o, i, u = move(s // inner, s % inner, t)
                found.append((s * ways + t, (o * inner + i) * ways + u))
        return found

    def over_tgt(block, step):
        return send(block, pairs(lambda o, i, t: (o, i, partner(t, step, ways))))

    given = (
        particle_position, particle_strength, core_radius, boundary_points,
        vorticity, swirl, diffusivity, intersection_source, intersection_target,
    )
    *messages, own, source, target = pl.pallas_call(
        functools.partial(particles_kernel, inner, outer),
        out_shape=(shape(tiles, ROWS, LANES),) * outer + (
            shape(5, angles, LANES),
            jax.ShapeDtypeStruct(intersection_source.shape, jnp.int32),
            jax.ShapeDtypeStruct(intersection_target.shape, jnp.int32),
        ),
        in_specs=[hbm()] * 9,
        out_specs=(vmem(),) * (outer + 3),
        scratch_shapes=[pltpu.VMEM(a.shape, f32) for a in given[0:4]]
        + [pltpu.SemaphoreType.DMA((11,))],
        compiler_params=limit(4),
        name="particles",
    )(*stay(*given))
    line = [messages[0]] + [
        send(
            message,
            pairs(lambda o, i, t: (partner(o, k, outer), i, partner(t, turn(k, ways), ways))),
        )
        for k, message in zip(line_order(outer)[1:], messages[1:])
    ]

    edges = pl.pallas_call(
        edges_kernel,
        out_shape=shape(11, ROWS, LANES),
        in_specs=[vmem()] * 3,
        out_specs=vmem(),
        compiler_params=limit(4),
        cost_estimate=cost(1 << 31, 1 << 10),
        name="edges",
    )(own, source, target)
    steps = tgt_order(ways)
    around = [edges] + [over_tgt(edges, k) for k in steps[1:]]

    rows = 3 * total // LANES
    slots = blocks
    sums_shape = shape(-(-rows // ROWS) * ROWS, LANES)
    along_shape = (ROWS, angles)
    terms_shape = (angles, TERMS)
    others_shape = (TERMS, per_device)
    early = outer - 2

    def held_shapes(count):
        return (
            shape(count, tiles, ROWS, LANES),
            jax.ShapeDtypeStruct((count, *others_shape), bf16),
            shape(count, *along_shape),
            jax.ShapeDtypeStruct((count, *terms_shape), bf16),
        )

    before, *held = pl.pallas_call(
        functools.partial(early_kernel, scale, outer, inner, early),
        out_shape=(shape(early, ROWS, LANES), *held_shapes(early)),
        in_specs=[vmem()] * (early + 1),
        out_specs=(vmem(),) * 5,
        compiler_params=limit(12),
        cost_estimate=cost(1 << 10, 1 << 10),
        name="early",
    )(*line[:early], edges)
    before, *second = pl.pallas_call(
        functools.partial(second_kernel, scale, outer, inner),
        out_shape=(shape(early + 1, ROWS, LANES), *held_shapes(1)),
        in_specs=[vmem()] * 6,
        out_specs=(vmem(),) * 5,
        compiler_params=limit(12),
        cost_estimate=cost(1 << 10, 1 << 10),
        name="second",
    )(line[early], before, *held)
    for_partner, last_moments, last_others = pl.pallas_call(
        functools.partial(late_kernel, scale, ways, outer, inner),
        out_shape=(
            sums_shape,
            shape(tiles, ROWS, LANES),
            jax.ShapeDtypeStruct(others_shape, bf16),
        ),
        in_specs=[vmem()] * 10,
        out_specs=(vmem(),) * 3,
        scratch_shapes=[
            pltpu.VMEM((outer, ROWS, LANES), f32),
            pltpu.VMEM((ways, ROWS, LANES), f32),
        ],
        compiler_params=limit(12),
        cost_estimate=cost(1 << 30, 1 << 10),
        name="late",
    )(line[-1], before, *held, *second)
    arrived = send(
        for_partner, pairs(lambda o, i, t: (o, inner - 1 - i, t ^ 1 if ways % 2 == 0 else t))
    )
    own_sum = pl.pallas_call(
        functools.partial(own_kernel, scale, ways, outer, inner),
        out_shape=sums_shape,
        in_specs=[vmem()] * (outer + 7),
        out_specs=vmem(),
        scratch_shapes=[
            pltpu.VMEM((outer, *along_shape), f32),
            pltpu.VMEM((outer, *terms_shape), bf16),
            pltpu.VMEM((outer, ROWS, LANES), f32),
            pltpu.VMEM((ways, ROWS, LANES), f32),
        ],
        compiler_params=limit(12),
        cost_estimate=cost(1 << 31, 1 << 10),
        name="own",
    )(*line, *held[0:2], *second[0:2], last_moments, last_others, for_partner)
    still, picks = pl.pallas_call(
        functools.partial(still_kernel, ways),
        out_shape=(
            shape(3, angles, LANES),
            shape(slots, LANES),
        ),
        in_specs=[vmem()] * (ways + 3),
        out_specs=(vmem(),) * 2,
        scratch_shapes=[
            pltpu.VMEM((ways, 5, ROWS, LANES), f32),
            pltpu.SMEM(source.shape, jnp.int32),
            pltpu.SemaphoreType.DMA,
        ],
        compiler_params=limit(8),
        name="still",
    )(*around, own, source, own_sum)
    partial_sum = pl.pallas_call(
        functools.partial(merge_kernel, rows),
        out_shape=shape(-(-(rows + blocks) // ROWS) * ROWS, LANES),
        in_specs=[vmem()] * 3,
        out_specs=vmem(),
        compiler_params=limit(4),
        name="merge",
    )(own_sum, arrived, picks)
    inner_cells, index = pl.pallas_call(
        functools.partial(prepare_kernel, ways, angles, blocks),
        out_shape=(
            shape(5, ROWS, total),
            jax.ShapeDtypeStruct((1, LANES), jnp.int32),
        ),
        in_specs=[vmem()] * (ways + 1),
        out_specs=(vmem(),) * 2,
        scratch_shapes=[pltpu.VMEM((ways, 5, ROWS, LANES), f32)],
        compiler_params=limit(8),
        name="prepare",
    )(*around, partial_sum)
    partials = [partial_sum] + [over_tgt(partial_sum, k) for k in steps[1:]]

    wall, grid, new_strength = pl.pallas_call(
        functools.partial(wall_kernel, ways),
        out_shape=(shape(3, planes, angles), shape(*vorticity.shape), shape(3, per_device)),
        in_specs=[vmem()] * (ways + 4),
        out_specs=(vmem(),) * 3,
        scratch_shapes=[
            pltpu.VMEM((3 * total + slots, LANES), f32),
            pltpu.VMEM((slots * ways + slots, LANES), f32),
            pltpu.VMEM((ways, ROWS, LANES), f32),
            pltpu.SMEM(index.shape, jnp.int32),
            pltpu.SemaphoreType.DMA,
        ],
        compiler_params=limit(16),
        name="wall",
    )(*partials, still, inner_cells, particle_strength, index)
    return (wall, grid, new_strength)


def solution(mesh):
    in_specs = (
        P(None, ("src", "tgt")),
        P(None, ("src", "tgt")),
        P(None, ("src", "tgt")),
        P(None, None, "tgt"),
        P("src", None, "tgt", None),
        P("src", "tgt", None),
        P("src", "tgt", None),
        P("src", "tgt", None),
        P("src", "tgt", None),
    )
    out_specs = (P(None, "src", "tgt"), P("src", None, "tgt", None), P(None, ("src", "tgt")))
    return jax.shard_map(
        on_device, mesh=mesh, in_specs=in_specs, out_specs=out_specs, check_vma=False
    )
```

```python
import functools
import math

import jax
import jax.numpy as jnp
from jax import lax
from jax.experimental import pallas as pl
from jax.experimental.pallas import tpu as pltpu
from jax.sharding import PartitionSpec as P

SUBSTEPS = 3
LANES = 128
ROWS = 8
TOGETHER = 2
TERMS = 48
UNROLLED = 4
swirl_gain = 0.2
f32 = jnp.float32
bf16 = jnp.bfloat16


def vmem():
    return pl.BlockSpec(memory_space=pltpu.VMEM)


def smem():
    return pl.BlockSpec(memory_space=pltpu.SMEM)


def hbm():
    return pl.BlockSpec(memory_space=pltpu.HBM)


def stay(*arrays):
    return [pltpu.with_memory_space_constraint(a, pltpu.HBM) for a in arrays]


def shape(*dims):
    return jax.ShapeDtypeStruct(dims, f32)


def limit(megabytes):
    return pltpu.CompilerParams(vmem_limit_bytes=megabytes << 20)


def cost(flops, size):
    return pl.CostEstimate(flops=flops, bytes_accessed=size, transcendentals=0)


def divisor(number, most):
    return max(c for c in range(1, min(number, most) + 1) if number % c == 0)


def power_of_two(number):
    return number & (number - 1) == 0


def partner(index, step, count):
    return index ^ step if power_of_two(count) else (index + step) % count


def source_of(index, step, count):
    return index ^ step if power_of_two(count) else (index - step) % count


def line_order(outer):
    return [0, *range(outer // 2, outer), *range(1, outer // 2)]


def tgt_order(ways):
    return [0, *range(ways // 2, ways), *range(1, ways // 2)]


def turn(step, ways):
    return {1: 3, 3: 1}.get(step % ways, step % ways)


def particles_kernel(inner, outer, *refs):
    given, messages = refs[:9], refs[9 : 9 + outer]
    own, lists, held, sems = refs[9 + outer], refs[10 + outer : 12 + outer], refs[12 + outer : -1], refs[-1]
    vort, swirl, diff = given[4:7]
    targets = (*held, *[own.at[c] for c in range(5)], *lists)
    sources = (*given[0:4], *[vort.at[0, m] for m in range(3)], swirl.at[0], diff.at[0], *given[7:9])
    copies = [
        pltpu.make_async_copy(a, b, sems.at[i]) for i, (a, b) in enumerate(zip(sources, targets))
    ]
    for copy in copies:
        copy.start()
    for copy in copies[0:4]:
        copy.wait()
    pos, strength, radius, points = held
    tiles = pos.shape[1] // LANES
    angles = points.shape[2]
    src = lax.axis_index("src")
    core = radius[...] * radius[...]
    parts = [slice(k * LANES, (k + 1) * LANES) for k in range(tiles)]
    bare = [
        jnp.concatenate(
            [pos[:, part], strength[:, part], core[:, part], jnp.zeros((1, LANES), f32)], axis=0
        )
        for part in parts
    ]
    last = lax.broadcasted_iota(jnp.int32, (ROWS, LANES), 0) == ROWS - 1
    for step, message in zip(line_order(outer), messages):
        there = partner(src // inner, step, outer) * inner
        planes = (there + src % inner, there + inner - 1 - src % inner)
        for k in range(tiles):
            if k < 3:
                both = [points[k, pl.ds(plane, 1), :] for plane in planes]
                both.append(jnp.zeros((1, LANES - 2 * angles), f32))
                both = [p for p in both if p.shape[1]]
                message[k] = jnp.where(last, jnp.concatenate(both, axis=1), bare[k])
            else:
                message[k] = bare[k]
    for copy in copies[4:]:
        copy.wait()


def edges_kernel(own, own_source, own_target, message):
    angles = own.shape[1]
    blocks = own_source.shape[2]
    total = angles * lax.axis_size("tgt")
    half = ROWS // 2
    for c in range(5):
        message[c, :, 0:angles] = jnp.transpose(own[c])[0:ROWS, :]
        message[c, :, angles:LANES] = jnp.zeros((ROWS, LANES - angles), f32)
        message[6 + c, 0:half, :] = own[c, 0:half]
        message[6 + c, half:ROWS, :] = own[c, angles - half : angles]
    message[5] = jnp.full((ROWS, LANES), -1.0, f32)
    q = own_source[0]
    row = (q // angles) * total + lax.axis_index("tgt") * angles + q % angles
    message[5, 0:1, 0:blocks] = row.astype(f32)
    message[5, 1:2, 0:blocks] = own_target[0].astype(f32)


def inner_step(field, local_swirl, local_diff, speed, first):
    total = field[0].shape[1]
    transport = 0.5 * (local_swirl + swirl_gain * field[2])
    renewed = []
    for m in range(3):
        center = field[m]
        eastern = pltpu.roll(center, total - 1, 1)
        western = pltpu.roll(center, 1, 1)
        outward = pltpu.roll(center, ROWS - 1, 0)
        inward = jnp.where(first, speed[m], pltpu.roll(center, 1, 0))
        renewed.append(
            center
            + local_diff * (eastern + western + outward + inward - 4.0 * center)
            - transport * (eastern - western)
        )
    return renewed


def still_kernel(ways, *refs):
    messages = refs[:ways]
    own, lists, after, grid, picks, placed, source, sem = refs[ways:]
    copy = pltpu.make_async_copy(lists, source, sem)
    copy.start()
    angles = own.shape[1]
    height = angles + ROWS
    blocks = lists.shape[2]
    me = lax.axis_index("tgt")
    for step, message in zip(tgt_order(ways), messages):
        placed[source_of(me, step, ways)] = message[6:11]

    upper = lax.broadcasted_iota(jnp.int32, (ROWS, LANES), 0) < ROWS // 2
    east = lax.rem(me + 1, ways)
    west = lax.rem(me + ways - 1, ways)
    cells = [
        jnp.concatenate(
            [own[c], jnp.where(upper, placed[east, c], placed[west, c])], axis=0
        )
        for c in range(5)
    ]
    field, local_swirl, local_diff = cells[0:3], cells[3], cells[4]
    lane = lax.broadcasted_iota(jnp.int32, (height, LANES), 1)
    for counter in range(SUBSTEPS):
        transport = 0.5 * (local_swirl + swirl_gain * field[2])
        renewed = []
        for m in range(3):
            center = field[m]
            eastern = pltpu.roll(center, height - 1, 0)
            western = pltpu.roll(center, 1, 0)
            outward = jnp.where(lane == LANES - 1, 0.0, pltpu.roll(center, LANES - 1, 1))
            inward = jnp.where(lane == 0, 0.0, pltpu.roll(center, 1, 1))
            renewed.append(
                center
                + local_diff * (eastern + western + outward + inward - 4.0 * center)
                - transport * (eastern - western)
            )
        field = renewed
    for m in range(3):
        grid[m] = field[m][0:angles]
    picks[...] = jnp.zeros(picks.shape, f32)
    copy.wait()
    for i in range(blocks):
        q = source[0, 0, i]
        picks[i : i + 1, :] = grid[q // angles, pl.ds(q % angles, 1), :]


def three_parts(value):
    high = value.astype(bf16).astype(f32)
    rest = value - high
    middle = rest.astype(bf16).astype(f32)
    return high, middle, rest - middle


def middle_of(outer, inner):
    here = (lax.axis_index("src") // inner).astype(f32)
    return 0.5, 0.5, (here + 0.5) * (1.0 / outer)


def point_terms(message, lane, angles, middle):
    x, y, z = [message[m, 7:8, lane : lane + angles] - middle[m] for m in range(3)]
    nothing = jnp.zeros((3, angles), f32)
    vector = jnp.concatenate(
        [-2.0 * x, -2.0 * y, -2.0 * z, jnp.ones_like(x), x * x + y * y + z * z, nothing], axis=0
    )
    high, middling, low = three_parts(vector)
    terms = jnp.transpose(jnp.concatenate([high, middling, low, high, middling, high], axis=0))
    return jnp.concatenate([x, y, z, nothing, nothing[0:2]], axis=0), terms.astype(bf16)


def tile_terms(message, middle, moments, others):
    one = jnp.ones((1, LANES), f32)
    nothing = jnp.zeros((3, LANES), f32)
    for k in range(message.shape[0]):
        px, py, pz = [message[k, r : r + 1, :] - middle[r] for r in range(3)]
        sx, sy, sz, cc = [message[k, r : r + 1, :] for r in range(3, 7)]
        moments[k] = jnp.concatenate(
            [sx, sy, sz, sy * pz - sz * py, sz * px - sx * pz, sx * py - sy * px, nothing[0:2]],
            axis=0,
        )
        vector = jnp.concatenate(
            [px, py, pz, px * px + py * py + (pz * pz + cc), one, nothing], axis=0
        )
        high, middling, low = three_parts(vector)
        others[:, k * LANES : (k + 1) * LANES] = jnp.concatenate(
            [high, high, high, middling, middling, low], axis=0
        ).astype(bf16)


def quarter(terms, blocks):
    tall = terms.shape[0]
    diagonal = lax.broadcasted_iota(jnp.int32, (ROWS, LANES), 1) - lax.broadcasted_iota(
        jnp.int32, (ROWS, LANES), 0
    )
    distances = [
        jnp.dot(terms, others[...], preferred_element_type=f32) for moments, others in blocks
    ]
    rows = [jnp.zeros((ROWS, LANES), f32)] * 6
    for start in range(0, tall // ROWS, TOGETHER):
        held = [jnp.zeros((ROWS, LANES), f32)] * (6 * TOGETHER)
        for distance, (moments, others) in zip(distances, blocks):
            for k in range(moments.shape[0]):
                summed = [moments[k, r : r + 1, :] for r in range(6)]
                for i in range(TOGETHER):
                    low = (start + i) * ROWS
                    inverse = lax.rsqrt(distance[low : low + ROWS, k * LANES : (k + 1) * LANES])
                    weight = inverse * inverse * inverse
                    for r in range(6):
                        held[6 * i + r] += weight * summed[r]
        for i in range(TOGETHER):
            mask = diagonal == (start + i) * ROWS
            for r in range(6):
                value = jnp.sum(held[6 * i + r], axis=1, keepdims=True)
                rows[r] = rows[r] + jnp.where(mask, value, 0.0)
    return rows


def repeat(count, body, carried):
    if count <= UNROLLED:
        for i in range(count):
            carried = body(i, carried)
        return carried
    return lax.fori_loop(0, count, body, carried)


def quarter_speed(scale, along, terms, blocks):
    if isinstance(blocks, list):
        rows = quarter(terms, blocks)
    else:
        moments, others = blocks
        count = others.shape[0]
        if count <= UNROLLED:
            rows = quarter(terms, [(moments.at[i], others.at[i]) for i in range(count)])
        else:

            def add(i, rows):
                more = quarter(terms, [(moments.at[i], others.at[i])])
                return tuple(a + b for a, b in zip(rows, more))

            rows = lax.fori_loop(0, count, add, (jnp.zeros((ROWS, LANES), f32),) * 6)
    angles = terms.shape[0]
    ax, ay, az, bx, by, bz = [jnp.sum(r, axis=0, keepdims=True) for r in rows]
    tx, ty, tz = [
        jnp.concatenate([along[m : m + 1, :], jnp.zeros((1, LANES - angles), f32)], axis=1)
        for m in range(3)
    ]
    return jnp.concatenate(
        [
            scale * (ay * tz - az * ty - bx),
            scale * (az * tx - ax * tz - by),
            scale * (ax * ty - ay * tx - bz),
            jnp.zeros((ROWS - 3, LANES), f32),
        ],
        axis=0,
    )


def place_quarters(outer, ways, angles, speeds, placed, result):
    per = LANES // angles
    me = lax.axis_index("tgt")
    for i, step in enumerate(line_order(outer)):
        if step < ways:
            placed[source_of(me, turn(step, ways), ways)] = speeds[i]
    result[...] = jnp.zeros(result.shape, f32)
    for k in range(ways // per):
        block = placed[k * per]
        for i in range(1, per):
            block = block + pltpu.roll(placed[k * per + i], i * angles, 1)
        result[3 * k : 3 * k + 3, :] = block[0:3]


def early_kernel(scale, outer, inner, count, *refs):
    messages, (after, speeds, moments, others, along, terms) = refs[:count], refs[count : count + 6]
    own_speeds, own_along, own_terms = refs[count + 6 :]
    middle = middle_of(outer, inner)
    angles = along.shape[2]
    for i, message in enumerate(messages):
        tile_terms(message, middle, moments.at[i], others.at[i])
        along[i], terms[i] = point_terms(message, angles, angles, middle)
        own_along[i], own_terms[i] = point_terms(message, 0, angles, middle)

    def one(i, unused):
        speeds[i] = quarter_speed(scale, along.at[i], terms[i], (moments, others))
        own_speeds[i] = quarter_speed(scale, own_along.at[i], own_terms[i], (moments, others))
        return unused

    repeat(count, one, 0)


def over_groups(scale, along, terms, groups, more):
    count = sum(others.shape[0] for moments, others, *rest in groups)
    if count <= UNROLLED:
        blocks = [
            (moments.at[i], others.at[i])
            for moments, others, *rest in groups
            for i in range(others.shape[0])
        ]
        return quarter_speed(scale, along, terms, blocks + more)
    total = quarter_speed(scale, along, terms, more)
    for moments, others, *rest in groups:
        total = total + quarter_speed(scale, along, terms, (moments, others))
    return total


def add_message(scale, middle, message, before, groups, moments, others, speeds):
    angles = groups[0][2].shape[2]
    tile_terms(message, middle, moments, others)
    along, terms = point_terms(message, angles, angles, middle)
    start = 0
    for there_moments, there_others, there_along, there_terms in groups:

        def one(i, unused, start=start, there_along=there_along, there_terms=there_terms):
            speeds[start + i] = before[start + i] + quarter_speed(
                scale, there_along.at[i], there_terms[i], [(moments, others)]
            )
            return unused

        repeat(there_others.shape[0], one, 0)
        start += there_others.shape[0]
    speeds[start] = over_groups(scale, along, terms, groups, [(moments, others)])
    return along, terms


def second_kernel(scale, outer, inner, *refs):
    message, before, *held, speeds, moments, others, along, terms = refs
    along[0], terms[0] = add_message(
        scale, middle_of(outer, inner), message, before, [held], moments.at[0], others.at[0], speeds
    )


def late_kernel(scale, ways, outer, inner, *refs):
    message, before = refs[:2]
    result, moments, others, speeds, placed = refs[10:]
    groups = [refs[2:6], refs[6:10]]
    add_message(scale, middle_of(outer, inner), message, before, groups, moments, others, speeds)
    place_quarters(outer, ways, groups[0][2].shape[2], speeds, placed, result)


def own_kernel(scale, ways, outer, inner, *refs):
    (*line, before, along, terms, moments, others, second_moments, second_others,
     last_moments, last_others, after, result, late_along, late_terms, speeds, placed) = refs
    second, last = (second_moments, second_others), [(last_moments, last_others)]
    middle = middle_of(outer, inner)
    angles = along.shape[2]
    early = before.shape[0]
    messages = line[early:]
    for i, message in enumerate(messages):
        late_along[i], late_terms[i] = point_terms(message, 0, angles, middle)

    def one(i, unused):
        speeds[i] = before[i] + over_groups(scale, along.at[i], terms[i], [second], last)
        return unused

    repeat(early, one, 0)
    for i in range(len(messages)):
        speeds[early + i] = over_groups(
            scale, late_along.at[i], late_terms[i], [(moments, others), second], last
        )
    place_quarters(outer, ways, angles, speeds, placed, result)


def prepare_kernel(ways, angles, blocks, *refs):
    messages = refs[:ways]
    after, inner_cells, index, placed = refs[ways:]
    me = lax.axis_index("tgt")
    for step, message in zip(tgt_order(ways), messages):
        placed[source_of(me, step, ways)] = message[0:5]

    cells = [
        jnp.concatenate([placed[t, c, :, 0:angles] for t in range(ways)], axis=1)
        for c in range(5)
    ]
    first = lax.broadcasted_iota(jnp.int32, cells[0].shape, 0) == 0
    for m, center in enumerate(inner_step(cells[0:3], cells[3], cells[4], [0.0] * 3, first)):
        inner_cells[m] = center
    inner_cells[3] = cells[3]
    inner_cells[4] = cells[4]

    shaped = (16 * ((blocks + 15) // 16), LANES)
    name = (me * blocks + lax.broadcasted_iota(jnp.int32, shaped, 0)).astype(f32)
    lane = lax.broadcasted_iota(jnp.int32, shaped, 1).astype(f32)
    row = jnp.full(shaped, -1.0, f32)
    slot = jnp.zeros(shaped, f32)
    for step, message in enumerate(messages):
        match = message[5, 1:2, :] == name
        row = jnp.maximum(row, jnp.where(match, message[5, 0:1, :], -1.0))
        slot = jnp.maximum(slot, jnp.where(match, lane + float(step * blocks), 0.0))
    row = jnp.max(row, axis=1, keepdims=True)
    slot = jnp.max(slot, axis=1, keepdims=True)
    block = lax.broadcasted_iota(jnp.int32, shaped, 0).astype(f32)
    kept = row < 0.0
    row = jnp.where(kept, float(3 * angles * ways) + block, row)
    slot = jnp.where(kept, float(ways * blocks) + block, slot)
    half = LANES // 2
    across = jnp.where(lane == block, row, 0.0) + jnp.where(lane == block + float(half), slot, 0.0)
    index[...] = jnp.sum(across, axis=0, keepdims=True).astype(jnp.int32)


def merge_kernel(rows, own, arrived, picks, result):
    result[...] = jnp.zeros(result.shape, f32)
    result[0:rows, :] = own[0:rows, :] + arrived[0:rows, :]
    result[rows : rows + picks.shape[0], :] = picks[...]


def wall_kernel(ways, *refs):
    partials = refs[:ways]
    (still, inner_cells, strength, index, wall, grid, new_strength,
     fixed, picked, halves, rows, sem) = refs[ways:]
    angles = grid.shape[2]
    total = angles * ways
    parts = total // LANES
    per = LANES // angles
    rows_of = 3 * parts
    pieces = strength.shape[1] // LANES
    slots = 3 * pieces
    me = lax.axis_index("tgt")
    copy = pltpu.make_async_copy(index, rows, sem)
    copy.start()
    places = [
        (b, b // pieces, slice((b % pieces) * LANES, (b % pieces + 1) * LANES))
        for b in range(3 * pieces)
    ]
    for step, partial in enumerate(partials):
        picked[step * slots : (step + 1) * slots, :] = partial[rows_of : rows_of + slots, :]
    for b, c, part in places:
        picked[ways * slots + b : ways * slots + b + 1, :] = strength[c : c + 1, part]
        fixed[3 * total + b : 3 * total + b + 1, :] = strength[c : c + 1, part]
    added = partials[0][0:rows_of, :]
    for partial in partials[1:]:
        added = added + partial[0:rows_of, :]
    speed = [
        jnp.concatenate([added[3 * k + m : 3 * k + m + 1] for k in range(parts)], axis=1)
        for m in range(3)
    ]
    for i in range(per):
        moved = added if i == 0 else pltpu.roll(added, LANES - i * angles, 1)
        for k in range(parts):
            halves[k * per + i, 0:3, :] = moved[3 * k : 3 * k + 3]
    for m in range(3):
        wall[m] = halves[me, m : m + 1, 0:angles]

    first = lax.broadcasted_iota(jnp.int32, (ROWS, total), 0) == 0
    local_swirl = inner_cells[3]
    local_diff = inner_cells[4]
    gain = jnp.where(first, local_diff, 0.0)
    field = [inner_cells[m] + gain * speed[m] for m in range(3)]
    for counter in range(1, SUBSTEPS):
        field = inner_step(field, local_swirl, local_diff, speed, first)
    stacked = jnp.concatenate(field + [jnp.zeros((LANES - 3 * ROWS, total), f32)], axis=0)
    for k in range(parts):
        turned = jnp.transpose(stacked[:, k * LANES : (k + 1) * LANES])
        for m in range(3):
            place = m * total + k * LANES
            fixed[place : place + LANES, :] = turned if m == 0 else pltpu.roll(
                turned, LANES - m * ROWS, 1
            )
    near = lax.broadcasted_iota(jnp.int32, (angles, LANES), 1) < SUBSTEPS
    for m in range(3):
        place = pl.multiple_of(m * total + me * angles, ROWS)
        grid[0, m] = jnp.where(near, fixed[pl.ds(place, angles), :], still[m])
    near = lax.broadcasted_iota(jnp.int32, (1, LANES), 1) < SUBSTEPS
    copy.wait()
    for b, c, part in places:
        new_strength[c : c + 1, part] = jnp.where(
            near, fixed[pl.ds(rows[0, b], 1), :], picked[pl.ds(rows[0, LANES // 2 + b], 1), :]
        )


def send(block, pairs):
    return lax.ppermute(block, ("src", "tgt"), pairs)


def on_device(
    particle_position,
    particle_strength,
    core_radius,
    boundary_points,
    vorticity,
    swirl,
    diffusivity,
    intersection_source,
    intersection_target,
):
    sources = lax.axis_size("src")
    ways = lax.axis_size("tgt")
    planes, comps, angles, radial = vorticity.shape
    per_device = particle_position.shape[1]
    tiles = per_device // LANES
    blocks = intersection_source.shape[2]
    inner = 2 if sources % 2 == 0 else 1
    outer = sources // inner
    total = angles * ways
    scale = 1.6 / (4.0 * math.pi * math.sqrt(per_device * ways * sources))

    def pairs(move):
        found = []
        for s in range(sources):
            for t in range(ways):
                o, i, u = move(s // inner, s % inner, t)
                found.append((s * ways + t, (o * inner + i) * ways + u))
        return found

    def over_tgt(block, step):
        return send(block, pairs(lambda o, i, t: (o, i, partner(t, step, ways))))

    given = (
        particle_position, particle_strength, core_radius, boundary_points,
        vorticity, swirl, diffusivity, intersection_source, intersection_target,
    )
    *messages, own, source, target = pl.pallas_call(
        functools.partial(particles_kernel, inner, outer),
        out_shape=(shape(tiles, ROWS, LANES),) * outer + (
            shape(5, angles, LANES),
            jax.ShapeDtypeStruct(intersection_source.shape, jnp.int32),
            jax.ShapeDtypeStruct(intersection_target.shape, jnp.int32),
        ),
        in_specs=[hbm()] * 9,
        out_specs=(vmem(),) * (outer + 3),
        scratch_shapes=[pltpu.VMEM(a.shape, f32) for a in given[0:4]]
        + [pltpu.SemaphoreType.DMA((11,))],
        compiler_params=limit(4),
        name="particles",
    )(*stay(*given))
    line = [messages[0]] + [
        send(
            message,
            pairs(lambda o, i, t: (partner(o, k, outer), i, partner(t, turn(k, ways), ways))),
        )
        for k, message in zip(line_order(outer)[1:], messages[1:])
    ]

    edges = pl.pallas_call(
        edges_kernel,
        out_shape=shape(11, ROWS, LANES),
        in_specs=[vmem()] * 3,
        out_specs=vmem(),
        compiler_params=limit(4),
        cost_estimate=cost(1 << 31, 1 << 10),
        name="edges",
    )(own, source, target)
    steps = tgt_order(ways)
    around = [edges] + [over_tgt(edges, k) for k in steps[1:]]

    rows = 3 * total // LANES
    slots = blocks
    sums_shape = shape(-(-rows // ROWS) * ROWS, LANES)
    along_shape = (ROWS, angles)
    terms_shape = (angles, TERMS)
    others_shape = (TERMS, per_device)
    early = outer - 2

    def held_shapes(count):
        return (
            shape(count, tiles, ROWS, LANES),
            jax.ShapeDtypeStruct((count, *others_shape), bf16),
            shape(count, *along_shape),
            jax.ShapeDtypeStruct((count, *terms_shape), bf16),
        )

    before, *held = pl.pallas_call(
        functools.partial(early_kernel, scale, outer, inner, early),
        out_shape=(
            shape(early, ROWS, LANES),
            *held_shapes(early),
            shape(early, ROWS, LANES),
            *held_shapes(early)[2:],
        ),
        in_specs=[vmem()] * (early + 1),
        out_specs=(vmem(),) * 8,
        compiler_params=limit(12),
        cost_estimate=cost(1 << 10, 1 << 10),
        name="early",
    )(*line[:early], edges)
    held, own_held = held[:4], held[4:]
    before, *second = pl.pallas_call(
        functools.partial(second_kernel, scale, outer, inner),
        out_shape=(shape(early + 1, ROWS, LANES), *held_shapes(1)),
        in_specs=[vmem()] * 6,
        out_specs=(vmem(),) * 5,
        compiler_params=limit(12),
        cost_estimate=cost(1 << 10, 1 << 10),
        name="second",
    )(line[early], before, *held)
    for_partner, last_moments, last_others = pl.pallas_call(
        functools.partial(late_kernel, scale, ways, outer, inner),
        out_shape=(
            sums_shape,
            shape(tiles, ROWS, LANES),
            jax.ShapeDtypeStruct(others_shape, bf16),
        ),
        in_specs=[vmem()] * 10,
        out_specs=(vmem(),) * 3,
        scratch_shapes=[
            pltpu.VMEM((outer, ROWS, LANES), f32),
            pltpu.VMEM((ways, ROWS, LANES), f32),
        ],
        compiler_params=limit(12),
        cost_estimate=cost(1 << 30, 1 << 10),
        name="late",
    )(line[-1], before, *held, *second)
    arrived = send(
        for_partner, pairs(lambda o, i, t: (o, inner - 1 - i, t ^ 1 if ways % 2 == 0 else t))
    )
    own_sum = pl.pallas_call(
        functools.partial(own_kernel, scale, ways, outer, inner),
        out_shape=sums_shape,
        in_specs=[vmem()] * (outer + 10),
        out_specs=vmem(),
        scratch_shapes=[
            pltpu.VMEM((2, *along_shape), f32),
            pltpu.VMEM((2, *terms_shape), bf16),
            pltpu.VMEM((outer, ROWS, LANES), f32),
            pltpu.VMEM((ways, ROWS, LANES), f32),
        ],
        compiler_params=limit(12),
        cost_estimate=cost(1 << 31, 1 << 10),
        name="own",
    )(
        *line, *own_held, *held[0:2], *second[0:2],
        last_moments, last_others, for_partner,
    )
    still, picks = pl.pallas_call(
        functools.partial(still_kernel, ways),
        out_shape=(
            shape(3, angles, LANES),
            shape(slots, LANES),
        ),
        in_specs=[vmem()] * (ways + 3),
        out_specs=(vmem(),) * 2,
        scratch_shapes=[
            pltpu.VMEM((ways, 5, ROWS, LANES), f32),
            pltpu.SMEM(source.shape, jnp.int32),
            pltpu.SemaphoreType.DMA,
        ],
        compiler_params=limit(8),
        name="still",
    )(*around, own, source, own_sum)
    partial_sum = pl.pallas_call(
        functools.partial(merge_kernel, rows),
        out_shape=shape(-(-(rows + blocks) // ROWS) * ROWS, LANES),
        in_specs=[vmem()] * 3,
        out_specs=vmem(),
        compiler_params=limit(4),
        name="merge",
    )(own_sum, arrived, picks)
    inner_cells, index = pl.pallas_call(
        functools.partial(prepare_kernel, ways, angles, blocks),
        out_shape=(
            shape(5, ROWS, total),
            jax.ShapeDtypeStruct((1, LANES), jnp.int32),
        ),
        in_specs=[vmem()] * (ways + 1),
        out_specs=(vmem(),) * 2,
        scratch_shapes=[pltpu.VMEM((ways, 5, ROWS, LANES), f32)],
        compiler_params=limit(8),
        name="prepare",
    )(*around, partial_sum)
    partials = [partial_sum] + [over_tgt(partial_sum, k) for k in steps[1:]]

    wall, grid, new_strength = pl.pallas_call(
        functools.partial(wall_kernel, ways),
        out_shape=(shape(3, planes, angles), shape(*vorticity.shape), shape(3, per_device)),
        in_specs=[vmem()] * (ways + 4),
        out_specs=(vmem(),) * 3,
        scratch_shapes=[
            pltpu.VMEM((3 * total + slots, LANES), f32),
            pltpu.VMEM((slots * ways + slots, LANES), f32),
            pltpu.VMEM((ways, ROWS, LANES), f32),
            pltpu.SMEM(index.shape, jnp.int32),
            pltpu.SemaphoreType.DMA,
        ],
        compiler_params=limit(16),
        name="wall",
    )(*partials, still, inner_cells, particle_strength, index)
    return (wall, grid, new_strength)


def solution(mesh):
    in_specs = (
        P(None, ("src", "tgt")),
        P(None, ("src", "tgt")),
        P(None, ("src", "tgt")),
        P(None, None, "tgt"),
        P("src", None, "tgt", None),
        P("src", "tgt", None),
        P("src", "tgt", None),
        P("src", "tgt", None),
        P("src", "tgt", None),
    )
    out_specs = (P(None, "src", "tgt"), P("src", None, "tgt", None), P(None, ("src", "tgt")))
    return jax.shard_map(
        on_device, mesh=mesh, in_specs=in_specs, out_specs=out_specs, check_vma=False
    )
```

```python
import functools
import math

import jax
import jax.numpy as jnp
from jax import lax
from jax.experimental import pallas as pl
from jax.experimental.pallas import tpu as pltpu
from jax.sharding import PartitionSpec as P

SUBSTEPS = 3
LANES = 128
ROWS = 8
TOGETHER = 2
TERMS = 48
UNROLLED = 4
swirl_gain = 0.2
f32 = jnp.float32
bf16 = jnp.bfloat16


def vmem():
    return pl.BlockSpec(memory_space=pltpu.VMEM)


def smem():
    return pl.BlockSpec(memory_space=pltpu.SMEM)


def hbm():
    return pl.BlockSpec(memory_space=pltpu.HBM)


def stay(*arrays):
    return [pltpu.with_memory_space_constraint(a, pltpu.HBM) for a in arrays]


def shape(*dims):
    return jax.ShapeDtypeStruct(dims, f32)


def limit(megabytes):
    return pltpu.CompilerParams(vmem_limit_bytes=megabytes << 20)


def cost(flops, size):
    return pl.CostEstimate(flops=flops, bytes_accessed=size, transcendentals=0)


def divisor(number, most):
    return max(c for c in range(1, min(number, most) + 1) if number % c == 0)


def power_of_two(number):
    return number & (number - 1) == 0


def partner(index, step, count):
    return index ^ step if power_of_two(count) else (index + step) % count


def source_of(index, step, count):
    return index ^ step if power_of_two(count) else (index - step) % count


def line_order(outer):
    return [0, *range(outer // 2, outer), *range(1, outer // 2)]


def tgt_order(ways):
    return [0, *range(ways // 2, ways), *range(1, ways // 2)]


def turn(step, ways):
    return {1: 2, 2: 3, 3: 1}.get(step % ways, step % ways)


def particles_kernel(inner, outer, *refs):
    given, messages = refs[:9], refs[9 : 9 + outer]
    own, lists, held, sems = refs[9 + outer], refs[10 + outer : 12 + outer], refs[12 + outer : -1], refs[-1]
    vort, swirl, diff = given[4:7]
    targets = (*held, *[own.at[c] for c in range(5)], *lists)
    sources = (*given[0:4], *[vort.at[0, m] for m in range(3)], swirl.at[0], diff.at[0], *given[7:9])
    copies = [
        pltpu.make_async_copy(a, b, sems.at[i]) for i, (a, b) in enumerate(zip(sources, targets))
    ]
    for copy in copies:
        copy.start()
    for copy in copies[0:4]:
        copy.wait()
    pos, strength, radius, points = held
    tiles = pos.shape[1] // LANES
    angles = points.shape[2]
    src = lax.axis_index("src")
    core = radius[...] * radius[...]
    parts = [slice(k * LANES, (k + 1) * LANES) for k in range(tiles)]
    bare = [
        jnp.concatenate(
            [pos[:, part], strength[:, part], core[:, part], jnp.zeros((1, LANES), f32)], axis=0
        )
        for part in parts
    ]
    last = lax.broadcasted_iota(jnp.int32, (ROWS, LANES), 0) == ROWS - 1
    for step, message in zip(line_order(outer), messages):
        there = partner(src // inner, step, outer) * inner
        planes = (there + src % inner, there + inner - 1 - src % inner)
        for k in range(tiles):
            if k < 3:
                both = [points[k, pl.ds(plane, 1), :] for plane in planes]
                both.append(jnp.zeros((1, LANES - 2 * angles), f32))
                both = [p for p in both if p.shape[1]]
                message[k] = jnp.where(last, jnp.concatenate(both, axis=1), bare[k])
            else:
                message[k] = bare[k]
    for copy in copies[4:]:
        copy.wait()


def edges_kernel(own, own_source, own_target, message):
    angles = own.shape[1]
    blocks = own_source.shape[2]
    total = angles * lax.axis_size("tgt")
    half = ROWS // 2
    for c in range(5):
        message[c, :, 0:angles] = jnp.transpose(own[c])[0:ROWS, :]
        message[c, :, angles:LANES] = jnp.zeros((ROWS, LANES - angles), f32)
        message[6 + c, 0:half, :] = own[c, 0:half]
        message[6 + c, half:ROWS, :] = own[c, angles - half : angles]
    message[5] = jnp.full((ROWS, LANES), -1.0, f32)
    q = own_source[0]
    row = (q // angles) * total + lax.axis_index("tgt") * angles + q % angles
    message[5, 0:1, 0:blocks] = row.astype(f32)
    message[5, 1:2, 0:blocks] = own_target[0].astype(f32)


def inner_step(field, local_swirl, local_diff, speed, first):
    total = field[0].shape[1]
    transport = 0.5 * (local_swirl + swirl_gain * field[2])
    renewed = []
    for m in range(3):
        center = field[m]
        eastern = pltpu.roll(center, total - 1, 1)
        western = pltpu.roll(center, 1, 1)
        outward = pltpu.roll(center, ROWS - 1, 0)
        inward = jnp.where(first, speed[m], pltpu.roll(center, 1, 0))
        renewed.append(
            center
            + local_diff * (eastern + western + outward + inward - 4.0 * center)
            - transport * (eastern - western)
        )
    return renewed


def still_kernel(ways, *refs):
    messages = refs[:ways]
    own, lists, after, grid, picks, placed, source, sem = refs[ways:]
    copy = pltpu.make_async_copy(lists, source, sem)
    copy.start()
    angles = own.shape[1]
    height = angles + ROWS
    blocks = lists.shape[2]
    me = lax.axis_index("tgt")
    for step, message in zip(tgt_order(ways), messages):
        placed[source_of(me, step, ways)] = message[6:11]

    upper = lax.broadcasted_iota(jnp.int32, (ROWS, LANES), 0) < ROWS // 2
    east = lax.rem(me + 1, ways)
    west = lax.rem(me + ways - 1, ways)
    cells = [
        jnp.concatenate(
            [own[c], jnp.where(upper, placed[east, c], placed[west, c])], axis=0
        )
        for c in range(5)
    ]
    field, local_swirl, local_diff = cells[0:3], cells[3], cells[4]
    lane = lax.broadcasted_iota(jnp.int32, (height, LANES), 1)
    for counter in range(SUBSTEPS):
        transport = 0.5 * (local_swirl + swirl_gain * field[2])
        renewed = []
        for m in range(3):
            center = field[m]
            eastern = pltpu.roll(center, height - 1, 0)
            western = pltpu.roll(center, 1, 0)
            outward = jnp.where(lane == LANES - 1, 0.0, pltpu.roll(center, LANES - 1, 1))
            inward = jnp.where(lane == 0, 0.0, pltpu.roll(center, 1, 1))
            renewed.append(
                center
                + local_diff * (eastern + western + outward + inward - 4.0 * center)
                - transport * (eastern - western)
            )
        field = renewed
    for m in range(3):
        grid[m] = field[m][0:angles]
    picks[...] = jnp.zeros(picks.shape, f32)
    copy.wait()
    for i in range(blocks):
        q = source[0, 0, i]
        picks[i : i + 1, :] = grid[q // angles, pl.ds(q % angles, 1), :]


def three_parts(value):
    high = value.astype(bf16).astype(f32)
    rest = value - high
    middle = rest.astype(bf16).astype(f32)
    return high, middle, rest - middle


def middle_of(outer, inner):
    here = (lax.axis_index("src") // inner).astype(f32)
    return 0.5, 0.5, (here + 0.5) * (1.0 / outer)


def point_terms(message, lane, angles, middle):
    x, y, z = [message[m, 7:8, lane : lane + angles] - middle[m] for m in range(3)]
    nothing = jnp.zeros((3, angles), f32)
    vector = jnp.concatenate(
        [-2.0 * x, -2.0 * y, -2.0 * z, jnp.ones_like(x), x * x + y * y + z * z, nothing], axis=0
    )
    high, middling, low = three_parts(vector)
    terms = jnp.transpose(jnp.concatenate([high, middling, low, high, middling, high], axis=0))
    return jnp.concatenate([x, y, z, nothing, nothing[0:2]], axis=0), terms.astype(bf16)


def tile_terms(message, middle, moments, others):
    one = jnp.ones((1, LANES), f32)
    nothing = jnp.zeros((3, LANES), f32)
    for k in range(message.shape[0]):
        px, py, pz = [message[k, r : r + 1, :] - middle[r] for r in range(3)]
        sx, sy, sz, cc = [message[k, r : r + 1, :] for r in range(3, 7)]
        moments[k] = jnp.concatenate(
            [sx, sy, sz, sy * pz - sz * py, sz * px - sx * pz, sx * py - sy * px, nothing[0:2]],
            axis=0,
        )
        vector = jnp.concatenate(
            [px, py, pz, px * px + py * py + (pz * pz + cc), one, nothing], axis=0
        )
        high, middling, low = three_parts(vector)
        others[:, k * LANES : (k + 1) * LANES] = jnp.concatenate(
            [high, high, high, middling, middling, low], axis=0
        ).astype(bf16)


def quarter(terms, blocks):
    tall = terms.shape[0]
    diagonal = lax.broadcasted_iota(jnp.int32, (ROWS, LANES), 1) - lax.broadcasted_iota(
        jnp.int32, (ROWS, LANES), 0
    )
    distances = [
        jnp.dot(terms, others[...], preferred_element_type=f32) for moments, others in blocks
    ]
    rows = [jnp.zeros((ROWS, LANES), f32)] * 6
    for start in range(0, tall // ROWS, TOGETHER):
        held = [jnp.zeros((ROWS, LANES), f32)] * (6 * TOGETHER)
        for distance, (moments, others) in zip(distances, blocks):
            for k in range(moments.shape[0]):
                summed = [moments[k, r : r + 1, :] for r in range(6)]
                for i in range(TOGETHER):
                    low = (start + i) * ROWS
                    inverse = lax.rsqrt(distance[low : low + ROWS, k * LANES : (k + 1) * LANES])
                    weight = inverse * inverse * inverse
                    for r in range(6):
                        held[6 * i + r] += weight * summed[r]
        for i in range(TOGETHER):
            mask = diagonal == (start + i) * ROWS
            for r in range(6):
                value = jnp.sum(held[6 * i + r], axis=1, keepdims=True)
                rows[r] = rows[r] + jnp.where(mask, value, 0.0)
    return rows


def repeat(count, body, carried):
    if count <= UNROLLED:
        for i in range(count):
            carried = body(i, carried)
        return carried
    return lax.fori_loop(0, count, body, carried)


def quarter_speed(scale, along, terms, blocks):
    if isinstance(blocks, list):
        rows = quarter(terms, blocks)
    else:
        moments, others = blocks
        count = others.shape[0]
        if count <= UNROLLED:
            rows = quarter(terms, [(moments.at[i], others.at[i]) for i in range(count)])
        else:

            def add(i, rows):
                more = quarter(terms, [(moments.at[i], others.at[i])])
                return tuple(a + b for a, b in zip(rows, more))

            rows = lax.fori_loop(0, count, add, (jnp.zeros((ROWS, LANES), f32),) * 6)
    angles = terms.shape[0]
    ax, ay, az, bx, by, bz = [jnp.sum(r, axis=0, keepdims=True) for r in rows]
    tx, ty, tz = [
        jnp.concatenate([along[m : m + 1, :], jnp.zeros((1, LANES - angles), f32)], axis=1)
        for m in range(3)
    ]
    return jnp.concatenate(
        [
            scale * (ay * tz - az * ty - bx),
            scale * (az * tx - ax * tz - by),
            scale * (ax * ty - ay * tx - bz),
            jnp.zeros((ROWS - 3, LANES), f32),
        ],
        axis=0,
    )


def place_quarters(outer, ways, angles, speeds, placed, result):
    per = LANES // angles
    me = lax.axis_index("tgt")
    for i, step in enumerate(line_order(outer)):
        if step < ways:
            placed[source_of(me, turn(step, ways), ways)] = speeds[i]
    result[...] = jnp.zeros(result.shape, f32)
    for k in range(ways // per):
        block = placed[k * per]
        for i in range(1, per):
            block = block + pltpu.roll(placed[k * per + i], i * angles, 1)
        result[3 * k : 3 * k + 3, :] = block[0:3]


def early_kernel(scale, outer, inner, count, *refs):
    messages, (after, speeds, moments, others, along, terms) = refs[:count], refs[count : count + 6]
    own_speeds, own_along, own_terms = refs[count + 6 :]
    middle = middle_of(outer, inner)
    angles = along.shape[2]
    for i, message in enumerate(messages):
        tile_terms(message, middle, moments.at[i], others.at[i])
        along[i], terms[i] = point_terms(message, angles, angles, middle)
        own_along[i], own_terms[i] = point_terms(message, 0, angles, middle)

    def one(i, unused):
        speeds[i] = quarter_speed(scale, along.at[i], terms[i], (moments, others))
        own_speeds[i] = quarter_speed(scale, own_along.at[i], own_terms[i], (moments, others))
        return unused

    repeat(count, one, 0)


def over_groups(scale, along, terms, groups, more):
    count = sum(others.shape[0] for moments, others, *rest in groups)
    if count <= UNROLLED:
        blocks = [
            (moments.at[i], others.at[i])
            for moments, others, *rest in groups
            for i in range(others.shape[0])
        ]
        return quarter_speed(scale, along, terms, blocks + more)
    total = quarter_speed(scale, along, terms, more)
    for moments, others, *rest in groups:
        total = total + quarter_speed(scale, along, terms, (moments, others))
    return total


def add_message(scale, middle, message, before, groups, moments, others, speeds):
    angles = groups[0][2].shape[2]
    tile_terms(message, middle, moments, others)
    along, terms = point_terms(message, angles, angles, middle)
    start = 0
    for there_moments, there_others, there_along, there_terms in groups:

        def one(i, unused, start=start, there_along=there_along, there_terms=there_terms):
            speeds[start + i] = before[start + i] + quarter_speed(
                scale, there_along.at[i], there_terms[i], [(moments, others)]
            )
            return unused

        repeat(there_others.shape[0], one, 0)
        start += there_others.shape[0]
    speeds[start] = over_groups(scale, along, terms, groups, [(moments, others)])
    return along, terms


def second_kernel(scale, outer, inner, *refs):
    message, before, *held, speeds, moments, others, along, terms = refs
    along[0], terms[0] = add_message(
        scale, middle_of(outer, inner), message, before, [held], moments.at[0], others.at[0], speeds
    )


def late_kernel(scale, ways, outer, inner, *refs):
    message, before = refs[:2]
    result, moments, others, speeds, placed = refs[10:]
    groups = [refs[2:6], refs[6:10]]
    add_message(scale, middle_of(outer, inner), message, before, groups, moments, others, speeds)
    place_quarters(outer, ways, groups[0][2].shape[2], speeds, placed, result)


def own_kernel(scale, ways, outer, inner, *refs):
    (*line, before, along, terms, moments, others, second_moments, second_others,
     last_moments, last_others, after, result, late_along, late_terms, speeds, placed) = refs
    second, last = (second_moments, second_others), [(last_moments, last_others)]
    middle = middle_of(outer, inner)
    angles = along.shape[2]
    early = before.shape[0]
    messages = line[early:]
    for i, message in enumerate(messages):
        late_along[i], late_terms[i] = point_terms(message, 0, angles, middle)

    def one(i, unused):
        speeds[i] = before[i] + over_groups(scale, along.at[i], terms[i], [second], last)
        return unused

    repeat(early, one, 0)
    for i in range(len(messages)):
        speeds[early + i] = over_groups(
            scale, late_along.at[i], late_terms[i], [(moments, others), second], last
        )
    place_quarters(outer, ways, angles, speeds, placed, result)


def prepare_kernel(ways, angles, blocks, *refs):
    messages = refs[:ways]
    after, inner_cells, index, placed = refs[ways:]
    me = lax.axis_index("tgt")
    for step, message in zip(tgt_order(ways), messages):
        placed[source_of(me, step, ways)] = message[0:5]

    cells = [
        jnp.concatenate([placed[t, c, :, 0:angles] for t in range(ways)], axis=1)
        for c in range(5)
    ]
    first = lax.broadcasted_iota(jnp.int32, cells[0].shape, 0) == 0
    for m, center in enumerate(inner_step(cells[0:3], cells[3], cells[4], [0.0] * 3, first)):
        inner_cells[m] = center
    inner_cells[3] = cells[3]
    inner_cells[4] = cells[4]

    shaped = (16 * ((blocks + 15) // 16), LANES)
    name = (me * blocks + lax.broadcasted_iota(jnp.int32, shaped, 0)).astype(f32)
    lane = lax.broadcasted_iota(jnp.int32, shaped, 1).astype(f32)
    row = jnp.full(shaped, -1.0, f32)
    slot = jnp.zeros(shaped, f32)
    for step, message in enumerate(messages):
        match = message[5, 1:2, :] == name
        row = jnp.maximum(row, jnp.where(match, message[5, 0:1, :], -1.0))
        slot = jnp.maximum(slot, jnp.where(match, lane + float(step * blocks), 0.0))
    row = jnp.max(row, axis=1, keepdims=True)
    slot = jnp.max(slot, axis=1, keepdims=True)
    block = lax.broadcasted_iota(jnp.int32, shaped, 0).astype(f32)
    kept = row < 0.0
    row = jnp.where(kept, float(3 * angles * ways) + block, row)
    slot = jnp.where(kept, float(ways * blocks) + block, slot)
    half = LANES // 2
    across = jnp.where(lane == block, row, 0.0) + jnp.where(lane == block + float(half), slot, 0.0)
    index[...] = jnp.sum(across, axis=0, keepdims=True).astype(jnp.int32)


def merge_kernel(rows, own, arrived, picks, result):
    result[...] = jnp.zeros(result.shape, f32)
    result[0:rows, :] = own[0:rows, :] + arrived[0:rows, :]
    result[rows : rows + picks.shape[0], :] = picks[...]


def wall_kernel(ways, *refs):
    partials = refs[:ways]
    (still, inner_cells, strength, index, wall, grid, new_strength,
     fixed, picked, halves, rows, sem) = refs[ways:]
    angles = grid.shape[2]
    total = angles * ways
    parts = total // LANES
    per = LANES // angles
    rows_of = 3 * parts
    pieces = strength.shape[1] // LANES
    slots = 3 * pieces
    me = lax.axis_index("tgt")
    copy = pltpu.make_async_copy(index, rows, sem)
    copy.start()
    places = [
        (b, b // pieces, slice((b % pieces) * LANES, (b % pieces + 1) * LANES))
        for b in range(3 * pieces)
    ]
    for step, partial in enumerate(partials):
        picked[step * slots : (step + 1) * slots, :] = partial[rows_of : rows_of + slots, :]
    for b, c, part in places:
        picked[ways * slots + b : ways * slots + b + 1, :] = strength[c : c + 1, part]
        fixed[3 * total + b : 3 * total + b + 1, :] = strength[c : c + 1, part]
    added = partials[0][0:rows_of, :]
    for partial in partials[1:]:
        added = added + partial[0:rows_of, :]
    speed = [
        jnp.concatenate([added[3 * k + m : 3 * k + m + 1] for k in range(parts)], axis=1)
        for m in range(3)
    ]
    for i in range(per):
        moved = added if i == 0 else pltpu.roll(added, LANES - i * angles, 1)
        for k in range(parts):
            halves[k * per + i, 0:3, :] = moved[3 * k : 3 * k + 3]
    for m in range(3):
        wall[m] = halves[me, m : m + 1, 0:angles]

    first = lax.broadcasted_iota(jnp.int32, (ROWS, total), 0) == 0
    local_swirl = inner_cells[3]
    local_diff = inner_cells[4]
    gain = jnp.where(first, local_diff, 0.0)
    field = [inner_cells[m] + gain * speed[m] for m in range(3)]
    for counter in range(1, SUBSTEPS):
        field = inner_step(field, local_swirl, local_diff, speed, first)
    stacked = jnp.concatenate(field + [jnp.zeros((LANES - 3 * ROWS, total), f32)], axis=0)
    for k in range(parts):
        turned = jnp.transpose(stacked[:, k * LANES : (k + 1) * LANES])
        for m in range(3):
            place = m * total + k * LANES
            fixed[place : place + LANES, :] = turned if m == 0 else pltpu.roll(
                turned, LANES - m * ROWS, 1
            )
    near = lax.broadcasted_iota(jnp.int32, (angles, LANES), 1) < SUBSTEPS
    for m in range(3):
        place = pl.multiple_of(m * total + me * angles, ROWS)
        grid[0, m] = jnp.where(near, fixed[pl.ds(place, angles), :], still[m])
    near = lax.broadcasted_iota(jnp.int32, (1, LANES), 1) < SUBSTEPS
    copy.wait()
    for b, c, part in places:
        new_strength[c : c + 1, part] = jnp.where(
            near, fixed[pl.ds(rows[0, b], 1), :], picked[pl.ds(rows[0, LANES // 2 + b], 1), :]
        )


def send(block, pairs):
    return lax.ppermute(block, ("src", "tgt"), pairs)


def on_device(
    particle_position,
    particle_strength,
    core_radius,
    boundary_points,
    vorticity,
    swirl,
    diffusivity,
    intersection_source,
    intersection_target,
):
    sources = lax.axis_size("src")
    ways = lax.axis_size("tgt")
    planes, comps, angles, radial = vorticity.shape
    per_device = particle_position.shape[1]
    tiles = per_device // LANES
    blocks = intersection_source.shape[2]
    inner = 2 if sources % 2 == 0 else 1
    outer = sources // inner
    total = angles * ways
    scale = 1.6 / (4.0 * math.pi * math.sqrt(per_device * ways * sources))

    def pairs(move):
        found = []
        for s in range(sources):
            for t in range(ways):
                o, i, u = move(s // inner, s % inner, t)
                found.append((s * ways + t, (o * inner + i) * ways + u))
        return found

    def over_tgt(block, step):
        return send(block, pairs(lambda o, i, t: (o, i, partner(t, step, ways))))

    given = (
        particle_position, particle_strength, core_radius, boundary_points,
        vorticity, swirl, diffusivity, intersection_source, intersection_target,
    )
    *messages, own, source, target = pl.pallas_call(
        functools.partial(particles_kernel, inner, outer),
        out_shape=(shape(tiles, ROWS, LANES),) * outer + (
            shape(5, angles, LANES),
            jax.ShapeDtypeStruct(intersection_source.shape, jnp.int32),
            jax.ShapeDtypeStruct(intersection_target.shape, jnp.int32),
        ),
        in_specs=[hbm()] * 9,
        out_specs=(vmem(),) * (outer + 3),
        scratch_shapes=[pltpu.VMEM(a.shape, f32) for a in given[0:4]]
        + [pltpu.SemaphoreType.DMA((11,))],
        compiler_params=limit(4),
        name="particles",
    )(*stay(*given))
    line = [messages[0]] + [
        send(
            message,
            pairs(lambda o, i, t: (partner(o, k, outer), i, partner(t, turn(k, ways), ways))),
        )
        for k, message in zip(line_order(outer)[1:], messages[1:])
    ]

    edges = pl.pallas_call(
        edges_kernel,
        out_shape=shape(11, ROWS, LANES),
        in_specs=[vmem()] * 3,
        out_specs=vmem(),
        compiler_params=limit(4),
        cost_estimate=cost(1 << 31, 1 << 10),
        name="edges",
    )(own, source, target)
    steps = tgt_order(ways)
    around = [edges] + [over_tgt(edges, k) for k in steps[1:]]

    rows = 3 * total // LANES
    slots = blocks
    sums_shape = shape(-(-rows // ROWS) * ROWS, LANES)
    along_shape = (ROWS, angles)
    terms_shape = (angles, TERMS)
    others_shape = (TERMS, per_device)
    early = outer - 2

    def held_shapes(count):
        return (
            shape(count, tiles, ROWS, LANES),
            jax.ShapeDtypeStruct((count, *others_shape), bf16),
            shape(count, *along_shape),
            jax.ShapeDtypeStruct((count, *terms_shape), bf16),
        )

    before, *held = pl.pallas_call(
        functools.partial(early_kernel, scale, outer, inner, early),
        out_shape=(
            shape(early, ROWS, LANES),
            *held_shapes(early),
            shape(early, ROWS, LANES),
            *held_shapes(early)[2:],
        ),
        in_specs=[vmem()] * (early + 1),
        out_specs=(vmem(),) * 8,
        compiler_params=limit(12),
        cost_estimate=cost(1 << 10, 1 << 10),
        name="early",
    )(*line[:early], edges)
    held, own_held = held[:4], held[4:]
    before, *second = pl.pallas_call(
        functools.partial(second_kernel, scale, outer, inner),
        out_shape=(shape(early + 1, ROWS, LANES), *held_shapes(1)),
        in_specs=[vmem()] * 6,
        out_specs=(vmem(),) * 5,
        compiler_params=limit(12),
        cost_estimate=cost(1 << 10, 1 << 10),
        name="second",
    )(line[early], before, *held)
    for_partner, last_moments, last_others = pl.pallas_call(
        functools.partial(late_kernel, scale, ways, outer, inner),
        out_shape=(
            sums_shape,
            shape(tiles, ROWS, LANES),
            jax.ShapeDtypeStruct(others_shape, bf16),
        ),
        in_specs=[vmem()] * 10,
        out_specs=(vmem(),) * 3,
        scratch_shapes=[
            pltpu.VMEM((outer, ROWS, LANES), f32),
            pltpu.VMEM((ways, ROWS, LANES), f32),
        ],
        compiler_params=limit(12),
        cost_estimate=cost(1 << 30, 1 << 10),
        name="late",
    )(line[-1], before, *held, *second)
    arrived = send(
        for_partner, pairs(lambda o, i, t: (o, inner - 1 - i, t ^ 1 if ways % 2 == 0 else t))
    )
    own_sum = pl.pallas_call(
        functools.partial(own_kernel, scale, ways, outer, inner),
        out_shape=sums_shape,
        in_specs=[vmem()] * (outer + 10),
        out_specs=vmem(),
        scratch_shapes=[
            pltpu.VMEM((2, *along_shape), f32),
            pltpu.VMEM((2, *terms_shape), bf16),
            pltpu.VMEM((outer, ROWS, LANES), f32),
            pltpu.VMEM((ways, ROWS, LANES), f32),
        ],
        compiler_params=limit(12),
        cost_estimate=cost(1 << 31, 1 << 10),
        name="own",
    )(
        *line, *own_held, *held[0:2], *second[0:2],
        last_moments, last_others, for_partner,
    )
    still, picks = pl.pallas_call(
        functools.partial(still_kernel, ways),
        out_shape=(
            shape(3, angles, LANES),
            shape(slots, LANES),
        ),
        in_specs=[vmem()] * (ways + 3),
        out_specs=(vmem(),) * 2,
        scratch_shapes=[
            pltpu.VMEM((ways, 5, ROWS, LANES), f32),
            pltpu.SMEM(source.shape, jnp.int32),
            pltpu.SemaphoreType.DMA,
        ],
        compiler_params=limit(8),
        name="still",
    )(*around, own, source, own_sum)
    partial_sum = pl.pallas_call(
        functools.partial(merge_kernel, rows),
        out_shape=shape(-(-(rows + blocks) // ROWS) * ROWS, LANES),
        in_specs=[vmem()] * 3,
        out_specs=vmem(),
        compiler_params=limit(4),
        name="merge",
    )(own_sum, arrived, picks)
    inner_cells, index = pl.pallas_call(
        functools.partial(prepare_kernel, ways, angles, blocks),
        out_shape=(
            shape(5, ROWS, total),
            jax.ShapeDtypeStruct((1, LANES), jnp.int32),
        ),
        in_specs=[vmem()] * (ways + 1),
        out_specs=(vmem(),) * 2,
        scratch_shapes=[pltpu.VMEM((ways, 5, ROWS, LANES), f32)],
        compiler_params=limit(8),
        name="prepare",
    )(*around, partial_sum)
    partials = [partial_sum] + [over_tgt(partial_sum, k) for k in steps[1:]]

    wall, grid, new_strength = pl.pallas_call(
        functools.partial(wall_kernel, ways),
        out_shape=(shape(3, planes, angles), shape(*vorticity.shape), shape(3, per_device)),
        in_specs=[vmem()] * (ways + 4),
        out_specs=(vmem(),) * 3,
        scratch_shapes=[
            pltpu.VMEM((3 * total + slots, LANES), f32),
            pltpu.VMEM((slots * ways + slots, LANES), f32),
            pltpu.VMEM((ways, ROWS, LANES), f32),
            pltpu.SMEM(index.shape, jnp.int32),
            pltpu.SemaphoreType.DMA,
        ],
        compiler_params=limit(16),
        name="wall",
    )(*partials, still, inner_cells, particle_strength, index)
    return (wall, grid, new_strength)


def solution(mesh):
    in_specs = (
        P(None, ("src", "tgt")),
        P(None, ("src", "tgt")),
        P(None, ("src", "tgt")),
        P(None, None, "tgt"),
        P("src", None, "tgt", None),
        P("src", "tgt", None),
        P("src", "tgt", None),
        P("src", "tgt", None),
        P("src", "tgt", None),
    )
    out_specs = (P(None, "src", "tgt"), P("src", None, "tgt", None), P(None, ("src", "tgt")))
    return jax.shard_map(
        on_device, mesh=mesh, in_specs=in_specs, out_specs=out_specs, check_vma=False
    )
```

```python
import functools
import math

import jax
import jax.numpy as jnp
from jax import lax
from jax.experimental import pallas as pl
from jax.experimental.pallas import tpu as pltpu
from jax.sharding import PartitionSpec as P

SUBSTEPS = 3
LANES = 128
ROWS = 8
TOGETHER = 4
TERMS = 48
UNROLLED = 4
swirl_gain = 0.2
f32 = jnp.float32
bf16 = jnp.bfloat16


def vmem():
    return pl.BlockSpec(memory_space=pltpu.VMEM)


def smem():
    return pl.BlockSpec(memory_space=pltpu.SMEM)


def hbm():
    return pl.BlockSpec(memory_space=pltpu.HBM)


def stay(*arrays):
    return [pltpu.with_memory_space_constraint(a, pltpu.HBM) for a in arrays]


def shape(*dims):
    return jax.ShapeDtypeStruct(dims, f32)


def limit(megabytes):
    return pltpu.CompilerParams(vmem_limit_bytes=megabytes << 20)


def cost(flops, size):
    return pl.CostEstimate(flops=flops, bytes_accessed=size, transcendentals=0)


def divisor(number, most):
    return max(c for c in range(1, min(number, most) + 1) if number % c == 0)


def power_of_two(number):
    return number & (number - 1) == 0


def partner(index, step, count):
    return index ^ step if power_of_two(count) else (index + step) % count


def source_of(index, step, count):
    return index ^ step if power_of_two(count) else (index - step) % count


def line_order(outer):
    return [0, *range(outer // 2, outer), *range(1, outer // 2)]


def tgt_order(ways):
    return [0, *range(ways // 2, ways), *range(1, ways // 2)]


def turn(step, ways):
    return {1: 3, 3: 1}.get(step % ways, step % ways)


def particles_kernel(inner, outer, *refs):
    given, messages = refs[:9], refs[9 : 9 + outer]
    own, lists, held, sems = refs[9 + outer], refs[10 + outer : 12 + outer], refs[12 + outer : -1], refs[-1]
    vort, swirl, diff = given[4:7]
    targets = (*held, *[own.at[c] for c in range(5)], *lists)
    sources = (*given[0:4], *[vort.at[0, m] for m in range(3)], swirl.at[0], diff.at[0], *given[7:9])
    copies = [
        pltpu.make_async_copy(a, b, sems.at[i]) for i, (a, b) in enumerate(zip(sources, targets))
    ]
    for copy in copies:
        copy.start()
    for copy in copies[0:4]:
        copy.wait()
    pos, strength, radius, points = held
    tiles = pos.shape[1] // LANES
    angles = points.shape[2]
    src = lax.axis_index("src")
    core = radius[...] * radius[...]
    parts = [slice(k * LANES, (k + 1) * LANES) for k in range(tiles)]
    bare = [
        jnp.concatenate(
            [pos[:, part], strength[:, part], core[:, part], jnp.zeros((1, LANES), f32)], axis=0
        )
        for part in parts
    ]
    last = lax.broadcasted_iota(jnp.int32, (ROWS, LANES), 0) == ROWS - 1
    for step, message in zip(line_order(outer), messages):
        there = partner(src // inner, step, outer) * inner
        planes = (there + src % inner, there + inner - 1 - src % inner)
        for k in range(tiles):
            if k < 3:
                both = [points[k, pl.ds(plane, 1), :] for plane in planes]
                both.append(jnp.zeros((1, LANES - 2 * angles), f32))
                both = [p for p in both if p.shape[1]]
                message[k] = jnp.where(last, jnp.concatenate(both, axis=1), bare[k])
            else:
                message[k] = bare[k]
    for copy in copies[4:]:
        copy.wait()


def edges_kernel(own, own_source, own_target, message):
    angles = own.shape[1]
    blocks = own_source.shape[2]
    total = angles * lax.axis_size("tgt")
    half = ROWS // 2
    for c in range(5):
        message[c, :, 0:angles] = jnp.transpose(own[c])[0:ROWS, :]
        message[c, :, angles:LANES] = jnp.zeros((ROWS, LANES - angles), f32)
        message[6 + c, 0:half, :] = own[c, 0:half]
        message[6 + c, half:ROWS, :] = own[c, angles - half : angles]
    message[5] = jnp.full((ROWS, LANES), -1.0, f32)
    q = own_source[0]
    row = (q // angles) * total + lax.axis_index("tgt") * angles + q % angles
    message[5, 0:1, 0:blocks] = row.astype(f32)
    message[5, 1:2, 0:blocks] = own_target[0].astype(f32)


def inner_step(field, local_swirl, local_diff, speed, first):
    total = field[0].shape[1]
    transport = 0.5 * (local_swirl + swirl_gain * field[2])
    renewed = []
    for m in range(3):
        center = field[m]
        eastern = pltpu.roll(center, total - 1, 1)
        western = pltpu.roll(center, 1, 1)
        outward = pltpu.roll(center, ROWS - 1, 0)
        inward = jnp.where(first, speed[m], pltpu.roll(center, 1, 0))
        renewed.append(
            center
            + local_diff * (eastern + western + outward + inward - 4.0 * center)
            - transport * (eastern - western)
        )
    return renewed


def still_kernel(ways, *refs):
    messages = refs[:ways]
    own, lists, after, grid, picks, placed, source, sem = refs[ways:]
    copy = pltpu.make_async_copy(lists, source, sem)
    copy.start()
    angles = own.shape[1]
    height = angles + ROWS
    blocks = lists.shape[2]
    me = lax.axis_index("tgt")
    for step, message in zip(tgt_order(ways), messages):
        placed[source_of(me, step, ways)] = message[6:11]

    upper = lax.broadcasted_iota(jnp.int32, (ROWS, LANES), 0) < ROWS // 2
    east = lax.rem(me + 1, ways)
    west = lax.rem(me + ways - 1, ways)
    cells = [
        jnp.concatenate(
            [own[c], jnp.where(upper, placed[east, c], placed[west, c])], axis=0
        )
        for c in range(5)
    ]
    field, local_swirl, local_diff = cells[0:3], cells[3], cells[4]
    lane = lax.broadcasted_iota(jnp.int32, (height, LANES), 1)
    for counter in range(SUBSTEPS):
        transport = 0.5 * (local_swirl + swirl_gain * field[2])
        renewed = []
        for m in range(3):
            center = field[m]
            eastern = pltpu.roll(center, height - 1, 0)
            western = pltpu.roll(center, 1, 0)
            outward = jnp.where(lane == LANES - 1, 0.0, pltpu.roll(center, LANES - 1, 1))
            inward = jnp.where(lane == 0, 0.0, pltpu.roll(center, 1, 1))
            renewed.append(
                center
                + local_diff * (eastern + western + outward + inward - 4.0 * center)
                - transport * (eastern - western)
            )
        field = renewed
    for m in range(3):
        grid[m] = field[m][0:angles]
    picks[...] = jnp.zeros(picks.shape, f32)
    copy.wait()
    for i in range(blocks):
        q = source[0, 0, i]
        picks[i : i + 1, :] = grid[q // angles, pl.ds(q % angles, 1), :]


def three_parts(value):
    high = value.astype(bf16).astype(f32)
    rest = value - high
    middle = rest.astype(bf16).astype(f32)
    return high, middle, rest - middle


def middle_of(outer, inner):
    here = (lax.axis_index("src") // inner).astype(f32)
    return 0.5, 0.5, (here + 0.5) * (1.0 / outer)


def point_terms(message, lane, angles, middle):
    x, y, z = [message[m, 7:8, lane : lane + angles] - middle[m] for m in range(3)]
    nothing = jnp.zeros((3, angles), f32)
    vector = jnp.concatenate(
        [-2.0 * x, -2.0 * y, -2.0 * z, jnp.ones_like(x), x * x + y * y + z * z, nothing], axis=0
    )
    high, middling, low = three_parts(vector)
    terms = jnp.transpose(jnp.concatenate([high, middling, low, high, middling, high], axis=0))
    return jnp.concatenate([x, y, z, nothing, nothing[0:2]], axis=0), terms.astype(bf16)


def tile_terms(message, middle, moments, others):
    one = jnp.ones((1, LANES), f32)
    nothing = jnp.zeros((3, LANES), f32)
    for k in range(message.shape[0]):
        px, py, pz = [message[k, r : r + 1, :] - middle[r] for r in range(3)]
        sx, sy, sz, cc = [message[k, r : r + 1, :] for r in range(3, 7)]
        moments[k] = jnp.concatenate(
            [sx, sy, sz, sy * pz - sz * py, sz * px - sx * pz, sx * py - sy * px, nothing[0:2]],
            axis=0,
        )
        vector = jnp.concatenate(
            [px, py, pz, px * px + py * py + (pz * pz + cc), one, nothing], axis=0
        )
        high, middling, low = three_parts(vector)
        others[:, k * LANES : (k + 1) * LANES] = jnp.concatenate(
            [high, high, high, middling, middling, low], axis=0
        ).astype(bf16)


def quarter(terms, blocks):
    tall = terms.shape[0]
    diagonal = lax.broadcasted_iota(jnp.int32, (ROWS, LANES), 1) - lax.broadcasted_iota(
        jnp.int32, (ROWS, LANES), 0
    )
    distances = [
        jnp.dot(terms, others[...], preferred_element_type=f32) for moments, others in blocks
    ]
    rows = [jnp.zeros((ROWS, LANES), f32)] * 6
    for start in range(0, tall // ROWS, TOGETHER):
        held = [jnp.zeros((ROWS, LANES), f32)] * (6 * TOGETHER)
        for distance, (moments, others) in zip(distances, blocks):
            for k in range(moments.shape[0]):
                summed = [moments[k, r : r + 1, :] for r in range(6)]
                for i in range(TOGETHER):
                    low = (start + i) * ROWS
                    inverse = lax.rsqrt(distance[low : low + ROWS, k * LANES : (k + 1) * LANES])
                    weight = inverse * inverse * inverse
                    for r in range(6):
                        held[6 * i + r] += weight * summed[r]
        for i in range(TOGETHER):
            mask = diagonal == (start + i) * ROWS
            for r in range(6):
                value = jnp.sum(held[6 * i + r], axis=1, keepdims=True)
                rows[r] = rows[r] + jnp.where(mask, value, 0.0)
    return rows


def repeat(count, body, carried):
    if count <= UNROLLED:
        for i in range(count):
            carried = body(i, carried)
        return carried
    return lax.fori_loop(0, count, body, carried)


def quarter_speed(scale, along, terms, blocks):
    if isinstance(blocks, list):
        rows = quarter(terms, blocks)
    else:
        moments, others = blocks
        count = others.shape[0]
        if count <= UNROLLED:
            rows = quarter(terms, [(moments.at[i], others.at[i]) for i in range(count)])
        else:

            def add(i, rows):
                more = quarter(terms, [(moments.at[i], others.at[i])])
                return tuple(a + b for a, b in zip(rows, more))

            rows = lax.fori_loop(0, count, add, (jnp.zeros((ROWS, LANES), f32),) * 6)
    angles = terms.shape[0]
    ax, ay, az, bx, by, bz = [jnp.sum(r, axis=0, keepdims=True) for r in rows]
    tx, ty, tz = [
        jnp.concatenate([along[m : m + 1, :], jnp.zeros((1, LANES - angles), f32)], axis=1)
        for m in range(3)
    ]
    return jnp.concatenate(
        [
            scale * (ay * tz - az * ty - bx),
            scale * (az * tx - ax * tz - by),
            scale * (ax * ty - ay * tx - bz),
            jnp.zeros((ROWS - 3, LANES), f32),
        ],
        axis=0,
    )


def place_quarters(outer, ways, angles, speeds, placed, result):
    per = LANES // angles
    me = lax.axis_index("tgt")
    for i, step in enumerate(line_order(outer)):
        if step < ways:
            placed[source_of(me, turn(step, ways), ways)] = speeds[i]
    result[...] = jnp.zeros(result.shape, f32)
    for k in range(ways // per):
        block = placed[k * per]
        for i in range(1, per):
            block = block + pltpu.roll(placed[k * per + i], i * angles, 1)
        result[3 * k : 3 * k + 3, :] = block[0:3]


def early_kernel(scale, outer, inner, count, *refs):
    messages, (after, speeds, moments, others, along, terms) = refs[:count], refs[count : count + 6]
    own_speeds, own_along, own_terms = refs[count + 6 :]
    middle = middle_of(outer, inner)
    angles = along.shape[2]
    for i, message in enumerate(messages):
        tile_terms(message, middle, moments.at[i], others.at[i])
        along[i], terms[i] = point_terms(message, angles, angles, middle)
        own_along[i], own_terms[i] = point_terms(message, 0, angles, middle)

    def one(i, unused):
        speeds[i] = quarter_speed(scale, along.at[i], terms[i], (moments, others))
        own_speeds[i] = quarter_speed(scale, own_along.at[i], own_terms[i], (moments, others))
        return unused

    repeat(count, one, 0)


def over_groups(scale, along, terms, groups, more):
    count = sum(others.shape[0] for moments, others, *rest in groups)
    if count <= UNROLLED:
        blocks = [
            (moments.at[i], others.at[i])
            for moments, others, *rest in groups
            for i in range(others.shape[0])
        ]
        return quarter_speed(scale, along, terms, blocks + more)
    total = quarter_speed(scale, along, terms, more)
    for moments, others, *rest in groups:
        total = total + quarter_speed(scale, along, terms, (moments, others))
    return total


def add_message(scale, middle, message, before, groups, moments, others, speeds):
    angles = groups[0][2].shape[2]
    tile_terms(message, middle, moments, others)
    along, terms = point_terms(message, angles, angles, middle)
    start = 0
    for there_moments, there_others, there_along, there_terms in groups:

        def one(i, unused, start=start, there_along=there_along, there_terms=there_terms):
            speeds[start + i] = before[start + i] + quarter_speed(
                scale, there_along.at[i], there_terms[i], [(moments, others)]
            )
            return unused

        repeat(there_others.shape[0], one, 0)
        start += there_others.shape[0]
    speeds[start] = over_groups(scale, along, terms, groups, [(moments, others)])
    return along, terms


def second_kernel(scale, outer, inner, *refs):
    message, before, *held, speeds, moments, others, along, terms = refs
    along[0], terms[0] = add_message(
        scale, middle_of(outer, inner), message, before, [held], moments.at[0], others.at[0], speeds
    )


def late_kernel(scale, ways, outer, inner, *refs):
    message, before = refs[:2]
    result, moments, others, speeds, placed = refs[10:]
    groups = [refs[2:6], refs[6:10]]
    add_message(scale, middle_of(outer, inner), message, before, groups, moments, others, speeds)
    place_quarters(outer, ways, groups[0][2].shape[2], speeds, placed, result)


def own_kernel(scale, ways, outer, inner, *refs):
    (*line, before, along, terms, moments, others, second_moments, second_others,
     last_moments, last_others, after, result, late_along, late_terms, speeds, placed) = refs
    second, last = (second_moments, second_others), [(last_moments, last_others)]
    middle = middle_of(outer, inner)
    angles = along.shape[2]
    early = before.shape[0]
    messages = line[early:]
    for i, message in enumerate(messages):
        late_along[i], late_terms[i] = point_terms(message, 0, angles, middle)

    def one(i, unused):
        speeds[i] = before[i] + over_groups(scale, along.at[i], terms[i], [second], last)
        return unused

    repeat(early, one, 0)
    for i in range(len(messages)):
        speeds[early + i] = over_groups(
            scale, late_along.at[i], late_terms[i], [(moments, others), second], last
        )
    place_quarters(outer, ways, angles, speeds, placed, result)


def prepare_kernel(ways, angles, blocks, *refs):
    messages = refs[:ways]
    after, inner_cells, index, placed = refs[ways:]
    me = lax.axis_index("tgt")
    for step, message in zip(tgt_order(ways), messages):
        placed[source_of(me, step, ways)] = message[0:5]

    cells = [
        jnp.concatenate([placed[t, c, :, 0:angles] for t in range(ways)], axis=1)
        for c in range(5)
    ]
    first = lax.broadcasted_iota(jnp.int32, cells[0].shape, 0) == 0
    for m, center in enumerate(inner_step(cells[0:3], cells[3], cells[4], [0.0] * 3, first)):
        inner_cells[m] = center
    inner_cells[3] = cells[3]
    inner_cells[4] = cells[4]

    shaped = (16 * ((blocks + 15) // 16), LANES)
    name = (me * blocks + lax.broadcasted_iota(jnp.int32, shaped, 0)).astype(f32)
    lane = lax.broadcasted_iota(jnp.int32, shaped, 1).astype(f32)
    row = jnp.full(shaped, -1.0, f32)
    slot = jnp.zeros(shaped, f32)
    for step, message in enumerate(messages):
        match = message[5, 1:2, :] == name
        row = jnp.maximum(row, jnp.where(match, message[5, 0:1, :], -1.0))
        slot = jnp.maximum(slot, jnp.where(match, lane + float(step * blocks), 0.0))
    row = jnp.max(row, axis=1, keepdims=True)
    slot = jnp.max(slot, axis=1, keepdims=True)
    block = lax.broadcasted_iota(jnp.int32, shaped, 0).astype(f32)
    kept = row < 0.0
    row = jnp.where(kept, float(3 * angles * ways) + block, row)
    slot = jnp.where(kept, float(ways * blocks) + block, slot)
    half = LANES // 2
    across = jnp.where(lane == block, row, 0.0) + jnp.where(lane == block + float(half), slot, 0.0)
    index[...] = jnp.sum(across, axis=0, keepdims=True).astype(jnp.int32)


def merge_kernel(rows, own, arrived, picks, result):
    result[...] = jnp.zeros(result.shape, f32)
    result[0:rows, :] = own[0:rows, :] + arrived[0:rows, :]
    result[rows : rows + picks.shape[0], :] = picks[...]


def wall_kernel(ways, *refs):
    partials = refs[:ways]
    (still, inner_cells, strength, index, wall, grid, new_strength,
     fixed, picked, halves, rows, sem) = refs[ways:]
    angles = grid.shape[2]
    total = angles * ways
    parts = total // LANES
    per = LANES // angles
    rows_of = 3 * parts
    pieces = strength.shape[1] // LANES
    slots = 3 * pieces
    me = lax.axis_index("tgt")
    copy = pltpu.make_async_copy(index, rows, sem)
    copy.start()
    places = [
        (b, b // pieces, slice((b % pieces) * LANES, (b % pieces + 1) * LANES))
        for b in range(3 * pieces)
    ]
    for step, partial in enumerate(partials):
        picked[step * slots : (step + 1) * slots, :] = partial[rows_of : rows_of + slots, :]
    for b, c, part in places:
        picked[ways * slots + b : ways * slots + b + 1, :] = strength[c : c + 1, part]
        fixed[3 * total + b : 3 * total + b + 1, :] = strength[c : c + 1, part]
    added = partials[0][0:rows_of, :]
    for partial in partials[1:]:
        added = added + partial[0:rows_of, :]
    speed = [
        jnp.concatenate([added[3 * k + m : 3 * k + m + 1] for k in range(parts)], axis=1)
        for m in range(3)
    ]
    for i in range(per):
        moved = added if i == 0 else pltpu.roll(added, LANES - i * angles, 1)
        for k in range(parts):
            halves[k * per + i, 0:3, :] = moved[3 * k : 3 * k + 3]
    for m in range(3):
        wall[m] = halves[me, m : m + 1, 0:angles]

    first = lax.broadcasted_iota(jnp.int32, (ROWS, total), 0) == 0
    local_swirl = inner_cells[3]
    local_diff = inner_cells[4]
    gain = jnp.where(first, local_diff, 0.0)
    field = [inner_cells[m] + gain * speed[m] for m in range(3)]
    for counter in range(1, SUBSTEPS):
        field = inner_step(field, local_swirl, local_diff, speed, first)
    stacked = jnp.concatenate(field + [jnp.zeros((LANES - 3 * ROWS, total), f32)], axis=0)
    for k in range(parts):
        turned = jnp.transpose(stacked[:, k * LANES : (k + 1) * LANES])
        for m in range(3):
            place = m * total + k * LANES
            fixed[place : place + LANES, :] = turned if m == 0 else pltpu.roll(
                turned, LANES - m * ROWS, 1
            )
    near = lax.broadcasted_iota(jnp.int32, (angles, LANES), 1) < SUBSTEPS
    for m in range(3):
        place = pl.multiple_of(m * total + me * angles, ROWS)
        grid[0, m] = jnp.where(near, fixed[pl.ds(place, angles), :], still[m])
    near = lax.broadcasted_iota(jnp.int32, (1, LANES), 1) < SUBSTEPS
    copy.wait()
    for b, c, part in places:
        new_strength[c : c + 1, part] = jnp.where(
            near, fixed[pl.ds(rows[0, b], 1), :], picked[pl.ds(rows[0, LANES // 2 + b], 1), :]
        )


def send(block, pairs):
    return lax.ppermute(block, ("src", "tgt"), pairs)


def on_device(
    particle_position,
    particle_strength,
    core_radius,
    boundary_points,
    vorticity,
    swirl,
    diffusivity,
    intersection_source,
    intersection_target,
):
    sources = lax.axis_size("src")
    ways = lax.axis_size("tgt")
    planes, comps, angles, radial = vorticity.shape
    per_device = particle_position.shape[1]
    tiles = per_device // LANES
    blocks = intersection_source.shape[2]
    inner = 2 if sources % 2 == 0 else 1
    outer = sources // inner
    total = angles * ways
    scale = 1.6 / (4.0 * math.pi * math.sqrt(per_device * ways * sources))

    def pairs(move):
        found = []
        for s in range(sources):
            for t in range(ways):
                o, i, u = move(s // inner, s % inner, t)
                found.append((s * ways + t, (o * inner + i) * ways + u))
        return found

    def over_tgt(block, step):
        return send(block, pairs(lambda o, i, t: (o, i, partner(t, step, ways))))

    given = (
        particle_position, particle_strength, core_radius, boundary_points,
        vorticity, swirl, diffusivity, intersection_source, intersection_target,
    )
    *messages, own, source, target = pl.pallas_call(
        functools.partial(particles_kernel, inner, outer),
        out_shape=(shape(tiles, ROWS, LANES),) * outer + (
            shape(5, angles, LANES),
            jax.ShapeDtypeStruct(intersection_source.shape, jnp.int32),
            jax.ShapeDtypeStruct(intersection_target.shape, jnp.int32),
        ),
        in_specs=[hbm()] * 9,
        out_specs=(vmem(),) * (outer + 3),
        scratch_shapes=[pltpu.VMEM(a.shape, f32) for a in given[0:4]]
        + [pltpu.SemaphoreType.DMA((11,))],
        compiler_params=limit(4),
        name="particles",
    )(*stay(*given))
    line = [messages[0]] + [
        send(
            message,
            pairs(lambda o, i, t: (partner(o, k, outer), i, partner(t, turn(k, ways), ways))),
        )
        for k, message in zip(line_order(outer)[1:], messages[1:])
    ]

    edges = pl.pallas_call(
        edges_kernel,
        out_shape=shape(11, ROWS, LANES),
        in_specs=[vmem()] * 3,
        out_specs=vmem(),
        compiler_params=limit(4),
        cost_estimate=cost(1 << 31, 1 << 10),
        name="edges",
    )(own, source, target)
    steps = tgt_order(ways)
    around = [edges] + [over_tgt(edges, k) for k in steps[1:]]

    rows = 3 * total // LANES
    slots = blocks
    sums_shape = shape(-(-rows // ROWS) * ROWS, LANES)
    along_shape = (ROWS, angles)
    terms_shape = (angles, TERMS)
    others_shape = (TERMS, per_device)
    early = outer - 2

    def held_shapes(count):
        return (
            shape(count, tiles, ROWS, LANES),
            jax.ShapeDtypeStruct((count, *others_shape), bf16),
            shape(count, *along_shape),
            jax.ShapeDtypeStruct((count, *terms_shape), bf16),
        )

    before, *held = pl.pallas_call(
        functools.partial(early_kernel, scale, outer, inner, early),
        out_shape=(
            shape(early, ROWS, LANES),
            *held_shapes(early),
            shape(early, ROWS, LANES),
            *held_shapes(early)[2:],
        ),
        in_specs=[vmem()] * (early + 1),
        out_specs=(vmem(),) * 8,
        compiler_params=limit(12),
        cost_estimate=cost(1 << 10, 1 << 10),
        name="early",
    )(*line[:early], edges)
    held, own_held = held[:4], held[4:]
    before, *second = pl.pallas_call(
        functools.partial(second_kernel, scale, outer, inner),
        out_shape=(shape(early + 1, ROWS, LANES), *held_shapes(1)),
        in_specs=[vmem()] * 6,
        out_specs=(vmem(),) * 5,
        compiler_params=limit(12),
        cost_estimate=cost(1 << 10, 1 << 10),
        name="second",
    )(line[early], before, *held)
    for_partner, last_moments, last_others = pl.pallas_call(
        functools.partial(late_kernel, scale, ways, outer, inner),
        out_shape=(
            sums_shape,
            shape(tiles, ROWS, LANES),
            jax.ShapeDtypeStruct(others_shape, bf16),
        ),
        in_specs=[vmem()] * 10,
        out_specs=(vmem(),) * 3,
        scratch_shapes=[
            pltpu.VMEM((outer, ROWS, LANES), f32),
            pltpu.VMEM((ways, ROWS, LANES), f32),
        ],
        compiler_params=limit(12),
        cost_estimate=cost(1 << 30, 1 << 10),
        name="late",
    )(line[-1], before, *held, *second)
    arrived = send(
        for_partner, pairs(lambda o, i, t: (o, inner - 1 - i, t ^ 1 if ways % 2 == 0 else t))
    )
    own_sum = pl.pallas_call(
        functools.partial(own_kernel, scale, ways, outer, inner),
        out_shape=sums_shape,
        in_specs=[vmem()] * (outer + 10),
        out_specs=vmem(),
        scratch_shapes=[
            pltpu.VMEM((2, *along_shape), f32),
            pltpu.VMEM((2, *terms_shape), bf16),
            pltpu.VMEM((outer, ROWS, LANES), f32),
            pltpu.VMEM((ways, ROWS, LANES), f32),
        ],
        compiler_params=limit(12),
        cost_estimate=cost(1 << 31, 1 << 10),
        name="own",
    )(
        *line, *own_held, *held[0:2], *second[0:2],
        last_moments, last_others, for_partner,
    )
    still, picks = pl.pallas_call(
        functools.partial(still_kernel, ways),
        out_shape=(
            shape(3, angles, LANES),
            shape(slots, LANES),
        ),
        in_specs=[vmem()] * (ways + 3),
        out_specs=(vmem(),) * 2,
        scratch_shapes=[
            pltpu.VMEM((ways, 5, ROWS, LANES), f32),
            pltpu.SMEM(source.shape, jnp.int32),
            pltpu.SemaphoreType.DMA,
        ],
        compiler_params=limit(8),
        name="still",
    )(*around, own, source, own_sum)
    partial_sum = pl.pallas_call(
        functools.partial(merge_kernel, rows),
        out_shape=shape(-(-(rows + blocks) // ROWS) * ROWS, LANES),
        in_specs=[vmem()] * 3,
        out_specs=vmem(),
        compiler_params=limit(4),
        name="merge",
    )(own_sum, arrived, picks)
    inner_cells, index = pl.pallas_call(
        functools.partial(prepare_kernel, ways, angles, blocks),
        out_shape=(
            shape(5, ROWS, total),
            jax.ShapeDtypeStruct((1, LANES), jnp.int32),
        ),
        in_specs=[vmem()] * (ways + 1),
        out_specs=(vmem(),) * 2,
        scratch_shapes=[pltpu.VMEM((ways, 5, ROWS, LANES), f32)],
        compiler_params=limit(8),
        name="prepare",
    )(*around, partial_sum)
    partials = [partial_sum] + [over_tgt(partial_sum, k) for k in steps[1:]]

    wall, grid, new_strength = pl.pallas_call(
        functools.partial(wall_kernel, ways),
        out_shape=(shape(3, planes, angles), shape(*vorticity.shape), shape(3, per_device)),
        in_specs=[vmem()] * (ways + 4),
        out_specs=(vmem(),) * 3,
        scratch_shapes=[
            pltpu.VMEM((3 * total + slots, LANES), f32),
            pltpu.VMEM((slots * ways + slots, LANES), f32),
            pltpu.VMEM((ways, ROWS, LANES), f32),
            pltpu.SMEM(index.shape, jnp.int32),
            pltpu.SemaphoreType.DMA,
        ],
        compiler_params=limit(16),
        name="wall",
    )(*partials, still, inner_cells, particle_strength, index)
    return (wall, grid, new_strength)


def solution(mesh):
    in_specs = (
        P(None, ("src", "tgt")),
        P(None, ("src", "tgt")),
        P(None, ("src", "tgt")),
        P(None, None, "tgt"),
        P("src", None, "tgt", None),
        P("src", "tgt", None),
        P("src", "tgt", None),
        P("src", "tgt", None),
        P("src", "tgt", None),
    )
    out_specs = (P(None, "src", "tgt"), P("src", None, "tgt", None), P(None, ("src", "tgt")))
    return jax.shard_map(
        on_device, mesh=mesh, in_specs=in_specs, out_specs=out_specs, check_vma=False
    )
```
